32 devices in a mesh: groups: 2 (over x), seq: 16 (over z, y, core).
Axes of the slice: x: 2, y: 2, z: 4, core: 2. Of those that a mesh axis runs over, the one named last changes fastest.
Arguments:
- hidden: bfloat16 [4, 2560, 8192], P('groups', 'seq'), parts along dimension 0, may hold values from -6 to 6
- key_weight: bfloat16 [8192, 512], P('seq'), may hold values from -0.0625 to 0.0625
- value_weight: bfloat16 [8192, 512], P('seq'), may hold values from -0.0625 to 0.0625
- lengths: int32 [4], P('groups'), parts along dimension 0, may hold values from 320 to 2560, as said below
- owner: int32 [16], P('groups'), parts along dimension 0, may hold values from 0 to 7, each once
- dec_query: bfloat16 [16, 4, 1024], P('groups'), parts along dimension 0, may hold values from -124 to 124
- dec_key: bfloat16 [16, 4, 128], P('groups'), parts along dimension 0, may hold values from -4 to 4
- dec_value: bfloat16 [16, 4, 128], P('groups'), parts along dimension 0, may hold values from -6 to 6
Outputs:
- cache_out: bfloat16 [32, 1280, 256], P(('groups', 'seq')), parts along dimension 0
- attended: bfloat16 [8, 8192], P('groups', 'seq'), parts along dimension 0
The draws below stay inside these ranges and needn't reach their ends.
There are 2 independent parts, one for each index of `groups`. The reference program is written for one: setup_inputs(seed, part) draws one part's arguments, and reference() takes and returns one part's arrays. A program takes and returns all parts, laid end to end along the dimension named above; an argument that names none is the same for every part. Nothing has to cross between parts.
Inputs may be any that keep to these rules, and one draw needn't show every extreme that they name: `lengths`: one request's length is exactly 2560. Each decode owner serves exactly one pair of request and key-value head.
All inputs are finite; a program needn't handle non-finite values.
Results may differ from the reference program's by a relative error of at most 0.0079.
Values may be sent and summed in bfloat16 or wider, within the bound.
No kernel may reach another device: no remote copies, remote signals or barrier semaphores. Data moves between devices by JAX's collectives and lax.ppermute only.
A program may use at most 128 MiB of HBM per device.

```python
import jax
import jax.numpy as jnp
from jax import lax

MODEL_WIDTH = 8192
HEAD_SIZE = 128
KEY_VALUE_HEADS = 4
QPK = 8
STEPS = 4
REQ = 2
PROMPT_SLOTS = 2560
DECODERS = 8
SPLIT = 2


def shared_keys(key):
    return jnp.clip(jax.random.normal(key, (DECODERS, STEPS, HEAD_SIZE), jnp.float32), -4.0, 4.0)


def draw_lengths(key, part):
    key = jax.random.fold_in(key, 5)
    pick_key, rest_key = jax.random.split(key, 2)
    longest = jax.random.randint(pick_key, (), 0, REQ)
    others = jax.random.randint(rest_key, (REQ,), PROMPT_SLOTS // 8, PROMPT_SLOTS + 1)
    return jnp.where(jnp.arange(REQ) == longest, PROMPT_SLOTS, others).astype(jnp.int32)


def draw_dec_key(key, part):
    base = shared_keys(key)
    return base.astype(jnp.bfloat16)


def draw_dec_query(key, part):
    key = jax.random.fold_in(key, 9)
    noise_key = jax.random.fold_in(key, 0)
    noise = jnp.clip(jax.random.normal(noise_key, (DECODERS, STEPS, QPK, HEAD_SIZE), jnp.float32), -4.0, 4.0)
    values_out = noise
    return values_out.reshape(DECODERS, STEPS, QPK * HEAD_SIZE).astype(jnp.bfloat16)


def levels(key, dims, pieces, least, largest):
    gain, own = 1.0, jax.random.fold_in(key, 6)
    for position, blocks in pieces:
        draws = jnp.exp(jax.random.uniform(jax.random.fold_in(own, position), (blocks,), jnp.float32, least / len(pieces), largest / len(pieces)))
        gain = gain * jnp.repeat(draws, dims[position] // blocks).reshape([-1 if axis == position else 1 for axis in range(len(dims))])
    return gain


def gaussian(stream_key, dims, width, bound, shards=(), held_as=jnp.bfloat16):
    loudness = levels(stream_key, dims, shards, -0.22, 0.18) if shards else 1.0
    values = jax.random.normal(stream_key, dims, jnp.float32) * width * loudness
    return jnp.minimum(jnp.maximum(values, -bound), bound).astype(held_as)


def setup_inputs(seed: int = 0, part: int = 0) -> dict:
    seeds = jax.random.split(jax.random.key(seed), 9)
    own_keys = jax.random.split(jax.random.fold_in(seeds[8], part), 9)
    return {
        "hidden": gaussian(own_keys[0], (REQ, PROMPT_SLOTS, MODEL_WIDTH), 1.0, 6.0, ((1, 16),)),
        "key_weight": gaussian(seeds[1], (MODEL_WIDTH, KEY_VALUE_HEADS * HEAD_SIZE), MODEL_WIDTH ** -0.5, 0.0625, ((0, 16),)),
        "value_weight": gaussian(seeds[2], (MODEL_WIDTH, KEY_VALUE_HEADS * HEAD_SIZE), MODEL_WIDTH ** -0.5, 0.0625, ((0, 16),)),
        "lengths": draw_lengths(jax.random.fold_in(jax.random.fold_in(seeds[8], part), 71), part),
        "owner": jax.random.permutation(own_keys[4], DECODERS).astype(jnp.int32),
        "dec_query": draw_dec_query(jax.random.fold_in(jax.random.fold_in(seeds[8], part), 71), part),
        "dec_key": draw_dec_key(jax.random.fold_in(jax.random.fold_in(seeds[8], part), 71), part),
        "dec_value": gaussian(own_keys[7], (DECODERS, STEPS, HEAD_SIZE), 1.0, 6.0),
    }


ROPE_BASE = 500000.0

def rope_table(positions, head_dim):
    freq = ROPE_BASE ** (-(jnp.arange(head_dim // 2, dtype=jnp.float32) * 2.0) / head_dim)
    angle = positions.astype(jnp.float32)[:, None] * freq[None, :]
    return (jnp.cos(angle), jnp.sin(angle))

def rotate(values_in, cosine, sine_part):
    half_dim = values_in.shape[-1] // 2
    lower_half = values_in[..., :half_dim]
    upper_half = values_in[..., half_dim:]
    return jnp.concatenate([lower_half * cosine - upper_half * sine_part, upper_half * cosine + lower_half * sine_part], -1)

def decode_one(cache_rows, length, query, new_key, new_value):
    step_pos = length + jnp.arange(STEPS, dtype=jnp.int32)
    cosine, sine_part = rope_table(step_pos, HEAD_SIZE)
    query_rot = rotate(query.astype(jnp.float32).reshape(STEPS, QPK, HEAD_SIZE), cosine[:, None, :], sine_part[:, None, :]).astype(jnp.bfloat16)
    new_keys = rotate(new_key.astype(jnp.float32), cosine, sine_part).astype(jnp.bfloat16)
    key_part = cache_rows[:, :HEAD_SIZE]
    value_part = cache_rows[:, HEAD_SIZE:]
    score_scale = 1.0 / HEAD_SIZE ** 0.5
    old_scores = jnp.einsum('sjd,id->sji', query_rot.astype(jnp.float32), key_part.astype(jnp.float32)) * score_scale
    new_scores = jnp.einsum('sjd,td->sjt', query_rot.astype(jnp.float32), new_keys.astype(jnp.float32)) * score_scale
    old_live = jnp.arange(PROMPT_SLOTS, dtype=jnp.int32) < length
    new_live = jnp.arange(STEPS)[None, :] <= jnp.arange(STEPS)[:, None]
    old_scores = jnp.where(old_live[None, None, :], old_scores, -1e+30)
    new_scores = jnp.where(new_live[:, None, :], new_scores, -1e+30)
    row_max = jnp.maximum(lax.optimization_barrier(jnp.max(old_scores, -1)), lax.optimization_barrier(jnp.max(new_scores, -1)))[..., None]
    old_exp = jnp.exp(old_scores - row_max)
    new_exp = jnp.exp(new_scores - row_max)
    denom = lax.optimization_barrier(jnp.sum(old_exp, -1, keepdims=True)) + lax.optimization_barrier(jnp.sum(new_exp, -1, keepdims=True))
    old_probs = (old_exp / denom).astype(jnp.bfloat16)
    new_probs = (new_exp / denom).astype(jnp.bfloat16)
    result = jnp.einsum('sji,id->sjd', old_probs.astype(jnp.float32), value_part.astype(jnp.float32))
    result = result + jnp.einsum('sjt,td->sjd', new_probs.astype(jnp.float32), new_value.astype(jnp.float32))
    return result.reshape(STEPS, QPK * HEAD_SIZE).astype(jnp.bfloat16)

def reference(hidden, key_weight, value_weight, lengths, owner, dec_query, dec_key, dec_value):
    cosine, sine_part = rope_table(jnp.arange(PROMPT_SLOTS, dtype=jnp.int32), HEAD_SIZE)

    def project(request_rows):
        widened = request_rows.astype(jnp.float32)
        normalized_input = (widened * lax.rsqrt(lax.optimization_barrier(jnp.mean(widened * widened, -1, keepdims=True)) + 1e-05)).astype(jnp.bfloat16)
        unrotated_key = jnp.dot(normalized_input, key_weight, preferred_element_type=jnp.float32).reshape(PROMPT_SLOTS, KEY_VALUE_HEADS, HEAD_SIZE)
        value_matrix_rows = jnp.dot(normalized_input, value_weight, preferred_element_type=jnp.float32).astype(jnp.bfloat16).reshape(PROMPT_SLOTS, KEY_VALUE_HEADS, HEAD_SIZE)
        key_rows = rotate(unrotated_key, cosine[:, None, :], sine_part[:, None, :]).astype(jnp.bfloat16)
        return jnp.concatenate([key_rows, value_matrix_rows], -1)
    key_value_pair = lax.map(project, hidden)
    live_rows = jnp.arange(PROMPT_SLOTS, dtype=jnp.int32)[None, :] < lengths[:, None]
    key_value_pair = jnp.where(live_rows[:, :, None, None], key_value_pair, jnp.zeros_like(key_value_pair))
    pair_ids = jnp.arange(DECODERS, dtype=jnp.int32)
    matches = owner[None, :] == pair_ids[:, None]
    inverse_order = lax.optimization_barrier(jnp.sum(jnp.where(matches, pair_ids[None, :], 0), axis=1)).astype(jnp.int32)
    source_request = (inverse_order // KEY_VALUE_HEADS).astype(jnp.int32)
    request_ids = jnp.arange(REQ, dtype=jnp.int32)
    decode_peer_lengths = lax.optimization_barrier(jnp.sum(jnp.where(request_ids[None, :] == source_request[:, None], lengths[None, :], 0), axis=1)).astype(jnp.int32)
    pair_rows = jnp.transpose(key_value_pair, (0, 2, 1, 3)).reshape(DECODERS, PROMPT_SLOTS, 2 * HEAD_SIZE)
    cache_full = pair_rows[inverse_order]
    attended_rows = jax.vmap(decode_one)(cache_full, decode_peer_lengths, dec_query, dec_key, dec_value)
    cache_out = jnp.transpose(cache_full.reshape(DECODERS, PROMPT_SLOTS // SPLIT, SPLIT, 2 * HEAD_SIZE), (0, 2, 1, 3)).reshape(DECODERS * SPLIT, PROMPT_SLOTS // SPLIT, 2 * HEAD_SIZE)
    attended = jnp.transpose(attended_rows, (1, 0, 2)).reshape(STEPS, DECODERS * QPK * HEAD_SIZE)
    return (cache_out, attended)
```

```python
import jax
import jax.numpy as jnp
from jax import lax
from jax.sharding import PartitionSpec as P

HEAD_SIZE = 128
KEY_VALUE_HEADS = 4
QPK = 8
STEPS = 4


ROPE_BASE = 500000.0


def swapped(block, axis, bit):
    count = lax.axis_size(axis)
    route = []
    for low in range(count):
        high = low | 1 << bit
        if high != low and high < count:
            route += [(low, high), (high, low)]
    return lax.ppermute(block, axis, route)


def rope_table(positions, head_dim):
    freq = ROPE_BASE ** (-(jnp.arange(head_dim // 2, dtype=jnp.float32) * 2.0) / head_dim)
    angle = positions.astype(jnp.float32)[:, None] * freq[None, :]
    return (jnp.cos(angle), jnp.sin(angle))


def rotate(values_in, cosine, sine_part):
    half_dim = values_in.shape[-1] // 2
    lower_half = values_in[..., :half_dim]
    upper_half = values_in[..., half_dim:]
    return jnp.concatenate(
        [
            lower_half * cosine - upper_half * sine_part,
            upper_half * cosine + lower_half * sine_part,
        ],
        -1,
    )


def spread(count):
    side = 1
    while side * side < count:
        side *= 2
    return (side, count // side)


def moved(block, rule):
    groups, seq = lax.axis_size("groups"), lax.axis_size("seq")
    low = spread(seq // 2)[1]
    route = []
    for g in range(groups):
        for s in range(seq):
            place = rule(g, s // 2 // low, s // 2 % low, s % 2)
            if place is not None:
                tg, tz, ty, tc = place
                route.append((g * seq + s, tg * seq + (tz * low + ty) * 2 + tc))
    return lax.ppermute(block, ("groups", "seq"), route)


def to_core(g, z, y, c):
    return (g, z, y, 1 - c)


def to_row(g, z, y, c):
    return (g, z, 1 - y, c)


def to_group(g, z, y, c):
    return (1 - g, z, y, c)


def to_pair(g, z, y, c):
    return (g, z ^ 1, y, c)


def to_middle(g, z, y, c):
    return (g, 3 - z, y, c) if z in (1, 2) else None


def to_end(g, z, y, c):
    return (g, 0 if z == 1 else 3, y, c) if z in (1, 2) else None


def mirrored(block, axis, flag):
    quarter = block.shape[axis] // 4
    parts = [lax.slice_in_dim(block, i * quarter, (i + 1) * quarter, axis=axis) for i in range(4)]
    return jnp.where(flag, jnp.concatenate(parts[::-1], axis), block)


def gathered_blocks(weight, z, y, g):
    quarter = weight.shape[0] // 4
    own = mirrored(weight, 0, g == 1)
    is_end = (z == 0) | (z == 3)
    main = own[: 3 * quarter]
    near = moved(main, to_pair)
    mid_b = moved(main, to_middle)
    mid_c = moved(near, to_middle)
    end_b = moved(mid_b, to_end)
    end_c = moved(mid_c, to_end)
    slot_b = jnp.where(is_end, end_b, mid_b)
    slot_c = jnp.where(is_end, end_c, mid_c)
    z_a, z_b, z_c = z ^ 1, jnp.where(z < 2, 2, 1), jnp.where(z < 2, 3, 0)
    pieces = [(z, y, 0, own)]
    for zz, block, share in ((z, main, 2), (z_a, near, 2), (z_b, slot_b, 3), (z_c, slot_c, 3)):
        if block is not main:
            pieces.append((zz, y, 0, block))
            pieces.append((zz, y, 3 * quarter, moved(block[:quarter], to_group)))
        across = moved(block[: share * quarter], to_row)
        pieces.append((zz, 1 - y, 0, across))
        if share == 2:
            onward = jnp.concatenate([across[quarter:], across[:quarter]], 0)
        else:
            onward = across[:quarter]
        pieces.append((zz, 1 - y, share * quarter, moved(onward, to_group)))
    return pieces


def body(hidden, key_weight, value_weight, lengths, owner, dec_query, dec_key, dec_value):
    count_requests, count_rows, width = hidden.shape
    device_id = lax.axis_index("seq")
    group_id = lax.axis_index("groups")
    seq = lax.axis_size("seq")
    planned = seq == 16 and lax.axis_size("groups") == 2
    decode_peers = count_requests * KEY_VALUE_HEADS
    split_point = seq // decode_peers
    tree_levels = split_point.bit_length() - 1
    rows_per_peer = count_rows // split_point
    positions = device_id * count_rows + jnp.arange(count_rows, dtype=jnp.int32)
    total_rows = count_requests * count_rows
    flat = hidden.reshape(total_rows, width)
    widened = flat.astype(jnp.float32)
    row_scale = lax.rsqrt(jnp.mean(widened * widened, -1, keepdims=True) + 1e-05)

    if planned:
        core = device_id % 2
        z, y = device_id // 4, device_id // 2 % 2
        blocks = seq // 2
        depth = width // seq
        split_cols = flat.reshape(total_rows, blocks, 2, depth)
        ordered = mirrored(split_cols, 3, group_id == 1)
        mine = jnp.where(core == 0, ordered[:, :, 0], ordered[:, :, 1])
        other = jnp.where(core == 0, ordered[:, :, 1], ordered[:, :, 0])
        mine = jnp.transpose(mine, (1, 0, 2))
        other = moved(jnp.transpose(other, (1, 0, 2)), to_core)
        left = jnp.concatenate([mine, other], 1)

        def project(weight):
            total = jnp.zeros((2 * total_rows, weight.shape[1]), jnp.float32)
            for zz, yy, first, piece in gathered_blocks(weight, z, y, group_id):
                part = lax.dynamic_index_in_dim(left, zz * 2 + yy, 0, keepdims=False)
                part = part[:, first : first + piece.shape[0]]
                total = total + jnp.dot(part, piece, preferred_element_type=jnp.float32)
            return total[:total_rows] + moved(total[total_rows:], to_core)
    else:

        def project(weight):
            whole = lax.all_gather(weight, "seq", axis=0, tiled=True)
            return jnp.dot(flat, whole, preferred_element_type=jnp.float32)

    pair_ids = jnp.arange(decode_peers, dtype=jnp.int32)
    matches = owner[None, :] == pair_ids[:, None]
    inverse_order = jnp.sum(jnp.where(matches, pair_ids[None, :], 0), axis=1)
    live_rows = positions[None, :] < lengths[:, None]

    def handed_over(rows):
        rows = jnp.where(live_rows[:, :, None, None], rows, jnp.zeros_like(rows))
        pair_rows = jnp.transpose(rows, (0, 2, 1, 3)).reshape(decode_peers, count_rows, HEAD_SIZE)
        sorted_rows = pair_rows[inverse_order].reshape(
            decode_peers, rows_per_peer, split_point, HEAD_SIZE
        )
        outgoing = jnp.transpose(sorted_rows, (0, 2, 1, 3)).reshape(
            decode_peers * split_point, rows_per_peer, HEAD_SIZE
        )
        return lax.all_to_all(outgoing, "seq", split_axis=0, concat_axis=1, tiled=True)[0]

    shape = (count_requests, count_rows, KEY_VALUE_HEADS, HEAD_SIZE)
    unrotated_key = (project(key_weight) * row_scale).reshape(shape)
    cosine, sine_part = rope_table(positions, HEAD_SIZE)
    key_rows = rotate(unrotated_key, cosine[:, None, :], sine_part[:, None, :]).astype(jnp.bfloat16)
    cache_keys = handed_over(key_rows)
    value_rows = (project(value_weight) * row_scale).astype(jnp.bfloat16).reshape(shape)
    cache_values = handed_over(value_rows)
    slot_count = cache_keys.shape[0]
    decode_peer = device_id // split_point
    block = device_id % split_point
    source_pair = jnp.sum(jnp.where(owner == decode_peer, pair_ids, 0))
    source_request = source_pair // KEY_VALUE_HEADS
    length = jnp.sum(
        jnp.where(jnp.arange(count_requests, dtype=jnp.int32) == source_request, lengths, 0)
    )
    query = lax.dynamic_index_in_dim(dec_query, decode_peer, 0, keepdims=False)
    new_key = lax.dynamic_index_in_dim(dec_key, decode_peer, 0, keepdims=False)
    new_value = lax.dynamic_index_in_dim(dec_value, decode_peer, 0, keepdims=False)
    step_pos = length + jnp.arange(STEPS, dtype=jnp.int32)
    step_cos, step_sin = rope_table(step_pos, HEAD_SIZE)
    query_rot = rotate(
        query.astype(jnp.float32).reshape(STEPS, QPK, HEAD_SIZE),
        step_cos[:, None, :],
        step_sin[:, None, :],
    ).astype(jnp.bfloat16)
    new_keys = rotate(new_key.astype(jnp.float32), step_cos, step_sin).astype(jnp.bfloat16)
    score_scale = 1.0 / HEAD_SIZE**0.5
    old_scores = (
        jnp.einsum(
            "sjd,id->sji", query_rot, cache_keys, preferred_element_type=jnp.float32
        )
        * score_scale
    )
    new_scores = (
        jnp.einsum("sjd,td->sjt", query_rot, new_keys, preferred_element_type=jnp.float32)
        * score_scale
    )
    slot_ids = jnp.arange(slot_count, dtype=jnp.int32) * split_point + block
    old_live = slot_ids < length
    new_live = (jnp.arange(STEPS)[None, :] <= jnp.arange(STEPS)[:, None]) & (block == 0)
    old_scores = jnp.where(old_live[None, None, :], old_scores, -1e30)
    new_scores = jnp.where(new_live[:, None, :], new_scores, -1e30)
    row_max = jnp.maximum(jnp.max(old_scores, -1), jnp.max(new_scores, -1))
    for bit in range(tree_levels):
        row_max = jnp.maximum(row_max, swapped(row_max, "seq", bit))
    old_exp = jnp.exp(old_scores - row_max[..., None])
    new_exp = jnp.exp(new_scores - row_max[..., None])
    denom = jnp.sum(old_exp, -1) + jnp.sum(new_exp, -1)
    for bit in range(tree_levels):
        denom = denom + swapped(denom, "seq", bit)
    old_probs = (old_exp / denom[..., None]).astype(jnp.bfloat16)
    new_probs = (new_exp / denom[..., None]).astype(jnp.bfloat16)
    partial_sum = jnp.einsum(
        "sji,id->sjd", old_probs, cache_values, preferred_element_type=jnp.float32
    )
    partial_sum = partial_sum + jnp.einsum(
        "sjt,td->sjd", new_probs, new_value, preferred_element_type=jnp.float32
    )
    flat_rows = partial_sum.reshape(STEPS, QPK * HEAD_SIZE)
    for bit in range(tree_levels):
        flat_rows = flat_rows + swapped(flat_rows, "seq", bit)
    share = flat_rows.shape[1] // split_point
    mine = lax.dynamic_slice_in_dim(flat_rows, block * share, share, 1)
    cache = jnp.concatenate([cache_keys, cache_values], 1)[None]
    return (cache, mine.astype(jnp.bfloat16))


def solution(mesh):
    placed = (
        P("groups", "seq", None),
        P("seq", None),
        P("seq", None),
        P("groups"),
        P("groups"),
        P("groups", None, None),
        P("groups", None, None),
        P("groups", None, None),
    )
    return jax.shard_map(
        body,
        mesh=mesh,
        in_specs=placed,
        out_specs=(P(("groups", "seq"), None, None), P("groups", "seq")),
        check_vma=False,
    )
```

```python
import functools

import jax
import jax.numpy as jnp
from jax import lax
from jax.experimental import pallas as pl
from jax.experimental.pallas import tpu as pltpu
from jax.sharding import PartitionSpec as P

HEAD_SIZE = 128
KEY_VALUE_HEADS = 4
QPK = 8
STEPS = 4


ROPE_BASE = 500000.0


def swapped(block, axis, bit):
    count = lax.axis_size(axis)
    route = []
    for low in range(count):
        high = low | 1 << bit
        if high != low and high < count:
            route += [(low, high), (high, low)]
    return lax.ppermute(block, axis, route)


def rope_table(positions, head_dim):
    freq = ROPE_BASE ** (-(jnp.arange(head_dim // 2, dtype=jnp.float32) * 2.0) / head_dim)
    angle = positions.astype(jnp.float32)[:, None] * freq[None, :]
    return (jnp.cos(angle), jnp.sin(angle))


def rotate(values_in, cosine, sine_part):
    half_dim = values_in.shape[-1] // 2
    lower_half = values_in[..., :half_dim]
    upper_half = values_in[..., half_dim:]
    return jnp.concatenate(
        [
            lower_half * cosine - upper_half * sine_part,
            upper_half * cosine + lower_half * sine_part,
        ],
        -1,
    )


def spread(count):
    side = 1
    while side * side < count:
        side *= 2
    return (side, count // side)


def moved(block, rule):
    groups, seq = lax.axis_size("groups"), lax.axis_size("seq")
    low = spread(seq // 2)[1]
    route = []
    for g in range(groups):
        for s in range(seq):
            place = rule(g, s // 2 // low, s // 2 % low, s % 2)
            if place is not None:
                tg, tz, ty, tc = place
                route.append((g * seq + s, tg * seq + (tz * low + ty) * 2 + tc))
    return lax.ppermute(block, ("groups", "seq"), route)


def to_core(g, z, y, c):
    return (g, z, y, 1 - c)


def to_row(g, z, y, c):
    return (g, z, 1 - y, c)


def to_group(g, z, y, c):
    return (1 - g, z, y, c)


def to_pair(g, z, y, c):
    return (g, z ^ 1, y, c)


def to_middle(g, z, y, c):
    return (g, 3 - z, y, c) if z in (1, 2) else None


def to_end(g, z, y, c):
    return (g, 0 if z == 1 else 3, y, c) if z in (1, 2) else None


def mirrored(block, axis, flag):
    quarter = block.shape[axis] // 4
    parts = [lax.slice_in_dim(block, i * quarter, (i + 1) * quarter, axis=axis) for i in range(4)]
    return jnp.where(flag, jnp.concatenate(parts[::-1], axis), block)


def small_cost():
    return pl.CostEstimate(flops=1000, bytes_accessed=1000, transcendentals=0)


def whole_block(array):
    return pl.BlockSpec(array.shape, lambda *_: (0,) * array.ndim)


def prepare_kernel(place, rows_in, mine, other):
    blocks, _, depth = mine.shape
    quarter = depth // 4
    wide = rows_in[...].astype(jnp.float32)
    scale = lax.rsqrt(jnp.mean(wide * wide, -1, keepdims=True) + 1e-05)
    for g in range(2):
        for core in range(2):

            @pl.when((place[0] == g) & (place[1] == core))
            def _():
                for j in range(blocks):
                    for c in range(2):
                        target = mine if c == core else other
                        for q in range(4):
                            first = (2 * j + c) * depth + q * quarter
                            part = rows_in[:, first : first + quarter].astype(jnp.float32)
                            spot = 3 - q if g else q
                            target[j, :, spot * quarter : (spot + 1) * quarter] = (
                                part * scale
                            ).astype(jnp.bfloat16)


def prepared(flat, group_id, core, blocks):
    rows, width = flat.shape
    depth = width // (2 * blocks)
    tile = 64 if rows % 64 == 0 else rows
    out = jax.ShapeDtypeStruct((blocks, rows, depth), jnp.bfloat16)
    spec = pl.BlockSpec((blocks, tile, depth), lambda i, place: (0, i, 0))
    return pl.pallas_call(
        prepare_kernel,
        grid_spec=pltpu.PrefetchScalarGridSpec(
            num_scalar_prefetch=1,
            grid=(rows // tile,),
            in_specs=[pl.BlockSpec((tile, width), lambda i, place: (i, 0))],
            out_specs=[spec, spec],
        ),
        out_shape=[out, out],
        compiler_params=pltpu.CompilerParams(vmem_limit_bytes=32 << 20),
        cost_estimate=small_cost(),
        name="normed_halves",
    )(jnp.stack([group_id, core]).astype(jnp.int32), flat)


def product_kernel(count_near, has_total, which, *refs):
    left = refs[:4]
    pieces = [ref[...] for ref in refs[4 : -2 - 2 * has_total]]
    near = jnp.concatenate(pieces[:count_near], 0) if count_near > 1 else pieces[0]
    far = jnp.concatenate(pieces[count_near:], 0)
    for half in range(2):
        total = jnp.dot(left[2 * half][0], near, preferred_element_type=jnp.float32)
        total += jnp.dot(left[2 * half + 1][0], far, preferred_element_type=jnp.float32)
        if has_total:
            total += refs[half - 4][...]
        refs[half - 2][...] = total


def product(which, mine, other, near, far, totals):
    _, rows, depth = mine.shape
    columns = near[0].shape[1]
    operands = [*near, *far, *totals]
    left_specs = [
        pl.BlockSpec((1, rows, depth), functools.partial(lambda k, _, which: (which[k], 0, 0), k))
        for k in (0, 1)
    ]
    out = jax.ShapeDtypeStruct((rows, columns), jnp.float32)
    first_total = 1 + 4 + len(near) + len(far)
    return pl.pallas_call(
        functools.partial(product_kernel, len(near), len(totals) // 2),
        grid_spec=pltpu.PrefetchScalarGridSpec(
            num_scalar_prefetch=1,
            grid=(1,),
            in_specs=left_specs * 2 + [whole_block(piece) for piece in operands],
            out_specs=[whole_block(out)] * 2,
        ),
        out_shape=[out, out],
        input_output_aliases={first_total + i: i for i in range(len(totals))},
        compiler_params=pltpu.CompilerParams(vmem_limit_bytes=32 << 20),
        cost_estimate=small_cost(),
        name="add_product",
    )(which, mine, mine, other, other, *operands)


def rows_kernel(rotated, place, lengths, owner, *refs):
    out, scratch = refs[-2:]
    total, came = refs[:2]
    count_requests, count_rows = lengths.shape[0], scratch.shape[0]
    first = place[0] * count_rows
    index = first + lax.broadcasted_iota(jnp.int32, scratch.shape, 0)
    for r in range(count_requests):
        live = index < lengths[r]
        for h in range(KEY_VALUE_HEADS):
            area = (
                slice(r * count_rows, (r + 1) * count_rows),
                slice(h * HEAD_SIZE, (h + 1) * HEAD_SIZE),
            )
            rows = total[area] + came[area]
            if rotated:
                turned = jnp.concatenate([rows[:, HEAD_SIZE // 2 :], rows[:, : HEAD_SIZE // 2]], 1)
                rows = rows * refs[2][...] + turned * refs[3][...]
            scratch[...] = jnp.where(live, rows, 0.0)
            peer = owner[r * KEY_VALUE_HEADS + h]
            for b in range(2):
                picked = scratch[pl.ds(b, count_rows // 2, stride=2), :]
                out[peer * 2 + b] = picked.astype(jnp.bfloat16)


def outgoing_rows(total, came, place, lengths, owner, turn):
    count_rows = total.shape[0] // lengths.shape[0]
    operands = [total, came, *turn]
    peers = owner.shape[0] * 2
    out = jax.ShapeDtypeStruct((peers, count_rows // 2, HEAD_SIZE), jnp.bfloat16)
    return pl.pallas_call(
        functools.partial(rows_kernel, bool(turn)),
        grid_spec=pltpu.PrefetchScalarGridSpec(
            num_scalar_prefetch=3,
            grid=(1,),
            in_specs=[whole_block(x) for x in operands],
            out_specs=whole_block(out),
            scratch_shapes=[pltpu.VMEM((count_rows, HEAD_SIZE), jnp.float32)],
        ),
        out_shape=out,
        compiler_params=pltpu.CompilerParams(vmem_limit_bytes=32 << 20),
        cost_estimate=small_cost(),
        name="cache_rows",
    )(place, lengths, owner, *operands)


def planned_totals(weight, mine, other, z, y, g):
    quarter = weight.shape[0] // 4
    own = mirrored(weight, 0, g == 1)
    is_end = (z == 0) | (z == 3)
    main = own[: 3 * quarter]
    near = moved(main, to_pair)
    mid_b = moved(main, to_middle)
    mid_c = moved(near, to_middle)
    end_b = moved(mid_b, to_end)
    end_c = moved(mid_c, to_end)
    slot_b = jnp.where(is_end, end_b, mid_b)
    slot_c = jnp.where(is_end, end_c, mid_c)
    z_a, z_b, z_c = z ^ 1, jnp.where(z < 2, 2, 1), jnp.where(z < 2, 3, 0)
    totals = []
    for zz, block, share in ((z, own, 2), (z_a, near, 2), (z_b, slot_b, 3), (z_c, slot_c, 3)):
        here = [block]
        if block is not own:
            here.append(moved(block[:quarter], to_group))
        across = moved(block[: share * quarter], to_row)
        if share == 2:
            onward = jnp.concatenate([across[quarter:], across[:quarter]], 0)
        else:
            onward = across[:quarter]
        there = [across, moved(onward, to_group)]
        which = jnp.stack([zz * 2 + y, zz * 2 + 1 - y]).astype(jnp.int32)
        totals = product(which, mine, other, here, there, totals)
    return totals


def body(hidden, key_weight, value_weight, lengths, owner, dec_query, dec_key, dec_value):
    count_requests, count_rows, width = hidden.shape
    device_id = lax.axis_index("seq")
    group_id = lax.axis_index("groups")
    seq = lax.axis_size("seq")
    planned = seq == 16 and lax.axis_size("groups") == 2
    decode_peers = count_requests * KEY_VALUE_HEADS
    split_point = seq // decode_peers
    tree_levels = split_point.bit_length() - 1
    rows_per_peer = count_rows // split_point
    positions = device_id * count_rows + jnp.arange(count_rows, dtype=jnp.int32)
    total_rows = count_requests * count_rows
    flat = hidden.reshape(total_rows, width)
    if planned:
        core = device_id % 2
        z, y = device_id // 4, device_id // 2 % 2
        mine, other = prepared(flat, group_id, core, seq // 2)
        other = moved(other, to_core)
    else:
        widened = flat.astype(jnp.float32)
        normed = (
            widened * lax.rsqrt(jnp.mean(widened * widened, -1, keepdims=True) + 1e-05)
        ).astype(jnp.bfloat16)

        def project(weight):
            whole = lax.all_gather(weight, "seq", axis=0, tiled=True)
            return jnp.dot(normed, whole, preferred_element_type=jnp.float32)

    pair_ids = jnp.arange(decode_peers, dtype=jnp.int32)
    matches = owner[None, :] == pair_ids[:, None]
    inverse_order = jnp.sum(jnp.where(matches, pair_ids[None, :], 0), axis=1)
    live_rows = positions[None, :] < lengths[:, None]

    def handed_over(rows):
        rows = jnp.where(live_rows[:, :, None, None], rows, jnp.zeros_like(rows))
        pair_rows = jnp.transpose(rows, (0, 2, 1, 3)).reshape(decode_peers, count_rows, HEAD_SIZE)
        sorted_rows = pair_rows[inverse_order].reshape(
            decode_peers, rows_per_peer, split_point, HEAD_SIZE
        )
        outgoing = jnp.transpose(sorted_rows, (0, 2, 1, 3)).reshape(
            decode_peers * split_point, rows_per_peer, HEAD_SIZE
        )
        return lax.all_to_all(outgoing, "seq", split_axis=0, concat_axis=1, tiled=True)[0]

    cosine, sine_part = rope_table(positions, HEAD_SIZE)
    if planned:
        turn = (
            jnp.concatenate([cosine, cosine], 1),
            jnp.concatenate([-sine_part, sine_part], 1),
        )
        place = device_id.astype(jnp.int32).reshape(1)

        def cached(weight, turn):
            total, came = planned_totals(weight, mine, other, z, y, group_id)
            came = moved(came, to_core)
            outgoing = outgoing_rows(total, came, place, lengths, owner, turn)
            return lax.all_to_all(outgoing, "seq", split_axis=0, concat_axis=1, tiled=True)[0]

        cache_keys = cached(key_weight, turn)
        cache_values = cached(value_weight, ())
    else:
        shape = (count_requests, count_rows, KEY_VALUE_HEADS, HEAD_SIZE)
        unrotated_key = project(key_weight).reshape(shape)
        key_rows = rotate(
            unrotated_key, cosine[:, None, :], sine_part[:, None, :]
        ).astype(jnp.bfloat16)
        cache_keys = handed_over(key_rows)
        cache_values = handed_over(project(value_weight).astype(jnp.bfloat16).reshape(shape))
    slot_count = cache_keys.shape[0]
    decode_peer = device_id // split_point
    block = device_id % split_point
    source_pair = jnp.sum(jnp.where(owner == decode_peer, pair_ids, 0))
    source_request = source_pair // KEY_VALUE_HEADS
    length = jnp.sum(
        jnp.where(jnp.arange(count_requests, dtype=jnp.int32) == source_request, lengths, 0)
    )
    query = lax.dynamic_index_in_dim(dec_query, decode_peer, 0, keepdims=False)
    new_key = lax.dynamic_index_in_dim(dec_key, decode_peer, 0, keepdims=False)
    new_value = lax.dynamic_index_in_dim(dec_value, decode_peer, 0, keepdims=False)
    step_pos = length + jnp.arange(STEPS, dtype=jnp.int32)
    step_cos, step_sin = rope_table(step_pos, HEAD_SIZE)
    query_rot = rotate(
        query.astype(jnp.float32).reshape(STEPS, QPK, HEAD_SIZE),
        step_cos[:, None, :],
        step_sin[:, None, :],
    ).astype(jnp.bfloat16)
    new_keys = rotate(new_key.astype(jnp.float32), step_cos, step_sin).astype(jnp.bfloat16)
    score_scale = 1.0 / HEAD_SIZE**0.5
    old_scores = (
        jnp.einsum(
            "sjd,id->sji", query_rot, cache_keys, preferred_element_type=jnp.float32
        )
        * score_scale
    )
    new_scores = (
        jnp.einsum("sjd,td->sjt", query_rot, new_keys, preferred_element_type=jnp.float32)
        * score_scale
    )
    slot_ids = jnp.arange(slot_count, dtype=jnp.int32) * split_point + block
    old_live = slot_ids < length
    new_live = (jnp.arange(STEPS)[None, :] <= jnp.arange(STEPS)[:, None]) & (block == 0)
    old_scores = jnp.where(old_live[None, None, :], old_scores, -1e30)
    new_scores = jnp.where(new_live[:, None, :], new_scores, -1e30)
    row_max = jnp.maximum(jnp.max(old_scores, -1), jnp.max(new_scores, -1))
    for bit in range(tree_levels):
        row_max = jnp.maximum(row_max, swapped(row_max, "seq", bit))
    old_exp = jnp.exp(old_scores - row_max[..., None])
    new_exp = jnp.exp(new_scores - row_max[..., None])
    denom = jnp.sum(old_exp, -1) + jnp.sum(new_exp, -1)
    for bit in range(tree_levels):
        denom = denom + swapped(denom, "seq", bit)
    old_probs = (old_exp / denom[..., None]).astype(jnp.bfloat16)
    new_probs = (new_exp / denom[..., None]).astype(jnp.bfloat16)
    partial_sum = jnp.einsum(
        "sji,id->sjd", old_probs, cache_values, preferred_element_type=jnp.float32
    )
    partial_sum = partial_sum + jnp.einsum(
        "sjt,td->sjd", new_probs, new_value, preferred_element_type=jnp.float32
    )
    flat_rows = partial_sum.reshape(STEPS, QPK * HEAD_SIZE)
    for bit in range(tree_levels):
        flat_rows = flat_rows + swapped(flat_rows, "seq", bit)
    share = flat_rows.shape[1] // split_point
    mine = lax.dynamic_slice_in_dim(flat_rows, block * share, share, 1)
    cache = jnp.concatenate([cache_keys, cache_values], 1)[None]
    return (cache, mine.astype(jnp.bfloat16))


def solution(mesh):
    placed = (
        P("groups", "seq", None),
        P("seq", None),
        P("seq", None),
        P("groups"),
        P("groups"),
        P("groups", None, None),
        P("groups", None, None),
        P("groups", None, None),
    )
    return jax.shard_map(
        body,
        mesh=mesh,
        in_specs=placed,
        out_specs=(P(("groups", "seq"), None, None), P("groups", "seq")),
        check_vma=False,
    )
```

```python
import functools

import jax
import jax.numpy as jnp
from jax import lax
from jax.experimental import pallas as pl
from jax.experimental.pallas import tpu as pltpu
from jax.sharding import PartitionSpec as P

HEAD_SIZE = 128
KEY_VALUE_HEADS = 4
QPK = 8
STEPS = 4


ROPE_BASE = 500000.0


def swapped(block, axis, bit):
    count = lax.axis_size(axis)
    route = []
    for low in range(count):
        high = low | 1 << bit
        if high != low and high < count:
            route += [(low, high), (high, low)]
    return lax.ppermute(block, axis, route)


def rope_table(positions, head_dim):
    freq = ROPE_BASE ** (-(jnp.arange(head_dim // 2, dtype=jnp.float32) * 2.0) / head_dim)
    angle = positions.astype(jnp.float32)[:, None] * freq[None, :]
    return (jnp.cos(angle), jnp.sin(angle))


def rotate(values_in, cosine, sine_part):
    half_dim = values_in.shape[-1] // 2
    lower_half = values_in[..., :half_dim]
    upper_half = values_in[..., half_dim:]
    return jnp.concatenate(
        [
            lower_half * cosine - upper_half * sine_part,
            upper_half * cosine + lower_half * sine_part,
        ],
        -1,
    )


def spread(count):
    side = 1
    while side * side < count:
        side *= 2
    return (side, count // side)


def moved(block, rule):
    groups, seq = lax.axis_size("groups"), lax.axis_size("seq")
    low = spread(seq // 2)[1]
    route = []
    for g in range(groups):
        for s in range(seq):
            place = rule(g, s // 2 // low, s // 2 % low, s % 2)
            if place is not None:
                tg, tz, ty, tc = place
                route.append((g * seq + s, tg * seq + (tz * low + ty) * 2 + tc))
    return lax.ppermute(block, ("groups", "seq"), route)


def to_core(g, z, y, c):
    return (g, z, y, 1 - c)


def to_row(g, z, y, c):
    return (g, z, 1 - y, c)


def to_group(g, z, y, c):
    return (1 - g, z, y, c)


def to_pair(g, z, y, c):
    return (g, z ^ 1, y, c)


def to_middle(g, z, y, c):
    return (g, 3 - z, y, c) if z in (1, 2) else None


def to_end(g, z, y, c):
    return (g, 0 if z == 1 else 3, y, c) if z in (1, 2) else None


def small_cost():
    return pl.CostEstimate(flops=1000, bytes_accessed=1000, transcendentals=0)


def whole_block(array):
    return pl.BlockSpec(array.shape, lambda *_: (0,) * array.ndim)


def prepare_kernel(place, rows_in, token, mine, other):
    blocks, _, depth = mine.shape
    quarter = depth // 4
    wide = rows_in[...].astype(jnp.float32)
    scale = lax.rsqrt(jnp.mean(wide * wide, -1, keepdims=True) + 1e-05)
    for g in range(2):
        for core in range(2):

            @pl.when((place[0] == g) & (place[1] == core))
            def _():
                for j in range(blocks):
                    for c in range(2):
                        target = mine if c == core else other
                        for q in range(4):
                            first = (2 * j + c) * depth + q * quarter
                            part = rows_in[:, first : first + quarter].astype(jnp.float32)
                            spot = 3 - q if g else q
                            target[j, :, spot * quarter : (spot + 1) * quarter] = (
                                part * scale
                            ).astype(jnp.bfloat16)


def prepared(flat, place, token, blocks):
    rows, width = flat.shape
    depth = width // (2 * blocks)
    tile = 64 if rows % 64 == 0 else rows
    out = jax.ShapeDtypeStruct((blocks, rows, depth), jnp.bfloat16)
    spec = pl.BlockSpec((blocks, tile, depth), lambda i, place: (0, i, 0))
    return pl.pallas_call(
        prepare_kernel,
        grid_spec=pltpu.PrefetchScalarGridSpec(
            num_scalar_prefetch=1,
            grid=(rows // tile,),
            in_specs=[pl.BlockSpec((tile, width), lambda i, place: (i, 0)), pl.BlockSpec(memory_space=pl.ANY)],
            out_specs=[spec, spec],
        ),
        out_shape=[out, out],
        compiler_params=pltpu.CompilerParams(vmem_limit_bytes=32 << 20),
        cost_estimate=pl.CostEstimate(
            flops=8 * rows * width, bytes_accessed=4 * rows * width, transcendentals=0
        ),
        name="normed_halves",
    )(place, flat, token)


VMEM_REF = pl.BlockSpec(memory_space=pltpu.VMEM)
SMEM_REF = pl.BlockSpec(memory_space=pltpu.SMEM)
ANY_REF = pl.BlockSpec(memory_space=pl.ANY)


def local_call(name, kernel, place, token, inputs, outs, flops=1000):
    def wrapped(place_ref, token_ref, *refs):
        kernel(place_ref, *refs)

    return pl.pallas_call(
        wrapped,
        in_specs=[SMEM_REF, ANY_REF] + [VMEM_REF] * len(inputs),
        out_specs=[VMEM_REF] * len(outs),
        out_shape=[jax.ShapeDtypeStruct(shape, dtype) for shape, dtype in outs],
        compiler_params=pltpu.CompilerParams(vmem_limit_bytes=24 << 20),
        cost_estimate=pl.CostEstimate(flops=flops, bytes_accessed=1000, transcendentals=0),
        name=name,
    )(place, token, *inputs)


def first_cut(place, *refs):
    count = len(refs) // 4
    for weight, own, main, across in zip(
        refs[:count], refs[count::3], refs[count + 1 :: 3], refs[count + 2 :: 3]
    ):
        quarter = weight.shape[0] // 4
        for g in range(2):

            @pl.when(place[0] == g)
            def _():
                for spot in range(4):
                    q = 3 - spot if g else spot
                    part = weight[q * quarter : (q + 1) * quarter]
                    area = slice(spot * quarter, (spot + 1) * quarter)
                    own[area] = part
                    if spot < 3:
                        main[area] = part
                    if spot < 2:
                        across[area] = part


def second_cut(place, near, across, onward, short):
    quarter = near.shape[0] // 3
    onward[:quarter] = near[:quarter]
    onward[quarter : 2 * quarter] = across[quarter:]
    onward[2 * quarter :] = across[:quarter]
    short[...] = near[: 2 * quarter]


def third_cut(place, end_b, mid_b, across_a, slot_b, onward):
    quarter = end_b.shape[0] // 3

    @pl.when(place[2] == 1)
    def _():
        slot_b[...] = end_b[...]
        onward[:quarter] = end_b[:quarter]

    @pl.when(place[2] == 0)
    def _():
        slot_b[...] = mid_b[...]
        onward[:quarter] = mid_b[:quarter]

    onward[quarter:] = across_a[:quarter]


def fourth_cut(place, end_c, mid_c, across_b, slot_c, onward):
    quarter = end_c.shape[0] // 2

    def put(block):
        slot_c[...] = block[...]
        onward[:quarter] = block[quarter:]
        onward[quarter : 2 * quarter] = block[:quarter]

    @pl.when(place[2] == 1)
    def _():
        put(end_c)

    @pl.when(place[2] == 0)
    def _():
        put(mid_c)

    onward[2 * quarter :] = across_b[:quarter]


def last_cut(place, across_c, onward):
    quarter = across_c.shape[0] // 2
    onward[:quarter] = across_c[quarter:]
    onward[quarter:] = across_c[:quarter]


def times(left, block, first, piece):
    part = left[block][:, first : first + piece.shape[0]]
    return jnp.dot(part, piece, preferred_element_type=jnp.float32)


def early_product(place, mine, other, own, near, across, slot_b, across_a, sent, *totals):
    quarter = own.shape[0] // 4
    for left, total in zip((mine, other), totals):
        home = jnp.concatenate([across[...], sent[quarter:]], 0)
        next_door = jnp.concatenate([near[...], sent[:quarter]], 0)
        value = times(left, place[4], 0, own[...])
        value += times(left, place[5], 0, home)
        value += times(left, place[6], 0, next_door)
        value += times(left, place[7], 0, across_a[...])
        value += times(left, place[8], 0, slot_b[...])
        total[...] = value


def late_product(
    place, mine, other, slot_c, across_b, across_c, sent_b, sent_c, mine_in, other_in, *totals
):
    quarter = slot_c.shape[0] // 2
    depth = 4 * quarter
    for left, before, total in zip((mine, other), (mine_in, other_in), totals):
        value = before[...]
        ends = jnp.concatenate(
            [left[place[8]][:, depth - quarter :], left[place[7]][:, depth - quarter :]], 1
        )
        value += jnp.dot(ends, sent_b[...], preferred_element_type=jnp.float32)
        full_b = jnp.concatenate([across_b[...], sent_c[2 * quarter :]], 0)
        value += times(left, place[9], 0, full_b)
        full_c = jnp.concatenate([slot_c[...], sent_c[: 2 * quarter]], 0)
        value += times(left, place[10], 0, full_c)
        value += times(left, place[11], 0, across_c[...])
        total[...] = value


def last_product(place, mine, other, sent, mine_in, other_in, *totals):
    for left, before, total in zip((mine, other), (mine_in, other_in), totals):
        total[...] = before[...] + times(left, place[11], sent.shape[0], sent[...])


def rows_kernel(rotated, place, lengths, owner, *refs):
    out, scratch = refs[-2:]
    total, came = refs[:2]
    count_requests, count_rows = lengths.shape[0], scratch.shape[0]
    first = place[0] * count_rows
    index = first + lax.broadcasted_iota(jnp.int32, scratch.shape, 0)
    for r in range(count_requests):
        live = index < lengths[r]
        for h in range(KEY_VALUE_HEADS):
            area = (
                slice(r * count_rows, (r + 1) * count_rows),
                slice(h * HEAD_SIZE, (h + 1) * HEAD_SIZE),
            )
            rows = total[area] + came[area]
            if rotated:
                turned = jnp.concatenate([rows[:, HEAD_SIZE // 2 :], rows[:, : HEAD_SIZE // 2]], 1)
                rows = rows * refs[2][...] + turned * refs[3][...]
            scratch[...] = jnp.where(live, rows, 0.0)
            peer = owner[r * KEY_VALUE_HEADS + h]
            for b in range(2):
                picked = scratch[pl.ds(b, count_rows // 2, stride=2), :]
                out[peer * 2 + b] = picked.astype(jnp.bfloat16)


def outgoing_rows(total, came, place, lengths, owner, turn):
    count_rows = total.shape[0] // lengths.shape[0]
    operands = [total, came, *turn]
    peers = owner.shape[0] * 2
    out = jax.ShapeDtypeStruct((peers, count_rows // 2, HEAD_SIZE), jnp.bfloat16)
    return pl.pallas_call(
        functools.partial(rows_kernel, bool(turn)),
        grid_spec=pltpu.PrefetchScalarGridSpec(
            num_scalar_prefetch=3,
            grid=(1,),
            in_specs=[whole_block(x) for x in operands],
            out_specs=whole_block(out),
            scratch_shapes=[pltpu.VMEM((count_rows, HEAD_SIZE), jnp.float32)],
        ),
        out_shape=out,
        compiler_params=pltpu.CompilerParams(vmem_limit_bytes=32 << 20),
        cost_estimate=small_cost(),
        name="cache_rows",
    )(place, lengths, owner, *operands)


def planned_totals(weights, mine_other, place, token):
    depth, columns = weights[0].shape
    quarter = depth // 4
    kind = weights[0].dtype

    def rows(count):
        return ((count * quarter, columns), kind)

    def round_of(name, kernel, inputs, *counts):
        nonlocal token
        outs = local_call(name, kernel, place, token, inputs, [rows(n) for n in counts])
        token = outs[0]
        return outs

    count = len(weights)
    cuts = round_of("cut_own", first_cut, weights, *[4, 3, 2] * count)
    states = [cuts[3 * i : 3 * i + 3] for i in range(count)]
    first = []
    for own, main, side in states:
        first.append((own, moved(main, to_pair), moved(main, to_middle), moved(side, to_row)))
    mine, other = mine_other(cuts[0])
    total_rows = mine.shape[1]
    sums = [((total_rows, columns), jnp.float32)] * 2
    flops = 2 * 2 * total_rows * columns * quarter

    second = []
    for own, near, mid_b, across in first:
        onward, short = round_of("cut_near", second_cut, [near, across], 3, 2)
        second.append(
            (moved(mid_b, to_end), moved(short, to_middle), moved(near, to_row), moved(onward, to_group))
        )
    third, totals = [], []
    for (own, near, mid_b, across), (end_b, mid_c, across_a, sent) in zip(first, second):
        slot_b, onward = round_of("cut_middle", third_cut, [end_b, mid_b, across_a], 3, 2)
        third.append((moved(mid_c, to_end), moved(slot_b, to_row), moved(onward, to_group)))
        operands = [mine, other, own, near, across, slot_b, across_a, sent]
        totals.append(
            local_call("early_product", early_product, place, slot_b, operands, sums, 18 * flops)
        )
    fourth = []
    for (_, mid_c, _, _), (end_c, across_b, sent_b) in zip(second, third):
        slot_c, onward = round_of("cut_far", fourth_cut, [end_c, mid_c, across_b], 2, 3)
        fourth.append((slot_c, moved(slot_c, to_row), moved(onward, to_group)))
    results = []
    for (_, across_b, sent_b), (slot_c, across_c, sent_c), total in zip(third, fourth, totals):
        (onward,) = round_of("cut_last", last_cut, [across_c], 2)
        last = moved(onward, to_group)
        operands = [mine, other, slot_c, across_b, across_c, sent_b, sent_c, *total]
        total = local_call("late_product", late_product, place, onward, operands, sums, 12 * flops)
        operands = [mine, other, last, *total]
        results.append(
            local_call("last_product", last_product, place, last, operands, sums, 2 * flops)
        )
    return results


def body(hidden, key_weight, value_weight, lengths, owner, dec_query, dec_key, dec_value):
    count_requests, count_rows, width = hidden.shape
    device_id = lax.axis_index("seq")
    group_id = lax.axis_index("groups")
    seq = lax.axis_size("seq")
    planned = seq == 16 and lax.axis_size("groups") == 2
    decode_peers = count_requests * KEY_VALUE_HEADS
    split_point = seq // decode_peers
    tree_levels = split_point.bit_length() - 1
    rows_per_peer = count_rows // split_point
    positions = device_id * count_rows + jnp.arange(count_rows, dtype=jnp.int32)
    total_rows = count_requests * count_rows
    flat = hidden.reshape(total_rows, width)
    if planned:
        core = device_id % 2
        z, y = device_id // 4, device_id // 2 % 2
        z_a, z_b, z_c = z ^ 1, jnp.where(z < 2, 2, 1), jnp.where(z < 2, 3, 0)
        place = [group_id, core, (z == 0) | (z == 3), 0, z * 2 + y, z * 2 + 1 - y, z_a * 2 + y]
        place += [z_a * 2 + 1 - y, z_b * 2 + y, z_b * 2 + 1 - y, z_c * 2 + y, z_c * 2 + 1 - y]
        place = jnp.stack([jnp.asarray(entry, jnp.int32) for entry in place])

        def mine_other(token):
            mine, other = prepared(flat, place, token, seq // 2)
            return mine, moved(other, to_core)
    else:
        widened = flat.astype(jnp.float32)
        normed = (
            widened * lax.rsqrt(jnp.mean(widened * widened, -1, keepdims=True) + 1e-05)
        ).astype(jnp.bfloat16)

        def project(weight):
            whole = lax.all_gather(weight, "seq", axis=0, tiled=True)
            return jnp.dot(normed, whole, preferred_element_type=jnp.float32)

    pair_ids = jnp.arange(decode_peers, dtype=jnp.int32)
    matches = owner[None, :] == pair_ids[:, None]
    inverse_order = jnp.sum(jnp.where(matches, pair_ids[None, :], 0), axis=1)
    live_rows = positions[None, :] < lengths[:, None]

    def handed_over(rows):
        rows = jnp.where(live_rows[:, :, None, None], rows, jnp.zeros_like(rows))
        pair_rows = jnp.transpose(rows, (0, 2, 1, 3)).reshape(decode_peers, count_rows, HEAD_SIZE)
        sorted_rows = pair_rows[inverse_order].reshape(
            decode_peers, rows_per_peer, split_point, HEAD_SIZE
        )
        outgoing = jnp.transpose(sorted_rows, (0, 2, 1, 3)).reshape(
            decode_peers * split_point, rows_per_peer, HEAD_SIZE
        )
        return lax.all_to_all(outgoing, "seq", split_axis=0, concat_axis=1, tiled=True)[0]

    cosine, sine_part = rope_table(positions, HEAD_SIZE)
    if planned:
        turn = (
            jnp.concatenate([cosine, cosine], 1),
            jnp.concatenate([-sine_part, sine_part], 1),
        )
        weights = (key_weight, value_weight)
        caches = []
        for (total, came), turned in zip(
            planned_totals(weights, mine_other, place, key_weight), (turn, ())
        ):
            came = moved(came, to_core)
            outgoing = outgoing_rows(total, came, device_id.reshape(1), lengths, owner, turned)
            caches.append(
                lax.all_to_all(outgoing, "seq", split_axis=0, concat_axis=1, tiled=True)[0]
            )
        cache_keys, cache_values = caches
    else:
        shape = (count_requests, count_rows, KEY_VALUE_HEADS, HEAD_SIZE)
        unrotated_key = project(key_weight).reshape(shape)
        key_rows = rotate(
            unrotated_key, cosine[:, None, :], sine_part[:, None, :]
        ).astype(jnp.bfloat16)
        cache_keys = handed_over(key_rows)
        cache_values = handed_over(project(value_weight).astype(jnp.bfloat16).reshape(shape))
    slot_count = cache_keys.shape[0]
    decode_peer = device_id // split_point
    block = device_id % split_point
    source_pair = jnp.sum(jnp.where(owner == decode_peer, pair_ids, 0))
    source_request = source_pair // KEY_VALUE_HEADS
    length = jnp.sum(
        jnp.where(jnp.arange(count_requests, dtype=jnp.int32) == source_request, lengths, 0)
    )
    query = lax.dynamic_index_in_dim(dec_query, decode_peer, 0, keepdims=False)
    new_key = lax.dynamic_index_in_dim(dec_key, decode_peer, 0, keepdims=False)
    new_value = lax.dynamic_index_in_dim(dec_value, decode_peer, 0, keepdims=False)
    step_pos = length + jnp.arange(STEPS, dtype=jnp.int32)
    step_cos, step_sin = rope_table(step_pos, HEAD_SIZE)
    query_rot = rotate(
        query.astype(jnp.float32).reshape(STEPS, QPK, HEAD_SIZE),
        step_cos[:, None, :],
        step_sin[:, None, :],
    ).astype(jnp.bfloat16)
    new_keys = rotate(new_key.astype(jnp.float32), step_cos, step_sin).astype(jnp.bfloat16)
    score_scale = 1.0 / HEAD_SIZE**0.5
    old_scores = (
        jnp.einsum(
            "sjd,id->sji", query_rot, cache_keys, preferred_element_type=jnp.float32
        )
        * score_scale
    )
    new_scores = (
        jnp.einsum("sjd,td->sjt", query_rot, new_keys, preferred_element_type=jnp.float32)
        * score_scale
    )
    slot_ids = jnp.arange(slot_count, dtype=jnp.int32) * split_point + block
    old_live = slot_ids < length
    new_live = (jnp.arange(STEPS)[None, :] <= jnp.arange(STEPS)[:, None]) & (block == 0)
    old_scores = jnp.where(old_live[None, None, :], old_scores, -1e30)
    new_scores = jnp.where(new_live[:, None, :], new_scores, -1e30)
    row_max = jnp.maximum(jnp.max(old_scores, -1), jnp.max(new_scores, -1))
    for bit in range(tree_levels):
        row_max = jnp.maximum(row_max, swapped(row_max, "seq", bit))
    old_exp = jnp.exp(old_scores - row_max[..., None])
    new_exp = jnp.exp(new_scores - row_max[..., None])
    denom = jnp.sum(old_exp, -1) + jnp.sum(new_exp, -1)
    for bit in range(tree_levels):
        denom = denom + swapped(denom, "seq", bit)
    old_probs = (old_exp / denom[..., None]).astype(jnp.bfloat16)
    new_probs = (new_exp / denom[..., None]).astype(jnp.bfloat16)
    partial_sum = jnp.einsum(
        "sji,id->sjd", old_probs, cache_values, preferred_element_type=jnp.float32
    )
    partial_sum = partial_sum + jnp.einsum(
        "sjt,td->sjd", new_probs, new_value, preferred_element_type=jnp.float32
    )
    flat_rows = partial_sum.reshape(STEPS, QPK * HEAD_SIZE)
    for bit in range(tree_levels):
        flat_rows = flat_rows + swapped(flat_rows, "seq", bit)
    share = flat_rows.shape[1] // split_point
    mine = lax.dynamic_slice_in_dim(flat_rows, block * share, share, 1)
    cache = jnp.concatenate([cache_keys, cache_values], 1)[None]
    return (cache, mine.astype(jnp.bfloat16))


def solution(mesh):
    placed = (
        P("groups", "seq", None),
        P("seq", None),
        P("seq", None),
        P("groups"),
        P("groups"),
        P("groups", None, None),
        P("groups", None, None),
        P("groups", None, None),
    )
    return jax.shard_map(
        body,
        mesh=mesh,
        in_specs=placed,
        out_specs=(P(("groups", "seq"), None, None), P("groups", "seq")),
        check_vma=False,
    )
```

```python
import functools

import jax
import jax.numpy as jnp
import numpy as np
from jax import lax
from jax.experimental import pallas as pl
from jax.experimental.pallas import tpu as pltpu
from jax.sharding import PartitionSpec as P

HEAD_SIZE = 128
KEY_VALUE_HEADS = 4
QPK = 8
STEPS = 4


ROPE_BASE = 500000.0


def swapped(block, axis, bit):
    count = lax.axis_size(axis)
    route = []
    for low in range(count):
        high = low | 1 << bit
        if high != low and high < count:
            route += [(low, high), (high, low)]
    return lax.ppermute(block, axis, route)


def rope_table(positions, head_dim):
    freq = ROPE_BASE ** (-(np.arange(head_dim // 2, dtype=np.float64) * 2.0) / head_dim)
    angle = positions.astype(jnp.float32)[:, None] * jnp.asarray(freq, jnp.float32)[None, :]
    return (jnp.cos(angle), jnp.sin(angle))


def rotate(values_in, cosine, sine_part):
    half_dim = values_in.shape[-1] // 2
    lower_half = values_in[..., :half_dim]
    upper_half = values_in[..., half_dim:]
    return jnp.concatenate(
        [
            lower_half * cosine - upper_half * sine_part,
            upper_half * cosine + lower_half * sine_part,
        ],
        -1,
    )


def spread(count):
    side = 1
    while side * side < count:
        side *= 2
    return (side, count // side)


def moved(block, rule):
    groups, seq = lax.axis_size("groups"), lax.axis_size("seq")
    low = spread(seq // 2)[1]
    route = []
    for g in range(groups):
        for s in range(seq):
            tg, tz, ty, tc = rule(g, s // 2 // low, s // 2 % low, s % 2)
            route.append((g * seq + s, tg * seq + (tz * low + ty) * 2 + tc))
    return lax.ppermute(block, ("groups", "seq"), route)


def to_core(g, z, y, c):
    return (g, z, y, 1 - c)


def to_row(g, z, y, c):
    return (g, z, 1 - y, c)


def to_group(g, z, y, c):
    return (1 - g, z, y, c)


def along(bits):
    return lambda g, z, y, c: (g, z ^ bits, y, c)


VMEM_REF = pl.BlockSpec(memory_space=pltpu.VMEM)
SMEM_REF = pl.BlockSpec(memory_space=pltpu.SMEM)
ANY_REF = pl.BlockSpec(memory_space=pl.ANY)
PARAMS = pltpu.CompilerParams(vmem_limit_bytes=56 << 20)


def cost(flops, moved_bytes):
    return pl.CostEstimate(flops=flops, bytes_accessed=moved_bytes, transcendentals=0)


def halves_kernel(place, *refs):
    sems = refs[-1]
    count = (len(refs) - 1) // 3
    rows = refs[count].shape[0]
    copies = []
    for k, weight in enumerate(refs[:count]):
        for part in range(2):
            first = (place[0] if part == 0 else 1 - place[0]) * rows
            source = weight.at[pl.ds(pl.multiple_of(first, rows), rows)]
            target = refs[count + 2 * k + part]
            copies.append(pltpu.make_async_copy(source, target, sems.at[2 * k + part]))
    for copy in copies:
        copy.start()
    for copy in copies:
        copy.wait()


def weight_halves(place, weights):
    rows, columns = weights[0].shape
    out = jax.ShapeDtypeStruct((rows // 2, columns), weights[0].dtype)
    outs = pl.pallas_call(
        halves_kernel,
        in_specs=[SMEM_REF] + [ANY_REF] * len(weights),
        out_specs=[ANY_REF] * (2 * len(weights)),
        out_shape=[out] * (2 * len(weights)),
        scratch_shapes=[pltpu.SemaphoreType.DMA((2 * len(weights),))],
        compiler_params=PARAMS,
        cost_estimate=cost(1000, 1000),
        name="weight_halves",
    )(place, *weights)
    return [outs[2 * k : 2 * k + 2] for k in range(len(weights))]


def prepare_kernel(place, rows_in, token, mine, other):
    depth = mine.shape[2]
    wide = rows_in[...].astype(jnp.float32)
    scale = lax.rsqrt(jnp.mean(wide * wide, -1, keepdims=True) + 1e-05)
    for core in range(2):

        @pl.when(place[1] == core)
        def _():
            for j in range(mine.shape[0] // 2):
                for c in range(2):
                    target = mine if c == core else other
                    for h in range(2):
                        first = (4 * j + 2 * c + h) * depth
                        part = rows_in[:, first : first + depth].astype(jnp.float32)
                        target[2 * j + h] = (part * scale).astype(jnp.bfloat16)


def prepared(flat, place, token, blocks):
    rows, width = flat.shape
    depth = width // (4 * blocks)
    tile = 64 if rows % 64 == 0 else rows
    out = jax.ShapeDtypeStruct((2 * blocks, rows, depth), jnp.bfloat16)
    spec = pl.BlockSpec((2 * blocks, tile, depth), lambda i, place: (0, i, 0))
    return pl.pallas_call(
        prepare_kernel,
        grid_spec=pltpu.PrefetchScalarGridSpec(
            num_scalar_prefetch=1,
            grid=(rows // tile,),
            in_specs=[pl.BlockSpec((tile, width), lambda i, place: (i, 0)), ANY_REF],
            out_specs=[spec, spec],
        ),
        out_shape=[out, out],
        compiler_params=PARAMS,
        cost_estimate=cost(1 << 36, 4 * rows * width),
        name="normed_halves",
    )(place, flat, token)


def fetch(source, target, sem):
    copy = pltpu.make_async_copy(source, target, sem)
    copy.start()
    return copy


def product_kernel(plan, group, with_total, place, mine, other, *refs):
    count = len(plan)
    pieces = refs[:count]
    totals_in = refs[count : count + 2 * with_total]
    outs = refs[count + 2 * with_total : count + 2 * with_total + 2]
    left, right, total, sems, total_sems = refs[-5:]
    rows, depth = mine.shape[1], mine.shape[2]
    waits = []
    for k, (entry, flipped, first) in enumerate(plan):
        half = (1 - place[0]) if flipped == 1 else place[0]
        half = first // depth if flipped is None else half
        index = place[entry] * 2 + half
        area = pl.ds((k % group) * depth, depth)
        slot = k // group
        waits.append(
            [
                fetch(mine.at[index], left.at[slot, pl.ds(0, rows), area], sems.at[3 * k]),
                fetch(other.at[index], left.at[slot, pl.ds(rows, rows), area], sems.at[3 * k + 1]),
                fetch(pieces[k].at[pl.ds(first, depth)], right.at[slot, area], sems.at[3 * k + 2]),
            ]
        )
    carried = [
        fetch(ref, total.at[pl.ds(k * rows, rows)], total_sems.at[k])
        for k, ref in enumerate(totals_in)
    ]
    for slot in range(count // group):
        for copies in waits[slot * group : (slot + 1) * group]:
            for copy in copies:
                copy.wait()
        value = jnp.dot(left[slot], right[slot], preferred_element_type=jnp.float32)
        if slot == 0:
            for copy in carried:
                copy.wait()
        if slot or with_total:
            value += total[...]
        if slot + 1 < count // group:
            total[...] = value
        else:
            outs[0][...] = value[:rows]
            outs[1][...] = value[rows:]


def product(place, mine, other, plan, pieces, totals, group, token):
    _, rows, depth = mine.shape
    columns = pieces[0].shape[1]
    count = len(plan)
    out = jax.ShapeDtypeStruct((rows, columns), jnp.float32)

    def kernel(place_ref, token_ref, *refs):
        product_kernel(plan, group, len(totals) // 2, place_ref, *refs)

    return pl.pallas_call(
        kernel,
        in_specs=[SMEM_REF] + [ANY_REF] * (3 + count + len(totals)),
        out_specs=[VMEM_REF] * 2,
        out_shape=[out, out],
        scratch_shapes=[
            pltpu.VMEM((count // group, 2 * rows, group * depth), mine.dtype),
            pltpu.VMEM((count // group, group * depth, columns), mine.dtype),
            pltpu.VMEM((2 * rows, columns), jnp.float32),
            pltpu.SemaphoreType.DMA((3 * count,)),
            pltpu.SemaphoreType.DMA((2,)),
        ],
        compiler_params=PARAMS,
        cost_estimate=cost(64 * rows * columns * depth * count, 1 << 22),
        name="add_product",
    )(place, token, mine, other, *pieces, *totals)


def rows_kernel(plan, rotated, place, lengths, owner, mine, kept, *refs):
    count = len(plan)
    pieces = refs[: 2 * count]
    total_in, came_in = refs[2 * count : 2 * count + 2]
    turn = refs[2 * count + 2 : 4 * count]
    out, left, right, total, came, scratch, sems = refs[-7:]
    rows, depth = mine.shape[1], mine.shape[2]
    waits = [fetch(total_in, total, sems.at[0]), fetch(came_in, came, sems.at[1])]
    sem = 2
    for k in range(2 * count):
        entry, flipped, first = plan[k // 2]
        half = (1 - place[0]) if flipped else place[0]
        source = (mine, kept)[k % 2]
        area = pl.ds(k * depth, depth)
        waits.append(fetch(source.at[place[entry] * 2 + half], left.at[:, area], sems.at[sem]))
        waits.append(fetch(pieces[k], right.at[area], sems.at[sem + 1]))
        sem += 2
    for copy in waits:
        copy.wait()
    total[...] += came[...]
    total[...] += jnp.dot(left[...], right[...], preferred_element_type=jnp.float32)
    count_requests, count_rows = lengths.shape[0], scratch.shape[0]
    index = place[2] * count_rows + lax.broadcasted_iota(jnp.int32, scratch.shape, 0)
    for r in range(count_requests):
        live = index < lengths[r]
        for h in range(KEY_VALUE_HEADS):
            part = total[
                r * count_rows : (r + 1) * count_rows, h * HEAD_SIZE : (h + 1) * HEAD_SIZE
            ]
            if rotated:
                turned = jnp.concatenate([part[:, HEAD_SIZE // 2 :], part[:, : HEAD_SIZE // 2]], 1)
                part = part * turn[0][...] + turned * turn[1][...]
            scratch[...] = jnp.where(live, part, 0.0)
            peer = owner[r * KEY_VALUE_HEADS + h]
            for b in range(2):
                picked = scratch[pl.ds(b, count_rows // 2, stride=2), :]
                out[peer * 2 + b] = picked.astype(jnp.bfloat16)


def outgoing_rows(place, lengths, owner, mine, kept, plan, pieces, total, came, turn, token):
    _, rows, depth = mine.shape
    columns = total.shape[1]
    count = len(plan)
    count_rows = rows // lengths.shape[0]
    out = jax.ShapeDtypeStruct((owner.shape[0] * 2, count_rows // 2, HEAD_SIZE), jnp.bfloat16)

    def kernel(place_ref, lengths_ref, owner_ref, token_ref, *refs):
        rows_kernel(plan, bool(turn), place_ref, lengths_ref, owner_ref, *refs)

    operands = [mine, kept, *pieces, total, came]
    return pl.pallas_call(
        kernel,
        in_specs=[SMEM_REF] * 3
        + [ANY_REF] * (1 + len(operands))
        + [VMEM_REF] * len(turn),
        out_specs=VMEM_REF,
        out_shape=out,
        scratch_shapes=[
            pltpu.VMEM((rows, 2 * count * depth), mine.dtype),
            pltpu.VMEM((2 * count * depth, columns), mine.dtype),
            pltpu.VMEM((rows, columns), jnp.float32),
            pltpu.VMEM((rows, columns), jnp.float32),
            pltpu.VMEM((count_rows, HEAD_SIZE), jnp.float32),
            pltpu.SemaphoreType.DMA((2 + 4 * count,)),
        ],
        compiler_params=PARAMS,
        cost_estimate=cost(4 * rows * columns * depth * count, 1 << 22),
        name="cache_rows",
    )(place, lengths, owner, token, *operands, *turn)


HERE, THERE = 3, 7


def body(hidden, key_weight, value_weight, lengths, owner, dec_query, dec_key, dec_value):
    count_requests, count_rows, width = hidden.shape
    device_id = lax.axis_index("seq")
    group_id = lax.axis_index("groups")
    seq = lax.axis_size("seq")
    planned = seq == 16 and lax.axis_size("groups") == 2
    decode_peers = count_requests * KEY_VALUE_HEADS
    split_point = seq // decode_peers
    tree_levels = split_point.bit_length() - 1
    rows_per_peer = count_rows // split_point
    positions = device_id * count_rows + jnp.arange(count_rows, dtype=jnp.int32)
    total_rows = count_requests * count_rows
    flat = hidden.reshape(total_rows, width)
    if planned:
        core = device_id % 2
        z, y = device_id // 4, device_id // 2 % 2
        place = [group_id, core, device_id]
        place += [(z ^ bits) * 2 + y for bits in range(4)]
        place += [(z ^ bits) * 2 + 1 - y for bits in range(4)]
        place = jnp.stack([jnp.asarray(entry, jnp.int32) for entry in place])
    else:
        widened = flat.astype(jnp.float32)
        normed = (
            widened * lax.rsqrt(jnp.mean(widened * widened, -1, keepdims=True) + 1e-05)
        ).astype(jnp.bfloat16)

        def project(weight):
            whole = lax.all_gather(weight, "seq", axis=0, tiled=True)
            return jnp.dot(normed, whole, preferred_element_type=jnp.float32)

    pair_ids = jnp.arange(decode_peers, dtype=jnp.int32)
    matches = owner[None, :] == pair_ids[:, None]
    inverse_order = jnp.sum(jnp.where(matches, pair_ids[None, :], 0), axis=1)
    live_rows = positions[None, :] < lengths[:, None]

    def handed_over(rows):
        rows = jnp.where(live_rows[:, :, None, None], rows, jnp.zeros_like(rows))
        pair_rows = jnp.transpose(rows, (0, 2, 1, 3)).reshape(decode_peers, count_rows, HEAD_SIZE)
        sorted_rows = pair_rows[inverse_order].reshape(
            decode_peers, rows_per_peer, split_point, HEAD_SIZE
        )
        outgoing = jnp.transpose(sorted_rows, (0, 2, 1, 3)).reshape(
            decode_peers * split_point, rows_per_peer, HEAD_SIZE
        )
        return lax.all_to_all(outgoing, "seq", split_axis=0, concat_axis=1, tiled=True)[0]

    cosine, sine_part = rope_table(positions, HEAD_SIZE)
    if planned:
        turn = (
            jnp.concatenate([cosine, cosine], 1),
            jnp.concatenate([-sine_part, sine_part], 1),
        )
        weights = (key_weight, value_weight)
        halves = weight_halves(place, weights)
        near = [moved(half, along(1)) for half, _ in halves]
        across = [moved(half, to_row) for half, _ in halves]
        far = [[moved(half, along(bits)) for bits in (2, 3)] for half, _ in halves]
        near_rest = [moved(rest, along(1)) for _, rest in halves]
        mine, kept = prepared(flat, place, halves[0][0], seq // 2)
        other = moved(kept, to_core)
        across_x = [moved(block, to_group) for block in across]
        near_y = [moved(block, to_row) for block in near]
        near_xy = [moved(block, to_group) for block in near_y]
        far_y = [[moved(block, to_row) for block in blocks] for blocks in far]
        far_x = [[moved(block, to_group) for block in blocks] for blocks in far]
        depth = key_weight.shape[0] // 2
        early = [(HERE, None, 0), (HERE, None, depth), (THERE, 0, 0), (THERE, 1, 0)]
        early += [(HERE + 1, 0, 0), (HERE + 1, 1, 0), (THERE + 1, 0, 0), (THERE + 1, 1, 0)]
        late = [(HERE + 2, 0, 0), (HERE + 2, 1, 0), (HERE + 3, 0, 0), (HERE + 3, 1, 0)]
        late += [(THERE + 2, 0, 0), (THERE + 3, 0, 0)]
        last = [(THERE + 2, 1, 0), (THERE + 3, 1, 0)]
        caches = []
        token = key_weight
        for k, turned in enumerate((turn, ())):
            pieces = [weights[k], weights[k], across[k], across_x[k]]
            pieces += [near[k], near_rest[k], near_y[k], near_xy[k]]
            totals = product(place, mine, other, early, pieces, (), 4, place)
            pieces = [far[k][0], far_x[k][0], far[k][1], far_x[k][1], *far_y[k]]
            total, sent = product(place, mine, other, late, pieces, totals, 6, place)
            came = moved(sent, to_core)
            ends = [moved(far_y[k][0], to_group), moved(far_x[k][1], to_row)]
            pieces = [piece for end in ends for piece in (end, moved(end, to_core))]
            outgoing = outgoing_rows(
                place, lengths, owner, mine, kept, last, pieces, total, came, turned, token
            )
            caches.append(
                lax.all_to_all(outgoing, "seq", split_axis=0, concat_axis=1, tiled=True)[0]
            )
            token = caches[0]
        cache_keys, cache_values = caches
    else:
        shape = (count_requests, count_rows, KEY_VALUE_HEADS, HEAD_SIZE)
        unrotated_key = project(key_weight).reshape(shape)
        key_rows = rotate(
            unrotated_key, cosine[:, None, :], sine_part[:, None, :]
        ).astype(jnp.bfloat16)
        cache_keys = handed_over(key_rows)
        cache_values = handed_over(project(value_weight).astype(jnp.bfloat16).reshape(shape))
    slot_count = cache_keys.shape[0]
    decode_peer = device_id // split_point
    block = device_id % split_point
    source_pair = jnp.sum(jnp.where(owner == decode_peer, pair_ids, 0))
    source_request = source_pair // KEY_VALUE_HEADS
    length = jnp.sum(
        jnp.where(jnp.arange(count_requests, dtype=jnp.int32) == source_request, lengths, 0)
    )
    query = lax.dynamic_index_in_dim(dec_query, decode_peer, 0, keepdims=False)
    new_key = lax.dynamic_index_in_dim(dec_key, decode_peer, 0, keepdims=False)
    new_value = lax.dynamic_index_in_dim(dec_value, decode_peer, 0, keepdims=False)
    step_pos = length + jnp.arange(STEPS, dtype=jnp.int32)
    step_cos, step_sin = rope_table(step_pos, HEAD_SIZE)
    query_rot = rotate(
        query.astype(jnp.float32).reshape(STEPS, QPK, HEAD_SIZE),
        step_cos[:, None, :],
        step_sin[:, None, :],
    ).astype(jnp.bfloat16)
    new_keys = rotate(new_key.astype(jnp.float32), step_cos, step_sin).astype(jnp.bfloat16)
    score_scale = 1.0 / HEAD_SIZE**0.5
    old_scores = (
        jnp.einsum(
            "sjd,id->sji", query_rot, cache_keys, preferred_element_type=jnp.float32
        )
        * score_scale
    )
    new_scores = (
        jnp.einsum("sjd,td->sjt", query_rot, new_keys, preferred_element_type=jnp.float32)
        * score_scale
    )
    slot_ids = jnp.arange(slot_count, dtype=jnp.int32) * split_point + block
    old_live = slot_ids < length
    new_live = (jnp.arange(STEPS)[None, :] <= jnp.arange(STEPS)[:, None]) & (block == 0)
    old_scores = jnp.where(old_live[None, None, :], old_scores, -1e30)
    new_scores = jnp.where(new_live[:, None, :], new_scores, -1e30)
    row_max = jnp.maximum(jnp.max(old_scores, -1), jnp.max(new_scores, -1))
    for bit in range(tree_levels):
        row_max = jnp.maximum(row_max, swapped(row_max, "seq", bit))
    old_exp = jnp.exp(old_scores - row_max[..., None])
    new_exp = jnp.exp(new_scores - row_max[..., None])
    denom = jnp.sum(old_exp, -1) + jnp.sum(new_exp, -1)
    for bit in range(tree_levels):
        denom = denom + swapped(denom, "seq", bit)
    old_probs = (old_exp / denom[..., None]).astype(jnp.bfloat16)
    new_probs = (new_exp / denom[..., None]).astype(jnp.bfloat16)
    partial_sum = jnp.einsum(
        "sji,id->sjd", old_probs, cache_values, preferred_element_type=jnp.float32
    )
    partial_sum = partial_sum + jnp.einsum(
        "sjt,td->sjd", new_probs, new_value, preferred_element_type=jnp.float32
    )
    flat_rows = partial_sum.reshape(STEPS, QPK * HEAD_SIZE)
    for bit in range(tree_levels):
        flat_rows = flat_rows + swapped(flat_rows, "seq", bit)
    share = flat_rows.shape[1] // split_point
    mine = lax.dynamic_slice_in_dim(flat_rows, block * share, share, 1)
    cache = jnp.concatenate([cache_keys, cache_values], 1)[None]
    return (cache, mine.astype(jnp.bfloat16))


def solution(mesh):
    placed = (
        P("groups", "seq", None),
        P("seq", None),
        P("seq", None),
        P("groups"),
        P("groups"),
        P("groups", None, None),
        P("groups", None, None),
        P("groups", None, None),
    )
    return jax.shard_map(
        body,
        mesh=mesh,
        in_specs=placed,
        out_specs=(P(("groups", "seq"), None, None), P("groups", "seq")),
        check_vma=False,
    )
```

```python
import functools

import jax
import jax.numpy as jnp
import numpy as np
from jax import lax
from jax.experimental import pallas as pl
from jax.experimental.pallas import tpu as pltpu
from jax.sharding import PartitionSpec as P

HEAD_SIZE = 128
KEY_VALUE_HEADS = 4
QPK = 8
STEPS = 4


ROPE_BASE = 500000.0


def swapped(block, axis, bit):
    count = lax.axis_size(axis)
    route = []
    for low in range(count):
        high = low | 1 << bit
        if high != low and high < count:
            route += [(low, high), (high, low)]
    return lax.ppermute(block, axis, route)


def rope_table(positions, head_dim):
    freq = ROPE_BASE ** (-(np.arange(head_dim // 2, dtype=np.float64) * 2.0) / head_dim)
    angle = positions.astype(jnp.float32)[:, None] * jnp.asarray(freq, jnp.float32)[None, :]
    return (jnp.cos(angle), jnp.sin(angle))


def rotate(values_in, cosine, sine_part):
    half_dim = values_in.shape[-1] // 2
    lower_half = values_in[..., :half_dim]
    upper_half = values_in[..., half_dim:]
    return jnp.concatenate(
        [
            lower_half * cosine - upper_half * sine_part,
            upper_half * cosine + lower_half * sine_part,
        ],
        -1,
    )


def swapped_core(block):
    count = lax.axis_size("seq")
    return lax.ppermute(block, "seq", [(i, i ^ 1) for i in range(count)])


def plane_gather(block):
    groups, seq = lax.axis_size("groups"), lax.axis_size("seq")
    planes = [[d for d in range(groups * seq) if d % 2 == core] for core in range(2)]
    return lax.all_gather(
        block, ("groups", "seq"), axis=0, tiled=True, axis_index_groups=planes
    )


VMEM_REF = pl.BlockSpec(memory_space=pltpu.VMEM)
SMEM_REF = pl.BlockSpec(memory_space=pltpu.SMEM)
ANY_REF = pl.BlockSpec(memory_space=pl.ANY)
PARAMS = pltpu.CompilerParams(vmem_limit_bytes=56 << 20)


def cost(flops, moved_bytes):
    return pl.CostEstimate(flops=flops, bytes_accessed=moved_bytes, transcendentals=0)


def whole_block(array):
    return pl.BlockSpec(array.shape, lambda *_: (0,) * array.ndim)


def prepare_kernel(place, rows_in, mine, other):
    steps, rows, depth = mine.shape
    half = depth // 2
    width = rows_in.shape[1]
    square = jnp.zeros((rows, half), jnp.float32)
    for first in range(0, width, half):
        part = rows_in[:, first : first + half].astype(jnp.float32)
        square += part * part
    scale = lax.rsqrt(jnp.sum(square, -1, keepdims=True) / width + 1e-05)
    for core in range(2):

        @pl.when(place[0] == core)
        def _():
            for first in range(0, width, half):
                j, c, h = first // (2 * depth), first // depth % 2, first // half % 2
                spot = h * steps + j
                target = mine if c == core else other
                part = rows_in[:, first : first + half].astype(jnp.float32)
                target[spot // 2, :, (spot % 2) * half : (spot % 2 + 1) * half] = (
                    part * scale
                ).astype(jnp.bfloat16)


def prepared(flat, place, steps):
    rows, width = flat.shape
    depth = width // (2 * steps)
    tile = 32 if rows % 32 == 0 else rows
    out = jax.ShapeDtypeStruct((steps, rows, depth), jnp.bfloat16)
    spec = pl.BlockSpec((steps, tile, depth), lambda i, place: (0, i, 0))
    return pl.pallas_call(
        prepare_kernel,
        grid_spec=pltpu.PrefetchScalarGridSpec(
            num_scalar_prefetch=1,
            grid=(rows // tile,),
            in_specs=[pl.BlockSpec((tile, width), lambda i, place: (i, 0))],
            out_specs=[spec, spec],
        ),
        out_shape=[out, out],
        compiler_params=PARAMS,
        cost_estimate=cost(8 * rows * width, 4 * rows * width),
        name="normed_halves",
    )(place, flat)


def product_kernel(token, mine, other, weight, *totals):
    for left, total in zip((mine, other), totals):
        part = jnp.dot(left[0], weight[...], preferred_element_type=jnp.float32)

        @pl.when(pl.program_id(0) == 0)
        def _():
            total[...] = part

        @pl.when(pl.program_id(0) > 0)
        def _():
            total[...] += part


def product(mine, other, weight, token):
    steps, rows, depth = mine.shape
    columns = weight.shape[1]
    out = jax.ShapeDtypeStruct((rows, columns), jnp.float32)
    left = pl.BlockSpec((1, rows, depth), lambda i: (i, 0, 0))
    return pl.pallas_call(
        product_kernel,
        grid=(steps,),
        in_specs=[ANY_REF, left, left, pl.BlockSpec((depth, columns), lambda i: (i, 0))],
        out_specs=[whole_block(out)] * 2,
        out_shape=[out, out],
        compiler_params=PARAMS,
        cost_estimate=cost(4 * rows * columns * depth * steps, 1 << 22),
        name="product",
    )(token, mine, other, weight)


def rows_kernel(rotated, place, lengths, owner, *refs):
    out, scratch = refs[-2:]
    total, came = refs[:2]
    count_requests, count_rows = lengths.shape[0], scratch.shape[0]
    first = place[0] * count_rows
    index = first + lax.broadcasted_iota(jnp.int32, scratch.shape, 0)
    for r in range(count_requests):
        live = index < lengths[r]
        for h in range(KEY_VALUE_HEADS):
            area = (
                slice(r * count_rows, (r + 1) * count_rows),
                slice(h * HEAD_SIZE, (h + 1) * HEAD_SIZE),
            )
            rows = total[area] + came[area]
            if rotated:
                turned = jnp.concatenate([rows[:, HEAD_SIZE // 2 :], rows[:, : HEAD_SIZE // 2]], 1)
                rows = rows * refs[2][...] + turned * refs[3][...]
            scratch[...] = jnp.where(live, rows, 0.0)
            peer = owner[r * KEY_VALUE_HEADS + h]
            for b in range(2):
                picked = scratch[pl.ds(b, count_rows // 2, stride=2), :]
                out[peer * 2 + b] = picked.astype(jnp.bfloat16)


def outgoing_rows(total, came, place, lengths, owner, turn):
    count_rows = total.shape[0] // lengths.shape[0]
    operands = [total, came, *turn]
    peers = owner.shape[0] * 2
    out = jax.ShapeDtypeStruct((peers, count_rows // 2, HEAD_SIZE), jnp.bfloat16)
    return pl.pallas_call(
        functools.partial(rows_kernel, bool(turn)),
        grid_spec=pltpu.PrefetchScalarGridSpec(
            num_scalar_prefetch=3,
            grid=(1,),
            in_specs=[whole_block(x) for x in operands],
            out_specs=whole_block(out),
            scratch_shapes=[pltpu.VMEM((count_rows, HEAD_SIZE), jnp.float32)],
        ),
        out_shape=out,
        compiler_params=pltpu.CompilerParams(vmem_limit_bytes=56 << 20),
        cost_estimate=cost(1 << 20, 1 << 21),
        name="cache_rows",
    )(place, lengths, owner, *operands)


def body(hidden, key_weight, value_weight, lengths, owner, dec_query, dec_key, dec_value):
    count_requests, count_rows, width = hidden.shape
    device_id = lax.axis_index("seq")
    group_id = lax.axis_index("groups")
    seq = lax.axis_size("seq")
    planned = seq == 16 and lax.axis_size("groups") == 2
    decode_peers = count_requests * KEY_VALUE_HEADS
    split_point = seq // decode_peers
    tree_levels = split_point.bit_length() - 1
    rows_per_peer = count_rows // split_point
    positions = device_id * count_rows + jnp.arange(count_rows, dtype=jnp.int32)
    total_rows = count_requests * count_rows
    flat = hidden.reshape(total_rows, width)
    if not planned:
        widened = flat.astype(jnp.float32)
        normed = (
            widened * lax.rsqrt(jnp.mean(widened * widened, -1, keepdims=True) + 1e-05)
        ).astype(jnp.bfloat16)

        def project(weight):
            whole = lax.all_gather(weight, "seq", axis=0, tiled=True)
            return jnp.dot(normed, whole, preferred_element_type=jnp.float32)

    pair_ids = jnp.arange(decode_peers, dtype=jnp.int32)
    matches = owner[None, :] == pair_ids[:, None]
    inverse_order = jnp.sum(jnp.where(matches, pair_ids[None, :], 0), axis=1)
    live_rows = positions[None, :] < lengths[:, None]

    def handed_over(rows):
        rows = jnp.where(live_rows[:, :, None, None], rows, jnp.zeros_like(rows))
        pair_rows = jnp.transpose(rows, (0, 2, 1, 3)).reshape(decode_peers, count_rows, HEAD_SIZE)
        sorted_rows = pair_rows[inverse_order].reshape(
            decode_peers, rows_per_peer, split_point, HEAD_SIZE
        )
        outgoing = jnp.transpose(sorted_rows, (0, 2, 1, 3)).reshape(
            decode_peers * split_point, rows_per_peer, HEAD_SIZE
        )
        return lax.all_to_all(outgoing, "seq", split_axis=0, concat_axis=1, tiled=True)[0]

    cosine, sine_part = rope_table(positions, HEAD_SIZE)
    if planned:
        turn = (
            jnp.concatenate([cosine, cosine], 1),
            jnp.concatenate([-sine_part, sine_part], 1),
        )
        depth = key_weight.shape[0] // 2
        halves = [
            lax.dynamic_slice_in_dim(weight, group_id * depth, depth, 0)
            for weight in (key_weight, value_weight)
        ]
        gathered = [plane_gather(half) for half in halves]
        mine, kept = prepared(flat, (device_id % 2).reshape(1), seq // 2)
        other = swapped_core(kept)
        caches = []
        token = mine
        for weight, turned in zip(gathered, (turn, ())):
            total, sent = product(mine, other, weight, token)
            outgoing = outgoing_rows(
                total, swapped_core(sent), device_id.reshape(1), lengths, owner, turned
            )
            caches.append(
                lax.all_to_all(outgoing, "seq", split_axis=0, concat_axis=1, tiled=True)[0]
            )
            token = caches[0]
        cache_keys, cache_values = caches
    else:
        shape = (count_requests, count_rows, KEY_VALUE_HEADS, HEAD_SIZE)
        unrotated_key = project(key_weight).reshape(shape)
        key_rows = rotate(
            unrotated_key, cosine[:, None, :], sine_part[:, None, :]
        ).astype(jnp.bfloat16)
        cache_keys = handed_over(key_rows)
        cache_values = handed_over(project(value_weight).astype(jnp.bfloat16).reshape(shape))
    slot_count = cache_keys.shape[0]
    decode_peer = device_id // split_point
    block = device_id % split_point
    source_pair = jnp.sum(jnp.where(owner == decode_peer, pair_ids, 0))
    source_request = source_pair // KEY_VALUE_HEADS
    length = jnp.sum(
        jnp.where(jnp.arange(count_requests, dtype=jnp.int32) == source_request, lengths, 0)
    )
    query = lax.dynamic_index_in_dim(dec_query, decode_peer, 0, keepdims=False)
    new_key = lax.dynamic_index_in_dim(dec_key, decode_peer, 0, keepdims=False)
    new_value = lax.dynamic_index_in_dim(dec_value, decode_peer, 0, keepdims=False)
    step_pos = length + jnp.arange(STEPS, dtype=jnp.int32)
    step_cos, step_sin = rope_table(step_pos, HEAD_SIZE)
    query_rot = rotate(
        query.astype(jnp.float32).reshape(STEPS, QPK, HEAD_SIZE),
        step_cos[:, None, :],
        step_sin[:, None, :],
    ).astype(jnp.bfloat16)
    new_keys = rotate(new_key.astype(jnp.float32), step_cos, step_sin).astype(jnp.bfloat16)
    score_scale = 1.0 / HEAD_SIZE**0.5
    old_scores = (
        jnp.einsum(
            "sjd,id->sji", query_rot, cache_keys, preferred_element_type=jnp.float32
        )
        * score_scale
    )
    new_scores = (
        jnp.einsum("sjd,td->sjt", query_rot, new_keys, preferred_element_type=jnp.float32)
        * score_scale
    )
    slot_ids = jnp.arange(slot_count, dtype=jnp.int32) * split_point + block
    old_live = slot_ids < length
    new_live = (jnp.arange(STEPS)[None, :] <= jnp.arange(STEPS)[:, None]) & (block == 0)
    old_scores = jnp.where(old_live[None, None, :], old_scores, -1e30)
    new_scores = jnp.where(new_live[:, None, :], new_scores, -1e30)
    row_max = jnp.maximum(jnp.max(old_scores, -1), jnp.max(new_scores, -1))
    for bit in range(tree_levels):
        row_max = jnp.maximum(row_max, swapped(row_max, "seq", bit))
    old_exp = jnp.exp(old_scores - row_max[..., None])
    new_exp = jnp.exp(new_scores - row_max[..., None])
    denom = jnp.sum(old_exp, -1) + jnp.sum(new_exp, -1)
    for bit in range(tree_levels):
        denom = denom + swapped(denom, "seq", bit)
    old_probs = (old_exp / denom[..., None]).astype(jnp.bfloat16)
    new_probs = (new_exp / denom[..., None]).astype(jnp.bfloat16)
    partial_sum = jnp.einsum(
        "sji,id->sjd", old_probs, cache_values, preferred_element_type=jnp.float32
    )
    partial_sum = partial_sum + jnp.einsum(
        "sjt,td->sjd", new_probs, new_value, preferred_element_type=jnp.float32
    )
    flat_rows = partial_sum.reshape(STEPS, QPK * HEAD_SIZE)
    for bit in range(tree_levels):
        flat_rows = flat_rows + swapped(flat_rows, "seq", bit)
    share = flat_rows.shape[1] // split_point
    mine = lax.dynamic_slice_in_dim(flat_rows, block * share, share, 1)
    cache = jnp.concatenate([cache_keys, cache_values], 1)[None]
    return (cache, mine.astype(jnp.bfloat16))


def solution(mesh):
    placed = (
        P("groups", "seq", None),
        P("seq", None),
        P("seq", None),
        P("groups"),
        P("groups"),
        P("groups", None, None),
        P("groups", None, None),
        P("groups", None, None),
    )
    return jax.shard_map(
        body,
        mesh=mesh,
        in_specs=placed,
        out_specs=(P(("groups", "seq"), None, None), P("groups", "seq")),
        check_vma=False,
    )
```

```python
import functools

import jax
import jax.numpy as jnp
import numpy as np
from jax import lax
from jax.experimental import pallas as pl
from jax.experimental.pallas import tpu as pltpu
from jax.sharding import PartitionSpec as P

HEAD_SIZE = 128
KEY_VALUE_HEADS = 4
QPK = 8
STEPS = 4


ROPE_BASE = 500000.0


def swapped(block, axis, bit):
    count = lax.axis_size(axis)
    route = []
    for low in range(count):
        high = low | 1 << bit
        if high != low and high < count:
            route += [(low, high), (high, low)]
    return lax.ppermute(block, axis, route)


def rope_table(positions, head_dim):
    freq = ROPE_BASE ** (-(np.arange(head_dim // 2, dtype=np.float64) * 2.0) / head_dim)
    angle = positions.astype(jnp.float32)[:, None] * jnp.asarray(freq, jnp.float32)[None, :]
    return (jnp.cos(angle), jnp.sin(angle))


def rotate(values_in, cosine, sine_part):
    half_dim = values_in.shape[-1] // 2
    lower_half = values_in[..., :half_dim]
    upper_half = values_in[..., half_dim:]
    return jnp.concatenate(
        [
            lower_half * cosine - upper_half * sine_part,
            upper_half * cosine + lower_half * sine_part,
        ],
        -1,
    )


def spread(count):
    side = 1
    while side * side < count:
        side *= 2
    return (side, count // side)


def moved(block, rule):
    groups, seq = lax.axis_size("groups"), lax.axis_size("seq")
    low = spread(seq // 2)[1]
    route = []
    for g in range(groups):
        for s in range(seq):
            tg, tz, ty, tc = rule(g, s // 2 // low, s // 2 % low, s % 2)
            route.append((g * seq + s, tg * seq + (tz * low + ty) * 2 + tc))
    return lax.ppermute(block, ("groups", "seq"), route)


def to_core(g, z, y, c):
    return (g, z, y, 1 - c)


def to_row(g, z, y, c):
    return (g, z, 1 - y, c)


def to_group(g, z, y, c):
    return (1 - g, z, y, c)


def along(bits):
    return lambda g, z, y, c: (g, z ^ bits, y, c)


VMEM_REF = pl.BlockSpec(memory_space=pltpu.VMEM)
SMEM_REF = pl.BlockSpec(memory_space=pltpu.SMEM)
ANY_REF = pl.BlockSpec(memory_space=pl.ANY)
PARAMS = pltpu.CompilerParams(vmem_limit_bytes=56 << 20)


def cost(flops, moved_bytes):
    return pl.CostEstimate(flops=flops, bytes_accessed=moved_bytes, transcendentals=0)


def halves_kernel(place, key_sent, value_sent, key_rest, value_rest, sent, rest, key, value):
    columns = key.shape[1]
    key[...] = key_sent[...]
    value[...] = value_sent[...]
    sent[:, :columns] = key_sent[...]
    sent[:, columns:] = value_sent[...]
    rest[:, :columns] = key_rest[...]
    rest[:, columns:] = value_rest[...]


def weight_halves(place, key_weight, value_weight):
    rows, columns = key_weight.shape
    depth = rows // 2
    both = jax.ShapeDtypeStruct((depth, 2 * columns), key_weight.dtype)
    one = jax.ShapeDtypeStruct((depth, columns), key_weight.dtype)
    sent = pl.BlockSpec((depth, columns), lambda i, place: (place[0], 0))
    rest = pl.BlockSpec((depth, columns), lambda i, place: (1 - place[0], 0))
    return pl.pallas_call(
        halves_kernel,
        grid_spec=pltpu.PrefetchScalarGridSpec(
            num_scalar_prefetch=1,
            grid=(1,),
            in_specs=[sent, sent, rest, rest],
            out_specs=[
                pl.BlockSpec(out.shape, lambda i, place: (0, 0)) for out in (both, both, one, one)
            ],
        ),
        out_shape=[both, both, one, one],
        compiler_params=PARAMS,
        cost_estimate=cost(1000, 1000),
        name="weight_halves",
    )(place, key_weight, value_weight, key_weight, value_weight)


def prepare_kernel(place, rows_in, token, mine, other):
    rows, depth = mine.shape[1], mine.shape[2]
    width = rows_in.shape[1]
    square = jnp.zeros((rows, depth), jnp.float32)
    for first in range(0, width, depth):
        part = rows_in[:, first : first + depth].astype(jnp.float32)
        square += part * part
    scale = lax.rsqrt(jnp.sum(square, -1, keepdims=True) / width + 1e-05)
    for core in range(2):

        @pl.when(place[1] == core)
        def _():
            for first in range(0, width, depth):
                j, c, h = first // (4 * depth), first // (2 * depth) % 2, first // depth % 2
                target = mine if c == core else other
                part = rows_in[:, first : first + depth].astype(jnp.float32)
                target[2 * j + h] = (part * scale).astype(jnp.bfloat16)


def prepared(flat, place, token, blocks):
    rows, width = flat.shape
    depth = width // (4 * blocks)
    tile = 80 if rows % 80 == 0 else rows
    out = jax.ShapeDtypeStruct((2 * blocks, rows, depth), jnp.bfloat16)
    spec = pl.BlockSpec((2 * blocks, tile, depth), lambda i, place: (0, i, 0))
    return pl.pallas_call(
        prepare_kernel,
        grid_spec=pltpu.PrefetchScalarGridSpec(
            num_scalar_prefetch=1,
            grid=(rows // tile,),
            in_specs=[pl.BlockSpec((tile, width), lambda i, place: (i, 0)), ANY_REF],
            out_specs=[spec, spec],
        ),
        out_shape=[out, out],
        compiler_params=PARAMS,
        cost_estimate=cost(1000, 1000),
        name="normed_halves",
    )(place, flat, token)


def fetch(source, target, sem):
    copy = pltpu.make_async_copy(source, target, sem)
    copy.start()
    return copy


def product_kernel(plan, group, parts, with_total, place, mine, other, *refs):
    count = len(plan)
    pieces = refs[:count]
    totals_in = refs[count : count + 2 * parts * with_total]
    outs = refs[len(refs) - 5 - 2 * parts : len(refs) - 5]
    left, right, total, sems, total_sems = refs[-5:]
    rows, depth = mine.shape[1], mine.shape[2]
    columns = pieces[0].shape[1] // parts
    waits = []
    for k, (entry, flipped) in enumerate(plan):
        half = (1 - place[0]) if flipped else place[0]
        index = place[entry] * 2 + half
        area = pl.ds((k % group) * depth, depth)
        slot = k // group
        waits.append(
            [
                fetch(mine.at[index], left.at[slot, pl.ds(0, rows), area], sems.at[3 * k]),
                fetch(other.at[index], left.at[slot, pl.ds(rows, rows), area], sems.at[3 * k + 1]),
                fetch(pieces[k], right.at[slot, area], sems.at[3 * k + 2]),
            ]
        )
    carried = [
        fetch(ref, total.at[pl.ds(k * rows, rows)], total_sems.at[k])
        for k, ref in enumerate(totals_in)
    ]
    for slot in range(count // group):
        for copies in waits[slot * group : (slot + 1) * group]:
            for copy in copies:
                copy.wait()
        value = jnp.dot(left[slot], right[slot], preferred_element_type=jnp.float32)
        if slot == 0:
            for copy in carried:
                copy.wait()
        if slot or with_total:
            value += total[...]
        if slot + 1 < count // group:
            total[...] = value
        else:
            for k, out in enumerate(outs):
                area = slice(k // 2 * columns, (k // 2 + 1) * columns)
                out[...] = value[k % 2 * rows : (k % 2 + 1) * rows, area]


def product(place, mine, other, plan, pieces, totals, group, parts):
    _, rows, depth = mine.shape
    columns = pieces[0].shape[1]
    count = len(plan)
    out = jax.ShapeDtypeStruct((rows, columns // parts), jnp.float32)
    return pl.pallas_call(
        functools.partial(product_kernel, plan, group, parts, bool(totals)),
        in_specs=[SMEM_REF] + [ANY_REF] * (2 + count + len(totals)),
        out_specs=[VMEM_REF] * (2 * parts),
        out_shape=[out] * (2 * parts),
        scratch_shapes=[
            pltpu.VMEM((count // group, 2 * rows, group * depth), mine.dtype),
            pltpu.VMEM((count // group, group * depth, columns), mine.dtype),
            pltpu.VMEM((2 * rows, columns), jnp.float32),
            pltpu.SemaphoreType.DMA((3 * count,)),
            pltpu.SemaphoreType.DMA((2,)),
        ],
        compiler_params=PARAMS,
        cost_estimate=cost(1000, 1000),
        name="add_product",
    )(place, mine, other, *pieces, *totals)


def rows_kernel(plan, rotated, place, lengths, owner, mine, kept, *refs):
    count = len(plan)
    pieces = refs[: 2 * count]
    total_in, came_in = refs[2 * count : 2 * count + 2]
    turn = refs[2 * count + 2 : 4 * count]
    out, left, right, total, came, scratch, sems = refs[-7:]
    rows, depth = mine.shape[1], mine.shape[2]
    waits = [fetch(total_in, total, sems.at[0]), fetch(came_in, came, sems.at[1])]
    sem = 2
    for k in range(2 * count):
        entry, flipped = plan[k // 2]
        half = (1 - place[0]) if flipped else place[0]
        source = (mine, kept)[k % 2]
        area = pl.ds(k * depth, depth)
        waits.append(fetch(source.at[place[entry] * 2 + half], left.at[:, area], sems.at[sem]))
        waits.append(fetch(pieces[k], right.at[area], sems.at[sem + 1]))
        sem += 2
    for copy in waits:
        copy.wait()
    total[...] += came[...]
    total[...] += jnp.dot(left[...], right[...], preferred_element_type=jnp.float32)
    count_requests, count_rows = lengths.shape[0], scratch.shape[0]
    index = place[2] * count_rows + lax.broadcasted_iota(jnp.int32, scratch.shape, 0)
    for r in range(count_requests):
        live = index < lengths[r]
        for h in range(KEY_VALUE_HEADS):
            part = total[
                r * count_rows : (r + 1) * count_rows, h * HEAD_SIZE : (h + 1) * HEAD_SIZE
            ]
            if rotated:
                turned = jnp.concatenate([part[:, HEAD_SIZE // 2 :], part[:, : HEAD_SIZE // 2]], 1)
                part = part * turn[0][...] + turned * turn[1][...]
            scratch[...] = jnp.where(live, part, 0.0)
            peer = owner[r * KEY_VALUE_HEADS + h]
            for b in range(2):
                picked = scratch[pl.ds(b, count_rows // 2, stride=2), :]
                out[peer * 2 + b] = picked.astype(jnp.bfloat16)


def outgoing_rows(place, lengths, owner, mine, kept, plan, pieces, total, came, turn, token):
    _, rows, depth = mine.shape
    columns = total.shape[1]
    count = len(plan)
    count_rows = rows // lengths.shape[0]
    out = jax.ShapeDtypeStruct((owner.shape[0] * 2, count_rows // 2, HEAD_SIZE), jnp.bfloat16)

    def kernel(place_ref, lengths_ref, owner_ref, token_ref, *refs):
        rows_kernel(plan, bool(turn), place_ref, lengths_ref, owner_ref, *refs)

    operands = [mine, kept, *pieces, total, came]
    return pl.pallas_call(
        kernel,
        in_specs=[SMEM_REF] * 3
        + [ANY_REF] * (1 + len(operands))
        + [VMEM_REF] * len(turn),
        out_specs=VMEM_REF,
        out_shape=out,
        scratch_shapes=[
            pltpu.VMEM((rows, 2 * count * depth), mine.dtype),
            pltpu.VMEM((2 * count * depth, columns), mine.dtype),
            pltpu.VMEM((rows, columns), jnp.float32),
            pltpu.VMEM((rows, columns), jnp.float32),
            pltpu.VMEM((count_rows, HEAD_SIZE), jnp.float32),
            pltpu.SemaphoreType.DMA((2 + 4 * count,)),
        ],
        compiler_params=PARAMS,
        cost_estimate=cost(1000, 1000),
        name="cache_rows",
    )(place, lengths, owner, token, *operands, *turn)


HERE, THERE = 3, 7


def body(hidden, key_weight, value_weight, lengths, owner, dec_query, dec_key, dec_value):
    count_requests, count_rows, width = hidden.shape
    device_id = lax.axis_index("seq")
    group_id = lax.axis_index("groups")
    seq = lax.axis_size("seq")
    planned = seq == 16 and lax.axis_size("groups") == 2
    decode_peers = count_requests * KEY_VALUE_HEADS
    split_point = seq // decode_peers
    tree_levels = split_point.bit_length() - 1
    rows_per_peer = count_rows // split_point
    positions = device_id * count_rows + jnp.arange(count_rows, dtype=jnp.int32)
    total_rows = count_requests * count_rows
    flat = hidden.reshape(total_rows, width)
    if planned:
        core = device_id % 2
        z, y = device_id // 4, device_id // 2 % 2
        place = [group_id, core, device_id]
        place += [(z ^ bits) * 2 + y for bits in range(4)]
        place += [(z ^ bits) * 2 + 1 - y for bits in range(4)]
        place = jnp.stack([jnp.asarray(entry, jnp.int32) for entry in place])
    else:
        widened = flat.astype(jnp.float32)
        normed = (
            widened * lax.rsqrt(jnp.mean(widened * widened, -1, keepdims=True) + 1e-05)
        ).astype(jnp.bfloat16)

        def project(weight):
            whole = lax.all_gather(weight, "seq", axis=0, tiled=True)
            return jnp.dot(normed, whole, preferred_element_type=jnp.float32)

    pair_ids = jnp.arange(decode_peers, dtype=jnp.int32)
    matches = owner[None, :] == pair_ids[:, None]
    inverse_order = jnp.sum(jnp.where(matches, pair_ids[None, :], 0), axis=1)
    live_rows = positions[None, :] < lengths[:, None]

    def handed_over(rows):
        rows = jnp.where(live_rows[:, :, None, None], rows, jnp.zeros_like(rows))
        pair_rows = jnp.transpose(rows, (0, 2, 1, 3)).reshape(decode_peers, count_rows, HEAD_SIZE)
        sorted_rows = pair_rows[inverse_order].reshape(
            decode_peers, rows_per_peer, split_point, HEAD_SIZE
        )
        outgoing = jnp.transpose(sorted_rows, (0, 2, 1, 3)).reshape(
            decode_peers * split_point, rows_per_peer, HEAD_SIZE
        )
        return lax.all_to_all(outgoing, "seq", split_axis=0, concat_axis=1, tiled=True)[0]

    cosine, sine_part = rope_table(positions, HEAD_SIZE)
    if planned:
        turn = (
            jnp.concatenate([cosine, cosine], 1),
            jnp.concatenate([-sine_part, sine_part], 1),
        )
        sent, rest, *alone = weight_halves(place, key_weight, value_weight)
        near = moved(sent, along(1))
        across = moved(sent, to_row)
        far = [[moved(half, along(bits)) for bits in (2, 3)] for half in alone]
        mine, kept = prepared(flat, place, sent, seq // 2)
        other = moved(kept, to_core)
        near_rest = moved(rest, along(1))
        across_x = moved(across, to_group)
        near_y = moved(near, to_row)
        near_xy = moved(near_y, to_group)
        early = [(HERE, 0), (HERE, 1), (THERE, 0), (THERE, 1)]
        early += [(HERE + 1, 0), (HERE + 1, 1), (THERE + 1, 0), (THERE + 1, 1)]
        late = [(HERE + 2, 0), (HERE + 2, 1), (HERE + 3, 0), (HERE + 3, 1)]
        late += [(THERE + 2, 0), (THERE + 3, 0)]
        last = [(THERE + 2, 1), (THERE + 3, 1)]
        pieces = [sent, rest, across, across_x, near, near_rest, near_y, near_xy]
        totals = product(place, mine, other, early, pieces, (), 4, 2)
        caches = []
        token = sent
        for k, turned in enumerate((turn, ())):
            far_y = [moved(block, to_row) for block in far[k]]
            far_x = [moved(block, to_group) for block in far[k]]
            pieces = [far[k][0], far_x[0], far[k][1], far_x[1], *far_y]
            total, given = product(
                place, mine, other, late, pieces, totals[2 * k : 2 * k + 2], 6, 1
            )
            came = moved(given, to_core)
            ends = [moved(far_y[0], to_group), moved(far_x[1], to_row)]
            pieces = [piece for end in ends for piece in (end, moved(end, to_core))]
            outgoing = outgoing_rows(
                place, lengths, owner, mine, kept, last, pieces, total, came, turned, token
            )
            caches.append(
                lax.all_to_all(outgoing, "seq", split_axis=0, concat_axis=1, tiled=True)[0]
            )
            token = caches[0]
        cache_keys, cache_values = caches
    else:
        shape = (count_requests, count_rows, KEY_VALUE_HEADS, HEAD_SIZE)
        unrotated_key = project(key_weight).reshape(shape)
        key_rows = rotate(
            unrotated_key, cosine[:, None, :], sine_part[:, None, :]
        ).astype(jnp.bfloat16)
        cache_keys = handed_over(key_rows)
        cache_values = handed_over(project(value_weight).astype(jnp.bfloat16).reshape(shape))
    slot_count = cache_keys.shape[0]
    decode_peer = device_id // split_point
    block = device_id % split_point
    source_pair = jnp.sum(jnp.where(owner == decode_peer, pair_ids, 0))
    source_request = source_pair // KEY_VALUE_HEADS
    length = jnp.sum(
        jnp.where(jnp.arange(count_requests, dtype=jnp.int32) == source_request, lengths, 0)
    )
    query = lax.dynamic_index_in_dim(dec_query, decode_peer, 0, keepdims=False)
    new_key = lax.dynamic_index_in_dim(dec_key, decode_peer, 0, keepdims=False)
    new_value = lax.dynamic_index_in_dim(dec_value, decode_peer, 0, keepdims=False)
    step_pos = length + jnp.arange(STEPS, dtype=jnp.int32)
    step_cos, step_sin = rope_table(step_pos, HEAD_SIZE)
    query_rot = rotate(
        query.astype(jnp.float32).reshape(STEPS, QPK, HEAD_SIZE),
        step_cos[:, None, :],
        step_sin[:, None, :],
    ).astype(jnp.bfloat16)
    new_keys = rotate(new_key.astype(jnp.float32), step_cos, step_sin).astype(jnp.bfloat16)
    score_scale = 1.0 / HEAD_SIZE**0.5
    old_scores = (
        jnp.einsum(
            "sjd,id->sji", query_rot, cache_keys, preferred_element_type=jnp.float32
        )
        * score_scale
    )
    new_scores = (
        jnp.einsum("sjd,td->sjt", query_rot, new_keys, preferred_element_type=jnp.float32)
        * score_scale
    )
    slot_ids = jnp.arange(slot_count, dtype=jnp.int32) * split_point + block
    old_live = slot_ids < length
    new_live = (jnp.arange(STEPS)[None, :] <= jnp.arange(STEPS)[:, None]) & (block == 0)
    old_scores = jnp.where(old_live[None, None, :], old_scores, -1e30)
    new_scores = jnp.where(new_live[:, None, :], new_scores, -1e30)
    row_max = jnp.maximum(jnp.max(old_scores, -1), jnp.max(new_scores, -1))
    for bit in range(tree_levels):
        row_max = jnp.maximum(row_max, swapped(row_max, "seq", bit))
    old_exp = jnp.exp(old_scores - row_max[..., None])
    new_exp = jnp.exp(new_scores - row_max[..., None])
    denom = jnp.sum(old_exp, -1) + jnp.sum(new_exp, -1)
    for bit in range(tree_levels):
        denom = denom + swapped(denom, "seq", bit)
    old_probs = (old_exp / denom[..., None]).astype(jnp.bfloat16)
    new_probs = (new_exp / denom[..., None]).astype(jnp.bfloat16)
    partial_sum = jnp.einsum(
        "sji,id->sjd", old_probs, cache_values, preferred_element_type=jnp.float32
    )
    partial_sum = partial_sum + jnp.einsum(
        "sjt,td->sjd", new_probs, new_value, preferred_element_type=jnp.float32
    )
    flat_rows = partial_sum.reshape(STEPS, QPK * HEAD_SIZE)
    for bit in range(tree_levels):
        flat_rows = flat_rows + swapped(flat_rows, "seq", bit)
    share = flat_rows.shape[1] // split_point
    mine = lax.dynamic_slice_in_dim(flat_rows, block * share, share, 1)
    cache = jnp.concatenate([cache_keys, cache_values], 1)[None]
    return (cache, mine.astype(jnp.bfloat16))


def solution(mesh):
    placed = (
        P("groups", "seq", None),
        P("seq", None),
        P("seq", None),
        P("groups"),
        P("groups"),
        P("groups", None, None),
        P("groups", None, None),
        P("groups", None, None),
    )
    return jax.shard_map(
        body,
        mesh=mesh,
        in_specs=placed,
        out_specs=(P(("groups", "seq"), None, None), P("groups", "seq")),
        check_vma=False,
    )
```

```python
import functools

import jax
import jax.numpy as jnp
import numpy as np
from jax import lax
from jax.experimental import pallas as pl
from jax.experimental.pallas import tpu as pltpu
from jax.sharding import PartitionSpec as P

HEAD_SIZE = 128
KEY_VALUE_HEADS = 4
QPK = 8
STEPS = 4


ROPE_BASE = 500000.0


def swapped(block, axis, bit):
    count = lax.axis_size(axis)
    route = []
    for low in range(count):
        high = low | 1 << bit
        if high != low and high < count:
            route += [(low, high), (high, low)]
    return lax.ppermute(block, axis, route)


def rope_table(positions, head_dim):
    freq = ROPE_BASE ** (-(np.arange(head_dim // 2, dtype=np.float64) * 2.0) / head_dim)
    angle = positions.astype(jnp.float32)[:, None] * jnp.asarray(freq, jnp.float32)[None, :]
    return (jnp.cos(angle), jnp.sin(angle))


def rotate(values_in, cosine, sine_part):
    half_dim = values_in.shape[-1] // 2
    lower_half = values_in[..., :half_dim]
    upper_half = values_in[..., half_dim:]
    return jnp.concatenate(
        [
            lower_half * cosine - upper_half * sine_part,
            upper_half * cosine + lower_half * sine_part,
        ],
        -1,
    )


def spread(count):
    side = 1
    while side * side < count:
        side *= 2
    return (side, count // side)


def moved(block, rule):
    groups, seq = lax.axis_size("groups"), lax.axis_size("seq")
    low = spread(seq // 2)[1]
    route = []
    for g in range(groups):
        for s in range(seq):
            tg, tz, ty, tc = rule(g, s // 2 // low, s // 2 % low, s % 2)
            route.append((g * seq + s, tg * seq + (tz * low + ty) * 2 + tc))
    return lax.ppermute(block, ("groups", "seq"), route)


def to_core(g, z, y, c):
    return (g, z, y, 1 - c)


def to_row(g, z, y, c):
    return (g, z, 1 - y, c)


def to_group(g, z, y, c):
    return (1 - g, z, y, c)


def along(bits):
    return lambda g, z, y, c: (g, z ^ bits, y, c)


VMEM_REF = pl.BlockSpec(memory_space=pltpu.VMEM)
SMEM_REF = pl.BlockSpec(memory_space=pltpu.SMEM)
ANY_REF = pl.BlockSpec(memory_space=pl.ANY)
PARAMS = pltpu.CompilerParams(vmem_limit_bytes=56 << 20)


def cost(flops, moved_bytes):
    return pl.CostEstimate(flops=flops, bytes_accessed=moved_bytes, transcendentals=0)


def halves_kernel(together, place, *refs):
    count = len(refs) // 2
    if together:
        columns = refs[0].shape[1]
        for k in range(len(refs) - 1):
            refs[-1][:, k * columns : (k + 1) * columns] = refs[k][...]
    else:
        for source, target in zip(refs[:count], refs[count:]):
            target[...] = source[...]


def sent_halves(place, blocks, together):
    rows, columns = blocks[0].shape
    depth, count = rows // 2, len(blocks)
    kind = blocks[0].dtype
    if together:
        outs = [jax.ShapeDtypeStruct((depth, count * columns), kind)]
    else:
        outs = [jax.ShapeDtypeStruct((depth, columns), kind)] * count
    return pl.pallas_call(
        functools.partial(halves_kernel, together),
        grid_spec=pltpu.PrefetchScalarGridSpec(
            num_scalar_prefetch=1,
            grid=(1,),
            in_specs=[pl.BlockSpec((depth, columns), lambda i, place: (place[0], 0))] * count,
            out_specs=[pl.BlockSpec(out.shape, lambda i, place: (0, 0)) for out in outs],
        ),
        out_shape=outs,
        compiler_params=PARAMS,
        cost_estimate=cost(1000, 1000),
        name="sent_halves",
    )(place, *blocks)


def prepare_kernel(place, *refs):
    left, kept = refs[-2:]
    rows, depth = kept.shape[1], kept.shape[2]
    width = refs[0].shape[1]
    for who, rows_in in enumerate(refs[:2]):
        square = jnp.zeros((rows, depth), jnp.float32)
        for first in range(0, width, depth):
            part = rows_in[:, first : first + depth].astype(jnp.float32)
            square += part * part
        scale = lax.rsqrt(jnp.sum(square, -1, keepdims=True) / width + 1e-05)
        for core in range(2):

            @pl.when(place[1] == core)
            def _():
                for first in range(0, width, depth):
                    j, c, h = first // (4 * depth), first // (2 * depth) % 2, first // depth % 2
                    if c == core or who == 0:
                        part = rows_in[:, first : first + depth].astype(jnp.float32)
                        part = (part * scale).astype(jnp.bfloat16)
                        if c == core:
                            left[2 * j + h, who] = part
                        else:
                            kept[2 * j + h] = part


def prepared(place, mine, other, blocks):
    rows, width = mine.shape
    depth = width // (4 * blocks)
    tile = 80 if rows % 80 == 0 else rows
    spec = pl.BlockSpec((tile, width), lambda i, place: (i, 0))
    return pl.pallas_call(
        prepare_kernel,
        grid_spec=pltpu.PrefetchScalarGridSpec(
            num_scalar_prefetch=1,
            grid=(rows // tile,),
            in_specs=[spec, spec],
            out_specs=[
                pl.BlockSpec((2 * blocks, 2, tile, depth), lambda i, place: (0, 0, i, 0)),
                pl.BlockSpec((2 * blocks, tile, depth), lambda i, place: (0, i, 0)),
            ],
        ),
        out_shape=[
            jax.ShapeDtypeStruct((2 * blocks, 2, rows, depth), jnp.bfloat16),
            jax.ShapeDtypeStruct((2 * blocks, rows, depth), jnp.bfloat16),
        ],
        compiler_params=PARAMS,
        cost_estimate=cost(1 << 36, 1000),
        name="normed_halves",
    )(place, mine, other)


def after(value, *events):
    return lax.optimization_barrier((value, *events))[0]


def fetch(source, target, sem):
    copy = pltpu.make_async_copy(source, target, sem)
    copy.start()
    return copy


def half_index(place, entry, kind):
    half = {0: place[0], 1: 1 - place[0], 2: 0, 3: 1}[kind]
    return place[entry] * 2 + half


def product_kernel(plan, group, with_total, place, both, *refs):
    count = len(plan)
    pieces = refs[:count]
    totals_in = refs[count : count + 2 * with_total]
    outs = refs[-7:-5]
    left, right, total, sems, total_sems = refs[-5:]
    rows, depth = both.shape[2], both.shape[3]
    columns = right.shape[2]
    waits = []
    for k, (entry, kind, row, column) in enumerate(plan):
        area = pl.ds((k % group) * depth, depth)
        slot = k // group
        piece = pieces[k].at[pl.ds(row, depth), pl.ds(column, columns)]
        waits.append(
            [
                fetch(both.at[half_index(place, entry, kind)], left.at[slot, :, :, area], sems.at[2 * k]),
                fetch(piece, right.at[slot, area], sems.at[2 * k + 1]),
            ]
        )
    carried = [
        fetch(ref, total.at[pl.ds(k * rows, rows)], total_sems.at[k])
        for k, ref in enumerate(totals_in)
    ]
    for slot in range(count // group):
        for copies in waits[slot * group : (slot + 1) * group]:
            for copy in copies:
                copy.wait()
        stacked = left[slot].reshape(2 * rows, group * depth)
        value = jnp.dot(stacked, right[slot], preferred_element_type=jnp.float32)
        if slot == 0:
            for copy in carried:
                copy.wait()
        if slot or with_total:
            value += total[...]
        if slot + 1 < count // group:
            total[...] = value
        else:
            outs[0][...] = value[:rows]
            outs[1][...] = value[rows:]


def product(place, both, plan, pieces, totals, group, columns):
    _, _, rows, depth = both.shape
    count = len(plan)
    out = jax.ShapeDtypeStruct((rows, columns), jnp.float32)
    return pl.pallas_call(
        functools.partial(product_kernel, plan, group, bool(totals)),
        in_specs=[SMEM_REF] + [ANY_REF] * (1 + count + len(totals)),
        out_specs=[VMEM_REF] * 2,
        out_shape=[out] * 2,
        scratch_shapes=[
            pltpu.VMEM((count // group, 2, rows, group * depth), both.dtype),
            pltpu.VMEM((count // group, group * depth, columns), both.dtype),
            pltpu.VMEM((2 * rows, columns), jnp.float32),
            pltpu.SemaphoreType.DMA((2 * count,)),
            pltpu.SemaphoreType.DMA((2,)),
        ],
        compiler_params=PARAMS,
        cost_estimate=cost(1000, 1000),
        name="add_product",
    )(place, both, *pieces, *totals)


def rows_kernel(plan, rotated, place, lengths, owner, both, kept, *refs):
    count = len(plan)
    pieces = refs[: 2 * count]
    total_in, came_in = refs[2 * count : 2 * count + 2]
    turn = refs[2 * count + 2 : 4 * count]
    out, left, right, total, came, scratch, sems = refs[-7:]
    rows, depth = kept.shape[1], kept.shape[2]
    waits = [fetch(total_in, total, sems.at[0]), fetch(came_in, came, sems.at[1])]
    sem = 2
    for k in range(2 * count):
        index = half_index(place, *plan[k // 2])
        source = kept.at[index] if k % 2 else both.at[index, 0]
        area = pl.ds(k * depth, depth)
        waits.append(fetch(source, left.at[:, area], sems.at[sem]))
        waits.append(fetch(pieces[k], right.at[area], sems.at[sem + 1]))
        sem += 2
    for copy in waits:
        copy.wait()
    total[...] += came[...]
    total[...] += jnp.dot(left[...], right[...], preferred_element_type=jnp.float32)
    count_requests, count_rows = lengths.shape[0], scratch.shape[0]
    index = place[2] * count_rows + lax.broadcasted_iota(jnp.int32, scratch.shape, 0)
    for r in range(count_requests):
        live = index < lengths[r]
        for h in range(KEY_VALUE_HEADS):
            part = total[
                r * count_rows : (r + 1) * count_rows, h * HEAD_SIZE : (h + 1) * HEAD_SIZE
            ]
            if rotated:
                turned = jnp.concatenate([part[:, HEAD_SIZE // 2 :], part[:, : HEAD_SIZE // 2]], 1)
                part = part * turn[0][...] + turned * turn[1][...]
            scratch[...] = jnp.where(live, part, 0.0)
            peer = owner[r * KEY_VALUE_HEADS + h]
            for b in range(2):
                picked = scratch[pl.ds(b, count_rows // 2, stride=2), :]
                out[peer * 2 + b] = picked.astype(jnp.bfloat16)


def outgoing_rows(place, lengths, owner, both, kept, plan, pieces, total, came, turn, token):
    _, rows, depth = kept.shape
    columns = total.shape[1]
    count = len(plan)
    count_rows = rows // lengths.shape[0]
    out = jax.ShapeDtypeStruct((owner.shape[0] * 2, count_rows // 2, HEAD_SIZE), jnp.bfloat16)

    def kernel(place_ref, lengths_ref, owner_ref, token_ref, *refs):
        rows_kernel(plan, bool(turn), place_ref, lengths_ref, owner_ref, *refs)

    operands = [both, kept, *pieces, total, came]
    return pl.pallas_call(
        kernel,
        in_specs=[SMEM_REF] * 3
        + [ANY_REF] * (1 + len(operands))
        + [VMEM_REF] * len(turn),
        out_specs=VMEM_REF,
        out_shape=out,
        scratch_shapes=[
            pltpu.VMEM((rows, 2 * count * depth), kept.dtype),
            pltpu.VMEM((2 * count * depth, columns), kept.dtype),
            pltpu.VMEM((rows, columns), jnp.float32),
            pltpu.VMEM((rows, columns), jnp.float32),
            pltpu.VMEM((count_rows, HEAD_SIZE), jnp.float32),
            pltpu.SemaphoreType.DMA((2 + 4 * count,)),
        ],
        compiler_params=PARAMS,
        cost_estimate=cost(1000, 1000),
        name="cache_rows",
    )(place, lengths, owner, token, *operands, *turn)


HERE, THERE = 3, 7


def body(hidden, key_weight, value_weight, lengths, owner, dec_query, dec_key, dec_value):
    count_requests, count_rows, width = hidden.shape
    device_id = lax.axis_index("seq")
    group_id = lax.axis_index("groups")
    seq = lax.axis_size("seq")
    planned = seq == 16 and lax.axis_size("groups") == 2
    decode_peers = count_requests * KEY_VALUE_HEADS
    split_point = seq // decode_peers
    tree_levels = split_point.bit_length() - 1
    rows_per_peer = count_rows // split_point
    positions = device_id * count_rows + jnp.arange(count_rows, dtype=jnp.int32)
    total_rows = count_requests * count_rows
    flat = hidden.reshape(total_rows, width)
    if planned:
        core = device_id % 2
        z, y = device_id // 4, device_id // 2 % 2
        place = [group_id, core, device_id]
        place += [(z ^ bits) * 2 + y for bits in range(4)]
        place += [(z ^ bits) * 2 + 1 - y for bits in range(4)]
        place = jnp.stack([jnp.asarray(entry, jnp.int32) for entry in place])
    else:
        widened = flat.astype(jnp.float32)
        normed = (
            widened * lax.rsqrt(jnp.mean(widened * widened, -1, keepdims=True) + 1e-05)
        ).astype(jnp.bfloat16)

        def project(weight):
            whole = lax.all_gather(weight, "seq", axis=0, tiled=True)
            return jnp.dot(normed, whole, preferred_element_type=jnp.float32)

    pair_ids = jnp.arange(decode_peers, dtype=jnp.int32)
    matches = owner[None, :] == pair_ids[:, None]
    inverse_order = jnp.sum(jnp.where(matches, pair_ids[None, :], 0), axis=1)
    live_rows = positions[None, :] < lengths[:, None]

    def handed_over(rows):
        rows = jnp.where(live_rows[:, :, None, None], rows, jnp.zeros_like(rows))
        pair_rows = jnp.transpose(rows, (0, 2, 1, 3)).reshape(decode_peers, count_rows, HEAD_SIZE)
        sorted_rows = pair_rows[inverse_order].reshape(
            decode_peers, rows_per_peer, split_point, HEAD_SIZE
        )
        outgoing = jnp.transpose(sorted_rows, (0, 2, 1, 3)).reshape(
            decode_peers * split_point, rows_per_peer, HEAD_SIZE
        )
        return lax.all_to_all(outgoing, "seq", split_axis=0, concat_axis=1, tiled=True)[0]

    cosine, sine_part = rope_table(positions, HEAD_SIZE)
    if planned:
        turn = (
            jnp.concatenate([cosine, cosine], 1),
            jnp.concatenate([-sine_part, sine_part], 1),
        )
        weights = (key_weight, value_weight)
        columns = key_weight.shape[1]
        depth = key_weight.shape[0] // 2
        other = moved(flat, to_core)
        halves = sent_halves(place, weights, False)
        lanes = {}

        def sent(lane, window, block, rule):
            held = lanes.setdefault(lane, [])
            if len(held) >= window:
                block = after(block, held[-window])
            held.append(moved(block, rule))
            return held[-1]

        near, across, far = [], [], []
        for weight, half in zip(weights, halves):
            near.append(sent("z", 3, weight, along(1)))
            across.append(sent("y", 1, weight, to_row))
            far.append([sent("z", 3, half, along(bits)) for bits in (2, 3)])
        both, kept = prepared(place, flat, other, seq // 2)
        (near_half,) = sent_halves(place, [after(block, other) for block in near], True)
        far_y, far_x, ends = [], [], []
        far_x.append([sent("x", 2, block, to_group) for block in far[0]])
        near_y = sent("y", 2, near_half, to_row)
        far_y.append([sent("y", 2, block, to_row) for block in far[0]])
        near_xy = sent("x", 2, near_y, to_group)
        ends.append([sent("x", 2, block, to_group) for block in far_y[0]])
        far_y.append([sent("y", 2, block, to_row) for block in far[1]])
        far_x.append([sent("x", 2, block, to_group) for block in far[1]])
        caches = []
        token = place
        for k, turned in enumerate((turn, ())):
            early = [(HERE, 2 + h, h * depth, 0) for h in range(2)]
            early += [(THERE, 2 + h, h * depth, 0) for h in range(2)]
            early += [(HERE + 1, 2 + h, h * depth, 0) for h in range(2)]
            early += [(THERE + 1, h, 0, k * columns) for h in range(2)]
            pieces = [weights[k]] * 2 + [across[k]] * 2 + [near[k]] * 2 + [near_y, near_xy]
            totals = product(place, both, early, pieces, (), 4, columns)
            late = [(HERE + 2, 0), (HERE + 2, 1), (HERE + 3, 0), (HERE + 3, 1)]
            late += [(THERE + 2, 0), (THERE + 3, 0)]
            pieces = [far[k][0], far_x[k][0], far[k][1], far_x[k][1], *far_y[k]]
            late = [(*entry, 0, 0) for entry in late]
            total, given = product(place, both, late, pieces, totals, 6, columns)
            came = moved(given, to_core)
            if k:
                ends.append([sent("x", 2, after(block, outgoing), to_group) for block in far_y[1]])
            pieces = [piece for end in ends[k] for piece in (end, moved(end, to_core))]
            last = [(THERE + 2, 1), (THERE + 3, 1)]
            outgoing = outgoing_rows(
                place, lengths, owner, both, kept, last, pieces, total, came, turned, token
            )
            caches.append(
                lax.all_to_all(outgoing, "seq", split_axis=0, concat_axis=1, tiled=True)[0]
            )
            token = caches[0]
        cache_keys, cache_values = caches
    else:
        shape = (count_requests, count_rows, KEY_VALUE_HEADS, HEAD_SIZE)
        unrotated_key = project(key_weight).reshape(shape)
        key_rows = rotate(
            unrotated_key, cosine[:, None, :], sine_part[:, None, :]
        ).astype(jnp.bfloat16)
        cache_keys = handed_over(key_rows)
        cache_values = handed_over(project(value_weight).astype(jnp.bfloat16).reshape(shape))
    slot_count = cache_keys.shape[0]
    decode_peer = device_id // split_point
    block = device_id % split_point
    source_pair = jnp.sum(jnp.where(owner == decode_peer, pair_ids, 0))
    source_request = source_pair // KEY_VALUE_HEADS
    length = jnp.sum(
        jnp.where(jnp.arange(count_requests, dtype=jnp.int32) == source_request, lengths, 0)
    )
    query = lax.dynamic_index_in_dim(dec_query, decode_peer, 0, keepdims=False)
    new_key = lax.dynamic_index_in_dim(dec_key, decode_peer, 0, keepdims=False)
    new_value = lax.dynamic_index_in_dim(dec_value, decode_peer, 0, keepdims=False)
    step_pos = length + jnp.arange(STEPS, dtype=jnp.int32)
    step_cos, step_sin = rope_table(step_pos, HEAD_SIZE)
    query_rot = rotate(
        query.astype(jnp.float32).reshape(STEPS, QPK, HEAD_SIZE),
        step_cos[:, None, :],
        step_sin[:, None, :],
    ).astype(jnp.bfloat16)
    new_keys = rotate(new_key.astype(jnp.float32), step_cos, step_sin).astype(jnp.bfloat16)
    score_scale = 1.0 / HEAD_SIZE**0.5
    old_scores = (
        jnp.einsum(
            "sjd,id->sji", query_rot, cache_keys, preferred_element_type=jnp.float32
        )
        * score_scale
    )
    new_scores = (
        jnp.einsum("sjd,td->sjt", query_rot, new_keys, preferred_element_type=jnp.float32)
        * score_scale
    )
    slot_ids = jnp.arange(slot_count, dtype=jnp.int32) * split_point + block
    old_live = slot_ids < length
    new_live = (jnp.arange(STEPS)[None, :] <= jnp.arange(STEPS)[:, None]) & (block == 0)
    old_scores = jnp.where(old_live[None, None, :], old_scores, -1e30)
    new_scores = jnp.where(new_live[:, None, :], new_scores, -1e30)
    row_max = jnp.maximum(jnp.max(old_scores, -1), jnp.max(new_scores, -1))
    for bit in range(tree_levels):
        row_max = jnp.maximum(row_max, swapped(row_max, "seq", bit))
    old_exp = jnp.exp(old_scores - row_max[..., None])
    new_exp = jnp.exp(new_scores - row_max[..., None])
    denom = jnp.sum(old_exp, -1) + jnp.sum(new_exp, -1)
    for bit in range(tree_levels):
        denom = denom + swapped(denom, "seq", bit)
    old_probs = (old_exp / denom[..., None]).astype(jnp.bfloat16)
    new_probs = (new_exp / denom[..., None]).astype(jnp.bfloat16)
    partial_sum = jnp.einsum(
        "sji,id->sjd", old_probs, cache_values, preferred_element_type=jnp.float32
    )
    partial_sum = partial_sum + jnp.einsum(
        "sjt,td->sjd", new_probs, new_value, preferred_element_type=jnp.float32
    )
    flat_rows = partial_sum.reshape(STEPS, QPK * HEAD_SIZE)
    for bit in range(tree_levels):
        flat_rows = flat_rows + swapped(flat_rows, "seq", bit)
    share = flat_rows.shape[1] // split_point
    mine = lax.dynamic_slice_in_dim(flat_rows, block * share, share, 1)
    cache = jnp.concatenate([cache_keys, cache_values], 1)[None]
    return (cache, mine.astype(jnp.bfloat16))


def solution(mesh):
    placed = (
        P("groups", "seq", None),
        P("seq", None),
        P("seq", None),
        P("groups"),
        P("groups"),
        P("groups", None, None),
        P("groups", None, None),
        P("groups", None, None),
    )
    return jax.shard_map(
        body,
        mesh=mesh,
        in_specs=placed,
        out_specs=(P(("groups", "seq"), None, None), P("groups", "seq")),
        check_vma=False,
    )
```

```python
import functools

import jax
import jax.numpy as jnp
import numpy as np
from jax import lax
from jax.experimental import pallas as pl
from jax.experimental.pallas import tpu as pltpu
from jax.sharding import PartitionSpec as P

HEAD_SIZE = 128
KEY_VALUE_HEADS = 4
QPK = 8
STEPS = 4


ROPE_BASE = 500000.0


def swapped(block, axis, bit):
    count = lax.axis_size(axis)
    route = []
    for low in range(count):
        high = low | 1 << bit
        if high != low and high < count:
            route += [(low, high), (high, low)]
    return lax.ppermute(block, axis, route)


def rope_table(positions, head_dim):
    freq = ROPE_BASE ** (-(np.arange(head_dim // 2, dtype=np.float64) * 2.0) / head_dim)
    angle = positions.astype(jnp.float32)[:, None] * jnp.asarray(freq, jnp.float32)[None, :]
    return (jnp.cos(angle), jnp.sin(angle))


def rotate(values_in, cosine, sine_part):
    half_dim = values_in.shape[-1] // 2
    lower_half = values_in[..., :half_dim]
    upper_half = values_in[..., half_dim:]
    return jnp.concatenate(
        [
            lower_half * cosine - upper_half * sine_part,
            upper_half * cosine + lower_half * sine_part,
        ],
        -1,
    )


def spread(count):
    side = 1
    while side * side < count:
        side *= 2
    return (side, count // side)


def moved(block, rule):
    groups, seq = lax.axis_size("groups"), lax.axis_size("seq")
    low = spread(seq // 2)[1]
    route = []
    for g in range(groups):
        for s in range(seq):
            place = rule(g, s // 2 // low, s // 2 % low, s % 2)
            if place is not None:
                tg, tz, ty, tc = place
                route.append((g * seq + s, tg * seq + (tz * low + ty) * 2 + tc))
    return lax.ppermute(block, ("groups", "seq"), route)


def to_core(g, z, y, c):
    return (g, z, y, 1 - c)


def to_row(g, z, y, c):
    return (g, z, 1 - y, c)


def to_group(g, z, y, c):
    return (1 - g, z, y, c)


def to_pair(g, z, y, c):
    return (g, z ^ 1, y, c)


def to_middle(g, z, y, c):
    return (g, 3 - z, y, c) if z in (1, 2) else None


def to_end(g, z, y, c):
    return (g, 0 if z == 1 else 3, y, c) if z in (1, 2) else None


VMEM_REF = pl.BlockSpec(memory_space=pltpu.VMEM)
SMEM_REF = pl.BlockSpec(memory_space=pltpu.SMEM)
ANY_REF = pl.BlockSpec(memory_space=pl.ANY)
PARAMS = pltpu.CompilerParams(vmem_limit_bytes=56 << 20)


def cost(flops, moved_bytes):
    return pl.CostEstimate(flops=flops, bytes_accessed=moved_bytes, transcendentals=0)


def halves_kernel(place, key_sent, value_sent, key_rest, value_rest, sent, rest):
    columns = key_sent.shape[1]
    sent[:, :columns] = key_sent[...]
    sent[:, columns:] = value_sent[...]
    rest[:, :columns] = key_rest[...]
    rest[:, columns:] = value_rest[...]


def weight_halves(place, key_weight, value_weight):
    rows, columns = key_weight.shape
    depth = rows // 2
    out = jax.ShapeDtypeStruct((depth, 2 * columns), key_weight.dtype)
    sent = pl.BlockSpec((depth, columns), lambda i, place: (place[0], 0))
    rest = pl.BlockSpec((depth, columns), lambda i, place: (1 - place[0], 0))
    return pl.pallas_call(
        halves_kernel,
        grid_spec=pltpu.PrefetchScalarGridSpec(
            num_scalar_prefetch=1,
            grid=(1,),
            in_specs=[sent, sent, rest, rest],
            out_specs=[pl.BlockSpec(out.shape, lambda i, place: (0, 0))] * 2,
        ),
        out_shape=[out, out],
        compiler_params=PARAMS,
        cost_estimate=cost(1000, 1000),
        name="weight_halves",
    )(place, key_weight, value_weight, key_weight, value_weight)


def prepare_kernel(place, *refs):
    left, kept = refs[-2:]
    rows, depth = kept.shape[1], kept.shape[2]
    width = refs[0].shape[1]
    for who, rows_in in enumerate(refs[:2]):
        square = jnp.zeros((rows, depth), jnp.float32)
        for first in range(0, width, depth):
            part = rows_in[:, first : first + depth].astype(jnp.float32)
            square += part * part
        scale = lax.rsqrt(jnp.sum(square, -1, keepdims=True) / width + 1e-05)
        for core in range(2):

            @pl.when(place[1] == core)
            def _():
                for first in range(0, width, depth):
                    j, c, h = first // (4 * depth), first // (2 * depth) % 2, first // depth % 2
                    if c == core or who == 0:
                        part = rows_in[:, first : first + depth].astype(jnp.float32)
                        part = (part * scale).astype(jnp.bfloat16)
                        if c == core:
                            left[2 * j + h, who] = part
                        else:
                            kept[2 * j + h] = part


def prepared(place, mine, other, blocks):
    rows, width = mine.shape
    depth = width // (4 * blocks)
    tile = 80 if rows % 80 == 0 else rows
    spec = pl.BlockSpec((tile, width), lambda i, place: (i, 0))
    return pl.pallas_call(
        prepare_kernel,
        grid_spec=pltpu.PrefetchScalarGridSpec(
            num_scalar_prefetch=1,
            grid=(rows // tile,),
            in_specs=[spec, spec],
            out_specs=[
                pl.BlockSpec((2 * blocks, 2, tile, depth), lambda i, place: (0, 0, i, 0)),
                pl.BlockSpec((2 * blocks, tile, depth), lambda i, place: (0, i, 0)),
            ],
        ),
        out_shape=[
            jax.ShapeDtypeStruct((2 * blocks, 2, rows, depth), jnp.bfloat16),
            jax.ShapeDtypeStruct((2 * blocks, rows, depth), jnp.bfloat16),
        ],
        compiler_params=PARAMS,
        cost_estimate=cost(1000, 1000),
        name="normed_halves",
    )(place, mine, other)


def after(value, *events):
    return lax.optimization_barrier((value, *events))[0]


def fetch(source, target, sem):
    copy = pltpu.make_async_copy(source, target, sem)
    copy.start()
    return copy


def half_index(place, entry, kind):
    half = {0: place[0], 1: 1 - place[0], 2: 0, 3: 1}[kind]
    return place[entry] * 2 + half


def product_kernel(plan, group, parts, with_total, place, both, *refs):
    count = len(plan)
    pieces = refs[:count]
    totals_in = refs[count : count + 2 * with_total * parts]
    outs = refs[-5 - 2 * parts : -5]
    left, right, total, sems, total_sems = refs[-5:]
    rows, depth = both.shape[2], both.shape[3]
    columns = right.shape[2]
    waits = []
    for k, (entry, kind, column) in enumerate(plan):
        area = pl.ds((k % group) * depth, depth)
        slot = k // group
        piece = pieces[k].at[:, pl.ds(column, columns)]
        waits.append(
            [
                fetch(both.at[half_index(place, entry, kind)], left.at[slot, :, :, area], sems.at[2 * k]),
                fetch(piece, right.at[slot, area], sems.at[2 * k + 1]),
            ]
        )
    width = columns // parts
    carried = [
        fetch(
            ref,
            total.at[pl.ds(k % 2 * rows, rows), pl.ds(k // 2 * width, width)],
            total_sems.at[k],
        )
        for k, ref in enumerate(totals_in)
    ]
    for slot in range(count // group):
        for copies in waits[slot * group : (slot + 1) * group]:
            for copy in copies:
                copy.wait()
        stacked = left[slot].reshape(2 * rows, group * depth)
        value = jnp.dot(stacked, right[slot], preferred_element_type=jnp.float32)
        if slot == 0:
            for copy in carried:
                copy.wait()
        if slot or with_total:
            value += total[...]
        if slot + 1 < count // group:
            total[...] = value
        else:
            for k, out in enumerate(outs):
                out[...] = value[
                    k % 2 * rows : (k % 2 + 1) * rows, k // 2 * width : (k // 2 + 1) * width
                ]


def product(place, both, plan, pieces, totals, group, columns, parts):
    _, _, rows, depth = both.shape
    count = len(plan)
    out = jax.ShapeDtypeStruct((rows, columns // parts), jnp.float32)
    return pl.pallas_call(
        functools.partial(product_kernel, plan, group, parts, bool(totals)),
        in_specs=[SMEM_REF] + [ANY_REF] * (1 + count + len(totals)),
        out_specs=[VMEM_REF] * (2 * parts),
        out_shape=[out] * (2 * parts),
        scratch_shapes=[
            pltpu.VMEM((count // group, 2, rows, group * depth), both.dtype),
            pltpu.VMEM((count // group, group * depth, columns), both.dtype),
            pltpu.VMEM((2 * rows, columns), jnp.float32),
            pltpu.SemaphoreType.DMA((2 * count,)),
            pltpu.SemaphoreType.DMA((2 * parts,)),
        ],
        compiler_params=PARAMS,
        cost_estimate=cost(1000, 1000),
        name="add_product",
    )(place, both, *pieces, *totals)


def rows_kernel(plan, rotated, place, lengths, owner, both, kept, *refs):
    count = len(plan)
    pieces = refs[: 2 * count]
    total_in, came_in = refs[2 * count : 2 * count + 2]
    turn = refs[2 * count + 2 : 2 * count + 2 + 2 * rotated]
    out, left, right, total, came, scratch, sems = refs[-7:]
    rows, depth = kept.shape[1], kept.shape[2]
    waits = [fetch(total_in, total, sems.at[0]), fetch(came_in, came, sems.at[1])]
    sem = 2
    for k in range(2 * count):
        index = half_index(place, *plan[k // 2])
        source = kept.at[index] if k % 2 else both.at[index, 0]
        area = pl.ds(k * depth, depth)
        waits.append(fetch(source, left.at[:, area], sems.at[sem]))
        waits.append(fetch(pieces[k], right.at[area], sems.at[sem + 1]))
        sem += 2
    for copy in waits:
        copy.wait()
    total[...] += came[...]
    total[...] += jnp.dot(left[...], right[...], preferred_element_type=jnp.float32)
    count_requests, count_rows = lengths.shape[0], scratch.shape[0]
    index = place[2] * count_rows + lax.broadcasted_iota(jnp.int32, scratch.shape, 0)
    for r in range(count_requests):
        live = index < lengths[r]
        for h in range(KEY_VALUE_HEADS):
            part = total[
                r * count_rows : (r + 1) * count_rows, h * HEAD_SIZE : (h + 1) * HEAD_SIZE
            ]
            if rotated:
                turned = jnp.concatenate([part[:, HEAD_SIZE // 2 :], part[:, : HEAD_SIZE // 2]], 1)
                part = part * turn[0][...] + turned * turn[1][...]
            scratch[...] = jnp.where(live, part, 0.0)
            peer = owner[r * KEY_VALUE_HEADS + h]
            for b in range(2):
                picked = scratch[pl.ds(b, count_rows // 2, stride=2), :]
                out[peer * 2 + b] = picked.astype(jnp.bfloat16)


def outgoing_rows(place, lengths, owner, both, kept, plan, pieces, total, came, turn, token):
    _, rows, depth = kept.shape
    columns = total.shape[1]
    count = len(plan)
    count_rows = rows // lengths.shape[0]
    out = jax.ShapeDtypeStruct((owner.shape[0] * 2, count_rows // 2, HEAD_SIZE), jnp.bfloat16)

    def kernel(place_ref, lengths_ref, owner_ref, token_ref, *refs):
        rows_kernel(plan, bool(turn), place_ref, lengths_ref, owner_ref, *refs)

    operands = [both, kept, *pieces, total, came]
    return pl.pallas_call(
        kernel,
        in_specs=[SMEM_REF] * 3
        + [ANY_REF] * (1 + len(operands))
        + [VMEM_REF] * len(turn),
        out_specs=VMEM_REF,
        out_shape=out,
        scratch_shapes=[
            pltpu.VMEM((rows, 2 * count * depth), kept.dtype),
            pltpu.VMEM((2 * count * depth, columns), kept.dtype),
            pltpu.VMEM((rows, columns), jnp.float32),
            pltpu.VMEM((rows, columns), jnp.float32),
            pltpu.VMEM((count_rows, HEAD_SIZE), jnp.float32),
            pltpu.SemaphoreType.DMA((2 + 4 * count,)),
        ],
        compiler_params=PARAMS,
        cost_estimate=cost(1000, 1000),
        name="cache_rows",
    )(place, lengths, owner, token, *operands, *turn)


HERE, THERE = 3, 7


def body(hidden, key_weight, value_weight, lengths, owner, dec_query, dec_key, dec_value):
    count_requests, count_rows, width = hidden.shape
    device_id = lax.axis_index("seq")
    group_id = lax.axis_index("groups")
    seq = lax.axis_size("seq")
    planned = seq == 16 and lax.axis_size("groups") == 2
    decode_peers = count_requests * KEY_VALUE_HEADS
    split_point = seq // decode_peers
    tree_levels = split_point.bit_length() - 1
    rows_per_peer = count_rows // split_point
    positions = device_id * count_rows + jnp.arange(count_rows, dtype=jnp.int32)
    total_rows = count_requests * count_rows
    flat = hidden.reshape(total_rows, width)
    if planned:
        core = device_id % 2
        z, y = device_id // 4, device_id // 2 % 2
        layers = [z, z ^ 1, jnp.where(z < 2, 2, 1), jnp.where(z < 2, 3, 0)]
        is_end = (z == 0) | (z == 3)
        place = [group_id, core, device_id]
        place += [layer * 2 + y for layer in layers]
        place += [layer * 2 + 1 - y for layer in layers]
        place = jnp.stack([jnp.asarray(entry, jnp.int32) for entry in place])
    else:
        widened = flat.astype(jnp.float32)
        normed = (
            widened * lax.rsqrt(jnp.mean(widened * widened, -1, keepdims=True) + 1e-05)
        ).astype(jnp.bfloat16)

        def project(weight):
            whole = lax.all_gather(weight, "seq", axis=0, tiled=True)
            return jnp.dot(normed, whole, preferred_element_type=jnp.float32)

    pair_ids = jnp.arange(decode_peers, dtype=jnp.int32)
    matches = owner[None, :] == pair_ids[:, None]
    inverse_order = jnp.sum(jnp.where(matches, pair_ids[None, :], 0), axis=1)
    live_rows = positions[None, :] < lengths[:, None]

    def handed_over(rows):
        rows = jnp.where(live_rows[:, :, None, None], rows, jnp.zeros_like(rows))
        pair_rows = jnp.transpose(rows, (0, 2, 1, 3)).reshape(decode_peers, count_rows, HEAD_SIZE)
        sorted_rows = pair_rows[inverse_order].reshape(
            decode_peers, rows_per_peer, split_point, HEAD_SIZE
        )
        outgoing = jnp.transpose(sorted_rows, (0, 2, 1, 3)).reshape(
            decode_peers * split_point, rows_per_peer, HEAD_SIZE
        )
        return lax.all_to_all(outgoing, "seq", split_axis=0, concat_axis=1, tiled=True)[0]

    cosine, sine_part = rope_table(positions, HEAD_SIZE)
    if planned:
        turn = (
            jnp.concatenate([cosine, cosine], 1),
            jnp.concatenate([-sine_part, sine_part], 1),
        )
        columns = key_weight.shape[1]

        def parts_of(block):
            return [block[:, k * columns : (k + 1) * columns] for k in range(2)]

        sent, rest = weight_halves(place, key_weight, value_weight)
        near = moved(sent, to_pair)
        middle = moved(sent, to_middle)
        across = moved(sent, to_row)
        other = moved(flat, to_core)
        came = (near, middle, across, other)
        end_b = moved(after(middle, *came), to_end)
        middle_c = moved(after(near, *came), to_middle)
        near_y = moved(after(near, *came), to_row)
        across_x = moved(after(across, *came), to_group)
        both, kept = prepared(place, after(flat, *came), other, seq // 2)
        came = (end_b, middle_c, near_y, across_x, both)
        end_c = moved(after(middle_c, *came), to_end)
        near_xy = moved(after(near_y, *came), to_group)
        block_b = jnp.where(is_end, after(end_b, *came), middle)
        block_yb = moved(block_b, to_row)
        plan = [(HERE, 0, 0), (HERE, 1, 0), (THERE, 0, 0), (THERE, 1, 0)]
        plan += [(HERE + 1, 0, 0), (THERE + 1, 0, 0)]
        pieces = [sent, rest, across, across_x, near, near_y]
        totals = product(place, after(both, *came), plan, pieces, (), 3, 2 * columns, 2)
        key_b, value_b = parts_of(block_b)
        came = (end_c, near_xy, block_yb, totals[0], key_b, value_b)
        near_rest = moved(after(rest, *came), to_pair)
        key_xb = moved(after(key_b, *came), to_group)
        key_c, value_c = parts_of(jnp.where(is_end, after(end_c, *came), middle_c))
        key_yc, value_yc = moved(key_c, to_row), moved(value_c, to_row)
        key_xc = moved(key_c, to_group)
        plan = [(THERE + 1, 1, 0), (HERE + 2, 0, 0), (THERE + 2, 0, 0)]
        pieces = [near_xy, block_b, block_yb]
        totals = product(place, after(both, *came), plan, pieces, totals, 3, 2 * columns, 2)
        came = (near_rest, key_xb, key_yc, value_yc, key_xc, totals[0])
        key_xyc = moved(after(key_yc, *came), to_group)
        key_yxb = moved(after(key_xb, *came), to_row)
        value_xb = moved(after(value_b, *came), to_group)
        plan = [(HERE + 1, 1, 0), (HERE + 2, 1, 0), (HERE + 3, 0, 0), (HERE + 3, 1, 0)]
        plan += [(THERE + 3, 0, 0)]
        pieces = [near_rest, key_xb, key_c, key_xc, key_yc]
        total, given = product(
            place, after(both, *came), plan, pieces, totals[:2], 5, columns, 1
        )
        came = (key_xyc, key_yxb, value_xb, total)
        value_yxb = moved(after(value_xb, *came), to_row)
        value_xc = moved(after(value_c, *came), to_group)
        value_xyc = moved(after(value_yc, *came), to_group)
        given = moved(after(given, *came), to_core)
        ends = [after(key_yxb, *came), after(key_xyc, *came)]
        pieces = [piece for end in ends for piece in (end, moved(end, to_core))]
        plan = [(THERE + 2, 1), (THERE + 3, 1)]
        outgoing = outgoing_rows(
            place, lengths, owner, both, kept, plan, pieces, total, given, turn, place
        )
        cache_keys = lax.all_to_all(outgoing, "seq", split_axis=0, concat_axis=1, tiled=True)[0]
        plan = [(HERE + 1, 1, columns), (HERE + 2, 1, 0), (HERE + 3, 0, 0), (THERE + 3, 0, 0)]
        pieces = [near_rest, value_xb, value_c, value_yc]
        total, given = product(
            place, after(both, outgoing), plan, pieces, totals[2:], 4, columns, 1
        )
        given = moved(given, to_core)
        came = (value_yxb, value_xc, value_xyc, total)
        ends = [after(end, *came) for end in came[:3]]
        pieces = [piece for end in ends for piece in (end, moved(end, to_core))]
        plan = [(THERE + 2, 1), (HERE + 3, 1), (THERE + 3, 1)]
        outgoing = outgoing_rows(
            place, lengths, owner, both, kept, plan, pieces, total, given, (), cache_keys
        )
        cache_values = lax.all_to_all(outgoing, "seq", split_axis=0, concat_axis=1, tiled=True)[0]
    else:
        shape = (count_requests, count_rows, KEY_VALUE_HEADS, HEAD_SIZE)
        unrotated_key = project(key_weight).reshape(shape)
        key_rows = rotate(
            unrotated_key, cosine[:, None, :], sine_part[:, None, :]
        ).astype(jnp.bfloat16)
        cache_keys = handed_over(key_rows)
        cache_values = handed_over(project(value_weight).astype(jnp.bfloat16).reshape(shape))
    slot_count = cache_keys.shape[0]
    decode_peer = device_id // split_point
    block = device_id % split_point
    source_pair = jnp.sum(jnp.where(owner == decode_peer, pair_ids, 0))
    source_request = source_pair // KEY_VALUE_HEADS
    length = jnp.sum(
        jnp.where(jnp.arange(count_requests, dtype=jnp.int32) == source_request, lengths, 0)
    )
    query = lax.dynamic_index_in_dim(dec_query, decode_peer, 0, keepdims=False)
    new_key = lax.dynamic_index_in_dim(dec_key, decode_peer, 0, keepdims=False)
    new_value = lax.dynamic_index_in_dim(dec_value, decode_peer, 0, keepdims=False)
    step_pos = length + jnp.arange(STEPS, dtype=jnp.int32)
    step_cos, step_sin = rope_table(step_pos, HEAD_SIZE)
    query_rot = rotate(
        query.astype(jnp.float32).reshape(STEPS, QPK, HEAD_SIZE),
        step_cos[:, None, :],
        step_sin[:, None, :],
    ).astype(jnp.bfloat16)
    new_keys = rotate(new_key.astype(jnp.float32), step_cos, step_sin).astype(jnp.bfloat16)
    score_scale = 1.0 / HEAD_SIZE**0.5
    old_scores = (
        jnp.einsum(
            "sjd,id->sji", query_rot, cache_keys, preferred_element_type=jnp.float32
        )
        * score_scale
    )
    new_scores = (
        jnp.einsum("sjd,td->sjt", query_rot, new_keys, preferred_element_type=jnp.float32)
        * score_scale
    )
    slot_ids = jnp.arange(slot_count, dtype=jnp.int32) * split_point + block
    old_live = slot_ids < length
    new_live = (jnp.arange(STEPS)[None, :] <= jnp.arange(STEPS)[:, None]) & (block == 0)
    old_scores = jnp.where(old_live[None, None, :], old_scores, -1e30)
    new_scores = jnp.where(new_live[:, None, :], new_scores, -1e30)
    row_max = jnp.maximum(jnp.max(old_scores, -1), jnp.max(new_scores, -1))
    for bit in range(tree_levels):
        row_max = jnp.maximum(row_max, swapped(row_max, "seq", bit))
    old_exp = jnp.exp(old_scores - row_max[..., None])
    new_exp = jnp.exp(new_scores - row_max[..., None])
    denom = jnp.sum(old_exp, -1) + jnp.sum(new_exp, -1)
    for bit in range(tree_levels):
        denom = denom + swapped(denom, "seq", bit)
    old_probs = (old_exp / denom[..., None]).astype(jnp.bfloat16)
    new_probs = (new_exp / denom[..., None]).astype(jnp.bfloat16)
    partial_sum = jnp.einsum(
        "sji,id->sjd", old_probs, cache_values, preferred_element_type=jnp.float32
    )
    partial_sum = partial_sum + jnp.einsum(
        "sjt,td->sjd", new_probs, new_value, preferred_element_type=jnp.float32
    )
    flat_rows = partial_sum.reshape(STEPS, QPK * HEAD_SIZE)
    for bit in range(tree_levels):
        flat_rows = flat_rows + swapped(flat_rows, "seq", bit)
    share = flat_rows.shape[1] // split_point
    mine = lax.dynamic_slice_in_dim(flat_rows, block * share, share, 1)
    cache = jnp.concatenate([cache_keys, cache_values], 1)[None]
    return (cache, mine.astype(jnp.bfloat16))


def solution(mesh):
    placed = (
        P("groups", "seq", None),
        P("seq", None),
        P("seq", None),
        P("groups"),
        P("groups"),
        P("groups", None, None),
        P("groups", None, None),
        P("groups", None, None),
    )
    return jax.shard_map(
        body,
        mesh=mesh,
        in_specs=placed,
        out_specs=(P(("groups", "seq"), None, None), P("groups", "seq")),
        check_vma=False,
    )
```

```python
import functools

import jax
import jax.numpy as jnp
import numpy as np
from jax import lax
from jax.experimental import pallas as pl
from jax.experimental.pallas import tpu as pltpu
from jax.sharding import PartitionSpec as P

HEAD_SIZE = 128
KEY_VALUE_HEADS = 4
QPK = 8
STEPS = 4


ROPE_BASE = 500000.0


def swapped(block, axis, bit):
    count = lax.axis_size(axis)
    route = []
    for low in range(count):
        high = low | 1 << bit
        if high != low and high < count:
            route += [(low, high), (high, low)]
    return lax.ppermute(block, axis, route)


def rope_table(positions, head_dim):
    freq = ROPE_BASE ** (-(np.arange(head_dim // 2, dtype=np.float64) * 2.0) / head_dim)
    angle = positions.astype(jnp.float32)[:, None] * jnp.asarray(freq, jnp.float32)[None, :]
    return (jnp.cos(angle), jnp.sin(angle))


def rotate(values_in, cosine, sine_part):
    half_dim = values_in.shape[-1] // 2
    lower_half = values_in[..., :half_dim]
    upper_half = values_in[..., half_dim:]
    return jnp.concatenate(
        [
            lower_half * cosine - upper_half * sine_part,
            upper_half * cosine + lower_half * sine_part,
        ],
        -1,
    )


def spread(count):
    side = 1
    while side * side < count:
        side *= 2
    return (side, count // side)


def moved(block, rule):
    groups, seq = lax.axis_size("groups"), lax.axis_size("seq")
    low = spread(seq // 2)[1]
    route = []
    for g in range(groups):
        for s in range(seq):
            place = rule(g, s // 2 // low, s // 2 % low, s % 2)
            if place is not None:
                tg, tz, ty, tc = place
                route.append((g * seq + s, tg * seq + (tz * low + ty) * 2 + tc))
    return lax.ppermute(block, ("groups", "seq"), route)


def to_core(g, z, y, c):
    return (g, z, y, 1 - c)


def to_row(g, z, y, c):
    return (g, z, 1 - y, c)


def to_group(g, z, y, c):
    return (1 - g, z, y, c)


def to_pair(g, z, y, c):
    return (g, z ^ 1, y, c)


def to_middle(g, z, y, c):
    return (g, 3 - z, y, c) if z in (1, 2) else None


def to_end(g, z, y, c):
    return (g, 0 if z == 1 else 3, y, c) if z in (1, 2) else None


VMEM_REF = pl.BlockSpec(memory_space=pltpu.VMEM)
SMEM_REF = pl.BlockSpec(memory_space=pltpu.SMEM)
ANY_REF = pl.BlockSpec(memory_space=pl.ANY)
PARAMS = pltpu.CompilerParams(vmem_limit_bytes=56 << 20)


def cost(flops, moved_bytes):
    return pl.CostEstimate(flops=flops, bytes_accessed=moved_bytes, transcendentals=0)


def fetch(source, target, sem):
    copy = pltpu.make_async_copy(source, target, sem)
    copy.start()
    return copy


def halves_kernel(kind, place, key_weight, value_weight, out, sems):
    depth, columns = out.shape[0], out.shape[1] // 2
    half = 1 - place[0] if kind else place[0]
    rows = pl.ds(pl.multiple_of(half * depth, depth), depth)
    copies = [
        fetch(weight.at[rows], out.at[:, pl.ds(k * columns, columns)], sems.at[k])
        for k, weight in enumerate((key_weight, value_weight))
    ]
    for copy in copies:
        copy.wait()


def weight_half(place, kind, key_weight, value_weight):
    rows, columns = key_weight.shape
    return pl.pallas_call(
        functools.partial(halves_kernel, kind),
        in_specs=[SMEM_REF, ANY_REF, ANY_REF],
        out_specs=VMEM_REF,
        out_shape=jax.ShapeDtypeStruct((rows // 2, 2 * columns), key_weight.dtype),
        scratch_shapes=[pltpu.SemaphoreType.DMA((2,))],
        compiler_params=PARAMS,
        cost_estimate=cost(1000, 1000),
        name="weight_half",
    )(place, key_weight, value_weight)


def prepare_kernel(place, *refs):
    left, kept = refs[-2:]
    rows, depth = kept.shape[1], kept.shape[2]
    width = refs[0].shape[1]
    for who, rows_in in enumerate(refs[:2]):
        square = jnp.zeros((rows, depth), jnp.float32)
        for first in range(0, width, depth):
            part = rows_in[:, first : first + depth].astype(jnp.float32)
            square += part * part
        scale = lax.rsqrt(jnp.sum(square, -1, keepdims=True) / width + 1e-05)
        for core in range(2):

            @pl.when(place[1] == core)
            def _():
                for first in range(0, width, depth):
                    j, c, h = first // (4 * depth), first // (2 * depth) % 2, first // depth % 2
                    if c == core or who == 0:
                        part = rows_in[:, first : first + depth].astype(jnp.float32)
                        part = (part * scale).astype(jnp.bfloat16)
                        if c == core:
                            left[2 * j + h, who] = part
                        else:
                            kept[2 * j + h] = part


def prepared(place, mine, other, blocks):
    rows, width = mine.shape
    depth = width // (4 * blocks)
    tile = 80 if rows % 80 == 0 else rows
    spec = pl.BlockSpec((tile, width), lambda i, place: (i, 0))
    return pl.pallas_call(
        prepare_kernel,
        grid_spec=pltpu.PrefetchScalarGridSpec(
            num_scalar_prefetch=1,
            grid=(rows // tile,),
            in_specs=[spec, spec],
            out_specs=[
                pl.BlockSpec((2 * blocks, 2, tile, depth), lambda i, place: (0, 0, i, 0)),
                pl.BlockSpec((2 * blocks, tile, depth), lambda i, place: (0, i, 0)),
            ],
        ),
        out_shape=[
            jax.ShapeDtypeStruct((2 * blocks, 2, rows, depth), jnp.bfloat16),
            jax.ShapeDtypeStruct((2 * blocks, rows, depth), jnp.bfloat16),
        ],
        compiler_params=PARAMS,
        cost_estimate=cost(1000, 1000),
        name="normed_halves",
    )(place, mine, other)


def after(value, *events):
    return lax.optimization_barrier((value, *events))[0]


def half_index(place, entry, kind):
    half = {0: place[0], 1: 1 - place[0], 2: 0, 3: 1}[kind]
    return place[entry] * 2 + half


def product_kernel(plan, group, parts, with_total, place, both, *refs):
    count = len(plan)
    taken = sum(pair for _, _, pair in plan)
    totals_in = refs[taken : taken + 2 * with_total * parts]
    next_ref = iter(refs)
    outs = refs[-5 - 2 * parts : -5]
    left, right, total, sems, total_sems = refs[-5:]
    rows, depth = both.shape[2], both.shape[3]
    columns = right.shape[2]
    waits = []
    width = columns // parts
    for k, (entry, kind, pair) in enumerate(plan):
        area = pl.ds((k % group) * depth, depth)
        slot = k // group
        index = half_index(place, entry, kind)
        waits.append([fetch(both.at[index], left.at[slot, :, :, area], sems.at[3 * k])])
        for p in range(pair):
            target = right.at[slot, area, pl.ds(p * columns // pair, columns // pair)]
            waits[-1].append(fetch(next(next_ref), target, sems.at[3 * k + 1 + p]))
    carried = [
        fetch(
            ref,
            total.at[pl.ds(k % 2 * rows, rows), pl.ds(k // 2 * width, width)],
            total_sems.at[k],
        )
        for k, ref in enumerate(totals_in)
    ]
    for slot in range(count // group):
        for copies in waits[slot * group : (slot + 1) * group]:
            for copy in copies:
                copy.wait()
        stacked = left[slot].reshape(2 * rows, group * depth)
        value = jnp.dot(stacked, right[slot], preferred_element_type=jnp.float32)
        if slot == 0:
            for copy in carried:
                copy.wait()
        if slot or with_total:
            value += total[...]
        if slot + 1 < count // group:
            total[...] = value
        else:
            for k, out in enumerate(outs):
                out[...] = value[
                    k % 2 * rows : (k % 2 + 1) * rows, k // 2 * width : (k // 2 + 1) * width
                ]


def product(place, both, pieces, totals, group, columns, parts):
    _, _, rows, depth = both.shape
    plan = [(entry, kind, len(arrays)) for entry, kind, *arrays in pieces]
    pieces_flat = [array for _, _, *arrays in pieces for array in arrays]
    count = len(plan)
    out = jax.ShapeDtypeStruct((rows, columns // parts), jnp.float32)
    return pl.pallas_call(
        functools.partial(product_kernel, plan, group, parts, bool(totals)),
        in_specs=[SMEM_REF] + [ANY_REF] * (1 + len(pieces_flat) + len(totals)),
        out_specs=[VMEM_REF] * (2 * parts),
        out_shape=[out] * (2 * parts),
        scratch_shapes=[
            pltpu.VMEM((count // group, 2, rows, group * depth), both.dtype),
            pltpu.VMEM((count // group, group * depth, columns), both.dtype),
            pltpu.VMEM((2 * rows, columns), jnp.float32),
            pltpu.SemaphoreType.DMA((3 * count,)),
            pltpu.SemaphoreType.DMA((2 * parts,)),
        ],
        compiler_params=PARAMS,
        cost_estimate=cost(1000, 1000),
        name="add_product",
    )(place, both, *pieces_flat, *totals)


def rows_kernel(plan, rotated, place, lengths, owner, both, kept, *refs):
    count = len(plan)
    pieces = refs[: 2 * count]
    total_in, came_in = refs[2 * count : 2 * count + 2]
    turn = refs[2 * count + 2 : 2 * count + 2 + 2 * rotated]
    out, left, right, total, came, scratch, sems = refs[-7:]
    rows, depth = kept.shape[1], kept.shape[2]
    waits = [fetch(total_in, total, sems.at[0]), fetch(came_in, came, sems.at[1])]
    sem = 2
    for k in range(2 * count):
        index = half_index(place, *plan[k // 2])
        source = kept.at[index] if k % 2 else both.at[index, 0]
        area = pl.ds(k * depth, depth)
        waits.append(fetch(source, left.at[:, area], sems.at[sem]))
        waits.append(fetch(pieces[k], right.at[area], sems.at[sem + 1]))
        sem += 2
    for copy in waits:
        copy.wait()
    total[...] += came[...]
    total[...] += jnp.dot(left[...], right[...], preferred_element_type=jnp.float32)
    count_requests, count_rows = lengths.shape[0], scratch.shape[0]
    index = place[2] * count_rows + lax.broadcasted_iota(jnp.int32, scratch.shape, 0)
    for r in range(count_requests):
        live = index < lengths[r]
        for h in range(KEY_VALUE_HEADS):
            part = total[
                r * count_rows : (r + 1) * count_rows, h * HEAD_SIZE : (h + 1) * HEAD_SIZE
            ]
            if rotated:
                turned = jnp.concatenate([part[:, HEAD_SIZE // 2 :], part[:, : HEAD_SIZE // 2]], 1)
                part = part * turn[0][...] + turned * turn[1][...]
            scratch[...] = jnp.where(live, part, 0.0)
            peer = owner[r * KEY_VALUE_HEADS + h]
            for b in range(2):
                picked = scratch[pl.ds(b, count_rows // 2, stride=2), :]
                out[peer * 2 + b] = picked.astype(jnp.bfloat16)


def outgoing_rows(place, lengths, owner, both, kept, plan, pieces, total, came, turn, token):
    _, rows, depth = kept.shape
    columns = total.shape[1]
    count = len(plan)
    count_rows = rows // lengths.shape[0]
    out = jax.ShapeDtypeStruct((owner.shape[0] * 2, count_rows // 2, HEAD_SIZE), jnp.bfloat16)

    def kernel(place_ref, lengths_ref, owner_ref, token_ref, *refs):
        rows_kernel(plan, bool(turn), place_ref, lengths_ref, owner_ref, *refs)

    operands = [both, kept, *pieces, total, came]
    return pl.pallas_call(
        kernel,
        in_specs=[SMEM_REF] * 3
        + [ANY_REF] * (1 + len(operands))
        + [VMEM_REF] * len(turn),
        out_specs=VMEM_REF,
        out_shape=out,
        scratch_shapes=[
            pltpu.VMEM((rows, 2 * count * depth), kept.dtype),
            pltpu.VMEM((2 * count * depth, columns), kept.dtype),
            pltpu.VMEM((rows, columns), jnp.float32),
            pltpu.VMEM((rows, columns), jnp.float32),
            pltpu.VMEM((count_rows, HEAD_SIZE), jnp.float32),
            pltpu.SemaphoreType.DMA((2 + 4 * count,)),
        ],
        compiler_params=PARAMS,
        cost_estimate=cost(1000, 1000),
        name="cache_rows",
    )(place, lengths, owner, token, *operands, *turn)


HERE, THERE = 3, 7


def body(hidden, key_weight, value_weight, lengths, owner, dec_query, dec_key, dec_value):
    count_requests, count_rows, width = hidden.shape
    device_id = lax.axis_index("seq")
    group_id = lax.axis_index("groups")
    seq = lax.axis_size("seq")
    planned = seq == 16 and lax.axis_size("groups") == 2
    decode_peers = count_requests * KEY_VALUE_HEADS
    split_point = seq // decode_peers
    tree_levels = split_point.bit_length() - 1
    rows_per_peer = count_rows // split_point
    positions = device_id * count_rows + jnp.arange(count_rows, dtype=jnp.int32)
    total_rows = count_requests * count_rows
    flat = hidden.reshape(total_rows, width)
    if planned:
        core = device_id % 2
        z, y = device_id // 4, device_id // 2 % 2
        layers = [z, z ^ 1, jnp.where(z < 2, 2, 1), jnp.where(z < 2, 3, 0)]
        is_end = (z == 0) | (z == 3)
        place = [group_id, core, device_id]
        place += [layer * 2 + y for layer in layers]
        place += [layer * 2 + 1 - y for layer in layers]
        place = jnp.stack([jnp.asarray(entry, jnp.int32) for entry in place])
    else:
        widened = flat.astype(jnp.float32)
        normed = (
            widened * lax.rsqrt(jnp.mean(widened * widened, -1, keepdims=True) + 1e-05)
        ).astype(jnp.bfloat16)

        def project(weight):
            whole = lax.all_gather(weight, "seq", axis=0, tiled=True)
            return jnp.dot(normed, whole, preferred_element_type=jnp.float32)

    pair_ids = jnp.arange(decode_peers, dtype=jnp.int32)
    matches = owner[None, :] == pair_ids[:, None]
    inverse_order = jnp.sum(jnp.where(matches, pair_ids[None, :], 0), axis=1)
    live_rows = positions[None, :] < lengths[:, None]

    def handed_over(rows):
        rows = jnp.where(live_rows[:, :, None, None], rows, jnp.zeros_like(rows))
        pair_rows = jnp.transpose(rows, (0, 2, 1, 3)).reshape(decode_peers, count_rows, HEAD_SIZE)
        sorted_rows = pair_rows[inverse_order].reshape(
            decode_peers, rows_per_peer, split_point, HEAD_SIZE
        )
        outgoing = jnp.transpose(sorted_rows, (0, 2, 1, 3)).reshape(
            decode_peers * split_point, rows_per_peer, HEAD_SIZE
        )
        return lax.all_to_all(outgoing, "seq", split_axis=0, concat_axis=1, tiled=True)[0]

    decode_peer = device_id // split_point
    block = device_id % split_point
    source_pair = jnp.sum(jnp.where(owner == decode_peer, pair_ids, 0))
    source_request = source_pair // KEY_VALUE_HEADS
    length = jnp.sum(
        jnp.where(jnp.arange(count_requests, dtype=jnp.int32) == source_request, lengths, 0)
    )
    query = lax.dynamic_index_in_dim(dec_query, decode_peer, 0, keepdims=False)
    new_key = lax.dynamic_index_in_dim(dec_key, decode_peer, 0, keepdims=False)
    new_value = lax.dynamic_index_in_dim(dec_value, decode_peer, 0, keepdims=False)
    step_pos = length + jnp.arange(STEPS, dtype=jnp.int32)
    step_cos, step_sin = rope_table(step_pos, HEAD_SIZE)
    query_rot = rotate(
        query.astype(jnp.float32).reshape(STEPS, QPK, HEAD_SIZE),
        step_cos[:, None, :],
        step_sin[:, None, :],
    ).astype(jnp.bfloat16)
    new_keys = rotate(new_key.astype(jnp.float32), step_cos, step_sin).astype(jnp.bfloat16)
    cosine, sine_part = rope_table(positions, HEAD_SIZE)
    if planned:
        turn = (
            jnp.concatenate([cosine, cosine], 1),
            jnp.concatenate([-sine_part, sine_part], 1),
        )
        columns = key_weight.shape[1]

        def parts_of(block):
            return [block[:, k * columns : (k + 1) * columns] for k in range(2)]

        sent = weight_half(place, 0, key_weight, value_weight)
        near = moved(sent, to_pair)
        middle = moved(sent, to_middle)
        across = moved(sent, to_row)
        other = moved(flat, to_core)
        rest = weight_half(place, 1, key_weight, after(value_weight, sent))
        came = (near, middle, across, other, rest, *turn, query_rot, new_keys)
        end_b = moved(after(middle, *came), to_end)
        middle_c = moved(after(near, *came), to_middle)
        near_y = moved(after(near, *came), to_row)
        across_x = moved(after(across, *came), to_group)
        both, kept = prepared(place, after(flat, *came), other, seq // 2)
        came = (end_b, middle_c, near_y, across_x, both)
        end_c = moved(after(middle_c, *came), to_end)
        block_b = jnp.where(is_end, after(end_b, *came), middle)
        block_yb = moved(block_b, to_row)
        block_xb = moved(block_b, to_group)
        pieces = [(HERE, 0, sent), (HERE, 1, rest), (THERE, 0, across), (THERE, 1, across_x)]
        pieces += [(HERE + 1, 0, near), (THERE + 1, 0, near_y)]
        totals = product(place, after(both, *came), pieces, (), 3, 2 * columns, 2)
        ends_x = parts_of(after(across_x, *came))
        came = (end_c, block_yb, block_xb, totals[0], *ends_x)
        near_rest = moved(after(rest, *came), to_pair)
        block_c = parts_of(jnp.where(is_end, after(end_c, *came), middle_c))
        block_xc = [moved(block_c[0], to_group)]
        block_yc = [moved(block_c[0], to_row)]
        block_xc.append(moved(block_c[1], to_group))
        block_yc.append(moved(block_c[1], to_row))
        pieces = [(HERE + 2, 0, block_b), (HERE + 2, 1, block_xb)]
        pieces += [(THERE + 2, 0, block_yb), (HERE + 3, 0, *block_c)]
        totals = product(place, after(both, *came), pieces, totals, 4, 2 * columns, 2)
        ends_yb = parts_of(after(block_yb, *came))
        came = (near_rest, *block_xc, *block_yc, totals[0], *ends_yb)
        ends = []
        for k in range(2):
            near_xy = moved(after(ends_x[k], *came), to_pair)
            ends.append([near_xy, moved(after(ends_yb[k], *came), to_group)])
            ends[k].append(moved(after(block_xc[k], *came), to_row))
        pieces = [(HERE + 1, 1, near_rest), (HERE + 3, 1, *block_xc), (THERE + 3, 0, *block_yc)]
        totals = product(place, after(both, ends[0][1]), pieces, totals, 3, 2 * columns, 2)
        plan = [(THERE + 1, 1), (THERE + 2, 1), (THERE + 3, 1)]
        caches = []
        token = place
        for k, turned in enumerate((turn, ())):
            given = moved(after(totals[2 * k + 1], token), to_core)
            swapped_ends = [moved(end, to_core) for end in ends[k]]
            pieces = [piece for pair in zip(ends[k], swapped_ends) for piece in pair]
            outgoing = outgoing_rows(
                place, lengths, owner, both, kept, plan, pieces, totals[2 * k], given, turned, token
            )
            caches.append(
                lax.all_to_all(outgoing, "seq", split_axis=0, concat_axis=1, tiled=True)[0]
            )
            token = outgoing
        cache_keys, cache_values = caches
    else:
        shape = (count_requests, count_rows, KEY_VALUE_HEADS, HEAD_SIZE)
        unrotated_key = project(key_weight).reshape(shape)
        key_rows = rotate(
            unrotated_key, cosine[:, None, :], sine_part[:, None, :]
        ).astype(jnp.bfloat16)
        cache_keys = handed_over(key_rows)
        cache_values = handed_over(project(value_weight).astype(jnp.bfloat16).reshape(shape))
    slot_count = cache_keys.shape[0]
    score_scale = 1.0 / HEAD_SIZE**0.5
    old_scores = (
        jnp.einsum(
            "sjd,id->sji", query_rot, cache_keys, preferred_element_type=jnp.float32
        )
        * score_scale
    )
    new_scores = (
        jnp.einsum("sjd,td->sjt", query_rot, new_keys, preferred_element_type=jnp.float32)
        * score_scale
    )
    slot_ids = jnp.arange(slot_count, dtype=jnp.int32) * split_point + block
    old_live = slot_ids < length
    new_live = (jnp.arange(STEPS)[None, :] <= jnp.arange(STEPS)[:, None]) & (block == 0)
    old_scores = jnp.where(old_live[None, None, :], old_scores, -1e30)
    new_scores = jnp.where(new_live[:, None, :], new_scores, -1e30)
    row_max = jnp.maximum(jnp.max(old_scores, -1), jnp.max(new_scores, -1))
    for bit in range(tree_levels):
        row_max = jnp.maximum(row_max, swapped(row_max, "seq", bit))
    old_exp = jnp.exp(old_scores - row_max[..., None])
    new_exp = jnp.exp(new_scores - row_max[..., None])
    denom = jnp.sum(old_exp, -1) + jnp.sum(new_exp, -1)
    for bit in range(tree_levels):
        denom = denom + swapped(denom, "seq", bit)
    old_probs = (old_exp / denom[..., None]).astype(jnp.bfloat16)
    new_probs = (new_exp / denom[..., None]).astype(jnp.bfloat16)
    partial_sum = jnp.einsum(
        "sji,id->sjd", old_probs, cache_values, preferred_element_type=jnp.float32
    )
    partial_sum = partial_sum + jnp.einsum(
        "sjt,td->sjd", new_probs, new_value, preferred_element_type=jnp.float32
    )
    flat_rows = partial_sum.reshape(STEPS, QPK * HEAD_SIZE)
    for bit in range(tree_levels):
        flat_rows = flat_rows + swapped(flat_rows, "seq", bit)
    share = flat_rows.shape[1] // split_point
    mine = lax.dynamic_slice_in_dim(flat_rows, block * share, share, 1)
    cache = jnp.concatenate([cache_keys, cache_values], 1)[None]
    return (cache, mine.astype(jnp.bfloat16))


def solution(mesh):
    placed = (
        P("groups", "seq", None),
        P("seq", None),
        P("seq", None),
        P("groups"),
        P("groups"),
        P("groups", None, None),
        P("groups", None, None),
        P("groups", None, None),
    )
    return jax.shard_map(
        body,
        mesh=mesh,
        in_specs=placed,
        out_specs=(P(("groups", "seq"), None, None), P("groups", "seq")),
        check_vma=False,
    )
```

```python
import functools

import jax
import jax.numpy as jnp
import numpy as np
from jax import lax
from jax.experimental import pallas as pl
from jax.experimental.pallas import tpu as pltpu
from jax.sharding import PartitionSpec as P

HEAD_SIZE = 128
KEY_VALUE_HEADS = 4
QPK = 8
STEPS = 4


ROPE_BASE = 500000.0


def swapped(block, axis, bit):
    count = lax.axis_size(axis)
    route = []
    for low in range(count):
        high = low | 1 << bit
        if high != low and high < count:
            route += [(low, high), (high, low)]
    return lax.ppermute(block, axis, route)


def rope_table(positions, head_dim):
    freq = ROPE_BASE ** (-(np.arange(head_dim // 2, dtype=np.float64) * 2.0) / head_dim)
    angle = positions.astype(jnp.float32)[:, None] * jnp.asarray(freq, jnp.float32)[None, :]
    return (jnp.cos(angle), jnp.sin(angle))


def rotate(values_in, cosine, sine_part):
    half_dim = values_in.shape[-1] // 2
    lower_half = values_in[..., :half_dim]
    upper_half = values_in[..., half_dim:]
    return jnp.concatenate(
        [
            lower_half * cosine - upper_half * sine_part,
            upper_half * cosine + lower_half * sine_part,
        ],
        -1,
    )


def spread(count):
    side = 1
    while side * side < count:
        side *= 2
    return (side, count // side)


def moved(block, rule):
    groups, seq = lax.axis_size("groups"), lax.axis_size("seq")
    low = spread(seq // 2)[1]
    route = []
    for g in range(groups):
        for s in range(seq):
            place = rule(g, s // 2 // low, s // 2 % low, s % 2)
            if place is not None:
                tg, tz, ty, tc = place
                route.append((g * seq + s, tg * seq + (tz * low + ty) * 2 + tc))
    return lax.ppermute(block, ("groups", "seq"), route)


def to_core(g, z, y, c):
    return (g, z, y, 1 - c)


def to_row(g, z, y, c):
    return (g, z, 1 - y, c)


def to_group(g, z, y, c):
    return (1 - g, z, y, c)


def to_pair(g, z, y, c):
    return (g, z ^ 1, y, c)


def to_middle(g, z, y, c):
    return (g, 3 - z, y, c) if z in (1, 2) else None


def to_end(g, z, y, c):
    return (g, 0 if z == 1 else 3, y, c) if z in (1, 2) else None


VMEM_REF = pl.BlockSpec(memory_space=pltpu.VMEM)
SMEM_REF = pl.BlockSpec(memory_space=pltpu.SMEM)
ANY_REF = pl.BlockSpec(memory_space=pl.ANY)
PARAMS = pltpu.CompilerParams(vmem_limit_bytes=56 << 20)


def cost(flops, moved_bytes):
    return pl.CostEstimate(flops=flops, bytes_accessed=moved_bytes, transcendentals=0)


def fetch(source, target, sem):
    copy = pltpu.make_async_copy(source, target, sem)
    copy.start()
    return copy


def halves_kernel(kind, place, key_weight, value_weight, out, sems):
    depth, columns = out.shape[0], out.shape[1] // 2
    half = 1 - place[0] if kind else place[0]
    rows = pl.ds(pl.multiple_of(half * depth, depth), depth)
    copies = [
        fetch(weight.at[rows], out.at[:, pl.ds(k * columns, columns)], sems.at[k])
        for k, weight in enumerate((key_weight, value_weight))
    ]
    for copy in copies:
        copy.wait()


def weight_half(place, kind, key_weight, value_weight):
    rows, columns = key_weight.shape
    return pl.pallas_call(
        functools.partial(halves_kernel, kind),
        in_specs=[SMEM_REF, ANY_REF, ANY_REF],
        out_specs=VMEM_REF,
        out_shape=jax.ShapeDtypeStruct((rows // 2, 2 * columns), key_weight.dtype),
        scratch_shapes=[pltpu.SemaphoreType.DMA((2,))],
        compiler_params=PARAMS,
        cost_estimate=cost(1000, 1000),
        name="weight_half",
    )(place, key_weight, value_weight)


def prepare_kernel(place, *refs):
    left, kept = refs[-2:]
    rows, depth = kept.shape[1], kept.shape[2]
    width = refs[0].shape[1]
    for who, rows_in in enumerate(refs[:2]):
        square = jnp.zeros((rows, depth), jnp.float32)
        for first in range(0, width, depth):
            part = rows_in[:, first : first + depth].astype(jnp.float32)
            square += part * part
        scale = lax.rsqrt(jnp.sum(square, -1, keepdims=True) / width + 1e-05)
        for core in range(2):

            @pl.when(place[1] == core)
            def _():
                for first in range(0, width, depth):
                    j, c, h = first // (4 * depth), first // (2 * depth) % 2, first // depth % 2
                    if c == core or who == 0:
                        part = rows_in[:, first : first + depth].astype(jnp.float32)
                        part = (part * scale).astype(jnp.bfloat16)
                        if c == core:
                            left[2 * j + h, who] = part
                        else:
                            kept[2 * j + h] = part


def prepared(place, mine, other, blocks):
    rows, width = mine.shape
    depth = width // (4 * blocks)
    tile = 80 if rows % 80 == 0 else rows
    spec = pl.BlockSpec((tile, width), lambda i, place: (i, 0))
    return pl.pallas_call(
        prepare_kernel,
        grid_spec=pltpu.PrefetchScalarGridSpec(
            num_scalar_prefetch=1,
            grid=(rows // tile,),
            in_specs=[spec, spec],
            out_specs=[
                pl.BlockSpec((2 * blocks, 2, tile, depth), lambda i, place: (0, 0, i, 0)),
                pl.BlockSpec((2 * blocks, tile, depth), lambda i, place: (0, i, 0)),
            ],
        ),
        out_shape=[
            jax.ShapeDtypeStruct((2 * blocks, 2, rows, depth), jnp.bfloat16),
            jax.ShapeDtypeStruct((2 * blocks, rows, depth), jnp.bfloat16),
        ],
        compiler_params=PARAMS,
        cost_estimate=cost(1000, 1000),
        name="normed_halves",
    )(place, mine, other)


def after(value, *events):
    return lax.optimization_barrier((value, *events))[0]


def half_index(place, entry, kind):
    half = {0: place[0], 1: 1 - place[0], 2: 0, 3: 1}[kind]
    return place[entry] * 2 + half


def product_kernel(plan, group, parts, with_total, place, both, *refs):
    count = len(plan)
    taken = sum(pair for _, _, pair in plan)
    totals_in = refs[taken : taken + 2 * with_total * parts]
    next_ref = iter(refs)
    outs = refs[-5 - 2 * parts : -5]
    left, right, total, sems, total_sems = refs[-5:]
    rows, depth = both.shape[2], both.shape[3]
    columns = right.shape[2]
    waits = []
    width = columns // parts
    for k, (entry, kind, pair) in enumerate(plan):
        area = pl.ds((k % group) * depth, depth)
        slot = k // group
        index = half_index(place, entry, kind)
        waits.append([fetch(both.at[index], left.at[slot, :, :, area], sems.at[3 * k])])
        for p in range(pair):
            target = right.at[slot, area, pl.ds(p * columns // pair, columns // pair)]
            waits[-1].append(fetch(next(next_ref), target, sems.at[3 * k + 1 + p]))
    carried = [
        fetch(
            ref,
            total.at[pl.ds(k % 2 * rows, rows), pl.ds(k // 2 * width, width)],
            total_sems.at[k],
        )
        for k, ref in enumerate(totals_in)
    ]
    for slot in range(count // group):
        for copies in waits[slot * group : (slot + 1) * group]:
            for copy in copies:
                copy.wait()
        stacked = left[slot].reshape(2 * rows, group * depth)
        value = jnp.dot(stacked, right[slot], preferred_element_type=jnp.float32)
        if slot == 0:
            for copy in carried:
                copy.wait()
        if slot or with_total:
            value += total[...]
        if slot + 1 < count // group:
            total[...] = value
        else:
            for k, out in enumerate(outs):
                out[...] = value[
                    k % 2 * rows : (k % 2 + 1) * rows, k // 2 * width : (k // 2 + 1) * width
                ]


def product(place, both, pieces, totals, group, columns, parts):
    _, _, rows, depth = both.shape
    plan = [(entry, kind, len(arrays)) for entry, kind, *arrays in pieces]
    pieces_flat = [array for _, _, *arrays in pieces for array in arrays]
    count = len(plan)
    out = jax.ShapeDtypeStruct((rows, columns // parts), jnp.float32)
    return pl.pallas_call(
        functools.partial(product_kernel, plan, group, parts, bool(totals)),
        in_specs=[SMEM_REF] + [ANY_REF] * (1 + len(pieces_flat) + len(totals)),
        out_specs=[VMEM_REF] * (2 * parts),
        out_shape=[out] * (2 * parts),
        scratch_shapes=[
            pltpu.VMEM((count // group, 2, rows, group * depth), both.dtype),
            pltpu.VMEM((count // group, group * depth, columns), both.dtype),
            pltpu.VMEM((2 * rows, columns), jnp.float32),
            pltpu.SemaphoreType.DMA((3 * count,)),
            pltpu.SemaphoreType.DMA((2 * parts,)),
        ],
        compiler_params=PARAMS,
        cost_estimate=cost(1 << 36, 1000),
        name="add_product",
    )(place, both, *pieces_flat, *totals)


def own_product_kernel(plan, place, both, kept, *refs):
    count = len(plan)
    pieces, sums_in = refs[: 2 * count], refs[2 * count : 2 * count + 2]
    outs = refs[2 * count + 2 : 2 * count + 4]
    left, right, total, came, sems = refs[-5:]
    depth, columns = kept.shape[2], outs[0].shape[1]
    waits = []
    for k in range(2 * count):
        index = half_index(place, *plan[k // 2])
        source = kept.at[index] if k % 2 else both.at[index, 0]
        area = pl.ds(k * depth, depth)
        waits.append(fetch(source, left.at[:, area], sems.at[2 * k]))
        waits.append(fetch(pieces[k], right.at[area], sems.at[2 * k + 1]))
    waits.append(fetch(sums_in[0], total, sems.at[4 * count]))
    waits.append(fetch(sums_in[1], came, sems.at[4 * count + 1]))
    for copy in waits:
        copy.wait()
    for k, out in enumerate(outs):
        area = slice(k * columns, (k + 1) * columns)
        out[...] = (total[:, area] + came[:, area]) + jnp.dot(
            left[...], right[:, area], preferred_element_type=jnp.float32
        )


def own_product(place, both, kept, pieces, sums):
    _, rows, depth = kept.shape
    columns = sums[0].shape[1]
    count = len(pieces)
    plan = [(entry, kind) for entry, kind, _, _ in pieces]
    operands = [block for _, _, *blocks in pieces for block in blocks]
    out = jax.ShapeDtypeStruct((rows, columns // 2), jnp.float32)
    return pl.pallas_call(
        functools.partial(own_product_kernel, plan),
        in_specs=[SMEM_REF] + [ANY_REF] * (4 + 2 * count),
        out_specs=[VMEM_REF] * 2,
        out_shape=[out] * 2,
        scratch_shapes=[
            pltpu.VMEM((rows, 2 * count * depth), kept.dtype),
            pltpu.VMEM((2 * count * depth, columns), kept.dtype),
            pltpu.VMEM((rows, columns), jnp.float32),
            pltpu.VMEM((rows, columns), jnp.float32),
            pltpu.SemaphoreType.DMA((4 * count + 2,)),
        ],
        compiler_params=PARAMS,
        cost_estimate=cost(1 << 36, 1000),
        name="own_product",
    )(place, both, kept, *operands, *sums)


def rows_kernel(plan, part, rotated, place, lengths, owner, both, kept, *refs):
    count = len(plan)
    pieces, refs = refs[: 2 * count], refs[2 * count :]
    turn = refs[1 : 1 + 2 * rotated]
    out, left, right, total, scratch, sems = refs[-6:]
    depth, columns = kept.shape[2], total.shape[1]
    waits, sem = [], 0
    for k in range(2 * count):
        index = half_index(place, *plan[k // 2])
        source = kept.at[index] if k % 2 else both.at[index, 0]
        area = pl.ds(k * depth, depth)
        waits.append(fetch(source, left.at[:, area], sems.at[sem]))
        piece = pieces[k].at[:, pl.ds(part * columns, columns)]
        waits.append(fetch(piece, right.at[area], sems.at[sem + 1]))
        sem += 2
    waits.append(fetch(refs[0], total, sems.at[sem]))
    for copy in waits:
        copy.wait()
    total[...] += jnp.dot(left[...], right[...], preferred_element_type=jnp.float32)
    count_requests, count_rows = lengths.shape[0], scratch.shape[0]
    index = place[2] * count_rows + lax.broadcasted_iota(jnp.int32, scratch.shape, 0)
    for r in range(count_requests):
        live = index < lengths[r]
        for h in range(KEY_VALUE_HEADS):
            part = total[
                r * count_rows : (r + 1) * count_rows, h * HEAD_SIZE : (h + 1) * HEAD_SIZE
            ]
            if rotated:
                turned = jnp.concatenate([part[:, HEAD_SIZE // 2 :], part[:, : HEAD_SIZE // 2]], 1)
                part = part * turn[0][...] + turned * turn[1][...]
            scratch[...] = jnp.where(live, part, 0.0)
            peer = owner[r * KEY_VALUE_HEADS + h]
            for b in range(2):
                picked = scratch[pl.ds(b, count_rows // 2, stride=2), :]
                out[peer * 2 + b] = picked.astype(jnp.bfloat16)


def outgoing_rows(place, lengths, owner, both, kept, plan, pieces, part, total, turn, token):
    _, rows, depth = kept.shape
    columns = total.shape[1]
    count = len(plan)
    count_rows = rows // lengths.shape[0]
    out = jax.ShapeDtypeStruct((owner.shape[0] * 2, count_rows // 2, HEAD_SIZE), jnp.bfloat16)

    def kernel(place_ref, lengths_ref, owner_ref, token_ref, *refs):
        rows_kernel(plan, part, bool(turn), place_ref, lengths_ref, owner_ref, *refs)

    operands = [both, kept, *pieces, total]
    return pl.pallas_call(
        kernel,
        in_specs=[SMEM_REF] * 3
        + [ANY_REF] * (1 + len(operands))
        + [VMEM_REF] * len(turn),
        out_specs=VMEM_REF,
        out_shape=out,
        scratch_shapes=[
            pltpu.VMEM((rows, 2 * count * depth), kept.dtype),
            pltpu.VMEM((2 * count * depth, columns), kept.dtype),
            pltpu.VMEM((rows, columns), jnp.float32),
            pltpu.VMEM((count_rows, HEAD_SIZE), jnp.float32),
            pltpu.SemaphoreType.DMA((4 * count + 1,)),
        ],
        compiler_params=PARAMS,
        cost_estimate=cost(1000, 1000),
        name="cache_rows",
    )(place, lengths, owner, token, *operands, *turn)


HERE, THERE = 3, 7


def body(hidden, key_weight, value_weight, lengths, owner, dec_query, dec_key, dec_value):
    count_requests, count_rows, width = hidden.shape
    device_id = lax.axis_index("seq")
    group_id = lax.axis_index("groups")
    seq = lax.axis_size("seq")
    planned = seq == 16 and lax.axis_size("groups") == 2
    decode_peers = count_requests * KEY_VALUE_HEADS
    split_point = seq // decode_peers
    tree_levels = split_point.bit_length() - 1
    rows_per_peer = count_rows // split_point
    positions = device_id * count_rows + jnp.arange(count_rows, dtype=jnp.int32)
    total_rows = count_requests * count_rows
    flat = hidden.reshape(total_rows, width)
    if planned:
        core = device_id % 2
        z, y = device_id // 4, device_id // 2 % 2
        layers = [z, z ^ 1, jnp.where(z < 2, 2, 1), jnp.where(z < 2, 3, 0)]
        is_end = (z == 0) | (z == 3)
        place = [group_id, core, device_id]
        place += [layer * 2 + y for layer in layers]
        place += [layer * 2 + 1 - y for layer in layers]
        place = jnp.stack([jnp.asarray(entry, jnp.int32) for entry in place])
    else:
        widened = flat.astype(jnp.float32)
        normed = (
            widened * lax.rsqrt(jnp.mean(widened * widened, -1, keepdims=True) + 1e-05)
        ).astype(jnp.bfloat16)

        def project(weight):
            whole = lax.all_gather(weight, "seq", axis=0, tiled=True)
            return jnp.dot(normed, whole, preferred_element_type=jnp.float32)

    pair_ids = jnp.arange(decode_peers, dtype=jnp.int32)
    matches = owner[None, :] == pair_ids[:, None]
    inverse_order = jnp.sum(jnp.where(matches, pair_ids[None, :], 0), axis=1)
    live_rows = positions[None, :] < lengths[:, None]

    def handed_over(rows):
        rows = jnp.where(live_rows[:, :, None, None], rows, jnp.zeros_like(rows))
        pair_rows = jnp.transpose(rows, (0, 2, 1, 3)).reshape(decode_peers, count_rows, HEAD_SIZE)
        sorted_rows = pair_rows[inverse_order].reshape(
            decode_peers, rows_per_peer, split_point, HEAD_SIZE
        )
        outgoing = jnp.transpose(sorted_rows, (0, 2, 1, 3)).reshape(
            decode_peers * split_point, rows_per_peer, HEAD_SIZE
        )
        return lax.all_to_all(outgoing, "seq", split_axis=0, concat_axis=1, tiled=True)[0]

    decode_peer = device_id // split_point
    block = device_id % split_point
    source_pair = jnp.sum(jnp.where(owner == decode_peer, pair_ids, 0))
    source_request = source_pair // KEY_VALUE_HEADS
    length = jnp.sum(
        jnp.where(jnp.arange(count_requests, dtype=jnp.int32) == source_request, lengths, 0)
    )
    query = lax.dynamic_index_in_dim(dec_query, decode_peer, 0, keepdims=False)
    new_key = lax.dynamic_index_in_dim(dec_key, decode_peer, 0, keepdims=False)
    new_value = lax.dynamic_index_in_dim(dec_value, decode_peer, 0, keepdims=False)
    step_pos = length + jnp.arange(STEPS, dtype=jnp.int32)
    step_cos, step_sin = rope_table(step_pos, HEAD_SIZE)
    query_rot = rotate(
        query.astype(jnp.float32).reshape(STEPS, QPK, HEAD_SIZE),
        step_cos[:, None, :],
        step_sin[:, None, :],
    ).astype(jnp.bfloat16)
    new_keys = rotate(new_key.astype(jnp.float32), step_cos, step_sin).astype(jnp.bfloat16)
    cosine, sine_part = rope_table(positions, HEAD_SIZE)
    if planned:
        turn = (
            jnp.concatenate([cosine, cosine], 1),
            jnp.concatenate([-sine_part, sine_part], 1),
        )
        columns = key_weight.shape[1]

        sent = weight_half(place, 0, key_weight, value_weight)
        near = moved(sent, to_pair)
        middle = moved(sent, to_middle)
        across = moved(sent, to_row)
        other = moved(flat, to_core)
        rest = weight_half(place, 1, key_weight, after(value_weight, sent))
        came = (near, middle, across, other, rest, *turn, query_rot, new_keys)
        end_b = moved(after(middle, *came), to_end)
        middle_c = moved(after(near, *came), to_middle)
        near_y = moved(after(near, *came), to_row)
        across_x = moved(after(across, *came), to_group)
        both, kept = prepared(place, after(flat, *came), other, seq // 2)
        came = (end_b, middle_c, near_y, across_x, both)
        end_c = moved(after(middle_c, *came), to_end)
        block_b = jnp.where(is_end, after(end_b, *came), middle)
        block_yb = moved(block_b, to_row)
        block_xb = moved(block_b, to_group)
        pieces = [(HERE, 0, sent), (HERE, 1, rest), (THERE, 0, across), (THERE, 1, across_x)]
        pieces += [(HERE + 1, 0, near), (THERE + 1, 0, near_y)]
        totals = product(place, after(both, *came), pieces, (), 3, 2 * columns, 1)
        came = (end_c, block_yb, block_xb, totals[0])
        near_rest = moved(after(rest, *came), to_pair)
        block_c = jnp.where(is_end, after(end_c, *came), middle_c)
        block_xc = moved(block_c, to_group)
        block_yc = moved(block_c, to_row)
        pieces = [(HERE + 2, 0, block_b), (HERE + 2, 1, block_xb)]
        pieces += [(THERE + 2, 0, block_yb), (HERE + 3, 0, block_c)]
        total, given = product(place, after(both, *came), pieces, totals, 4, 2 * columns, 1)
        came = (near_rest, block_xc, block_yc, total)
        ends = [moved(after(across_x, *came), to_pair), moved(after(block_yb, *came), to_group)]
        ends.append(moved(after(block_xc, *came), to_row))
        pieces = [(HERE + 1, 1, near_rest), (HERE + 3, 1, block_xc), (THERE + 3, 0, block_yc)]
        pieces = [
            (entry, kind, after(block, *came), moved(after(block, *came), to_core))
            for entry, kind, block in pieces
        ]
        given = moved(after(given, *came), to_core)
        sums = own_product(place, both, kept, pieces, (total, given))
        came = (*ends, *sums)
        pieces = []
        for end in ends:
            end = after(end, *came)
            pieces += [end, moved(end, to_core)]
        plan = [(THERE + 1, 1), (THERE + 2, 1), (THERE + 3, 1)]
        caches = []
        token = place
        for k, turned in enumerate((turn, ())):
            outgoing = outgoing_rows(
                place, lengths, owner, both, kept, plan, pieces, k, sums[k], turned, token
            )
            caches.append(
                lax.all_to_all(outgoing, "seq", split_axis=0, concat_axis=1, tiled=True)[0]
            )
            token = outgoing
        cache_keys, cache_values = caches
    else:
        shape = (count_requests, count_rows, KEY_VALUE_HEADS, HEAD_SIZE)
        unrotated_key = project(key_weight).reshape(shape)
        key_rows = rotate(
            unrotated_key, cosine[:, None, :], sine_part[:, None, :]
        ).astype(jnp.bfloat16)
        cache_keys = handed_over(key_rows)
        cache_values = handed_over(project(value_weight).astype(jnp.bfloat16).reshape(shape))
    slot_count = cache_keys.shape[0]
    score_scale = 1.0 / HEAD_SIZE**0.5
    old_scores = (
        jnp.einsum(
            "sjd,id->sji", query_rot, cache_keys, preferred_element_type=jnp.float32
        )
        * score_scale
    )
    new_scores = (
        jnp.einsum("sjd,td->sjt", query_rot, new_keys, preferred_element_type=jnp.float32)
        * score_scale
    )
    slot_ids = jnp.arange(slot_count, dtype=jnp.int32) * split_point + block
    old_live = slot_ids < length
    new_live = (jnp.arange(STEPS)[None, :] <= jnp.arange(STEPS)[:, None]) & (block == 0)
    old_scores = jnp.where(old_live[None, None, :], old_scores, -1e30)
    new_scores = jnp.where(new_live[:, None, :], new_scores, -1e30)
    row_max = jnp.maximum(jnp.max(old_scores, -1), jnp.max(new_scores, -1))
    for bit in range(tree_levels):
        row_max = jnp.maximum(row_max, swapped(row_max, "seq", bit))
    old_exp = jnp.exp(old_scores - row_max[..., None])
    new_exp = jnp.exp(new_scores - row_max[..., None])
    denom = jnp.sum(old_exp, -1) + jnp.sum(new_exp, -1)
    for bit in range(tree_levels):
        denom = denom + swapped(denom, "seq", bit)
    old_probs = (old_exp / denom[..., None]).astype(jnp.bfloat16)
    new_probs = (new_exp / denom[..., None]).astype(jnp.bfloat16)
    partial_sum = jnp.einsum(
        "sji,id->sjd", old_probs, cache_values, preferred_element_type=jnp.float32
    )
    partial_sum = partial_sum + jnp.einsum(
        "sjt,td->sjd", new_probs, new_value, preferred_element_type=jnp.float32
    )
    flat_rows = partial_sum.reshape(STEPS, QPK * HEAD_SIZE)
    for bit in range(tree_levels):
        flat_rows = flat_rows + swapped(flat_rows, "seq", bit)
    share = flat_rows.shape[1] // split_point
    mine = lax.dynamic_slice_in_dim(flat_rows, block * share, share, 1)
    cache = jnp.concatenate([cache_keys, cache_values], 1)[None]
    return (cache, mine.astype(jnp.bfloat16))


def solution(mesh):
    placed = (
        P("groups", "seq", None),
        P("seq", None),
        P("seq", None),
        P("groups"),
        P("groups"),
        P("groups", None, None),
        P("groups", None, None),
        P("groups", None, None),
    )
    return jax.shard_map(
        body,
        mesh=mesh,
        in_specs=placed,
        out_specs=(P(("groups", "seq"), None, None), P("groups", "seq")),
        check_vma=False,
    )
```

```python
import functools

import jax
import jax.numpy as jnp
import numpy as np
from jax import lax
from jax.experimental import pallas as pl
from jax.experimental.pallas import tpu as pltpu
from jax.sharding import PartitionSpec as P

HEAD_SIZE = 128
KEY_VALUE_HEADS = 4
QPK = 8
STEPS = 4


ROPE_BASE = 500000.0


def swapped(block, axis, bit):
    count = lax.axis_size(axis)
    route = []
    for low in range(count):
        high = low | 1 << bit
        if high != low and high < count:
            route += [(low, high), (high, low)]
    return lax.ppermute(block, axis, route)


def rope_table(positions, head_dim):
    freq = ROPE_BASE ** (-(np.arange(head_dim // 2, dtype=np.float64) * 2.0) / head_dim)
    angle = positions.astype(jnp.float32)[:, None] * jnp.asarray(freq, jnp.float32)[None, :]
    return (jnp.cos(angle), jnp.sin(angle))


def rotate(values_in, cosine, sine_part):
    half_dim = values_in.shape[-1] // 2
    lower_half = values_in[..., :half_dim]
    upper_half = values_in[..., half_dim:]
    return jnp.concatenate(
        [
            lower_half * cosine - upper_half * sine_part,
            upper_half * cosine + lower_half * sine_part,
        ],
        -1,
    )


def spread(count):
    side = 1
    while side * side < count:
        side *= 2
    return (side, count // side)


def moved(block, rule):
    groups, seq = lax.axis_size("groups"), lax.axis_size("seq")
    low = spread(seq // 2)[1]
    route = []
    for g in range(groups):
        for s in range(seq):
            place = rule(g, s // 2 // low, s // 2 % low, s % 2)
            if place is not None:
                tg, tz, ty, tc = place
                route.append((g * seq + s, tg * seq + (tz * low + ty) * 2 + tc))
    return lax.ppermute(block, ("groups", "seq"), route)


def to_core(g, z, y, c):
    return (g, z, y, 1 - c)


def to_row(g, z, y, c):
    return (g, z, 1 - y, c)


def to_group(g, z, y, c):
    return (1 - g, z, y, c)


def to_pair(g, z, y, c):
    return (g, z ^ 1, y, c)


def to_middle(g, z, y, c):
    return (g, 3 - z, y, c) if z in (1, 2) else None


def to_end(g, z, y, c):
    return (g, 0 if z == 1 else 3, y, c) if z in (1, 2) else None


VMEM_REF = pl.BlockSpec(memory_space=pltpu.VMEM)
SMEM_REF = pl.BlockSpec(memory_space=pltpu.SMEM)
ANY_REF = pl.BlockSpec(memory_space=pl.ANY)
PARAMS = pltpu.CompilerParams(vmem_limit_bytes=56 << 20)
SMALL = pltpu.CompilerParams(vmem_limit_bytes=16 << 20)


def cost(flops, moved_bytes):
    return pl.CostEstimate(flops=flops, bytes_accessed=moved_bytes, transcendentals=0)


def fetch(source, target, sem):
    copy = pltpu.make_async_copy(source, target, sem)
    copy.start()
    return copy


def weight_half(half, *weights):
    depth = weights[0].shape[0] // 2
    return jnp.concatenate(
        [lax.dynamic_slice_in_dim(weight, half * depth, depth, 0) for weight in weights], 1
    )


def prepare_kernel(place, *refs):
    left, kept = refs[-2:]
    rows, depth = kept.shape[1], kept.shape[2]
    width = refs[0].shape[1]
    for who, rows_in in enumerate(refs[:2]):
        square = jnp.zeros((rows, depth), jnp.float32)
        for first in range(0, width, depth):
            part = rows_in[:, first : first + depth].astype(jnp.float32)
            square += part * part
        scale = lax.rsqrt(jnp.sum(square, -1, keepdims=True) / width + 1e-05)
        for core in range(2):

            @pl.when(place[1] == core)
            def _():
                for first in range(0, width, depth):
                    j, c, h = first // (4 * depth), first // (2 * depth) % 2, first // depth % 2
                    if c == core or who == 0:
                        part = rows_in[:, first : first + depth].astype(jnp.float32)
                        part = (part * scale).astype(jnp.bfloat16)
                        if c == core:
                            left[2 * j + h, who] = part
                        else:
                            kept[2 * j + h] = part


def prepared(place, mine, other, blocks):
    rows, width = mine.shape
    depth = width // (4 * blocks)
    tile = 80 if rows % 80 == 0 else rows
    spec = pl.BlockSpec((tile, width), lambda i, place: (i, 0))
    return pl.pallas_call(
        prepare_kernel,
        grid_spec=pltpu.PrefetchScalarGridSpec(
            num_scalar_prefetch=1,
            grid=(rows // tile,),
            in_specs=[spec, spec],
            out_specs=[
                pl.BlockSpec((2 * blocks, 2, tile, depth), lambda i, place: (0, 0, i, 0)),
                pl.BlockSpec((2 * blocks, tile, depth), lambda i, place: (0, i, 0)),
            ],
        ),
        out_shape=[
            jax.ShapeDtypeStruct((2 * blocks, 2, rows, depth), jnp.bfloat16),
            jax.ShapeDtypeStruct((2 * blocks, rows, depth), jnp.bfloat16),
        ],
        compiler_params=PARAMS,
        cost_estimate=cost(1000, 1000),
        name="normed_halves",
    )(place, mine, other)


def after(value, *events):
    return lax.optimization_barrier((value, *events))[0]


def half_index(place, entry, kind):
    half = {0: place[0], 1: 1 - place[0], 2: 0, 3: 1}[kind]
    return place[entry] * 2 + half


def product_kernel(plan, group, parts, with_total, place, both, *refs):
    count = len(plan)
    taken = sum(pair for _, _, pair in plan)
    totals_in = refs[taken : taken + 2 * with_total * parts]
    next_ref = iter(refs)
    outs = refs[-5 - 2 * parts : -5]
    left, right, total, sems, total_sems = refs[-5:]
    rows, depth = both.shape[2], both.shape[3]
    columns = right.shape[2]
    waits = []
    width = columns // parts
    for k, (entry, kind, pair) in enumerate(plan):
        area = pl.ds((k % group) * depth, depth)
        slot = k // group
        index = half_index(place, entry, kind)
        waits.append([fetch(both.at[index], left.at[slot, :, :, area], sems.at[3 * k])])
        for p in range(pair):
            target = right.at[slot, area, pl.ds(p * columns // pair, columns // pair)]
            waits[-1].append(fetch(next(next_ref), target, sems.at[3 * k + 1 + p]))
    carried = [
        fetch(
            ref,
            total.at[pl.ds(k % 2 * rows, rows), pl.ds(k // 2 * width, width)],
            total_sems.at[k],
        )
        for k, ref in enumerate(totals_in)
    ]
    for slot in range(count // group):
        for copies in waits[slot * group : (slot + 1) * group]:
            for copy in copies:
                copy.wait()
        stacked = left[slot].reshape(2 * rows, group * depth)
        value = jnp.dot(stacked, right[slot], preferred_element_type=jnp.float32)
        if slot == 0:
            for copy in carried:
                copy.wait()
        if slot or with_total:
            value += total[...]
        if slot + 1 < count // group:
            total[...] = value
        else:
            for k, out in enumerate(outs):
                out[...] = value[
                    k % 2 * rows : (k % 2 + 1) * rows, k // 2 * width : (k // 2 + 1) * width
                ]


def product(place, both, pieces, totals, group, columns, parts, params=PARAMS):
    _, _, rows, depth = both.shape
    plan = [(entry, kind, len(arrays)) for entry, kind, *arrays in pieces]
    pieces_flat = [array for _, _, *arrays in pieces for array in arrays]
    count = len(plan)
    out = jax.ShapeDtypeStruct((rows, columns // parts), jnp.float32)
    return pl.pallas_call(
        functools.partial(product_kernel, plan, group, parts, bool(totals)),
        in_specs=[SMEM_REF] + [ANY_REF] * (1 + len(pieces_flat) + len(totals)),
        out_specs=[VMEM_REF] * (2 * parts),
        out_shape=[out] * (2 * parts),
        scratch_shapes=[
            pltpu.VMEM((count // group, 2, rows, group * depth), both.dtype),
            pltpu.VMEM((count // group, group * depth, columns), both.dtype),
            pltpu.VMEM((2 * rows, columns), jnp.float32),
            pltpu.SemaphoreType.DMA((3 * count,)),
            pltpu.SemaphoreType.DMA((2 * parts,)),
        ],
        compiler_params=params,
        cost_estimate=cost(1 << 36, 1000),
        name="add_product",
    )(place, both, *pieces_flat, *totals)


def rows_kernel(place, lengths, owner, total, came, cosine, sine, out, scratch):
    columns = total.shape[1] // 2
    count_requests, count_rows = lengths.shape[0], scratch.shape[0]
    index = place[2] * count_rows + lax.broadcasted_iota(jnp.int32, scratch.shape, 0)
    for r in range(count_requests):
        live = index < lengths[r]
        for h in range(KEY_VALUE_HEADS):
            for part in range(2):
                first = part * columns + h * HEAD_SIZE
                area = (
                    slice(r * count_rows, (r + 1) * count_rows),
                    slice(first, first + HEAD_SIZE),
                )
                rows = total[area] + came[area]
                if part == 0:
                    half = HEAD_SIZE // 2
                    turned = jnp.concatenate([rows[:, half:], rows[:, :half]], 1)
                    rows = rows * cosine[...] + turned * sine[...]
                scratch[...] = jnp.where(live, rows, 0.0)
                peer = owner[r * KEY_VALUE_HEADS + h]
                lanes = slice(part * HEAD_SIZE, (part + 1) * HEAD_SIZE)
                for b in range(2):
                    picked = scratch[pl.ds(b, count_rows // 2, stride=2), :]
                    out[peer * 2 + b, :, lanes] = picked.astype(jnp.bfloat16)


def outgoing_rows(place, lengths, owner, total, came, turn):
    count_rows = total.shape[0] // lengths.shape[0]
    out = (owner.shape[0] * 2, count_rows // 2, 2 * HEAD_SIZE)
    return pl.pallas_call(
        rows_kernel,
        in_specs=[SMEM_REF] * 3 + [VMEM_REF] * 4,
        out_specs=VMEM_REF,
        out_shape=jax.ShapeDtypeStruct(out, jnp.bfloat16),
        scratch_shapes=[pltpu.VMEM((count_rows, HEAD_SIZE), jnp.float32)],
        compiler_params=SMALL,
        cost_estimate=cost(1000, 1000),
        name="cache_rows",
    )(place, lengths, owner, total, came, *turn)


def decode_kernel(place, cache, query, new_keys, new_value, out):
    slots, queries = cache.shape[0], query.shape[0]
    block, length = place[0], place[1]
    contract = (((1,), (1,)), ((), ()))
    scale = 1.0 / HEAD_SIZE**0.5
    old = lax.dot_general(
        query[...], cache[:, :HEAD_SIZE], contract, preferred_element_type=jnp.float32
    )
    slot = lax.broadcasted_iota(jnp.int32, old.shape, 1) * 2 + block
    old = jnp.where(slot < length, old * scale, -1e30)
    new = lax.dot_general(query[...], new_keys[...], contract, preferred_element_type=jnp.float32)
    step = lax.broadcasted_iota(jnp.int32, new.shape, 0) // QPK
    token = lax.broadcasted_iota(jnp.int32, new.shape, 1)
    new = jnp.where((token <= step) & (block == 0), new * scale, -1e30)
    top = jnp.maximum(jnp.max(old, 1, keepdims=True), jnp.max(new, 1, keepdims=True))
    old, new = jnp.exp(old - top), jnp.exp(new - top)
    total = jnp.sum(old, 1, keepdims=True) + jnp.sum(new, 1, keepdims=True)
    sums = jnp.dot(
        old.astype(jnp.bfloat16), cache[:, HEAD_SIZE:], preferred_element_type=jnp.float32
    )
    out[:, :HEAD_SIZE] = sums + jnp.dot(
        new.astype(jnp.bfloat16), new_value[...], preferred_element_type=jnp.float32
    )
    half = (queries, HEAD_SIZE // 2)
    out[:, HEAD_SIZE : HEAD_SIZE + half[1]] = jnp.broadcast_to(top, half)
    out[:, HEAD_SIZE + half[1] :] = jnp.broadcast_to(total, half)


def decoded(block, length, cache, query, new_keys, new_value):
    pad = ((0, 16 - STEPS), (0, 0))
    new_keys, new_value = jnp.pad(new_keys, pad), jnp.pad(new_value, pad)
    mine = pl.pallas_call(
        decode_kernel,
        in_specs=[SMEM_REF] + [VMEM_REF] * 4,
        out_specs=VMEM_REF,
        out_shape=jax.ShapeDtypeStruct((STEPS * QPK, 2 * HEAD_SIZE), jnp.float32),
        compiler_params=SMALL,
        cost_estimate=cost(1000, 1000),
        name="decode",
    )(jnp.stack([block, length]), cache, query, new_keys, new_value)
    theirs = moved(mine, to_core)
    share = QPK // 2

    def heads(array):
        array = array.reshape(STEPS, QPK, 2 * HEAD_SIZE)
        array = lax.dynamic_slice_in_dim(array, block * share, share, 1)
        last = HEAD_SIZE + HEAD_SIZE // 2
        return array[..., :HEAD_SIZE], array[..., HEAD_SIZE : HEAD_SIZE + 1], array[..., last : last + 1]

    sums_a, top_a, total_a = heads(mine)
    sums_b, top_b, total_b = heads(theirs)
    top = jnp.maximum(top_a, top_b)
    scale_a, scale_b = jnp.exp(top_a - top), jnp.exp(top_b - top)
    sums = sums_a * scale_a + sums_b * scale_b
    return (sums / (total_a * scale_a + total_b * scale_b)).reshape(STEPS, share * HEAD_SIZE)


HERE, THERE = 3, 7


def body(hidden, key_weight, value_weight, lengths, owner, dec_query, dec_key, dec_value):
    count_requests, count_rows, width = hidden.shape
    device_id = lax.axis_index("seq")
    group_id = lax.axis_index("groups")
    seq = lax.axis_size("seq")
    planned = seq == 16 and lax.axis_size("groups") == 2
    decode_peers = count_requests * KEY_VALUE_HEADS
    split_point = seq // decode_peers
    tree_levels = split_point.bit_length() - 1
    rows_per_peer = count_rows // split_point
    positions = device_id * count_rows + jnp.arange(count_rows, dtype=jnp.int32)
    total_rows = count_requests * count_rows
    flat = hidden.reshape(total_rows, width)
    if planned:
        core = device_id % 2
        z, y = device_id // 4, device_id // 2 % 2
        layers = [z, z ^ 1, jnp.where(z < 2, 2, 1), jnp.where(z < 2, 3, 0)]
        is_end = (z == 0) | (z == 3)
        place = [group_id, core, device_id]
        place += [layer * 2 + y for layer in layers]
        place += [layer * 2 + 1 - y for layer in layers]
        place = jnp.stack([jnp.asarray(entry, jnp.int32) for entry in place])
    else:
        widened = flat.astype(jnp.float32)
        normed = (
            widened * lax.rsqrt(jnp.mean(widened * widened, -1, keepdims=True) + 1e-05)
        ).astype(jnp.bfloat16)

        def project(weight):
            whole = lax.all_gather(weight, "seq", axis=0, tiled=True)
            return jnp.dot(normed, whole, preferred_element_type=jnp.float32)

    pair_ids = jnp.arange(decode_peers, dtype=jnp.int32)
    matches = owner[None, :] == pair_ids[:, None]
    inverse_order = jnp.sum(jnp.where(matches, pair_ids[None, :], 0), axis=1)
    live_rows = positions[None, :] < lengths[:, None]

    def handed_over(rows):
        rows = jnp.where(live_rows[:, :, None, None], rows, jnp.zeros_like(rows))
        pair_rows = jnp.transpose(rows, (0, 2, 1, 3)).reshape(decode_peers, count_rows, HEAD_SIZE)
        sorted_rows = pair_rows[inverse_order].reshape(
            decode_peers, rows_per_peer, split_point, HEAD_SIZE
        )
        outgoing = jnp.transpose(sorted_rows, (0, 2, 1, 3)).reshape(
            decode_peers * split_point, rows_per_peer, HEAD_SIZE
        )
        return lax.all_to_all(outgoing, "seq", split_axis=0, concat_axis=1, tiled=True)[0]

    decode_peer = device_id // split_point
    block = device_id % split_point
    source_pair = jnp.sum(jnp.where(owner == decode_peer, pair_ids, 0))
    source_request = source_pair // KEY_VALUE_HEADS
    length = jnp.sum(
        jnp.where(jnp.arange(count_requests, dtype=jnp.int32) == source_request, lengths, 0)
    )
    query = lax.dynamic_index_in_dim(dec_query, decode_peer, 0, keepdims=False)
    new_key = lax.dynamic_index_in_dim(dec_key, decode_peer, 0, keepdims=False)
    new_value = lax.dynamic_index_in_dim(dec_value, decode_peer, 0, keepdims=False)
    step_pos = length + jnp.arange(STEPS, dtype=jnp.int32)
    step_cos, step_sin = rope_table(step_pos, HEAD_SIZE)
    query_rot = rotate(
        query.astype(jnp.float32).reshape(STEPS, QPK, HEAD_SIZE),
        step_cos[:, None, :],
        step_sin[:, None, :],
    ).astype(jnp.bfloat16)
    new_keys = rotate(new_key.astype(jnp.float32), step_cos, step_sin).astype(jnp.bfloat16)
    cosine, sine_part = rope_table(positions, HEAD_SIZE)
    if planned:
        turn = (
            jnp.concatenate([cosine, cosine], 1),
            jnp.concatenate([-sine_part, sine_part], 1),
        )
        columns = key_weight.shape[1]

        sent = weight_half(group_id, key_weight, value_weight)
        near = moved(sent, to_pair)
        middle = moved(sent, to_middle)
        across = moved(sent, to_row)
        other = moved(flat, to_core)
        rest = weight_half(1 - group_id, key_weight, after(value_weight, sent))
        came = (near, middle, across, other, rest, *turn, query_rot, new_keys)
        end_b = moved(after(middle, *came), to_end)
        middle_c = moved(after(near, *came), to_middle)
        near_y = moved(after(near, *came), to_row)
        across_x = moved(after(across, *came), to_group)
        both, kept = prepared(place, after(flat, *came), other, seq // 2)
        came = (end_b, middle_c, near_y, across_x, both)
        end_c = moved(after(middle_c, *came), to_end)
        block_b = jnp.where(is_end, after(end_b, *came), middle)
        block_yb = moved(block_b, to_row)
        block_xb = moved(block_b, to_group)
        pieces = [(HERE, 0, sent), (HERE, 1, rest), (THERE, 0, across), (THERE, 1, across_x)]
        pieces += [(HERE + 1, 0, near), (THERE + 1, 0, near_y)]
        totals = product(place, after(both, *came), pieces, (), 3, 2 * columns, 1)
        came = (end_c, block_yb, block_xb, totals[0])
        near_rest = moved(after(rest, *came), to_pair)
        block_c = jnp.where(is_end, after(end_c, *came), middle_c)
        block_xc = moved(block_c, to_group)
        block_yc = moved(block_c, to_row)
        pieces = [(HERE + 2, 0, block_b), (HERE + 2, 1, block_xb)]
        pieces += [(THERE + 2, 0, block_yb), (HERE + 3, 0, block_c)]
        total, given = product(place, after(both, *came), pieces, totals, 4, 2 * columns, 1)
        came = (near_rest, block_xc, block_yc, total)
        ends = [moved(after(across_x, *came), to_pair), moved(after(block_yb, *came), to_group)]
        ends.append(moved(after(block_xc, *came), to_row))
        pieces = [(HERE + 1, 1, near_rest), (HERE + 3, 1, block_xc), (THERE + 3, 0, block_yc)]
        totals = product(place, after(both, *came), pieces, (total, given), 3, 2 * columns, 1)
        came = (*ends, *totals)
        spots = (THERE + 1, THERE + 2, THERE + 3)
        pieces = [(spot, 1, after(end, *came)) for spot, end in zip(spots, ends)]
        total, given = product(place, both, pieces, totals, 3, 2 * columns, 1, SMALL)
        outgoing = outgoing_rows(place, lengths, owner, total, moved(given, to_core), turn)
        incoming = lax.all_to_all(outgoing, "seq", split_axis=0, concat_axis=1, tiled=True)
        mine = decoded(
            device_id % 2, length, incoming[0], query_rot.reshape(STEPS * QPK, HEAD_SIZE),
            new_keys, new_value,
        )
        return (incoming, mine.astype(jnp.bfloat16))
    else:
        shape = (count_requests, count_rows, KEY_VALUE_HEADS, HEAD_SIZE)
        unrotated_key = project(key_weight).reshape(shape)
        key_rows = rotate(
            unrotated_key, cosine[:, None, :], sine_part[:, None, :]
        ).astype(jnp.bfloat16)
        cache_keys = handed_over(key_rows)
        cache_values = handed_over(project(value_weight).astype(jnp.bfloat16).reshape(shape))
    slot_count = cache_keys.shape[0]
    score_scale = 1.0 / HEAD_SIZE**0.5
    old_scores = (
        jnp.einsum(
            "sjd,id->sji", query_rot, cache_keys, preferred_element_type=jnp.float32
        )
        * score_scale
    )
    new_scores = (
        jnp.einsum("sjd,td->sjt", query_rot, new_keys, preferred_element_type=jnp.float32)
        * score_scale
    )
    slot_ids = jnp.arange(slot_count, dtype=jnp.int32) * split_point + block
    old_live = slot_ids < length
    new_live = (jnp.arange(STEPS)[None, :] <= jnp.arange(STEPS)[:, None]) & (block == 0)
    old_scores = jnp.where(old_live[None, None, :], old_scores, -1e30)
    new_scores = jnp.where(new_live[:, None, :], new_scores, -1e30)
    row_max = jnp.maximum(jnp.max(old_scores, -1), jnp.max(new_scores, -1))
    for bit in range(tree_levels):
        row_max = jnp.maximum(row_max, swapped(row_max, "seq", bit))
    old_exp = jnp.exp(old_scores - row_max[..., None])
    new_exp = jnp.exp(new_scores - row_max[..., None])
    denom = jnp.sum(old_exp, -1) + jnp.sum(new_exp, -1)
    for bit in range(tree_levels):
        denom = denom + swapped(denom, "seq", bit)
    old_probs = (old_exp / denom[..., None]).astype(jnp.bfloat16)
    new_probs = (new_exp / denom[..., None]).astype(jnp.bfloat16)
    partial_sum = jnp.einsum(
        "sji,id->sjd", old_probs, cache_values, preferred_element_type=jnp.float32
    )
    partial_sum = partial_sum + jnp.einsum(
        "sjt,td->sjd", new_probs, new_value, preferred_element_type=jnp.float32
    )
    flat_rows = partial_sum.reshape(STEPS, QPK * HEAD_SIZE)
    for bit in range(tree_levels):
        flat_rows = flat_rows + swapped(flat_rows, "seq", bit)
    share = flat_rows.shape[1] // split_point
    mine = lax.dynamic_slice_in_dim(flat_rows, block * share, share, 1)
    cache = jnp.concatenate([cache_keys, cache_values], 1)[None]
    return (cache, mine.astype(jnp.bfloat16))


def solution(mesh):
    placed = (
        P("groups", "seq", None),
        P("seq", None),
        P("seq", None),
        P("groups"),
        P("groups"),
        P("groups", None, None),
        P("groups", None, None),
        P("groups", None, None),
    )
    return jax.shard_map(
        body,
        mesh=mesh,
        in_specs=placed,
        out_specs=(P(("groups", "seq"), None, None), P("groups", "seq")),
        check_vma=False,
    )
```

```python
import functools

import jax
import jax.numpy as jnp
import numpy as np
from jax import lax
from jax.experimental import pallas as pl
from jax.experimental.pallas import tpu as pltpu
from jax.sharding import PartitionSpec as P

HEAD_SIZE = 128
KEY_VALUE_HEADS = 4
QPK = 8
STEPS = 4


ROPE_BASE = 500000.0


def swapped(block, axis, bit):
    count = lax.axis_size(axis)
    route = []
    for low in range(count):
        high = low | 1 << bit
        if high != low and high < count:
            route += [(low, high), (high, low)]
    return lax.ppermute(block, axis, route)


def rope_table(positions, head_dim):
    freq = ROPE_BASE ** (-(np.arange(head_dim // 2, dtype=np.float64) * 2.0) / head_dim)
    angle = positions.astype(jnp.float32)[:, None] * jnp.asarray(freq, jnp.float32)[None, :]
    return (jnp.cos(angle), jnp.sin(angle))


def rotate(values_in, cosine, sine_part):
    half_dim = values_in.shape[-1] // 2
    lower_half = values_in[..., :half_dim]
    upper_half = values_in[..., half_dim:]
    return jnp.concatenate(
        [
            lower_half * cosine - upper_half * sine_part,
            upper_half * cosine + lower_half * sine_part,
        ],
        -1,
    )


def spread(count):
    side = 1
    while side * side < count:
        side *= 2
    return (side, count // side)


def moved(block, rule):
    groups, seq = lax.axis_size("groups"), lax.axis_size("seq")
    low = spread(seq // 2)[1]
    route = []
    for g in range(groups):
        for s in range(seq):
            place = rule(g, s // 2 // low, s // 2 % low, s % 2)
            if place is not None:
                tg, tz, ty, tc = place
                route.append((g * seq + s, tg * seq + (tz * low + ty) * 2 + tc))
    return lax.ppermute(block, ("groups", "seq"), route)


def to_core(g, z, y, c):
    return (g, z, y, 1 - c)


def to_row(g, z, y, c):
    return (g, z, 1 - y, c)


def to_group(g, z, y, c):
    return (1 - g, z, y, c)


def to_pair(g, z, y, c):
    return (g, z ^ 1, y, c)


def to_middle(g, z, y, c):
    return (g, 3 - z, y, c) if z in (1, 2) else None


def to_end(g, z, y, c):
    return (g, 0 if z == 1 else 3, y, c) if z in (1, 2) else None


VMEM_REF = pl.BlockSpec(memory_space=pltpu.VMEM)
SMEM_REF = pl.BlockSpec(memory_space=pltpu.SMEM)
ANY_REF = pl.BlockSpec(memory_space=pl.ANY)
PARAMS = pltpu.CompilerParams(vmem_limit_bytes=20 << 20)
SMALL = pltpu.CompilerParams(vmem_limit_bytes=16 << 20)


def cost(flops, moved_bytes):
    return pl.CostEstimate(flops=flops, bytes_accessed=moved_bytes, transcendentals=0)


def fetch(source, target, sem):
    copy = pltpu.make_async_copy(source, target, sem)
    copy.start()
    return copy


def weight_half(half, *weights):
    depth = weights[0].shape[0] // 2
    return jnp.concatenate(
        [lax.dynamic_slice_in_dim(weight, half * depth, depth, 0) for weight in weights], 1
    )


def prepare_kernel(place, *refs):
    left, kept = refs[-2:]
    rows, depth = kept.shape[1], kept.shape[2]
    width = refs[0].shape[1]
    for who, rows_in in enumerate(refs[:2]):
        square = jnp.zeros((rows, depth), jnp.float32)
        for first in range(0, width, depth):
            part = rows_in[:, first : first + depth].astype(jnp.float32)
            square += part * part
        scale = lax.rsqrt(jnp.sum(square, -1, keepdims=True) / width + 1e-05)
        for core in range(2):

            @pl.when(place[1] == core)
            def _():
                for first in range(0, width, depth):
                    j, c, h = first // (4 * depth), first // (2 * depth) % 2, first // depth % 2
                    if c == core or who == 0:
                        part = rows_in[:, first : first + depth].astype(jnp.float32)
                        part = (part * scale).astype(jnp.bfloat16)
                        if c == core:
                            left[2 * j + h, who] = part
                        else:
                            kept[2 * j + h] = part


def prepared(place, mine, other, blocks):
    rows, width = mine.shape
    depth = width // (4 * blocks)
    tile = 80 if rows % 80 == 0 else rows
    spec = pl.BlockSpec((tile, width), lambda i, place: (i, 0))
    return pl.pallas_call(
        prepare_kernel,
        grid_spec=pltpu.PrefetchScalarGridSpec(
            num_scalar_prefetch=1,
            grid=(rows // tile,),
            in_specs=[spec, spec],
            out_specs=[
                pl.BlockSpec((2 * blocks, 2, tile, depth), lambda i, place: (0, 0, i, 0)),
                pl.BlockSpec((2 * blocks, tile, depth), lambda i, place: (0, i, 0)),
            ],
        ),
        out_shape=[
            jax.ShapeDtypeStruct((2 * blocks, 2, rows, depth), jnp.bfloat16),
            jax.ShapeDtypeStruct((2 * blocks, rows, depth), jnp.bfloat16),
        ],
        compiler_params=PARAMS,
        cost_estimate=cost(1000, 1000),
        name="normed_halves",
    )(place, mine, other)


def after(value, *events):
    return lax.optimization_barrier((value, *events))[0]


def half_index(place, entry, kind):
    half = {0: place[0], 1: 1 - place[0], 2: 0, 3: 1}[kind]
    return place[entry] * 2 + half


def product_kernel(plan, group, parts, with_total, place, both, *refs):
    count = len(plan)
    taken = sum(pair for _, _, pair in plan)
    totals_in = refs[taken : taken + 2 * with_total * parts]
    next_ref = iter(refs)
    outs = refs[-5 - 2 * parts : -5]
    left, right, total, sems, total_sems = refs[-5:]
    rows, depth = both.shape[2], both.shape[3]
    columns = right.shape[2]
    waits = []
    width = columns // parts
    for k, (entry, kind, pair) in enumerate(plan):
        area = pl.ds((k % group) * depth, depth)
        slot = k // group
        index = half_index(place, entry, kind)
        waits.append([fetch(both.at[index], left.at[slot, :, :, area], sems.at[3 * k])])
        for p in range(pair):
            target = right.at[slot, area, pl.ds(p * columns // pair, columns // pair)]
            waits[-1].append(fetch(next(next_ref), target, sems.at[3 * k + 1 + p]))
    carried = [
        fetch(
            ref,
            total.at[pl.ds(k % 2 * rows, rows), pl.ds(k // 2 * width, width)],
            total_sems.at[k],
        )
        for k, ref in enumerate(totals_in)
    ]
    for slot in range(count // group):
        for copies in waits[slot * group : (slot + 1) * group]:
            for copy in copies:
                copy.wait()
        stacked = left[slot].reshape(2 * rows, group * depth)
        value = jnp.dot(stacked, right[slot], preferred_element_type=jnp.float32)
        if slot == 0:
            for copy in carried:
                copy.wait()
        if slot or with_total:
            value += total[...]
        if slot + 1 < count // group:
            total[...] = value
        else:
            for k, out in enumerate(outs):
                out[...] = value[
                    k % 2 * rows : (k % 2 + 1) * rows, k // 2 * width : (k // 2 + 1) * width
                ]


def product(place, both, pieces, totals, group, columns, parts, params=PARAMS):
    _, _, rows, depth = both.shape
    plan = [(entry, kind, len(arrays)) for entry, kind, *arrays in pieces]
    pieces_flat = [array for _, _, *arrays in pieces for array in arrays]
    count = len(plan)
    out = jax.ShapeDtypeStruct((rows, columns // parts), jnp.float32)
    return pl.pallas_call(
        functools.partial(product_kernel, plan, group, parts, bool(totals)),
        in_specs=[SMEM_REF] + [ANY_REF] * (1 + len(pieces_flat) + len(totals)),
        out_specs=[VMEM_REF] * (2 * parts),
        out_shape=[out] * (2 * parts),
        scratch_shapes=[
            pltpu.VMEM((count // group, 2, rows, group * depth), both.dtype),
            pltpu.VMEM((count // group, group * depth, columns), both.dtype),
            pltpu.VMEM((2 * rows, columns), jnp.float32),
            pltpu.SemaphoreType.DMA((3 * count,)),
            pltpu.SemaphoreType.DMA((2 * parts,)),
        ],
        compiler_params=params,
        cost_estimate=cost(1 << 36, 1000),
        name="add_product",
    )(place, both, *pieces_flat, *totals)


def rows_kernel(place, lengths, owner, total, came, cosine, sine, out, scratch):
    columns = total.shape[1] // 2
    count_requests, count_rows = lengths.shape[0], scratch.shape[0]
    index = place[2] * count_rows + lax.broadcasted_iota(jnp.int32, scratch.shape, 0)
    for r in range(count_requests):
        live = index < lengths[r]
        for h in range(KEY_VALUE_HEADS):
            for part in range(2):
                first = part * columns + h * HEAD_SIZE
                area = (
                    slice(r * count_rows, (r + 1) * count_rows),
                    slice(first, first + HEAD_SIZE),
                )
                rows = total[area] + came[area]
                if part == 0:
                    half = HEAD_SIZE // 2
                    turned = jnp.concatenate([rows[:, half:], rows[:, :half]], 1)
                    rows = rows * cosine[...] + turned * sine[...]
                scratch[...] = jnp.where(live, rows, 0.0)
                peer = owner[r * KEY_VALUE_HEADS + h]
                lanes = slice(part * HEAD_SIZE, (part + 1) * HEAD_SIZE)
                for b in range(2):
                    picked = scratch[pl.ds(b, count_rows // 2, stride=2), :]
                    out[peer * 2 + b, :, lanes] = picked.astype(jnp.bfloat16)


def outgoing_rows(place, lengths, owner, total, came, turn):
    count_rows = total.shape[0] // lengths.shape[0]
    out = (owner.shape[0] * 2, count_rows // 2, 2 * HEAD_SIZE)
    return pl.pallas_call(
        rows_kernel,
        in_specs=[SMEM_REF] * 3 + [VMEM_REF] * 4,
        out_specs=VMEM_REF,
        out_shape=jax.ShapeDtypeStruct(out, jnp.bfloat16),
        scratch_shapes=[pltpu.VMEM((count_rows, HEAD_SIZE), jnp.float32)],
        compiler_params=SMALL,
        cost_estimate=cost(1000, 1000),
        name="cache_rows",
    )(place, lengths, owner, total, came, *turn)


def decode_kernel(place, cache, query, new_keys, new_value, out):
    slots, queries = cache.shape[0], query.shape[0]
    block, length = place[0], place[1]
    contract = (((1,), (1,)), ((), ()))
    scale = 1.0 / HEAD_SIZE**0.5
    old = lax.dot_general(
        query[...], cache[:, :HEAD_SIZE], contract, preferred_element_type=jnp.float32
    )
    slot = lax.broadcasted_iota(jnp.int32, old.shape, 1) * 2 + block
    old = jnp.where(slot < length, old * scale, -1e30)
    new = lax.dot_general(query[...], new_keys[...], contract, preferred_element_type=jnp.float32)
    step = lax.broadcasted_iota(jnp.int32, new.shape, 0) // QPK
    token = lax.broadcasted_iota(jnp.int32, new.shape, 1)
    new = jnp.where((token <= step) & (block == 0), new * scale, -1e30)
    top = jnp.maximum(jnp.max(old, 1, keepdims=True), jnp.max(new, 1, keepdims=True))
    old, new = jnp.exp(old - top), jnp.exp(new - top)
    total = jnp.sum(old, 1, keepdims=True) + jnp.sum(new, 1, keepdims=True)
    sums = jnp.dot(
        old.astype(jnp.bfloat16), cache[:, HEAD_SIZE:], preferred_element_type=jnp.float32
    )
    out[:, :HEAD_SIZE] = sums + jnp.dot(
        new.astype(jnp.bfloat16), new_value[...], preferred_element_type=jnp.float32
    )
    half = (queries, HEAD_SIZE // 2)
    out[:, HEAD_SIZE : HEAD_SIZE + half[1]] = jnp.broadcast_to(top, half)
    out[:, HEAD_SIZE + half[1] :] = jnp.broadcast_to(total, half)


def decoded(block, length, cache, query, new_keys, new_value):
    pad = ((0, 16 - STEPS), (0, 0))
    new_keys, new_value = jnp.pad(new_keys, pad), jnp.pad(new_value, pad)
    mine = pl.pallas_call(
        decode_kernel,
        in_specs=[SMEM_REF] + [VMEM_REF] * 4,
        out_specs=VMEM_REF,
        out_shape=jax.ShapeDtypeStruct((STEPS * QPK, 2 * HEAD_SIZE), jnp.float32),
        compiler_params=SMALL,
        cost_estimate=cost(1000, 1000),
        name="decode",
    )(jnp.stack([block, length]), cache, query, new_keys, new_value)
    theirs = moved(mine, to_core)
    share = QPK // 2

    def heads(array):
        array = array.reshape(STEPS, QPK, 2 * HEAD_SIZE)
        array = lax.dynamic_slice_in_dim(array, block * share, share, 1)
        last = HEAD_SIZE + HEAD_SIZE // 2
        return array[..., :HEAD_SIZE], array[..., HEAD_SIZE : HEAD_SIZE + 1], array[..., last : last + 1]

    sums_a, top_a, total_a = heads(mine)
    sums_b, top_b, total_b = heads(theirs)
    top = jnp.maximum(top_a, top_b)
    scale_a, scale_b = jnp.exp(top_a - top), jnp.exp(top_b - top)
    sums = sums_a * scale_a + sums_b * scale_b
    return (sums / (total_a * scale_a + total_b * scale_b)).reshape(STEPS, share * HEAD_SIZE)


HERE, THERE = 3, 7


def body(hidden, key_weight, value_weight, lengths, owner, dec_query, dec_key, dec_value):
    count_requests, count_rows, width = hidden.shape
    device_id = lax.axis_index("seq")
    group_id = lax.axis_index("groups")
    seq = lax.axis_size("seq")
    planned = seq == 16 and lax.axis_size("groups") == 2
    decode_peers = count_requests * KEY_VALUE_HEADS
    split_point = seq // decode_peers
    tree_levels = split_point.bit_length() - 1
    rows_per_peer = count_rows // split_point
    positions = device_id * count_rows + jnp.arange(count_rows, dtype=jnp.int32)
    total_rows = count_requests * count_rows
    flat = hidden.reshape(total_rows, width)
    if planned:
        core = device_id % 2
        z, y = device_id // 4, device_id // 2 % 2
        layers = [z, z ^ 1, jnp.where(z < 2, 2, 1), jnp.where(z < 2, 3, 0)]
        is_end = (z == 0) | (z == 3)
        place = [group_id, core, device_id]
        place += [layer * 2 + y for layer in layers]
        place += [layer * 2 + 1 - y for layer in layers]
        place = jnp.stack([jnp.asarray(entry, jnp.int32) for entry in place])
    else:
        widened = flat.astype(jnp.float32)
        normed = (
            widened * lax.rsqrt(jnp.mean(widened * widened, -1, keepdims=True) + 1e-05)
        ).astype(jnp.bfloat16)

        def project(weight):
            whole = lax.all_gather(weight, "seq", axis=0, tiled=True)
            return jnp.dot(normed, whole, preferred_element_type=jnp.float32)

    pair_ids = jnp.arange(decode_peers, dtype=jnp.int32)
    matches = owner[None, :] == pair_ids[:, None]
    inverse_order = jnp.sum(jnp.where(matches, pair_ids[None, :], 0), axis=1)
    live_rows = positions[None, :] < lengths[:, None]

    def handed_over(rows):
        rows = jnp.where(live_rows[:, :, None, None], rows, jnp.zeros_like(rows))
        pair_rows = jnp.transpose(rows, (0, 2, 1, 3)).reshape(decode_peers, count_rows, HEAD_SIZE)
        sorted_rows = pair_rows[inverse_order].reshape(
            decode_peers, rows_per_peer, split_point, HEAD_SIZE
        )
        outgoing = jnp.transpose(sorted_rows, (0, 2, 1, 3)).reshape(
            decode_peers * split_point, rows_per_peer, HEAD_SIZE
        )
        return lax.all_to_all(outgoing, "seq", split_axis=0, concat_axis=1, tiled=True)[0]

    decode_peer = device_id // split_point
    block = device_id % split_point
    source_pair = jnp.sum(jnp.where(owner == decode_peer, pair_ids, 0))
    source_request = source_pair // KEY_VALUE_HEADS
    length = jnp.sum(
        jnp.where(jnp.arange(count_requests, dtype=jnp.int32) == source_request, lengths, 0)
    )
    query = lax.dynamic_index_in_dim(dec_query, decode_peer, 0, keepdims=False)
    new_key = lax.dynamic_index_in_dim(dec_key, decode_peer, 0, keepdims=False)
    new_value = lax.dynamic_index_in_dim(dec_value, decode_peer, 0, keepdims=False)
    step_pos = length + jnp.arange(STEPS, dtype=jnp.int32)
    step_cos, step_sin = rope_table(step_pos, HEAD_SIZE)
    query_rot = rotate(
        query.astype(jnp.float32).reshape(STEPS, QPK, HEAD_SIZE),
        step_cos[:, None, :],
        step_sin[:, None, :],
    ).astype(jnp.bfloat16)
    new_keys = rotate(new_key.astype(jnp.float32), step_cos, step_sin).astype(jnp.bfloat16)
    cosine, sine_part = rope_table(positions, HEAD_SIZE)
    if planned:
        turn = (
            jnp.concatenate([cosine, cosine], 1),
            jnp.concatenate([-sine_part, sine_part], 1),
        )
        columns = key_weight.shape[1]

        sent = weight_half(group_id, key_weight, value_weight)
        near = moved(sent, to_pair)
        middle = moved(sent, to_middle)
        across = moved(sent, to_row)
        other = moved(flat, to_core)
        rest = weight_half(1 - group_id, key_weight, after(value_weight, sent))
        came = (near, middle, across, other, rest, *turn, query_rot, new_keys)
        end_b = moved(after(middle, *came), to_end)
        middle_c = moved(after(near, *came), to_middle)
        near_y = moved(after(near, *came), to_row)
        across_x = moved(after(across, *came), to_group)
        both, kept = prepared(place, after(flat, *came), other, seq // 2)
        came = (end_b, middle_c, near_y, across_x, both)
        end_c = moved(after(middle_c, *came), to_end)
        block_b = jnp.where(is_end, after(end_b, *came), middle)
        block_yb = moved(block_b, to_row)
        block_xb = moved(block_b, to_group)
        pieces = [(HERE, 0, sent), (HERE, 1, rest), (THERE, 0, across), (THERE, 1, across_x)]
        pieces += [(HERE + 1, 0, near), (THERE + 1, 0, near_y)]
        totals = product(place, after(both, *came), pieces, (), 3, 2 * columns, 1)
        came = (end_c, block_yb, block_xb, totals[0])
        near_rest = moved(after(rest, *came), to_pair)
        block_c = jnp.where(is_end, after(end_c, *came), middle_c)
        block_xc = moved(block_c, to_group)
        block_yc = moved(block_c, to_row)
        pieces = [(HERE + 2, 0, block_b), (HERE + 2, 1, block_xb)]
        pieces += [(THERE + 2, 0, block_yb), (HERE + 3, 0, block_c)]
        total, given = product(place, after(both, *came), pieces, totals, 4, 2 * columns, 1)
        came = (near_rest, block_xc, block_yc, total)
        ends = [moved(after(across_x, *came), to_pair), moved(after(block_yb, *came), to_group)]
        ends.append(moved(after(block_xc, *came), to_row))
        pieces = [(HERE + 1, 1, near_rest), (HERE + 3, 1, block_xc), (THERE + 3, 0, block_yc)]
        totals = product(place, after(both, *came), pieces, (total, given), 3, 2 * columns, 1)
        came = (*ends, *totals)
        spots = (THERE + 1, THERE + 2, THERE + 3)
        pieces = [(spot, 1, after(end, *came)) for spot, end in zip(spots, ends)]
        total, given = product(place, both, pieces, totals, 3, 2 * columns, 1, SMALL)
        outgoing = outgoing_rows(place, lengths, owner, total, moved(given, to_core), turn)
        incoming = lax.all_to_all(outgoing, "seq", split_axis=0, concat_axis=1, tiled=True)
        mine = decoded(
            device_id % 2, length, incoming[0], query_rot.reshape(STEPS * QPK, HEAD_SIZE),
            new_keys, new_value,
        )
        return (incoming, mine.astype(jnp.bfloat16))
    else:
        shape = (count_requests, count_rows, KEY_VALUE_HEADS, HEAD_SIZE)
        unrotated_key = project(key_weight).reshape(shape)
        key_rows = rotate(
            unrotated_key, cosine[:, None, :], sine_part[:, None, :]
        ).astype(jnp.bfloat16)
        cache_keys = handed_over(key_rows)
        cache_values = handed_over(project(value_weight).astype(jnp.bfloat16).reshape(shape))
    slot_count = cache_keys.shape[0]
    score_scale = 1.0 / HEAD_SIZE**0.5
    old_scores = (
        jnp.einsum(
            "sjd,id->sji", query_rot, cache_keys, preferred_element_type=jnp.float32
        )
        * score_scale
    )
    new_scores = (
        jnp.einsum("sjd,td->sjt", query_rot, new_keys, preferred_element_type=jnp.float32)
        * score_scale
    )
    slot_ids = jnp.arange(slot_count, dtype=jnp.int32) * split_point + block
    old_live = slot_ids < length
    new_live = (jnp.arange(STEPS)[None, :] <= jnp.arange(STEPS)[:, None]) & (block == 0)
    old_scores = jnp.where(old_live[None, None, :], old_scores, -1e30)
    new_scores = jnp.where(new_live[:, None, :], new_scores, -1e30)
    row_max = jnp.maximum(jnp.max(old_scores, -1), jnp.max(new_scores, -1))
    for bit in range(tree_levels):
        row_max = jnp.maximum(row_max, swapped(row_max, "seq", bit))
    old_exp = jnp.exp(old_scores - row_max[..., None])
    new_exp = jnp.exp(new_scores - row_max[..., None])
    denom = jnp.sum(old_exp, -1) + jnp.sum(new_exp, -1)
    for bit in range(tree_levels):
        denom = denom + swapped(denom, "seq", bit)
    old_probs = (old_exp / denom[..., None]).astype(jnp.bfloat16)
    new_probs = (new_exp / denom[..., None]).astype(jnp.bfloat16)
    partial_sum = jnp.einsum(
        "sji,id->sjd", old_probs, cache_values, preferred_element_type=jnp.float32
    )
    partial_sum = partial_sum + jnp.einsum(
        "sjt,td->sjd", new_probs, new_value, preferred_element_type=jnp.float32
    )
    flat_rows = partial_sum.reshape(STEPS, QPK * HEAD_SIZE)
    for bit in range(tree_levels):
        flat_rows = flat_rows + swapped(flat_rows, "seq", bit)
    share = flat_rows.shape[1] // split_point
    mine = lax.dynamic_slice_in_dim(flat_rows, block * share, share, 1)
    cache = jnp.concatenate([cache_keys, cache_values], 1)[None]
    return (cache, mine.astype(jnp.bfloat16))


def solution(mesh):
    placed = (
        P("groups", "seq", None),
        P("seq", None),
        P("seq", None),
        P("groups"),
        P("groups"),
        P("groups", None, None),
        P("groups", None, None),
        P("groups", None, None),
    )
    return jax.shard_map(
        body,
        mesh=mesh,
        in_specs=placed,
        out_specs=(P(("groups", "seq"), None, None), P("groups", "seq")),
        check_vma=False,
    )
```

```python
import functools

import jax
import jax.numpy as jnp
import numpy as np
from jax import lax
from jax.experimental import pallas as pl
from jax.experimental.pallas import tpu as pltpu
from jax.sharding import PartitionSpec as P

HEAD_SIZE = 128
KEY_VALUE_HEADS = 4
QPK = 8
STEPS = 4


ROPE_BASE = 500000.0


def swapped(block, axis, bit):
    count = lax.axis_size(axis)
    route = []
    for low in range(count):
        high = low | 1 << bit
        if high != low and high < count:
            route += [(low, high), (high, low)]
    return lax.ppermute(block, axis, route)


def rope_table(positions, head_dim):
    freq = ROPE_BASE ** (-(np.arange(head_dim // 2, dtype=np.float64) * 2.0) / head_dim)
    angle = positions.astype(jnp.float32)[:, None] * jnp.asarray(freq, jnp.float32)[None, :]
    return (jnp.cos(angle), jnp.sin(angle))


def rotate(values_in, cosine, sine_part):
    half_dim = values_in.shape[-1] // 2
    lower_half = values_in[..., :half_dim]
    upper_half = values_in[..., half_dim:]
    return jnp.concatenate(
        [
            lower_half * cosine - upper_half * sine_part,
            upper_half * cosine + lower_half * sine_part,
        ],
        -1,
    )


def spread(count):
    side = 1
    while side * side < count:
        side *= 2
    return (side, count // side)


def moved(block, rule):
    groups, seq = lax.axis_size("groups"), lax.axis_size("seq")
    low = spread(seq // 2)[1]
    route = []
    for g in range(groups):
        for s in range(seq):
            place = rule(g, s // 2 // low, s // 2 % low, s % 2)
            if place is not None:
                tg, tz, ty, tc = place
                route.append((g * seq + s, tg * seq + (tz * low + ty) * 2 + tc))
    return lax.ppermute(block, ("groups", "seq"), route)


def to_core(g, z, y, c):
    return (g, z, y, 1 - c)


def to_row(g, z, y, c):
    return (g, z, 1 - y, c)


def to_group(g, z, y, c):
    return (1 - g, z, y, c)


def to_pair(g, z, y, c):
    return (g, z ^ 1, y, c)


def to_middle(g, z, y, c):
    return (g, 3 - z, y, c) if z in (1, 2) else None


def to_end(g, z, y, c):
    return (g, 0 if z == 1 else 3, y, c) if z in (1, 2) else None


VMEM_REF = pl.BlockSpec(memory_space=pltpu.VMEM)
SMEM_REF = pl.BlockSpec(memory_space=pltpu.SMEM)
ANY_REF = pl.BlockSpec(memory_space=pl.ANY)
PARAMS = pltpu.CompilerParams(vmem_limit_bytes=20 << 20)
SMALL = pltpu.CompilerParams(vmem_limit_bytes=16 << 20)


def cost(flops, moved_bytes):
    return pl.CostEstimate(flops=flops, bytes_accessed=moved_bytes, transcendentals=0)


def fetch(source, target, sem):
    copy = pltpu.make_async_copy(source, target, sem)
    copy.start()
    return copy


def prepare_kernel(place, rows_in, mine, kept):
    depth = mine.shape[2]
    rows, width = rows_in.shape
    square = jnp.zeros((rows, depth), jnp.float32)
    for first in range(0, width, depth):
        part = rows_in[:, first : first + depth].astype(jnp.float32)
        square += part * part
    scale = lax.rsqrt(jnp.sum(square, -1, keepdims=True) / width + 1e-05)
    for core in range(2):

        @pl.when(place[1] == core)
        def _():
            for first in range(0, width, depth):
                j, c, h = first // (4 * depth), first // (2 * depth) % 2, first // depth % 2
                target = mine if c == core else kept
                part = rows_in[:, first : first + depth].astype(jnp.float32)
                target[2 * j + h] = (part * scale).astype(jnp.bfloat16)


def prepared(place, flat, blocks):
    rows, width = flat.shape
    depth = width // (4 * blocks)
    tile = 80 if rows % 80 == 0 else rows
    out = jax.ShapeDtypeStruct((2 * blocks, rows, depth), jnp.bfloat16)
    spec = pl.BlockSpec((2 * blocks, tile, depth), lambda i, place: (0, i, 0))
    return pl.pallas_call(
        prepare_kernel,
        grid_spec=pltpu.PrefetchScalarGridSpec(
            num_scalar_prefetch=1,
            grid=(rows // tile,),
            in_specs=[pl.BlockSpec((tile, width), lambda i, place: (i, 0))],
            out_specs=[spec, spec],
        ),
        out_shape=[out, out],
        compiler_params=PARAMS,
        cost_estimate=cost(1000, 1000),
        name="normed_halves",
    )(place, flat)


def after(value, *events):
    return lax.optimization_barrier((value, *events))[0]


def half_index(place, entry, kind):
    half = {0: place[0], 1: 1 - place[0], 2: 0, 3: 1}[kind]
    return place[entry] * 2 + half


def product_kernel(plan, group, with_total, place, mine, other, *refs):
    count = len(plan)
    outs = refs[-7:-5]
    left, right, total, sems, total_sems = refs[-5:]
    rows, depth = mine.shape[1], mine.shape[2]
    waits = []
    for k, (entry, kind) in enumerate(plan):
        area = pl.ds((k % group) * depth, depth)
        slot = k // group
        index = half_index(place, entry, kind)
        sources = (mine.at[index], other.at[index], refs[k])
        targets = (left.at[slot, 0, :, area], left.at[slot, 1, :, area], right.at[slot, area])
        waits.append(
            [fetch(a, b, sems.at[3 * k + i]) for i, (a, b) in enumerate(zip(sources, targets))]
        )
    carried = [
        fetch(ref, total.at[pl.ds(k * rows, rows)], total_sems.at[k])
        for k, ref in enumerate(refs[count : count + 2 * with_total])
    ]
    for slot in range(count // group):
        for copies in waits[slot * group : (slot + 1) * group]:
            for copy in copies:
                copy.wait()
        stacked = left[slot].reshape(2 * rows, group * depth)
        value = jnp.dot(stacked, right[slot], preferred_element_type=jnp.float32)
        if slot == 0:
            for copy in carried:
                copy.wait()
        if slot or with_total:
            value += total[...]
        if slot + 1 < count // group:
            total[...] = value
        else:
            outs[0][...] = value[:rows]
            outs[1][...] = value[rows:]


def product(place, mine, other, pieces, totals, group, moved_bytes=1000):
    _, rows, depth = mine.shape
    columns = pieces[0][2].shape[1]
    plan = [(entry, kind) for entry, kind, _ in pieces]
    count = len(plan)
    out = jax.ShapeDtypeStruct((rows, columns), jnp.float32)
    return pl.pallas_call(
        functools.partial(product_kernel, plan, group, bool(totals)),
        in_specs=[SMEM_REF] + [ANY_REF] * (2 + count + len(totals)),
        out_specs=[VMEM_REF] * 2,
        out_shape=[out] * 2,
        scratch_shapes=[
            pltpu.VMEM((count // group, 2, rows, group * depth), mine.dtype),
            pltpu.VMEM((count // group, group * depth, columns), mine.dtype),
            pltpu.VMEM((2 * rows, columns), jnp.float32),
            pltpu.SemaphoreType.DMA((3 * count,)),
            pltpu.SemaphoreType.DMA((2,)),
        ],
        compiler_params=PARAMS,
        cost_estimate=cost(1000, moved_bytes),
        name="add_product",
    )(place, mine, other, *[array for _, _, array in pieces], *totals)


LOW = 64


def turn_tables(positions, rows):
    freq = ROPE_BASE ** (-(np.arange(HEAD_SIZE // 2) * 2.0) / HEAD_SIZE)
    tables = []
    for places in (np.arange(0, positions, LOW), np.arange(LOW), np.arange(rows)):
        angle = places[:, None] * freq[None, :]
        tables.append(np.concatenate([np.cos(angle), np.cos(angle)], 1))
        tables.append(np.concatenate([-np.sin(angle), np.sin(angle)], 1))
    return [jnp.asarray(table, jnp.float32) for table in tables]


def turned_by(start, tables, cosine, sine):
    high, low = pl.ds(start // LOW, 1), pl.ds(start % LOW, 1)
    for cos_row, sin_row in (
        (tables[0][high], tables[1][high]),
        (tables[2][low], tables[3][low]),
    ):
        cosine, sine = cosine * cos_row - sine * sin_row, sine * cos_row + cosine * sin_row
    return cosine, sine


def rotated(rows, cosine, sine):
    half = HEAD_SIZE // 2
    return rows * cosine + jnp.concatenate([rows[:, half:], rows[:, :half]], 1) * sine


def rows_kernel(place, lengths, owner, *refs):
    totals, came, tables, (out, scratch) = refs[:2], refs[2:4], refs[4:10], refs[10:]
    count_requests, count_rows = lengths.shape[0], scratch.shape[0]
    cosine, sine = turned_by(place[2] * count_rows, tables, tables[4][...], tables[5][...])
    index = place[2] * count_rows + lax.broadcasted_iota(jnp.int32, scratch.shape, 0)
    for r in range(count_requests):
        live = index < lengths[r]
        for h in range(KEY_VALUE_HEADS):
            for part in range(2):
                area = (
                    slice(r * count_rows, (r + 1) * count_rows),
                    slice(h * HEAD_SIZE, (h + 1) * HEAD_SIZE),
                )
                rows = totals[part][area] + came[part][area]
                if part == 0:
                    rows = rotated(rows, cosine, sine)
                scratch[...] = jnp.where(live, rows, 0.0)
                peer = owner[r * KEY_VALUE_HEADS + h]
                lanes = slice(part * HEAD_SIZE, (part + 1) * HEAD_SIZE)
                for b in range(2):
                    picked = scratch[pl.ds(b, count_rows // 2, stride=2), :]
                    out[peer * 2 + b, :, lanes] = picked.astype(jnp.bfloat16)


def outgoing_rows(place, lengths, owner, totals, came, tables):
    count_rows = totals[0].shape[0] // lengths.shape[0]
    out = (owner.shape[0] * 2, count_rows // 2, 2 * HEAD_SIZE)
    return pl.pallas_call(
        rows_kernel,
        in_specs=[SMEM_REF] * 3 + [VMEM_REF] * 10,
        out_specs=VMEM_REF,
        out_shape=jax.ShapeDtypeStruct(out, jnp.bfloat16),
        scratch_shapes=[pltpu.VMEM((count_rows, HEAD_SIZE), jnp.float32)],
        compiler_params=SMALL,
        cost_estimate=cost(1000, 1000),
        name="cache_rows",
    )(place, lengths, owner, *totals, *came, *tables)


def decode_kernel(place, lengths, owner, cache, dec_query, dec_key, dec_value, *refs):
    tables, out = refs[:4], refs[4]
    peer, block = place[2] // 2, place[2] % 2
    length = lengths[0]
    for pair in range(owner.shape[0]):
        length = jnp.where(owner[pair] == peer, lengths[pair // KEY_VALUE_HEADS], length)
    cosine, sine = turned_by(length, tables, tables[2][:STEPS], tables[3][:STEPS])

    def turned(rows):
        return rotated(rows.astype(jnp.float32), cosine, sine)

    def padded(rows):
        return jnp.concatenate([rows, jnp.zeros((16 - STEPS, HEAD_SIZE), jnp.float32)], 0)

    raw = dec_query[peer]
    heads = [raw[:, j * HEAD_SIZE : (j + 1) * HEAD_SIZE] for j in range(QPK)]
    query = jnp.concatenate([turned(head) for head in heads], 0).astype(jnp.bfloat16)
    new_keys = padded(turned(dec_key[peer])).astype(jnp.bfloat16)
    new_value = padded(dec_value[peer].astype(jnp.float32)).astype(jnp.bfloat16)
    contract = (((1,), (1,)), ((), ()))
    scale = 1.0 / HEAD_SIZE**0.5
    old = lax.dot_general(
        query, cache[:, :HEAD_SIZE], contract, preferred_element_type=jnp.float32
    )
    slot = lax.broadcasted_iota(jnp.int32, old.shape, 1) * 2 + block
    old = jnp.where(slot < length, old * scale, -1e30)
    new = lax.dot_general(query, new_keys, contract, preferred_element_type=jnp.float32)
    step = lax.broadcasted_iota(jnp.int32, new.shape, 0) % STEPS
    token = lax.broadcasted_iota(jnp.int32, new.shape, 1)
    new = jnp.where((token <= step) & (block == 0), new * scale, -1e30)
    top = jnp.maximum(jnp.max(old, 1, keepdims=True), jnp.max(new, 1, keepdims=True))
    old, new = jnp.exp(old - top), jnp.exp(new - top)
    total = jnp.sum(old, 1, keepdims=True) + jnp.sum(new, 1, keepdims=True)
    sums = jnp.dot(
        old.astype(jnp.bfloat16), cache[:, HEAD_SIZE:], preferred_element_type=jnp.float32
    )
    out[:, :HEAD_SIZE] = sums + jnp.dot(
        new.astype(jnp.bfloat16), new_value, preferred_element_type=jnp.float32
    )
    half = (QPK * STEPS, HEAD_SIZE // 2)
    out[:, HEAD_SIZE : HEAD_SIZE + half[1]] = jnp.broadcast_to(top, half)
    out[:, HEAD_SIZE + half[1] :] = jnp.broadcast_to(total, half)


def joined_kernel(place, mine, theirs, out):
    share = QPK // 2
    area = pl.ds(place[2] % 2 * share * STEPS, share * STEPS)
    last = HEAD_SIZE + HEAD_SIZE // 2
    sums, tops, totals = [], [], []
    for ref in (mine, theirs):
        sums.append(ref[area, :HEAD_SIZE])
        tops.append(ref[area, HEAD_SIZE : HEAD_SIZE + 1])
        totals.append(ref[area, last : last + 1])
    top = jnp.maximum(tops[0], tops[1])
    scales = [jnp.exp(one - top) for one in tops]
    total = totals[0] * scales[0] + totals[1] * scales[1]
    value = (sums[0] * scales[0] + sums[1] * scales[1]) / total
    for j in range(share):
        rows = value[j * STEPS : (j + 1) * STEPS]
        out[:, j * HEAD_SIZE : (j + 1) * HEAD_SIZE] = rows.astype(jnp.bfloat16)


def decoded(place, lengths, owner, cache, dec_query, dec_key, dec_value, tables):
    mine = pl.pallas_call(
        decode_kernel,
        in_specs=[SMEM_REF] * 3 + [VMEM_REF] * 8,
        out_specs=VMEM_REF,
        out_shape=jax.ShapeDtypeStruct((STEPS * QPK, 2 * HEAD_SIZE), jnp.float32),
        compiler_params=SMALL,
        cost_estimate=cost(1000, 1000),
        name="decode",
    )(place, lengths, owner, cache, dec_query, dec_key, dec_value, *tables[:4])
    return pl.pallas_call(
        joined_kernel,
        in_specs=[SMEM_REF] + [VMEM_REF] * 2,
        out_specs=VMEM_REF,
        out_shape=jax.ShapeDtypeStruct((STEPS, QPK // 2 * HEAD_SIZE), jnp.bfloat16),
        compiler_params=SMALL,
        cost_estimate=cost(1000, 1000),
        name="joined",
    )(place, mine, moved(mine, to_core))


HERE, THERE = 3, 7


def body(hidden, key_weight, value_weight, lengths, owner, dec_query, dec_key, dec_value):
    count_requests, count_rows, width = hidden.shape
    device_id = lax.axis_index("seq")
    group_id = lax.axis_index("groups")
    seq = lax.axis_size("seq")
    planned = seq == 16 and lax.axis_size("groups") == 2
    decode_peers = count_requests * KEY_VALUE_HEADS
    split_point = seq // decode_peers
    tree_levels = split_point.bit_length() - 1
    rows_per_peer = count_rows // split_point
    positions = device_id * count_rows + jnp.arange(count_rows, dtype=jnp.int32)
    total_rows = count_requests * count_rows
    flat = hidden.reshape(total_rows, width)
    if planned:
        core = device_id % 2
        z, y = device_id // 4, device_id // 2 % 2
        layers = [z, z ^ 1, jnp.where(z < 2, 2, 1), jnp.where(z < 2, 3, 0)]
        is_end = (z == 0) | (z == 3)
        place = [group_id, core, device_id]
        place += [layer * 2 + y for layer in layers]
        place += [layer * 2 + 1 - y for layer in layers]
        place = jnp.stack([jnp.asarray(entry, jnp.int32) for entry in place])
    else:
        widened = flat.astype(jnp.float32)
        normed = (
            widened * lax.rsqrt(jnp.mean(widened * widened, -1, keepdims=True) + 1e-05)
        ).astype(jnp.bfloat16)

        def project(weight):
            whole = lax.all_gather(weight, "seq", axis=0, tiled=True)
            return jnp.dot(normed, whole, preferred_element_type=jnp.float32)

    pair_ids = jnp.arange(decode_peers, dtype=jnp.int32)
    matches = owner[None, :] == pair_ids[:, None]
    inverse_order = jnp.sum(jnp.where(matches, pair_ids[None, :], 0), axis=1)
    live_rows = positions[None, :] < lengths[:, None]

    def handed_over(rows):
        rows = jnp.where(live_rows[:, :, None, None], rows, jnp.zeros_like(rows))
        pair_rows = jnp.transpose(rows, (0, 2, 1, 3)).reshape(decode_peers, count_rows, HEAD_SIZE)
        sorted_rows = pair_rows[inverse_order].reshape(
            decode_peers, rows_per_peer, split_point, HEAD_SIZE
        )
        outgoing = jnp.transpose(sorted_rows, (0, 2, 1, 3)).reshape(
            decode_peers * split_point, rows_per_peer, HEAD_SIZE
        )
        return lax.all_to_all(outgoing, "seq", split_axis=0, concat_axis=1, tiled=True)[0]

    if planned:
        weights = (key_weight, value_weight)
        depth = key_weight.shape[0] // 2
        sent = [lax.dynamic_slice_in_dim(w, group_id * depth, depth, 0) for w in weights]
        rest = [lax.dynamic_slice_in_dim(w, depth - group_id * depth, depth, 0) for w in weights]
        tables = turn_tables(count_rows * seq + STEPS, count_rows)
        steps = []

        def gated(value, k):
            return after(value, *steps[k]) if len(steps) > k else value

        near = [moved(block, to_pair) for block in sent]
        middle = [moved(block, to_middle) for block in sent]
        across = [moved(block, to_row) for block in sent]
        mine, kept = prepared(place, flat, seq // 2)
        steps = [[near[k], middle[k], across[k]] for k in range(2)]
        steps[0].append(mine)
        end_b = [moved(gated(middle[k], k), to_end) for k in range(2)]
        middle_c = [moved(gated(near[k], k), to_middle) for k in range(2)]
        near_y = [moved(gated(near[k], k), to_row) for k in range(2)]
        across_x = [moved(gated(across[k], k), to_group) for k in range(2)]
        other = moved(gated(kept, 0), to_core)
        steps = [[end_b[k], middle_c[k], near_y[k], across_x[k], other] for k in range(2)]
        end_c = [moved(gated(middle_c[k], k), to_end) for k in range(2)]
        block_b = [jnp.where(is_end, gated(end_b[k], k), middle[k]) for k in range(2)]
        block_yb = [moved(block, to_row) for block in block_b]
        block_xb = [moved(block, to_group) for block in block_b]
        totals = []
        for k in range(2):
            pieces = [(HERE, 0, sent[k]), (HERE, 1, rest[k]), (THERE, 0, across[k])]
            pieces += [(THERE, 1, across_x[k]), (HERE + 1, 0, near[k]), (THERE + 1, 0, near_y[k])]
            totals.append(product(place, gated(mine, k), other, pieces, (), 3))
        steps = [[end_c[k], block_yb[k], block_xb[k], totals[k][0]] for k in range(2)]
        near_rest = [moved(gated(rest[k], k), to_pair) for k in range(2)]
        block_c = [jnp.where(is_end, gated(end_c[k], k), middle_c[k]) for k in range(2)]
        block_xc = [moved(block, to_group) for block in block_c]
        block_yc = [moved(block, to_row) for block in block_c]
        for k in range(2):
            pieces = [(HERE + 2, 0, block_b[k]), (HERE + 2, 1, block_xb[k])]
            pieces += [(THERE + 2, 0, block_yb[k]), (HERE + 3, 0, block_c[k])]
            totals[k] = product(place, gated(mine, k), other, pieces, totals[k], 4)
        steps = [[near_rest[k], block_xc[k], block_yc[k], totals[k][0]] for k in range(2)]
        ends = []
        for k in range(2):
            ends.append([moved(gated(across_x[k], k), to_pair)])
            ends[k].append(moved(gated(block_yb[k], k), to_group))
            ends[k].append(moved(gated(block_xc[k], k), to_row))
            pieces = [(HERE + 1, 1, near_rest[k]), (HERE + 3, 1, block_xc[k])]
            pieces.append((THERE + 3, 0, block_yc[k]))
            totals[k] = product(place, gated(mine, k), other, pieces, totals[k], 3)
        steps = [[*ends[k], *totals[k]] for k in range(2)]
        sums, came = [], []
        spots = (THERE + 1, THERE + 2, THERE + 3)
        for k in range(2):
            pieces = [(spot, 1, gated(end, k)) for spot, end in zip(spots, ends[k])]
            left = after(mine, *sums)
            total, given = product(place, left, other, pieces, totals[k], 3, (1 - k) << 24)
            sums.append(total)
            came.append(moved(given, to_core))
        outgoing = outgoing_rows(place, lengths, owner, sums, came, tables)
        incoming = lax.all_to_all(outgoing, "seq", split_axis=0, concat_axis=1, tiled=True)
        attended = decoded(
            place, lengths, owner, incoming[0], dec_query, dec_key, dec_value, tables
        )
        return (incoming, attended)
    else:
        cosine, sine_part = rope_table(positions, HEAD_SIZE)
        shape = (count_requests, count_rows, KEY_VALUE_HEADS, HEAD_SIZE)
        unrotated_key = project(key_weight).reshape(shape)
        key_rows = rotate(
            unrotated_key, cosine[:, None, :], sine_part[:, None, :]
        ).astype(jnp.bfloat16)
        cache_keys = handed_over(key_rows)
        cache_values = handed_over(project(value_weight).astype(jnp.bfloat16).reshape(shape))
    slot_count = cache_keys.shape[0]
    decode_peer = device_id // split_point
    block = device_id % split_point
    source_pair = jnp.sum(jnp.where(owner == decode_peer, pair_ids, 0))
    source_request = source_pair // KEY_VALUE_HEADS
    length = jnp.sum(
        jnp.where(jnp.arange(count_requests, dtype=jnp.int32) == source_request, lengths, 0)
    )
    query = lax.dynamic_index_in_dim(dec_query, decode_peer, 0, keepdims=False)
    new_key = lax.dynamic_index_in_dim(dec_key, decode_peer, 0, keepdims=False)
    new_value = lax.dynamic_index_in_dim(dec_value, decode_peer, 0, keepdims=False)
    step_pos = length + jnp.arange(STEPS, dtype=jnp.int32)
    step_cos, step_sin = rope_table(step_pos, HEAD_SIZE)
    query_rot = rotate(
        query.astype(jnp.float32).reshape(STEPS, QPK, HEAD_SIZE),
        step_cos[:, None, :],
        step_sin[:, None, :],
    ).astype(jnp.bfloat16)
    new_keys = rotate(new_key.astype(jnp.float32), step_cos, step_sin).astype(jnp.bfloat16)
    score_scale = 1.0 / HEAD_SIZE**0.5
    old_scores = (
        jnp.einsum(
            "sjd,id->sji", query_rot, cache_keys, preferred_element_type=jnp.float32
        )
        * score_scale
    )
    new_scores = (
        jnp.einsum("sjd,td->sjt", query_rot, new_keys, preferred_element_type=jnp.float32)
        * score_scale
    )
    slot_ids = jnp.arange(slot_count, dtype=jnp.int32) * split_point + block
    old_live = slot_ids < length
    new_live = (jnp.arange(STEPS)[None, :] <= jnp.arange(STEPS)[:, None]) & (block == 0)
    old_scores = jnp.where(old_live[None, None, :], old_scores, -1e30)
    new_scores = jnp.where(new_live[:, None, :], new_scores, -1e30)
    row_max = jnp.maximum(jnp.max(old_scores, -1), jnp.max(new_scores, -1))
    for bit in range(tree_levels):
        row_max = jnp.maximum(row_max, swapped(row_max, "seq", bit))
    old_exp = jnp.exp(old_scores - row_max[..., None])
    new_exp = jnp.exp(new_scores - row_max[..., None])
    denom = jnp.sum(old_exp, -1) + jnp.sum(new_exp, -1)
    for bit in range(tree_levels):
        denom = denom + swapped(denom, "seq", bit)
    old_probs = (old_exp / denom[..., None]).astype(jnp.bfloat16)
    new_probs = (new_exp / denom[..., None]).astype(jnp.bfloat16)
    partial_sum = jnp.einsum(
        "sji,id->sjd", old_probs, cache_values, preferred_element_type=jnp.float32
    )
    partial_sum = partial_sum + jnp.einsum(
        "sjt,td->sjd", new_probs, new_value, preferred_element_type=jnp.float32
    )
    flat_rows = partial_sum.reshape(STEPS, QPK * HEAD_SIZE)
    for bit in range(tree_levels):
        flat_rows = flat_rows + swapped(flat_rows, "seq", bit)
    share = flat_rows.shape[1] // split_point
    mine = lax.dynamic_slice_in_dim(flat_rows, block * share, share, 1)
    cache = jnp.concatenate([cache_keys, cache_values], 1)[None]
    return (cache, mine.astype(jnp.bfloat16))


def solution(mesh):
    placed = (
        P("groups", "seq", None),
        P("seq", None),
        P("seq", None),
        P("groups"),
        P("groups"),
        P("groups", None, None),
        P("groups", None, None),
        P("groups", None, None),
    )
    return jax.shard_map(
        body,
        mesh=mesh,
        in_specs=placed,
        out_specs=(P(("groups", "seq"), None, None), P("groups", "seq")),
        check_vma=False,
    )
```

```python
import functools

import jax
import jax.numpy as jnp
import numpy as np
from jax import lax
from jax.experimental import pallas as pl
from jax.experimental.pallas import tpu as pltpu
from jax.sharding import PartitionSpec as P

HEAD_SIZE = 128
KEY_VALUE_HEADS = 4
QPK = 8
STEPS = 4


ROPE_BASE = 500000.0


def swapped(block, axis, bit):
    count = lax.axis_size(axis)
    route = []
    for low in range(count):
        high = low | 1 << bit
        if high != low and high < count:
            route += [(low, high), (high, low)]
    return lax.ppermute(block, axis, route)


def rope_table(positions, head_dim):
    freq = ROPE_BASE ** (-(np.arange(head_dim // 2, dtype=np.float64) * 2.0) / head_dim)
    angle = positions.astype(jnp.float32)[:, None] * jnp.asarray(freq, jnp.float32)[None, :]
    return (jnp.cos(angle), jnp.sin(angle))


def rotate(values_in, cosine, sine_part):
    half_dim = values_in.shape[-1] // 2
    lower_half = values_in[..., :half_dim]
    upper_half = values_in[..., half_dim:]
    return jnp.concatenate(
        [
            lower_half * cosine - upper_half * sine_part,
            upper_half * cosine + lower_half * sine_part,
        ],
        -1,
    )


def spread(count):
    side = 1
    while side * side < count:
        side *= 2
    return (side, count // side)


def moved(block, rule):
    groups, seq = lax.axis_size("groups"), lax.axis_size("seq")
    low = spread(seq // 2)[1]
    route = []
    for g in range(groups):
        for s in range(seq):
            place = rule(g, s // 2 // low, s // 2 % low, s % 2)
            if place is not None:
                tg, tz, ty, tc = place
                route.append((g * seq + s, tg * seq + (tz * low + ty) * 2 + tc))
    return lax.ppermute(block, ("groups", "seq"), route)


def to_core(g, z, y, c):
    return (g, z, y, 1 - c)


def to_row(g, z, y, c):
    return (g, z, 1 - y, c)


def to_group(g, z, y, c):
    return (1 - g, z, y, c)


def to_pair(g, z, y, c):
    return (g, z ^ 1, y, c)


def to_middle(g, z, y, c):
    return (g, 3 - z, y, c) if z in (1, 2) else None


def to_end(g, z, y, c):
    return (g, 0 if z == 1 else 3, y, c) if z in (1, 2) else None


VMEM_REF = pl.BlockSpec(memory_space=pltpu.VMEM)
SMEM_REF = pl.BlockSpec(memory_space=pltpu.SMEM)
ANY_REF = pl.BlockSpec(memory_space=pl.ANY)
PARAMS = pltpu.CompilerParams(vmem_limit_bytes=20 << 20)
SMALL = pltpu.CompilerParams(vmem_limit_bytes=16 << 20)


def cost(flops, moved_bytes):
    return pl.CostEstimate(flops=flops, bytes_accessed=moved_bytes, transcendentals=0)


def fetch(source, target, sem):
    copy = pltpu.make_async_copy(source, target, sem)
    copy.start()
    return copy


def prepare_kernel(place, rows_in, mine, kept):
    depth = mine.shape[2]
    rows, width = rows_in.shape
    square = jnp.zeros((rows, depth), jnp.float32)
    for first in range(0, width, depth):
        part = rows_in[:, first : first + depth].astype(jnp.float32)
        square += part * part
    scale = lax.rsqrt(jnp.sum(square, -1, keepdims=True) / width + 1e-05)
    for core in range(2):

        @pl.when(place[1] == core)
        def _():
            for first in range(0, width, depth):
                j, c, h = first // (4 * depth), first // (2 * depth) % 2, first // depth % 2
                target = mine if c == core else kept
                part = rows_in[:, first : first + depth].astype(jnp.float32)
                target[2 * j + h] = (part * scale).astype(jnp.bfloat16)


def prepared(place, flat, blocks):
    rows, width = flat.shape
    depth = width // (4 * blocks)
    tile = 80 if rows % 80 == 0 else rows
    out = jax.ShapeDtypeStruct((2 * blocks, rows, depth), jnp.bfloat16)
    spec = pl.BlockSpec((2 * blocks, tile, depth), lambda i, place: (0, i, 0))
    return pl.pallas_call(
        prepare_kernel,
        grid_spec=pltpu.PrefetchScalarGridSpec(
            num_scalar_prefetch=1,
            grid=(rows // tile,),
            in_specs=[pl.BlockSpec((tile, width), lambda i, place: (i, 0))],
            out_specs=[spec, spec],
        ),
        out_shape=[out, out],
        compiler_params=PARAMS,
        cost_estimate=cost(1000, 1000),
        name="normed_halves",
    )(place, flat)


def after(value, *events):
    return lax.optimization_barrier((value, *events))[0]


def half_index(place, entry, kind):
    half = {0: place[0], 1: 1 - place[0], 2: 0, 3: 1}[kind]
    return place[entry] * 2 + half


def product_kernel(plan, group, with_total, place, mine, other, *refs):
    count = len(plan)
    outs = refs[-7:-5]
    left, right, total, sems, total_sems = refs[-5:]
    rows, depth = mine.shape[1], mine.shape[2]
    waits = []
    for k, (entry, kind) in enumerate(plan):
        area = pl.ds((k % group) * depth, depth)
        slot = k // group
        index = half_index(place, entry, kind)
        sources = (mine.at[index], other.at[index], refs[k])
        targets = (left.at[slot, 0, :, area], left.at[slot, 1, :, area], right.at[slot, area])
        waits.append(
            [fetch(a, b, sems.at[3 * k + i]) for i, (a, b) in enumerate(zip(sources, targets))]
        )
    carried = [
        fetch(ref, total.at[pl.ds(k * rows, rows)], total_sems.at[k])
        for k, ref in enumerate(refs[count : count + 2 * with_total])
    ]
    for slot in range(count // group):
        for copies in waits[slot * group : (slot + 1) * group]:
            for copy in copies:
                copy.wait()
        stacked = left[slot].reshape(2 * rows, group * depth)
        value = jnp.dot(stacked, right[slot], preferred_element_type=jnp.float32)
        if slot == 0:
            for copy in carried:
                copy.wait()
        if slot or with_total:
            value += total[...]
        if slot + 1 < count // group:
            total[...] = value
        else:
            outs[0][...] = value[:rows]
            outs[1][...] = value[rows:]


def product(place, mine, other, pieces, totals, group, moved_bytes=1000):
    _, rows, depth = mine.shape
    columns = pieces[0][2].shape[1]
    plan = [(entry, kind) for entry, kind, _ in pieces]
    count = len(plan)
    out = jax.ShapeDtypeStruct((rows, columns), jnp.float32)
    return pl.pallas_call(
        functools.partial(product_kernel, plan, group, bool(totals)),
        in_specs=[SMEM_REF] + [ANY_REF] * (2 + count + len(totals)),
        out_specs=[VMEM_REF] * 2,
        out_shape=[out] * 2,
        scratch_shapes=[
            pltpu.VMEM((count // group, 2, rows, group * depth), mine.dtype),
            pltpu.VMEM((count // group, group * depth, columns), mine.dtype),
            pltpu.VMEM((2 * rows, columns), jnp.float32),
            pltpu.SemaphoreType.DMA((3 * count,)),
            pltpu.SemaphoreType.DMA((2,)),
        ],
        compiler_params=PARAMS,
        cost_estimate=cost(1000, moved_bytes),
        name="add_product",
    )(place, mine, other, *[array for _, _, array in pieces], *totals)


LOW = 64


def turn_tables(positions, rows):
    freq = ROPE_BASE ** (-(np.arange(HEAD_SIZE // 2) * 2.0) / HEAD_SIZE)
    tables = []
    for places in (np.arange(0, positions, LOW), np.arange(LOW), np.arange(rows)):
        angle = places[:, None] * freq[None, :]
        tables.append(np.concatenate([np.cos(angle), np.cos(angle)], 1))
        tables.append(np.concatenate([-np.sin(angle), np.sin(angle)], 1))
    return [jnp.asarray(table, jnp.float32) for table in tables]


def turned_by(start, tables, cosine, sine):
    high, low = pl.ds(start // LOW, 1), pl.ds(start % LOW, 1)
    for cos_row, sin_row in (
        (tables[0][high], tables[1][high]),
        (tables[2][low], tables[3][low]),
    ):
        cosine, sine = cosine * cos_row - sine * sin_row, sine * cos_row + cosine * sin_row
    return cosine, sine


def rotated(rows, cosine, sine):
    half = HEAD_SIZE // 2
    return rows * cosine + jnp.concatenate([rows[:, half:], rows[:, :half]], 1) * sine


def rows_kernel(place, lengths, owner, *refs):
    total, came, *tables, out, scratch = refs
    columns = total.shape[1] // 2
    count_requests, count_rows = lengths.shape[0], scratch.shape[0]
    cosine, sine = turned_by(place[2] * count_rows, tables, tables[4][...], tables[5][...])
    index = place[2] * count_rows + lax.broadcasted_iota(jnp.int32, scratch.shape, 0)
    for r in range(count_requests):
        live = index < lengths[r]
        for h in range(KEY_VALUE_HEADS):
            for part in range(2):
                first = part * columns + h * HEAD_SIZE
                area = (
                    slice(r * count_rows, (r + 1) * count_rows),
                    slice(first, first + HEAD_SIZE),
                )
                rows = total[area] + came[area]
                if part == 0:
                    rows = rotated(rows, cosine, sine)
                scratch[...] = jnp.where(live, rows, 0.0)
                peer = owner[r * KEY_VALUE_HEADS + h]
                lanes = slice(part * HEAD_SIZE, (part + 1) * HEAD_SIZE)
                for b in range(2):
                    picked = scratch[pl.ds(b, count_rows // 2, stride=2), :]
                    out[peer * 2 + b, :, lanes] = picked.astype(jnp.bfloat16)


def outgoing_rows(place, lengths, owner, total, came, tables):
    count_rows = total.shape[0] // lengths.shape[0]
    out = (owner.shape[0] * 2, count_rows // 2, 2 * HEAD_SIZE)
    return pl.pallas_call(
        rows_kernel,
        in_specs=[SMEM_REF] * 3 + [VMEM_REF] * 8,
        out_specs=VMEM_REF,
        out_shape=jax.ShapeDtypeStruct(out, jnp.bfloat16),
        scratch_shapes=[pltpu.VMEM((count_rows, HEAD_SIZE), jnp.float32)],
        compiler_params=SMALL,
        cost_estimate=cost(1000, 1000),
        name="cache_rows",
    )(place, lengths, owner, total, came, *tables)


def decode_kernel(place, lengths, owner, cache, dec_query, dec_key, dec_value, *refs):
    tables, out = refs[:4], refs[4]
    peer, block = place[2] // 2, place[2] % 2
    length = lengths[0]
    for pair in range(owner.shape[0]):
        length = jnp.where(owner[pair] == peer, lengths[pair // KEY_VALUE_HEADS], length)
    cosine, sine = turned_by(length, tables, tables[2][:STEPS], tables[3][:STEPS])

    def turned(rows):
        return rotated(rows.astype(jnp.float32), cosine, sine)

    def padded(rows):
        return jnp.concatenate([rows, jnp.zeros((16 - STEPS, HEAD_SIZE), jnp.float32)], 0)

    raw = dec_query[peer]
    heads = [raw[:, j * HEAD_SIZE : (j + 1) * HEAD_SIZE] for j in range(QPK)]
    query = jnp.concatenate([turned(head) for head in heads], 0).astype(jnp.bfloat16)
    new_keys = padded(turned(dec_key[peer])).astype(jnp.bfloat16)
    new_value = padded(dec_value[peer].astype(jnp.float32)).astype(jnp.bfloat16)
    contract = (((1,), (1,)), ((), ()))
    scale = 1.0 / HEAD_SIZE**0.5
    old = lax.dot_general(
        query, cache[:, :HEAD_SIZE], contract, preferred_element_type=jnp.float32
    )
    slot = lax.broadcasted_iota(jnp.int32, old.shape, 1) * 2 + block
    old = jnp.where(slot < length, old * scale, -1e30)
    new = lax.dot_general(query, new_keys, contract, preferred_element_type=jnp.float32)
    step = lax.broadcasted_iota(jnp.int32, new.shape, 0) % STEPS
    token = lax.broadcasted_iota(jnp.int32, new.shape, 1)
    new = jnp.where((token <= step) & (block == 0), new * scale, -1e30)
    top = jnp.maximum(jnp.max(old, 1, keepdims=True), jnp.max(new, 1, keepdims=True))
    old, new = jnp.exp(old - top), jnp.exp(new - top)
    total = jnp.sum(old, 1, keepdims=True) + jnp.sum(new, 1, keepdims=True)
    sums = jnp.dot(
        old.astype(jnp.bfloat16), cache[:, HEAD_SIZE:], preferred_element_type=jnp.float32
    )
    out[:, :HEAD_SIZE] = sums + jnp.dot(
        new.astype(jnp.bfloat16), new_value, preferred_element_type=jnp.float32
    )
    half = (QPK * STEPS, HEAD_SIZE // 2)
    out[:, HEAD_SIZE : HEAD_SIZE + half[1]] = jnp.broadcast_to(top, half)
    out[:, HEAD_SIZE + half[1] :] = jnp.broadcast_to(total, half)


def joined_kernel(place, mine, theirs, out):
    share = QPK // 2
    area = pl.ds(place[2] % 2 * share * STEPS, share * STEPS)
    last = HEAD_SIZE + HEAD_SIZE // 2
    sums, tops, totals = [], [], []
    for ref in (mine, theirs):
        sums.append(ref[area, :HEAD_SIZE])
        tops.append(ref[area, HEAD_SIZE : HEAD_SIZE + 1])
        totals.append(ref[area, last : last + 1])
    top = jnp.maximum(tops[0], tops[1])
    scales = [jnp.exp(one - top) for one in tops]
    total = totals[0] * scales[0] + totals[1] * scales[1]
    value = (sums[0] * scales[0] + sums[1] * scales[1]) / total
    for j in range(share):
        rows = value[j * STEPS : (j + 1) * STEPS]
        out[:, j * HEAD_SIZE : (j + 1) * HEAD_SIZE] = rows.astype(jnp.bfloat16)


def decoded(place, lengths, owner, cache, dec_query, dec_key, dec_value, tables):
    mine = pl.pallas_call(
        decode_kernel,
        in_specs=[SMEM_REF] * 3 + [VMEM_REF] * 8,
        out_specs=VMEM_REF,
        out_shape=jax.ShapeDtypeStruct((STEPS * QPK, 2 * HEAD_SIZE), jnp.float32),
        compiler_params=SMALL,
        cost_estimate=cost(1000, 1000),
        name="decode",
    )(place, lengths, owner, cache, dec_query, dec_key, dec_value, *tables[:4])
    return pl.pallas_call(
        joined_kernel,
        in_specs=[SMEM_REF] + [VMEM_REF] * 2,
        out_specs=VMEM_REF,
        out_shape=jax.ShapeDtypeStruct((STEPS, QPK // 2 * HEAD_SIZE), jnp.bfloat16),
        compiler_params=SMALL,
        cost_estimate=cost(1000, 1000),
        name="joined",
    )(place, mine, moved(mine, to_core))


HERE, THERE = 3, 7


def body(hidden, key_weight, value_weight, lengths, owner, dec_query, dec_key, dec_value):
    count_requests, count_rows, width = hidden.shape
    device_id = lax.axis_index("seq")
    group_id = lax.axis_index("groups")
    seq = lax.axis_size("seq")
    planned = seq == 16 and lax.axis_size("groups") == 2
    decode_peers = count_requests * KEY_VALUE_HEADS
    split_point = seq // decode_peers
    tree_levels = split_point.bit_length() - 1
    rows_per_peer = count_rows // split_point
    positions = device_id * count_rows + jnp.arange(count_rows, dtype=jnp.int32)
    total_rows = count_requests * count_rows
    flat = hidden.reshape(total_rows, width)
    if planned:
        core = device_id % 2
        z, y = device_id // 4, device_id // 2 % 2
        layers = [z, z ^ 1, jnp.where(z < 2, 2, 1), jnp.where(z < 2, 3, 0)]
        is_end = (z == 0) | (z == 3)
        place = [group_id, core, device_id]
        place += [layer * 2 + y for layer in layers]
        place += [layer * 2 + 1 - y for layer in layers]
        place = jnp.stack([jnp.asarray(entry, jnp.int32) for entry in place])
    else:
        widened = flat.astype(jnp.float32)
        normed = (
            widened * lax.rsqrt(jnp.mean(widened * widened, -1, keepdims=True) + 1e-05)
        ).astype(jnp.bfloat16)

        def project(weight):
            whole = lax.all_gather(weight, "seq", axis=0, tiled=True)
            return jnp.dot(normed, whole, preferred_element_type=jnp.float32)

    pair_ids = jnp.arange(decode_peers, dtype=jnp.int32)
    matches = owner[None, :] == pair_ids[:, None]
    inverse_order = jnp.sum(jnp.where(matches, pair_ids[None, :], 0), axis=1)
    live_rows = positions[None, :] < lengths[:, None]

    def handed_over(rows):
        rows = jnp.where(live_rows[:, :, None, None], rows, jnp.zeros_like(rows))
        pair_rows = jnp.transpose(rows, (0, 2, 1, 3)).reshape(decode_peers, count_rows, HEAD_SIZE)
        sorted_rows = pair_rows[inverse_order].reshape(
            decode_peers, rows_per_peer, split_point, HEAD_SIZE
        )
        outgoing = jnp.transpose(sorted_rows, (0, 2, 1, 3)).reshape(
            decode_peers * split_point, rows_per_peer, HEAD_SIZE
        )
        return lax.all_to_all(outgoing, "seq", split_axis=0, concat_axis=1, tiled=True)[0]

    if planned:
        depth = key_weight.shape[0] // 2

        def half_block(first):
            halves = [
                lax.dynamic_slice_in_dim(weight, first, depth, 0)
                for weight in (key_weight, value_weight)
            ]
            return jnp.concatenate(halves, 1)

        sent = half_block(group_id * depth)
        tables = turn_tables(count_rows * seq + STEPS, count_rows)
        near = moved(sent, to_pair)
        middle = moved(sent, to_middle)
        across = moved(sent, to_row)
        rest = half_block(depth - group_id * depth)
        mine, kept = prepared(place, flat, seq // 2)
        layers, rows = (near, middle), (across, mine, rest)
        end_b = moved(after(middle, *layers), to_end)
        middle_c = moved(after(near, *layers), to_middle)
        near_y = moved(after(near, *layers, *rows), to_row)
        across_x = moved(after(across, *layers, *rows), to_group)
        other = moved(after(kept, *layers, *rows), to_core)
        layers, rows, before = (end_b, middle_c), (near_y, across_x, other), rows
        end_c = moved(after(middle_c, *layers, *before), to_end)
        block_b = jnp.where(is_end, after(end_b, *layers), middle)
        block_yb = moved(after(block_b, *rows), to_row)
        block_xb = moved(after(block_b, *rows), to_group)
        pieces = [(HERE, 0, sent), (HERE, 1, rest), (THERE, 0, across)]
        pieces += [(THERE, 1, across_x), (HERE + 1, 0, near), (THERE + 1, 0, near_y)]
        totals = product(place, after(mine, *rows, block_b), other, pieces, (), 3)
        layers, rows, before = (end_c,), (block_yb, block_xb, totals[0]), rows
        near_rest = moved(after(rest, *layers, *before), to_pair)
        block_c = jnp.where(is_end, after(end_c, *layers), middle_c)
        block_xc = moved(after(block_c, *rows), to_group)
        block_yc = moved(after(block_c, *rows), to_row)
        pieces = [(HERE + 2, 0, block_b), (HERE + 2, 1, block_xb)]
        pieces += [(THERE + 2, 0, block_yb), (HERE + 3, 0, block_c)]
        totals = product(place, after(mine, *rows, block_c), other, pieces, totals, 4)
        layers, rows, before = (near_rest,), (block_xc, block_yc, totals[0]), rows
        end_a = moved(after(across_x, *layers, *before), to_pair)
        ends = [moved(after(block_yb, *rows), to_group), moved(after(block_xc, *rows), to_row)]
        pieces = [(HERE + 1, 1, near_rest), (HERE + 3, 1, block_xc)]
        pieces += [(THERE + 3, 0, block_yc), (THERE + 1, 1, end_a)]
        totals = product(place, after(mine, *rows, end_a), other, pieces, totals, 4, 1 << 24)
        pieces = [(THERE + 2, 1, ends[0]), (THERE + 3, 1, ends[1])]
        total, given = product(place, after(mine, *ends, *totals), other, pieces, totals, 2)
        outgoing = outgoing_rows(place, lengths, owner, total, moved(given, to_core), tables)
        incoming = lax.all_to_all(outgoing, "seq", split_axis=0, concat_axis=1, tiled=True)
        attended = decoded(
            place, lengths, owner, incoming[0], dec_query, dec_key, dec_value, tables
        )
        return (incoming, attended)
    else:
        cosine, sine_part = rope_table(positions, HEAD_SIZE)
        shape = (count_requests, count_rows, KEY_VALUE_HEADS, HEAD_SIZE)
        unrotated_key = project(key_weight).reshape(shape)
        key_rows = rotate(
            unrotated_key, cosine[:, None, :], sine_part[:, None, :]
        ).astype(jnp.bfloat16)
        cache_keys = handed_over(key_rows)
        cache_values = handed_over(project(value_weight).astype(jnp.bfloat16).reshape(shape))
    slot_count = cache_keys.shape[0]
    decode_peer = device_id // split_point
    block = device_id % split_point
    source_pair = jnp.sum(jnp.where(owner == decode_peer, pair_ids, 0))
    source_request = source_pair // KEY_VALUE_HEADS
    length = jnp.sum(
        jnp.where(jnp.arange(count_requests, dtype=jnp.int32) == source_request, lengths, 0)
    )
    query = lax.dynamic_index_in_dim(dec_query, decode_peer, 0, keepdims=False)
    new_key = lax.dynamic_index_in_dim(dec_key, decode_peer, 0, keepdims=False)
    new_value = lax.dynamic_index_in_dim(dec_value, decode_peer, 0, keepdims=False)
    step_pos = length + jnp.arange(STEPS, dtype=jnp.int32)
    step_cos, step_sin = rope_table(step_pos, HEAD_SIZE)
    query_rot = rotate(
        query.astype(jnp.float32).reshape(STEPS, QPK, HEAD_SIZE),
        step_cos[:, None, :],
        step_sin[:, None, :],
    ).astype(jnp.bfloat16)
    new_keys = rotate(new_key.astype(jnp.float32), step_cos, step_sin).astype(jnp.bfloat16)
    score_scale = 1.0 / HEAD_SIZE**0.5
    old_scores = (
        jnp.einsum(
            "sjd,id->sji", query_rot, cache_keys, preferred_element_type=jnp.float32
        )
        * score_scale
    )
    new_scores = (
        jnp.einsum("sjd,td->sjt", query_rot, new_keys, preferred_element_type=jnp.float32)
        * score_scale
    )
    slot_ids = jnp.arange(slot_count, dtype=jnp.int32) * split_point + block
    old_live = slot_ids < length
    new_live = (jnp.arange(STEPS)[None, :] <= jnp.arange(STEPS)[:, None]) & (block == 0)
    old_scores = jnp.where(old_live[None, None, :], old_scores, -1e30)
    new_scores = jnp.where(new_live[:, None, :], new_scores, -1e30)
    row_max = jnp.maximum(jnp.max(old_scores, -1), jnp.max(new_scores, -1))
    for bit in range(tree_levels):
        row_max = jnp.maximum(row_max, swapped(row_max, "seq", bit))
    old_exp = jnp.exp(old_scores - row_max[..., None])
    new_exp = jnp.exp(new_scores - row_max[..., None])
    denom = jnp.sum(old_exp, -1) + jnp.sum(new_exp, -1)
    for bit in range(tree_levels):
        denom = denom + swapped(denom, "seq", bit)
    old_probs = (old_exp / denom[..., None]).astype(jnp.bfloat16)
    new_probs = (new_exp / denom[..., None]).astype(jnp.bfloat16)
    partial_sum = jnp.einsum(
        "sji,id->sjd", old_probs, cache_values, preferred_element_type=jnp.float32
    )
    partial_sum = partial_sum + jnp.einsum(
        "sjt,td->sjd", new_probs, new_value, preferred_element_type=jnp.float32
    )
    flat_rows = partial_sum.reshape(STEPS, QPK * HEAD_SIZE)
    for bit in range(tree_levels):
        flat_rows = flat_rows + swapped(flat_rows, "seq", bit)
    share = flat_rows.shape[1] // split_point
    mine = lax.dynamic_slice_in_dim(flat_rows, block * share, share, 1)
    cache = jnp.concatenate([cache_keys, cache_values], 1)[None]
    return (cache, mine.astype(jnp.bfloat16))


def solution(mesh):
    placed = (
        P("groups", "seq", None),
        P("seq", None),
        P("seq", None),
        P("groups"),
        P("groups"),
        P("groups", None, None),
        P("groups", None, None),
        P("groups", None, None),
    )
    return jax.shard_map(
        body,
        mesh=mesh,
        in_specs=placed,
        out_specs=(P(("groups", "seq"), None, None), P("groups", "seq")),
        check_vma=False,
    )
```

```python
import functools

import jax
import jax.numpy as jnp
import numpy as np
from jax import lax
from jax.experimental import pallas as pl
from jax.experimental.pallas import tpu as pltpu
from jax.sharding import PartitionSpec as P

HEAD_SIZE = 128
KEY_VALUE_HEADS = 4
QPK = 8
STEPS = 4


ROPE_BASE = 500000.0


def swapped(block, axis, bit):
    count = lax.axis_size(axis)
    route = []
    for low in range(count):
        high = low | 1 << bit
        if high != low and high < count:
            route += [(low, high), (high, low)]
    return lax.ppermute(block, axis, route)


def rope_table(positions, head_dim):
    freq = ROPE_BASE ** (-(np.arange(head_dim // 2, dtype=np.float64) * 2.0) / head_dim)
    angle = positions.astype(jnp.float32)[:, None] * jnp.asarray(freq, jnp.float32)[None, :]
    return (jnp.cos(angle), jnp.sin(angle))


def rotate(values_in, cosine, sine_part):
    half_dim = values_in.shape[-1] // 2
    lower_half = values_in[..., :half_dim]
    upper_half = values_in[..., half_dim:]
    return jnp.concatenate(
        [
            lower_half * cosine - upper_half * sine_part,
            upper_half * cosine + lower_half * sine_part,
        ],
        -1,
    )


def spread(count):
    side = 1
    while side * side < count:
        side *= 2
    return (side, count // side)


def moved(block, rule):
    groups, seq = lax.axis_size("groups"), lax.axis_size("seq")
    low = spread(seq // 2)[1]
    route = []
    for g in range(groups):
        for s in range(seq):
            tg, tz, ty, tc = rule(g, s // 2 // low, s // 2 % low, s % 2)
            route.append((g * seq + s, tg * seq + (tz * low + ty) * 2 + tc))
    return lax.ppermute(block, ("groups", "seq"), route)


def to_core(g, z, y, c):
    return (g, z, y, 1 - c)


def to_row(g, z, y, c):
    return (g, z, 1 - y, c)


def to_group(g, z, y, c):
    return (1 - g, z, y, c)


def along(bits):
    return lambda g, z, y, c: (g, z ^ bits, y, c)


VMEM_REF = pl.BlockSpec(memory_space=pltpu.VMEM)
SMEM_REF = pl.BlockSpec(memory_space=pltpu.SMEM)
ANY_REF = pl.BlockSpec(memory_space=pl.ANY)
PARAMS = pltpu.CompilerParams(vmem_limit_bytes=20 << 20)
SMALL = pltpu.CompilerParams(vmem_limit_bytes=16 << 20)


def cost(flops, moved_bytes):
    return pl.CostEstimate(flops=flops, bytes_accessed=moved_bytes, transcendentals=0)


def fetch(source, target, sem):
    copy = pltpu.make_async_copy(source, target, sem)
    copy.start()
    return copy


def prepare_kernel(place, rows_in, mine, kept):
    depth = mine.shape[2]
    rows, width = rows_in.shape
    square = jnp.zeros((rows, depth), jnp.float32)
    for first in range(0, width, depth):
        part = rows_in[:, first : first + depth].astype(jnp.float32)
        square += part * part
    scale = lax.rsqrt(jnp.sum(square, -1, keepdims=True) / width + 1e-05)
    for core in range(2):

        @pl.when(place[1] == core)
        def _():
            for first in range(0, width, depth):
                j, c, h = first // (4 * depth), first // (2 * depth) % 2, first // depth % 2
                target = mine if c == core else kept
                part = rows_in[:, first : first + depth].astype(jnp.float32)
                target[2 * j + h] = (part * scale).astype(jnp.bfloat16)


def prepared(place, flat, blocks):
    rows, width = flat.shape
    depth = width // (4 * blocks)
    tile = 80 if rows % 80 == 0 else rows
    out = jax.ShapeDtypeStruct((2 * blocks, rows, depth), jnp.bfloat16)
    spec = pl.BlockSpec((2 * blocks, tile, depth), lambda i, place: (0, i, 0))
    return pl.pallas_call(
        prepare_kernel,
        grid_spec=pltpu.PrefetchScalarGridSpec(
            num_scalar_prefetch=1,
            grid=(rows // tile,),
            in_specs=[pl.BlockSpec((tile, width), lambda i, place: (i, 0))],
            out_specs=[spec, spec],
        ),
        out_shape=[out, out],
        compiler_params=PARAMS,
        cost_estimate=cost(1000, 1000),
        name="normed_halves",
    )(place, flat)


def after(value, *events):
    return lax.optimization_barrier((value, *events))[0]


def half_index(place, entry, kind):
    half = {0: place[0], 1: 1 - place[0], 2: 0, 3: 1}[kind]
    return place[entry] * 2 + half


def product_kernel(plan, group, with_total, place, mine, other, *refs):
    count = len(plan)
    outs = refs[-7:-5]
    left, right, total, sems, total_sems = refs[-5:]
    rows, depth = mine.shape[1], mine.shape[2]
    waits = []
    for k, (entry, kind) in enumerate(plan):
        area = pl.ds((k % group) * depth, depth)
        slot = k // group
        index = half_index(place, entry, kind)
        sources = (mine.at[index], other.at[index], refs[k])
        targets = (left.at[slot, 0, :, area], left.at[slot, 1, :, area], right.at[slot, area])
        waits.append(
            [fetch(a, b, sems.at[3 * k + i]) for i, (a, b) in enumerate(zip(sources, targets))]
        )
    carried = [
        fetch(ref, total.at[pl.ds(k * rows, rows)], total_sems.at[k])
        for k, ref in enumerate(refs[count : count + 2 * with_total])
    ]
    for slot in range(count // group):
        for copies in waits[slot * group : (slot + 1) * group]:
            for copy in copies:
                copy.wait()
        stacked = left[slot].reshape(2 * rows, group * depth)
        value = jnp.dot(stacked, right[slot], preferred_element_type=jnp.float32)
        if slot == 0:
            for copy in carried:
                copy.wait()
        if slot or with_total:
            value += total[...]
        if slot + 1 < count // group:
            total[...] = value
        else:
            outs[0][...] = value[:rows]
            outs[1][...] = value[rows:]


def product(place, mine, other, pieces, totals, group, moved_bytes=1000):
    _, rows, depth = mine.shape
    columns = pieces[0][2].shape[1]
    plan = [(entry, kind) for entry, kind, _ in pieces]
    count = len(plan)
    out = jax.ShapeDtypeStruct((rows, columns), jnp.float32)
    return pl.pallas_call(
        functools.partial(product_kernel, plan, group, bool(totals)),
        in_specs=[SMEM_REF] + [ANY_REF] * (2 + count + len(totals)),
        out_specs=[VMEM_REF] * 2,
        out_shape=[out] * 2,
        scratch_shapes=[
            pltpu.VMEM((count // group, 2, rows, group * depth), mine.dtype),
            pltpu.VMEM((count // group, group * depth, columns), mine.dtype),
            pltpu.VMEM((2 * rows, columns), jnp.float32),
            pltpu.SemaphoreType.DMA((3 * count,)),
            pltpu.SemaphoreType.DMA((2,)),
        ],
        compiler_params=PARAMS,
        cost_estimate=cost(1000, moved_bytes),
        name="add_product",
    )(place, mine, other, *[array for _, _, array in pieces], *totals)


LOW = 64


def turn_tables(positions, rows):
    freq = ROPE_BASE ** (-(np.arange(HEAD_SIZE // 2) * 2.0) / HEAD_SIZE)
    tables = []
    for places in (np.arange(0, positions, LOW), np.arange(LOW), np.arange(rows)):
        angle = places[:, None] * freq[None, :]
        tables.append(np.concatenate([np.cos(angle), np.cos(angle)], 1))
        tables.append(np.concatenate([-np.sin(angle), np.sin(angle)], 1))
    return [jnp.asarray(table, jnp.float32) for table in tables]


def turned_by(start, tables, cosine, sine):
    high, low = pl.ds(start // LOW, 1), pl.ds(start % LOW, 1)
    for cos_row, sin_row in (
        (tables[0][high], tables[1][high]),
        (tables[2][low], tables[3][low]),
    ):
        cosine, sine = cosine * cos_row - sine * sin_row, sine * cos_row + cosine * sin_row
    return cosine, sine


def rotated(rows, cosine, sine):
    half = HEAD_SIZE // 2
    return rows * cosine + jnp.concatenate([rows[:, half:], rows[:, :half]], 1) * sine


def rows_kernel(place, lengths, owner, *refs):
    total, came, *tables, out, scratch = refs
    columns = total.shape[1] // 2
    count_requests, count_rows = lengths.shape[0], scratch.shape[0]
    cosine, sine = turned_by(place[2] * count_rows, tables, tables[4][...], tables[5][...])
    index = place[2] * count_rows + lax.broadcasted_iota(jnp.int32, scratch.shape, 0)
    for r in range(count_requests):
        live = index < lengths[r]
        for h in range(KEY_VALUE_HEADS):
            for part in range(2):
                first = part * columns + h * HEAD_SIZE
                area = (
                    slice(r * count_rows, (r + 1) * count_rows),
                    slice(first, first + HEAD_SIZE),
                )
                rows = total[area] + came[area]
                if part == 0:
                    rows = rotated(rows, cosine, sine)
                scratch[...] = jnp.where(live, rows, 0.0)
                peer = owner[r * KEY_VALUE_HEADS + h]
                lanes = slice(part * HEAD_SIZE, (part + 1) * HEAD_SIZE)
                for b in range(2):
                    picked = scratch[pl.ds(b, count_rows // 2, stride=2), :]
                    out[peer * 2 + b, :, lanes] = picked.astype(jnp.bfloat16)


def outgoing_rows(place, lengths, owner, total, came, tables):
    count_rows = total.shape[0] // lengths.shape[0]
    out = (owner.shape[0] * 2, count_rows // 2, 2 * HEAD_SIZE)
    return pl.pallas_call(
        rows_kernel,
        in_specs=[SMEM_REF] * 3 + [VMEM_REF] * 8,
        out_specs=VMEM_REF,
        out_shape=jax.ShapeDtypeStruct(out, jnp.bfloat16),
        scratch_shapes=[pltpu.VMEM((count_rows, HEAD_SIZE), jnp.float32)],
        compiler_params=SMALL,
        cost_estimate=cost(1000, 1000),
        name="cache_rows",
    )(place, lengths, owner, total, came, *tables)


def decode_kernel(place, lengths, owner, cache, dec_query, dec_key, dec_value, *refs):
    tables, out = refs[:4], refs[4]
    peer, block = place[2] // 2, place[2] % 2
    length = lengths[0]
    for pair in range(owner.shape[0]):
        length = jnp.where(owner[pair] == peer, lengths[pair // KEY_VALUE_HEADS], length)
    cosine, sine = turned_by(length, tables, tables[2][:STEPS], tables[3][:STEPS])

    def turned(rows):
        return rotated(rows.astype(jnp.float32), cosine, sine)

    def padded(rows):
        return jnp.concatenate([rows, jnp.zeros((16 - STEPS, HEAD_SIZE), jnp.float32)], 0)

    raw = dec_query[peer]
    heads = [raw[:, j * HEAD_SIZE : (j + 1) * HEAD_SIZE] for j in range(QPK)]
    query = jnp.concatenate([turned(head) for head in heads], 0).astype(jnp.bfloat16)
    new_keys = padded(turned(dec_key[peer])).astype(jnp.bfloat16)
    new_value = padded(dec_value[peer].astype(jnp.float32)).astype(jnp.bfloat16)
    contract = (((1,), (1,)), ((), ()))
    scale = 1.0 / HEAD_SIZE**0.5
    old = lax.dot_general(
        query, cache[:, :HEAD_SIZE], contract, preferred_element_type=jnp.float32
    )
    slot = lax.broadcasted_iota(jnp.int32, old.shape, 1) * 2 + block
    old = jnp.where(slot < length, old * scale, -1e30)
    new = lax.dot_general(query, new_keys, contract, preferred_element_type=jnp.float32)
    step = lax.broadcasted_iota(jnp.int32, new.shape, 0) % STEPS
    token = lax.broadcasted_iota(jnp.int32, new.shape, 1)
    new = jnp.where((token <= step) & (block == 0), new * scale, -1e30)
    top = jnp.maximum(jnp.max(old, 1, keepdims=True), jnp.max(new, 1, keepdims=True))
    old, new = jnp.exp(old - top), jnp.exp(new - top)
    total = jnp.sum(old, 1, keepdims=True) + jnp.sum(new, 1, keepdims=True)
    sums = jnp.dot(
        old.astype(jnp.bfloat16), cache[:, HEAD_SIZE:], preferred_element_type=jnp.float32
    )
    out[:, :HEAD_SIZE] = sums + jnp.dot(
        new.astype(jnp.bfloat16), new_value, preferred_element_type=jnp.float32
    )
    half = (QPK * STEPS, HEAD_SIZE // 2)
    out[:, HEAD_SIZE : HEAD_SIZE + half[1]] = jnp.broadcast_to(top, half)
    out[:, HEAD_SIZE + half[1] :] = jnp.broadcast_to(total, half)


def joined_kernel(place, mine, theirs, out):
    share = QPK // 2
    area = pl.ds(place[2] % 2 * share * STEPS, share * STEPS)
    last = HEAD_SIZE + HEAD_SIZE // 2
    sums, tops, totals = [], [], []
    for ref in (mine, theirs):
        sums.append(ref[area, :HEAD_SIZE])
        tops.append(ref[area, HEAD_SIZE : HEAD_SIZE + 1])
        totals.append(ref[area, last : last + 1])
    top = jnp.maximum(tops[0], tops[1])
    scales = [jnp.exp(one - top) for one in tops]
    total = totals[0] * scales[0] + totals[1] * scales[1]
    value = (sums[0] * scales[0] + sums[1] * scales[1]) / total
    for j in range(share):
        rows = value[j * STEPS : (j + 1) * STEPS]
        out[:, j * HEAD_SIZE : (j + 1) * HEAD_SIZE] = rows.astype(jnp.bfloat16)


def decoded(place, lengths, owner, cache, dec_query, dec_key, dec_value, tables):
    mine = pl.pallas_call(
        decode_kernel,
        in_specs=[SMEM_REF] * 3 + [VMEM_REF] * 8,
        out_specs=VMEM_REF,
        out_shape=jax.ShapeDtypeStruct((STEPS * QPK, 2 * HEAD_SIZE), jnp.float32),
        compiler_params=SMALL,
        cost_estimate=cost(1000, 1000),
        name="decode",
    )(place, lengths, owner, cache, dec_query, dec_key, dec_value, *tables[:4])
    return pl.pallas_call(
        joined_kernel,
        in_specs=[SMEM_REF] + [VMEM_REF] * 2,
        out_specs=VMEM_REF,
        out_shape=jax.ShapeDtypeStruct((STEPS, QPK // 2 * HEAD_SIZE), jnp.bfloat16),
        compiler_params=SMALL,
        cost_estimate=cost(1000, 1000),
        name="joined",
    )(place, mine, moved(mine, to_core))


HERE, THERE = 3, 7


def body(hidden, key_weight, value_weight, lengths, owner, dec_query, dec_key, dec_value):
    count_requests, count_rows, width = hidden.shape
    device_id = lax.axis_index("seq")
    group_id = lax.axis_index("groups")
    seq = lax.axis_size("seq")
    planned = seq == 16 and lax.axis_size("groups") == 2
    decode_peers = count_requests * KEY_VALUE_HEADS
    split_point = seq // decode_peers
    tree_levels = split_point.bit_length() - 1
    rows_per_peer = count_rows // split_point
    positions = device_id * count_rows + jnp.arange(count_rows, dtype=jnp.int32)
    total_rows = count_requests * count_rows
    flat = hidden.reshape(total_rows, width)
    if planned:
        core = device_id % 2
        z, y = device_id // 4, device_id // 2 % 2
        place = [group_id, core, device_id]
        place += [(z ^ bits) * 2 + y for bits in range(4)]
        place += [(z ^ bits) * 2 + 1 - y for bits in range(4)]
        place = jnp.stack([jnp.asarray(entry, jnp.int32) for entry in place])
    else:
        widened = flat.astype(jnp.float32)
        normed = (
            widened * lax.rsqrt(jnp.mean(widened * widened, -1, keepdims=True) + 1e-05)
        ).astype(jnp.bfloat16)

        def project(weight):
            whole = lax.all_gather(weight, "seq", axis=0, tiled=True)
            return jnp.dot(normed, whole, preferred_element_type=jnp.float32)

    pair_ids = jnp.arange(decode_peers, dtype=jnp.int32)
    matches = owner[None, :] == pair_ids[:, None]
    inverse_order = jnp.sum(jnp.where(matches, pair_ids[None, :], 0), axis=1)
    live_rows = positions[None, :] < lengths[:, None]

    def handed_over(rows):
        rows = jnp.where(live_rows[:, :, None, None], rows, jnp.zeros_like(rows))
        pair_rows = jnp.transpose(rows, (0, 2, 1, 3)).reshape(decode_peers, count_rows, HEAD_SIZE)
        sorted_rows = pair_rows[inverse_order].reshape(
            decode_peers, rows_per_peer, split_point, HEAD_SIZE
        )
        outgoing = jnp.transpose(sorted_rows, (0, 2, 1, 3)).reshape(
            decode_peers * split_point, rows_per_peer, HEAD_SIZE
        )
        return lax.all_to_all(outgoing, "seq", split_axis=0, concat_axis=1, tiled=True)[0]

    if planned:
        depth = key_weight.shape[0] // 2

        def half_block(first):
            halves = [
                lax.dynamic_slice_in_dim(weight, first, depth, 0)
                for weight in (key_weight, value_weight)
            ]
            return jnp.concatenate(halves, 1)

        sent = half_block(group_id * depth)
        tables = turn_tables(count_rows * seq + STEPS, count_rows)
        layer_1 = moved(sent, along(1))
        layer_2 = moved(sent, along(2))
        row_0 = moved(sent, to_row)
        mine, kept = prepared(place, flat, seq // 2)
        rest = half_block(depth - group_id * depth)
        came = (layer_1, layer_2, row_0, mine, rest)
        other = moved(after(kept, *came), to_core)
        layer_3 = moved(after(sent, *came), along(3))
        rest_1 = moved(after(rest, *came), along(1))
        row_1 = moved(after(layer_1, *came), to_row)
        group_0 = moved(after(row_0, *came), to_group)
        row_2 = moved(after(layer_2, *came), to_row)
        group_2 = moved(after(layer_2, *came), to_group)
        pieces = [(HERE, 0, sent), (HERE, 1, rest), (THERE, 0, row_0)]
        pieces += [(HERE + 1, 0, layer_1), (HERE + 2, 0, layer_2)]
        totals = product(place, after(mine, *came), other, pieces, (), 5)
        came = (layer_3, rest_1, row_1, group_0, row_2, group_2, totals[0])
        row_3 = moved(after(layer_3, *came), to_row)
        group_3 = moved(after(layer_3, *came), to_group)
        pair_1 = moved(after(group_0, *came), along(1))
        pieces = [(THERE, 1, group_0), (THERE + 1, 0, row_1), (HERE + 1, 1, rest_1)]
        pieces += [(THERE + 2, 0, row_2), (HERE + 2, 1, group_2), (HERE + 3, 0, layer_3)]
        totals = product(place, after(mine, *came), other, pieces, totals, 3)
        came = (row_3, group_3, pair_1, totals[0])
        end_2 = moved(after(row_2, *came), to_group)
        end_3 = moved(after(group_3, *came), to_row)
        pieces = [(THERE + 1, 1, pair_1), (THERE + 3, 0, row_3), (HERE + 3, 1, group_3)]
        totals = product(place, after(mine, *came), other, pieces, totals, 3)
        came = (end_2, end_3, *totals)
        pieces = [(THERE + 2, 1, end_2), (THERE + 3, 1, end_3)]
        total, given = product(place, after(mine, *came), other, pieces, totals, 2)
        outgoing = outgoing_rows(place, lengths, owner, total, moved(given, to_core), tables)
        incoming = lax.all_to_all(outgoing, "seq", split_axis=0, concat_axis=1, tiled=True)
        attended = decoded(
            place, lengths, owner, incoming[0], dec_query, dec_key, dec_value, tables
        )
        return (incoming, attended)
    else:
        cosine, sine_part = rope_table(positions, HEAD_SIZE)
        shape = (count_requests, count_rows, KEY_VALUE_HEADS, HEAD_SIZE)
        unrotated_key = project(key_weight).reshape(shape)
        key_rows = rotate(
            unrotated_key, cosine[:, None, :], sine_part[:, None, :]
        ).astype(jnp.bfloat16)
        cache_keys = handed_over(key_rows)
        cache_values = handed_over(project(value_weight).astype(jnp.bfloat16).reshape(shape))
    slot_count = cache_keys.shape[0]
    decode_peer = device_id // split_point
    block = device_id % split_point
    source_pair = jnp.sum(jnp.where(owner == decode_peer, pair_ids, 0))
    source_request = source_pair // KEY_VALUE_HEADS
    length = jnp.sum(
        jnp.where(jnp.arange(count_requests, dtype=jnp.int32) == source_request, lengths, 0)
    )
    query = lax.dynamic_index_in_dim(dec_query, decode_peer, 0, keepdims=False)
    new_key = lax.dynamic_index_in_dim(dec_key, decode_peer, 0, keepdims=False)
    new_value = lax.dynamic_index_in_dim(dec_value, decode_peer, 0, keepdims=False)
    step_pos = length + jnp.arange(STEPS, dtype=jnp.int32)
    step_cos, step_sin = rope_table(step_pos, HEAD_SIZE)
    query_rot = rotate(
        query.astype(jnp.float32).reshape(STEPS, QPK, HEAD_SIZE),
        step_cos[:, None, :],
        step_sin[:, None, :],
    ).astype(jnp.bfloat16)
    new_keys = rotate(new_key.astype(jnp.float32), step_cos, step_sin).astype(jnp.bfloat16)
    score_scale = 1.0 / HEAD_SIZE**0.5
    old_scores = (
        jnp.einsum(
            "sjd,id->sji", query_rot, cache_keys, preferred_element_type=jnp.float32
        )
        * score_scale
    )
    new_scores = (
        jnp.einsum("sjd,td->sjt", query_rot, new_keys, preferred_element_type=jnp.float32)
        * score_scale
    )
    slot_ids = jnp.arange(slot_count, dtype=jnp.int32) * split_point + block
    old_live = slot_ids < length
    new_live = (jnp.arange(STEPS)[None, :] <= jnp.arange(STEPS)[:, None]) & (block == 0)
    old_scores = jnp.where(old_live[None, None, :], old_scores, -1e30)
    new_scores = jnp.where(new_live[:, None, :], new_scores, -1e30)
    row_max = jnp.maximum(jnp.max(old_scores, -1), jnp.max(new_scores, -1))
    for bit in range(tree_levels):
        row_max = jnp.maximum(row_max, swapped(row_max, "seq", bit))
    old_exp = jnp.exp(old_scores - row_max[..., None])
    new_exp = jnp.exp(new_scores - row_max[..., None])
    denom = jnp.sum(old_exp, -1) + jnp.sum(new_exp, -1)
    for bit in range(tree_levels):
        denom = denom + swapped(denom, "seq", bit)
    old_probs = (old_exp / denom[..., None]).astype(jnp.bfloat16)
    new_probs = (new_exp / denom[..., None]).astype(jnp.bfloat16)
    partial_sum = jnp.einsum(
        "sji,id->sjd", old_probs, cache_values, preferred_element_type=jnp.float32
    )
    partial_sum = partial_sum + jnp.einsum(
        "sjt,td->sjd", new_probs, new_value, preferred_element_type=jnp.float32
    )
    flat_rows = partial_sum.reshape(STEPS, QPK * HEAD_SIZE)
    for bit in range(tree_levels):
        flat_rows = flat_rows + swapped(flat_rows, "seq", bit)
    share = flat_rows.shape[1] // split_point
    mine = lax.dynamic_slice_in_dim(flat_rows, block * share, share, 1)
    cache = jnp.concatenate([cache_keys, cache_values], 1)[None]
    return (cache, mine.astype(jnp.bfloat16))


def solution(mesh):
    placed = (
        P("groups", "seq", None),
        P("seq", None),
        P("seq", None),
        P("groups"),
        P("groups"),
        P("groups", None, None),
        P("groups", None, None),
        P("groups", None, None),
    )
    return jax.shard_map(
        body,
        mesh=mesh,
        in_specs=placed,
        out_specs=(P(("groups", "seq"), None, None), P("groups", "seq")),
        check_vma=False,
    )
```

```python
import functools

import jax
import jax.numpy as jnp
import numpy as np
from jax import lax
from jax.experimental import pallas as pl
from jax.experimental.pallas import tpu as pltpu
from jax.sharding import PartitionSpec as P

HEAD_SIZE = 128
KEY_VALUE_HEADS = 4
QPK = 8
STEPS = 4


ROPE_BASE = 500000.0


def swapped(block, axis, bit):
    count = lax.axis_size(axis)
    route = []
    for low in range(count):
        high = low | 1 << bit
        if high != low and high < count:
            route += [(low, high), (high, low)]
    return lax.ppermute(block, axis, route)


def rope_table(positions, head_dim):
    freq = ROPE_BASE ** (-(np.arange(head_dim // 2, dtype=np.float64) * 2.0) / head_dim)
    angle = positions.astype(jnp.float32)[:, None] * jnp.asarray(freq, jnp.float32)[None, :]
    return (jnp.cos(angle), jnp.sin(angle))


def rotate(values_in, cosine, sine_part):
    half_dim = values_in.shape[-1] // 2
    lower_half = values_in[..., :half_dim]
    upper_half = values_in[..., half_dim:]
    return jnp.concatenate(
        [
            lower_half * cosine - upper_half * sine_part,
            upper_half * cosine + lower_half * sine_part,
        ],
        -1,
    )


def spread(count):
    side = 1
    while side * side < count:
        side *= 2
    return (side, count // side)


def moved(block, rule):
    groups, seq = lax.axis_size("groups"), lax.axis_size("seq")
    low = spread(seq // 2)[1]
    route = []
    for g in range(groups):
        for s in range(seq):
            place = rule(g, s // 2 // low, s // 2 % low, s % 2)
            if place is not None:
                tg, tz, ty, tc = place
                route.append((g * seq + s, tg * seq + (tz * low + ty) * 2 + tc))
    return lax.ppermute(block, ("groups", "seq"), route)


def to_core(g, z, y, c):
    return (g, z, y, 1 - c)


def to_row(g, z, y, c):
    return (g, z, 1 - y, c)


def to_group(g, z, y, c):
    return (1 - g, z, y, c)


def to_pair(g, z, y, c):
    return (g, z ^ 1, y, c)


def to_middle(g, z, y, c):
    return (g, 3 - z if z in (1, 2) else z, y, c)


VMEM_REF = pl.BlockSpec(memory_space=pltpu.VMEM)
SMEM_REF = pl.BlockSpec(memory_space=pltpu.SMEM)
ANY_REF = pl.BlockSpec(memory_space=pl.ANY)
PARAMS = pltpu.CompilerParams(vmem_limit_bytes=20 << 20)
SMALL = pltpu.CompilerParams(vmem_limit_bytes=16 << 20)


def cost(flops, moved_bytes):
    return pl.CostEstimate(flops=flops, bytes_accessed=moved_bytes, transcendentals=0)


def fetch(source, target, sem):
    copy = pltpu.make_async_copy(source, target, sem)
    copy.start()
    return copy


def prepare_kernel(place, rows_in, mine, kept):
    depth = mine.shape[2]
    rows, width = rows_in.shape
    square = jnp.zeros((rows, depth), jnp.float32)
    for first in range(0, width, depth):
        part = rows_in[:, first : first + depth].astype(jnp.float32)
        square += part * part
    scale = lax.rsqrt(jnp.sum(square, -1, keepdims=True) / width + 1e-05)
    for core in range(2):

        @pl.when(place[1] == core)
        def _():
            for first in range(0, width, depth):
                j, c, h = first // (4 * depth), first // (2 * depth) % 2, first // depth % 2
                target = mine if c == core else kept
                part = rows_in[:, first : first + depth].astype(jnp.float32)
                target[2 * j + h] = (part * scale).astype(jnp.bfloat16)


def prepared(place, flat, blocks):
    rows, width = flat.shape
    depth = width // (4 * blocks)
    tile = 80 if rows % 80 == 0 else rows
    out = jax.ShapeDtypeStruct((2 * blocks, rows, depth), jnp.bfloat16)
    spec = pl.BlockSpec((2 * blocks, tile, depth), lambda i, place: (0, i, 0))
    return pl.pallas_call(
        prepare_kernel,
        grid_spec=pltpu.PrefetchScalarGridSpec(
            num_scalar_prefetch=1,
            grid=(rows // tile,),
            in_specs=[pl.BlockSpec((tile, width), lambda i, place: (i, 0))],
            out_specs=[spec, spec],
        ),
        out_shape=[out, out],
        compiler_params=PARAMS,
        cost_estimate=cost(1000, 1000),
        name="normed_halves",
    )(place, flat)


def after(value, *events):
    return lax.optimization_barrier((value, *events))[0]


def half_index(place, entry, kind):
    half = {0: place[0], 1: 1 - place[0], 2: 0, 3: 1}[kind]
    return place[entry] * 2 + half


def product_kernel(plan, group, with_total, place, mine, other, *refs):
    count = len(plan)
    outs = refs[-7:-5]
    left, right, total, sems, total_sems = refs[-5:]
    rows, depth = mine.shape[1], mine.shape[2]
    waits = []
    for k, (entry, kind) in enumerate(plan):
        area = pl.ds((k % group) * depth, depth)
        slot = k // group
        index = half_index(place, entry, kind)
        sources = (mine.at[index], other.at[index], refs[k])
        targets = (left.at[slot, 0, :, area], left.at[slot, 1, :, area], right.at[slot, area])
        waits.append(
            [fetch(a, b, sems.at[3 * k + i]) for i, (a, b) in enumerate(zip(sources, targets))]
        )
    carried = [
        fetch(ref, total.at[pl.ds(k * rows, rows)], total_sems.at[k])
        for k, ref in enumerate(refs[count : count + 2 * with_total])
    ]
    for slot in range(count // group):
        for copies in waits[slot * group : (slot + 1) * group]:
            for copy in copies:
                copy.wait()
        stacked = left[slot].reshape(2 * rows, group * depth)
        value = jnp.dot(stacked, right[slot], preferred_element_type=jnp.float32)
        if slot == 0:
            for copy in carried:
                copy.wait()
        if slot or with_total:
            value += total[...]
        if slot + 1 < count // group:
            total[...] = value
        else:
            outs[0][...] = value[:rows]
            outs[1][...] = value[rows:]


def product(place, mine, other, pieces, totals, group, moved_bytes=1000):
    _, rows, depth = mine.shape
    columns = pieces[0][2].shape[1]
    plan = [(entry, kind) for entry, kind, _ in pieces]
    count = len(plan)
    out = jax.ShapeDtypeStruct((rows, columns), jnp.float32)
    return pl.pallas_call(
        functools.partial(product_kernel, plan, group, bool(totals)),
        in_specs=[SMEM_REF] + [ANY_REF] * (2 + count + len(totals)),
        out_specs=[VMEM_REF] * 2,
        out_shape=[out] * 2,
        scratch_shapes=[
            pltpu.VMEM((count // group, 2, rows, group * depth), mine.dtype),
            pltpu.VMEM((count // group, group * depth, columns), mine.dtype),
            pltpu.VMEM((2 * rows, columns), jnp.float32),
            pltpu.SemaphoreType.DMA((3 * count,)),
            pltpu.SemaphoreType.DMA((2,)),
        ],
        compiler_params=PARAMS,
        cost_estimate=cost(1000, moved_bytes),
        name="add_product",
    )(place, mine, other, *[array for _, _, array in pieces], *totals)


LOW = 64


def turn_tables(positions, rows):
    freq = ROPE_BASE ** (-(np.arange(HEAD_SIZE // 2) * 2.0) / HEAD_SIZE)
    tables = []
    for places in (np.arange(0, positions, LOW), np.arange(LOW), np.arange(rows)):
        angle = places[:, None] * freq[None, :]
        tables.append(np.concatenate([np.cos(angle), np.cos(angle)], 1))
        tables.append(np.concatenate([-np.sin(angle), np.sin(angle)], 1))
    return [jnp.asarray(table, jnp.float32) for table in tables]


def turned_by(start, tables, cosine, sine):
    high, low = pl.ds(start // LOW, 1), pl.ds(start % LOW, 1)
    for cos_row, sin_row in (
        (tables[0][high], tables[1][high]),
        (tables[2][low], tables[3][low]),
    ):
        cosine, sine = cosine * cos_row - sine * sin_row, sine * cos_row + cosine * sin_row
    return cosine, sine


def rotated(rows, cosine, sine):
    half = HEAD_SIZE // 2
    return rows * cosine + jnp.concatenate([rows[:, half:], rows[:, :half]], 1) * sine


def rows_kernel(place, lengths, owner, *refs):
    total, came, *tables, out, scratch = refs
    columns = total.shape[1] // 2
    count_requests, count_rows = lengths.shape[0], scratch.shape[0]
    cosine, sine = turned_by(place[2] * count_rows, tables, tables[4][...], tables[5][...])
    index = place[2] * count_rows + lax.broadcasted_iota(jnp.int32, scratch.shape, 0)
    for r in range(count_requests):
        live = index < lengths[r]
        for h in range(KEY_VALUE_HEADS):
            for part in range(2):
                first = part * columns + h * HEAD_SIZE
                area = (
                    slice(r * count_rows, (r + 1) * count_rows),
                    slice(first, first + HEAD_SIZE),
                )
                rows = total[area] + came[area]
                if part == 0:
                    rows = rotated(rows, cosine, sine)
                scratch[...] = jnp.where(live, rows, 0.0)
                peer = owner[r * KEY_VALUE_HEADS + h]
                lanes = slice(part * HEAD_SIZE, (part + 1) * HEAD_SIZE)
                for b in range(2):
                    picked = scratch[pl.ds(b, count_rows // 2, stride=2), :]
                    out[peer * 2 + b, :, lanes] = picked.astype(jnp.bfloat16)


def outgoing_rows(place, lengths, owner, total, came, tables):
    count_rows = total.shape[0] // lengths.shape[0]
    out = (owner.shape[0] * 2, count_rows // 2, 2 * HEAD_SIZE)
    return pl.pallas_call(
        rows_kernel,
        in_specs=[SMEM_REF] * 3 + [VMEM_REF] * 8,
        out_specs=VMEM_REF,
        out_shape=jax.ShapeDtypeStruct(out, jnp.bfloat16),
        scratch_shapes=[pltpu.VMEM((count_rows, HEAD_SIZE), jnp.float32)],
        compiler_params=SMALL,
        cost_estimate=cost(1000, 1000),
        name="cache_rows",
    )(place, lengths, owner, total, came, *tables)


def decode_kernel(place, lengths, owner, cache, dec_query, dec_key, dec_value, *refs):
    tables, out = refs[:4], refs[4]
    peer, block = place[2] // 2, place[2] % 2
    length = lengths[0]
    for pair in range(owner.shape[0]):
        length = jnp.where(owner[pair] == peer, lengths[pair // KEY_VALUE_HEADS], length)
    cosine, sine = turned_by(length, tables, tables[2][:STEPS], tables[3][:STEPS])

    def turned(rows):
        return rotated(rows.astype(jnp.float32), cosine, sine)

    def padded(rows):
        return jnp.concatenate([rows, jnp.zeros((16 - STEPS, HEAD_SIZE), jnp.float32)], 0)

    raw = dec_query[peer]
    heads = [raw[:, j * HEAD_SIZE : (j + 1) * HEAD_SIZE] for j in range(QPK)]
    query = jnp.concatenate([turned(head) for head in heads], 0).astype(jnp.bfloat16)
    new_keys = padded(turned(dec_key[peer])).astype(jnp.bfloat16)
    new_value = padded(dec_value[peer].astype(jnp.float32)).astype(jnp.bfloat16)
    contract = (((1,), (1,)), ((), ()))
    scale = 1.0 / HEAD_SIZE**0.5
    old = lax.dot_general(
        query, cache[:, :HEAD_SIZE], contract, preferred_element_type=jnp.float32
    )
    slot = lax.broadcasted_iota(jnp.int32, old.shape, 1) * 2 + block
    old = jnp.where(slot < length, old * scale, -1e30)
    new = lax.dot_general(query, new_keys, contract, preferred_element_type=jnp.float32)
    step = lax.broadcasted_iota(jnp.int32, new.shape, 0) % STEPS
    token = lax.broadcasted_iota(jnp.int32, new.shape, 1)
    new = jnp.where((token <= step) & (block == 0), new * scale, -1e30)
    top = jnp.maximum(jnp.max(old, 1, keepdims=True), jnp.max(new, 1, keepdims=True))
    old, new = jnp.exp(old - top), jnp.exp(new - top)
    total = jnp.sum(old, 1, keepdims=True) + jnp.sum(new, 1, keepdims=True)
    sums = jnp.dot(
        old.astype(jnp.bfloat16), cache[:, HEAD_SIZE:], preferred_element_type=jnp.float32
    )
    out[:, :HEAD_SIZE] = sums + jnp.dot(
        new.astype(jnp.bfloat16), new_value, preferred_element_type=jnp.float32
    )
    half = (QPK * STEPS, HEAD_SIZE // 2)
    out[:, HEAD_SIZE : HEAD_SIZE + half[1]] = jnp.broadcast_to(top, half)
    out[:, HEAD_SIZE + half[1] :] = jnp.broadcast_to(total, half)


def joined_kernel(place, mine, theirs, out):
    share = QPK // 2
    area = pl.ds(place[2] % 2 * share * STEPS, share * STEPS)
    last = HEAD_SIZE + HEAD_SIZE // 2
    sums, tops, totals = [], [], []
    for ref in (mine, theirs):
        sums.append(ref[area, :HEAD_SIZE])
        tops.append(ref[area, HEAD_SIZE : HEAD_SIZE + 1])
        totals.append(ref[area, last : last + 1])
    top = jnp.maximum(tops[0], tops[1])
    scales = [jnp.exp(one - top) for one in tops]
    total = totals[0] * scales[0] + totals[1] * scales[1]
    value = (sums[0] * scales[0] + sums[1] * scales[1]) / total
    for j in range(share):
        rows = value[j * STEPS : (j + 1) * STEPS]
        out[:, j * HEAD_SIZE : (j + 1) * HEAD_SIZE] = rows.astype(jnp.bfloat16)


def decoded(place, lengths, owner, cache, dec_query, dec_key, dec_value, tables):
    mine = pl.pallas_call(
        decode_kernel,
        in_specs=[SMEM_REF] * 3 + [VMEM_REF] * 8,
        out_specs=VMEM_REF,
        out_shape=jax.ShapeDtypeStruct((STEPS * QPK, 2 * HEAD_SIZE), jnp.float32),
        compiler_params=SMALL,
        cost_estimate=cost(1000, 1000),
        name="decode",
    )(place, lengths, owner, cache, dec_query, dec_key, dec_value, *tables[:4])
    return pl.pallas_call(
        joined_kernel,
        in_specs=[SMEM_REF] + [VMEM_REF] * 2,
        out_specs=VMEM_REF,
        out_shape=jax.ShapeDtypeStruct((STEPS, QPK // 2 * HEAD_SIZE), jnp.bfloat16),
        compiler_params=SMALL,
        cost_estimate=cost(1000, 1000),
        name="joined",
    )(place, mine, moved(mine, to_core))


HERE, THERE = 3, 7


def body(hidden, key_weight, value_weight, lengths, owner, dec_query, dec_key, dec_value):
    count_requests, count_rows, width = hidden.shape
    device_id = lax.axis_index("seq")
    group_id = lax.axis_index("groups")
    seq = lax.axis_size("seq")
    planned = seq == 16 and lax.axis_size("groups") == 2
    decode_peers = count_requests * KEY_VALUE_HEADS
    split_point = seq // decode_peers
    tree_levels = split_point.bit_length() - 1
    rows_per_peer = count_rows // split_point
    positions = device_id * count_rows + jnp.arange(count_rows, dtype=jnp.int32)
    total_rows = count_requests * count_rows
    flat = hidden.reshape(total_rows, width)
    if planned:
        core = device_id % 2
        z, y = device_id // 4, device_id // 2 % 2
        layers = [z, z ^ 1, jnp.where(z < 2, 2, 1), jnp.where(z < 2, 3, 0)]
        is_end = (z == 0) | (z == 3)
        place = [group_id, core, device_id]
        place += [layer * 2 + y for layer in layers]
        place += [layer * 2 + 1 - y for layer in layers]
        place = jnp.stack([jnp.asarray(entry, jnp.int32) for entry in place])
    else:
        widened = flat.astype(jnp.float32)
        normed = (
            widened * lax.rsqrt(jnp.mean(widened * widened, -1, keepdims=True) + 1e-05)
        ).astype(jnp.bfloat16)

        def project(weight):
            whole = lax.all_gather(weight, "seq", axis=0, tiled=True)
            return jnp.dot(normed, whole, preferred_element_type=jnp.float32)

    pair_ids = jnp.arange(decode_peers, dtype=jnp.int32)
    matches = owner[None, :] == pair_ids[:, None]
    inverse_order = jnp.sum(jnp.where(matches, pair_ids[None, :], 0), axis=1)
    live_rows = positions[None, :] < lengths[:, None]

    def handed_over(rows):
        rows = jnp.where(live_rows[:, :, None, None], rows, jnp.zeros_like(rows))
        pair_rows = jnp.transpose(rows, (0, 2, 1, 3)).reshape(decode_peers, count_rows, HEAD_SIZE)
        sorted_rows = pair_rows[inverse_order].reshape(
            decode_peers, rows_per_peer, split_point, HEAD_SIZE
        )
        outgoing = jnp.transpose(sorted_rows, (0, 2, 1, 3)).reshape(
            decode_peers * split_point, rows_per_peer, HEAD_SIZE
        )
        return lax.all_to_all(outgoing, "seq", split_axis=0, concat_axis=1, tiled=True)[0]

    if planned:
        depth = key_weight.shape[0] // 2

        def half_block(first):
            halves = [
                lax.dynamic_slice_in_dim(weight, first, depth, 0)
                for weight in (key_weight, value_weight)
            ]
            return jnp.concatenate(halves, 1)

        sent = half_block(group_id * depth)
        tables = turn_tables(count_rows * seq + STEPS, count_rows)
        near = moved(sent, to_pair)
        middle = moved(sent, to_middle)
        across = moved(sent, to_row)
        rest = half_block(depth - group_id * depth)
        mine, kept = prepared(place, flat, seq // 2)
        layers, rows = (near, middle), (across, mine, rest)
        end_b = moved(after(middle, *layers), to_pair)
        middle_c = moved(after(near, *layers), to_middle)
        near_y = moved(after(near, *layers, *rows), to_row)
        across_x = moved(after(across, *layers, *rows), to_group)
        other = moved(after(kept, *layers, *rows), to_core)
        layers, rows, before = (end_b, middle_c), (near_y, across_x, other), rows
        end_c = moved(after(middle_c, *layers, *before), to_pair)
        block_b = jnp.where(is_end, after(end_b, *layers), middle)
        block_yb = moved(after(block_b, *rows), to_row)
        block_xb = moved(after(block_b, *rows), to_group)
        pieces = [(HERE, 0, sent), (HERE, 1, rest), (THERE, 0, across)]
        pieces += [(THERE, 1, across_x), (HERE + 1, 0, near), (THERE + 1, 0, near_y)]
        totals = product(place, after(mine, *rows, block_b), other, pieces, (), 3)
        layers, rows, before = (end_c,), (block_yb, block_xb, totals[0]), rows
        near_rest = moved(after(rest, *layers, *before), to_pair)
        block_c = jnp.where(is_end, after(end_c, *layers), middle_c)
        block_xc = moved(after(block_c, *rows), to_group)
        block_yc = moved(after(block_c, *rows), to_row)
        pieces = [(HERE + 2, 0, block_b), (HERE + 2, 1, block_xb)]
        pieces += [(THERE + 2, 0, block_yb), (HERE + 3, 0, block_c)]
        totals = product(place, after(mine, *rows, block_c), other, pieces, totals, 4)
        layers, rows, before = (near_rest,), (block_xc, block_yc, totals[0]), rows
        end_a = moved(after(across_x, *layers, *before), to_pair)
        ends = [moved(after(block_yb, *rows), to_group), moved(after(block_xc, *rows), to_row)]
        pieces = [(HERE + 1, 1, near_rest), (HERE + 3, 1, block_xc)]
        pieces += [(THERE + 3, 0, block_yc), (THERE + 1, 1, end_a)]
        totals = product(place, after(mine, *rows, end_a), other, pieces, totals, 4, 1 << 24)
        pieces = [(THERE + 2, 1, ends[0]), (THERE + 3, 1, ends[1])]
        total, given = product(place, after(mine, *ends, *totals), other, pieces, totals, 2)
        outgoing = outgoing_rows(place, lengths, owner, total, moved(given, to_core), tables)
        incoming = lax.all_to_all(outgoing, "seq", split_axis=0, concat_axis=1, tiled=True)
        attended = decoded(
            place, lengths, owner, incoming[0], dec_query, dec_key, dec_value, tables
        )
        return (incoming, attended)
    else:
        cosine, sine_part = rope_table(positions, HEAD_SIZE)
        shape = (count_requests, count_rows, KEY_VALUE_HEADS, HEAD_SIZE)
        unrotated_key = project(key_weight).reshape(shape)
        key_rows = rotate(
            unrotated_key, cosine[:, None, :], sine_part[:, None, :]
        ).astype(jnp.bfloat16)
        cache_keys = handed_over(key_rows)
        cache_values = handed_over(project(value_weight).astype(jnp.bfloat16).reshape(shape))
    slot_count = cache_keys.shape[0]
    decode_peer = device_id // split_point
    block = device_id % split_point
    source_pair = jnp.sum(jnp.where(owner == decode_peer, pair_ids, 0))
    source_request = source_pair // KEY_VALUE_HEADS
    length = jnp.sum(
        jnp.where(jnp.arange(count_requests, dtype=jnp.int32) == source_request, lengths, 0)
    )
    query = lax.dynamic_index_in_dim(dec_query, decode_peer, 0, keepdims=False)
    new_key = lax.dynamic_index_in_dim(dec_key, decode_peer, 0, keepdims=False)
    new_value = lax.dynamic_index_in_dim(dec_value, decode_peer, 0, keepdims=False)
    step_pos = length + jnp.arange(STEPS, dtype=jnp.int32)
    step_cos, step_sin = rope_table(step_pos, HEAD_SIZE)
    query_rot = rotate(
        query.astype(jnp.float32).reshape(STEPS, QPK, HEAD_SIZE),
        step_cos[:, None, :],
        step_sin[:, None, :],
    ).astype(jnp.bfloat16)
    new_keys = rotate(new_key.astype(jnp.float32), step_cos, step_sin).astype(jnp.bfloat16)
    score_scale = 1.0 / HEAD_SIZE**0.5
    old_scores = (
        jnp.einsum(
            "sjd,id->sji", query_rot, cache_keys, preferred_element_type=jnp.float32
        )
        * score_scale
    )
    new_scores = (
        jnp.einsum("sjd,td->sjt", query_rot, new_keys, preferred_element_type=jnp.float32)
        * score_scale
    )
    slot_ids = jnp.arange(slot_count, dtype=jnp.int32) * split_point + block
    old_live = slot_ids < length
    new_live = (jnp.arange(STEPS)[None, :] <= jnp.arange(STEPS)[:, None]) & (block == 0)
    old_scores = jnp.where(old_live[None, None, :], old_scores, -1e30)
    new_scores = jnp.where(new_live[:, None, :], new_scores, -1e30)
    row_max = jnp.maximum(jnp.max(old_scores, -1), jnp.max(new_scores, -1))
    for bit in range(tree_levels):
        row_max = jnp.maximum(row_max, swapped(row_max, "seq", bit))
    old_exp = jnp.exp(old_scores - row_max[..., None])
    new_exp = jnp.exp(new_scores - row_max[..., None])
    denom = jnp.sum(old_exp, -1) + jnp.sum(new_exp, -1)
    for bit in range(tree_levels):
        denom = denom + swapped(denom, "seq", bit)
    old_probs = (old_exp / denom[..., None]).astype(jnp.bfloat16)
    new_probs = (new_exp / denom[..., None]).astype(jnp.bfloat16)
    partial_sum = jnp.einsum(
        "sji,id->sjd", old_probs, cache_values, preferred_element_type=jnp.float32
    )
    partial_sum = partial_sum + jnp.einsum(
        "sjt,td->sjd", new_probs, new_value, preferred_element_type=jnp.float32
    )
    flat_rows = partial_sum.reshape(STEPS, QPK * HEAD_SIZE)
    for bit in range(tree_levels):
        flat_rows = flat_rows + swapped(flat_rows, "seq", bit)
    share = flat_rows.shape[1] // split_point
    mine = lax.dynamic_slice_in_dim(flat_rows, block * share, share, 1)
    cache = jnp.concatenate([cache_keys, cache_values], 1)[None]
    return (cache, mine.astype(jnp.bfloat16))


def solution(mesh):
    placed = (
        P("groups", "seq", None),
        P("seq", None),
        P("seq", None),
        P("groups"),
        P("groups"),
        P("groups", None, None),
        P("groups", None, None),
        P("groups", None, None),
    )
    return jax.shard_map(
        body,
        mesh=mesh,
        in_specs=placed,
        out_specs=(P(("groups", "seq"), None, None), P("groups", "seq")),
        check_vma=False,
    )
```

```python
import functools

import jax
import jax.numpy as jnp
import numpy as np
from jax import lax
from jax.experimental import pallas as pl
from jax.experimental.pallas import tpu as pltpu
from jax.sharding import PartitionSpec as P

HEAD_SIZE = 128
KEY_VALUE_HEADS = 4
QPK = 8
STEPS = 4


ROPE_BASE = 500000.0


def swapped(block, axis, bit):
    count = lax.axis_size(axis)
    route = []
    for low in range(count):
        high = low | 1 << bit
        if high != low and high < count:
            route += [(low, high), (high, low)]
    return lax.ppermute(block, axis, route)


def rope_table(positions, head_dim):
    freq = ROPE_BASE ** (-(np.arange(head_dim // 2, dtype=np.float64) * 2.0) / head_dim)
    angle = positions.astype(jnp.float32)[:, None] * jnp.asarray(freq, jnp.float32)[None, :]
    return (jnp.cos(angle), jnp.sin(angle))


def rotate(values_in, cosine, sine_part):
    half_dim = values_in.shape[-1] // 2
    lower_half = values_in[..., :half_dim]
    upper_half = values_in[..., half_dim:]
    return jnp.concatenate(
        [
            lower_half * cosine - upper_half * sine_part,
            upper_half * cosine + lower_half * sine_part,
        ],
        -1,
    )


def spread(count):
    side = 1
    while side * side < count:
        side *= 2
    return (side, count // side)


def moved(block, rule):
    groups, seq = lax.axis_size("groups"), lax.axis_size("seq")
    low = spread(seq // 2)[1]
    route = []
    for g in range(groups):
        for s in range(seq):
            place = rule(g, s // 2 // low, s // 2 % low, s % 2)
            if place is not None:
                tg, tz, ty, tc = place
                route.append((g * seq + s, tg * seq + (tz * low + ty) * 2 + tc))
    return lax.ppermute(block, ("groups", "seq"), route)


def to_core(g, z, y, c):
    return (g, z, y, 1 - c)


def to_row(g, z, y, c):
    return (g, z, 1 - y, c)


def to_group(g, z, y, c):
    return (1 - g, z, y, c)


def to_pair(g, z, y, c):
    return (g, z ^ 1, y, c)


def to_middle(g, z, y, c):
    return (g, 3 - z, y, c) if z in (1, 2) else None


def to_end(g, z, y, c):
    return (g, 0 if z == 1 else 3, y, c) if z in (1, 2) else None


VMEM_REF = pl.BlockSpec(memory_space=pltpu.VMEM)
SMEM_REF = pl.BlockSpec(memory_space=pltpu.SMEM)
ANY_REF = pl.BlockSpec(memory_space=pl.ANY)
PARAMS = pltpu.CompilerParams(vmem_limit_bytes=20 << 20)
SMALL = pltpu.CompilerParams(vmem_limit_bytes=16 << 20)


def cost(flops, moved_bytes):
    return pl.CostEstimate(flops=flops, bytes_accessed=moved_bytes, transcendentals=0)


def fetch(source, target, sem):
    copy = pltpu.make_async_copy(source, target, sem)
    copy.start()
    return copy


def prepare_kernel(place, rows_in, mine, kept):
    depth = mine.shape[2]
    rows, width = rows_in.shape
    square = jnp.zeros((rows, depth), jnp.float32)
    for first in range(0, width, depth):
        part = rows_in[:, first : first + depth].astype(jnp.float32)
        square += part * part
    scale = lax.rsqrt(jnp.sum(square, -1, keepdims=True) / width + 1e-05)
    for core in range(2):

        @pl.when(place[1] == core)
        def _():
            for first in range(0, width, depth):
                j, c, h = first // (4 * depth), first // (2 * depth) % 2, first // depth % 2
                target = mine if c == core else kept
                part = rows_in[:, first : first + depth].astype(jnp.float32)
                target[2 * j + h] = (part * scale).astype(jnp.bfloat16)


def prepared(place, flat, blocks):
    rows, width = flat.shape
    depth = width // (4 * blocks)
    tile = 80 if rows % 80 == 0 else rows
    out = jax.ShapeDtypeStruct((2 * blocks, rows, depth), jnp.bfloat16)
    spec = pl.BlockSpec((2 * blocks, tile, depth), lambda i, place: (0, i, 0))
    return pl.pallas_call(
        prepare_kernel,
        grid_spec=pltpu.PrefetchScalarGridSpec(
            num_scalar_prefetch=1,
            grid=(rows // tile,),
            in_specs=[pl.BlockSpec((tile, width), lambda i, place: (i, 0))],
            out_specs=[spec, spec],
        ),
        out_shape=[out, out],
        compiler_params=PARAMS,
        cost_estimate=cost(1000, 1000),
        name="normed_halves",
    )(place, flat)


def after(value, *events):
    return lax.optimization_barrier((value, *events))[0]


def half_index(place, entry, kind):
    half = {0: place[0], 1: 1 - place[0], 2: 0, 3: 1}[kind]
    return place[entry] * 2 + half


def product_kernel(plan, group, with_total, place, mine, other, *refs):
    count = len(plan)
    outs = refs[-7:-5]
    left, right, total, sems, total_sems = refs[-5:]
    rows, depth = mine.shape[1], mine.shape[2]
    waits = []
    for k, (entry, kind) in enumerate(plan):
        area = pl.ds((k % group) * depth, depth)
        slot = k // group
        index = half_index(place, entry, kind)
        sources = (mine.at[index], other.at[index], refs[k])
        targets = (left.at[slot, 0, :, area], left.at[slot, 1, :, area], right.at[slot, area])
        waits.append(
            [fetch(a, b, sems.at[3 * k + i]) for i, (a, b) in enumerate(zip(sources, targets))]
        )
    carried = [
        fetch(ref, total.at[pl.ds(k * rows, rows)], total_sems.at[k])
        for k, ref in enumerate(refs[count : count + 2 * with_total])
    ]
    for slot in range(count // group):
        for copies in waits[slot * group : (slot + 1) * group]:
            for copy in copies:
                copy.wait()
        stacked = left[slot].reshape(2 * rows, group * depth)
        value = jnp.dot(stacked, right[slot], preferred_element_type=jnp.float32)
        if slot == 0:
            for copy in carried:
                copy.wait()
        if slot or with_total:
            value += total[...]
        if slot + 1 < count // group:
            total[...] = value
        else:
            outs[0][...] = value[:rows]
            outs[1][...] = value[rows:]


def product(place, mine, other, pieces, totals, group, moved_bytes=1000):
    _, rows, depth = mine.shape
    columns = pieces[0][2].shape[1]
    plan = [(entry, kind) for entry, kind, _ in pieces]
    count = len(plan)
    out = jax.ShapeDtypeStruct((rows, columns), jnp.float32)
    return pl.pallas_call(
        functools.partial(product_kernel, plan, group, bool(totals)),
        in_specs=[SMEM_REF] + [ANY_REF] * (2 + count + len(totals)),
        out_specs=[VMEM_REF] * 2,
        out_shape=[out] * 2,
        scratch_shapes=[
            pltpu.VMEM((count // group, 2, rows, group * depth), mine.dtype),
            pltpu.VMEM((count // group, group * depth, columns), mine.dtype),
            pltpu.VMEM((2 * rows, columns), jnp.float32),
            pltpu.SemaphoreType.DMA((3 * count,)),
            pltpu.SemaphoreType.DMA((2,)),
        ],
        compiler_params=PARAMS,
        cost_estimate=cost(1000, moved_bytes),
        name="add_product",
    )(place, mine, other, *[array for _, _, array in pieces], *totals)


LOW = 64


def turn_tables(positions, rows):
    freq = ROPE_BASE ** (-(np.arange(HEAD_SIZE // 2) * 2.0) / HEAD_SIZE)
    tables = []
    for places in (np.arange(0, positions, LOW), np.arange(LOW), np.arange(rows)):
        angle = places[:, None] * freq[None, :]
        tables.append(np.concatenate([np.cos(angle), np.cos(angle)], 1))
        tables.append(np.concatenate([-np.sin(angle), np.sin(angle)], 1))
    return [jnp.asarray(table, jnp.float32) for table in tables]


def turned_by(start, tables, cosine, sine):
    high, low = pl.ds(start // LOW, 1), pl.ds(start % LOW, 1)
    for cos_row, sin_row in (
        (tables[0][high], tables[1][high]),
        (tables[2][low], tables[3][low]),
    ):
        cosine, sine = cosine * cos_row - sine * sin_row, sine * cos_row + cosine * sin_row
    return cosine, sine


def rotated(rows, cosine, sine):
    half = HEAD_SIZE // 2
    return rows * cosine + jnp.concatenate([rows[:, half:], rows[:, :half]], 1) * sine


def rows_kernel(place, lengths, owner, *refs):
    total, came, *tables, out, scratch = refs
    columns = total.shape[1] // 2
    count_requests, count_rows = lengths.shape[0], scratch.shape[0]
    cosine, sine = turned_by(place[2] * count_rows, tables, tables[4][...], tables[5][...])
    index = place[2] * count_rows + lax.broadcasted_iota(jnp.int32, scratch.shape, 0)
    for r in range(count_requests):
        live = index < lengths[r]
        for h in range(KEY_VALUE_HEADS):
            for part in range(2):
                first = part * columns + h * HEAD_SIZE
                area = (
                    slice(r * count_rows, (r + 1) * count_rows),
                    slice(first, first + HEAD_SIZE),
                )
                rows = total[area] + came[area]
                if part == 0:
                    rows = rotated(rows, cosine, sine)
                scratch[...] = jnp.where(live, rows, 0.0)
                peer = owner[r * KEY_VALUE_HEADS + h]
                lanes = slice(part * HEAD_SIZE, (part + 1) * HEAD_SIZE)
                for b in range(2):
                    picked = scratch[pl.ds(b, count_rows // 2, stride=2), :]
                    out[peer * 2 + b, :, lanes] = picked.astype(jnp.bfloat16)


def outgoing_rows(place, lengths, owner, total, came, tables):
    count_rows = total.shape[0] // lengths.shape[0]
    out = (owner.shape[0] * 2, count_rows // 2, 2 * HEAD_SIZE)
    return pl.pallas_call(
        rows_kernel,
        in_specs=[SMEM_REF] * 3 + [VMEM_REF] * 8,
        out_specs=VMEM_REF,
        out_shape=jax.ShapeDtypeStruct(out, jnp.bfloat16),
        scratch_shapes=[pltpu.VMEM((count_rows, HEAD_SIZE), jnp.float32)],
        compiler_params=SMALL,
        cost_estimate=cost(1000, 1000),
        name="cache_rows",
    )(place, lengths, owner, total, came, *tables)


def decode_kernel(place, lengths, owner, cache, dec_query, dec_key, dec_value, *refs):
    tables, out = refs[:4], refs[4]
    peer, block = place[2] // 2, place[2] % 2
    length = lengths[0]
    for pair in range(owner.shape[0]):
        length = jnp.where(owner[pair] == peer, lengths[pair // KEY_VALUE_HEADS], length)
    cosine, sine = turned_by(length, tables, tables[2][:STEPS], tables[3][:STEPS])

    def turned(rows):
        return rotated(rows.astype(jnp.float32), cosine, sine)

    def padded(rows):
        return jnp.concatenate([rows, jnp.zeros((16 - STEPS, HEAD_SIZE), jnp.float32)], 0)

    raw = dec_query[peer]
    heads = [raw[:, j * HEAD_SIZE : (j + 1) * HEAD_SIZE] for j in range(QPK)]
    query = jnp.concatenate([turned(head) for head in heads], 0).astype(jnp.bfloat16)
    new_keys = padded(turned(dec_key[peer])).astype(jnp.bfloat16)
    new_value = padded(dec_value[peer].astype(jnp.float32)).astype(jnp.bfloat16)
    contract = (((1,), (1,)), ((), ()))
    scale = 1.0 / HEAD_SIZE**0.5
    old = lax.dot_general(
        query, cache[:, :HEAD_SIZE], contract, preferred_element_type=jnp.float32
    )
    slot = lax.broadcasted_iota(jnp.int32, old.shape, 1) * 2 + block
    old = jnp.where(slot < length, old * scale, -1e30)
    new = lax.dot_general(query, new_keys, contract, preferred_element_type=jnp.float32)
    step = lax.broadcasted_iota(jnp.int32, new.shape, 0) % STEPS
    token = lax.broadcasted_iota(jnp.int32, new.shape, 1)
    new = jnp.where((token <= step) & (block == 0), new * scale, -1e30)
    top = jnp.maximum(jnp.max(old, 1, keepdims=True), jnp.max(new, 1, keepdims=True))
    old, new = jnp.exp(old - top), jnp.exp(new - top)
    total = jnp.sum(old, 1, keepdims=True) + jnp.sum(new, 1, keepdims=True)
    sums = jnp.dot(
        old.astype(jnp.bfloat16), cache[:, HEAD_SIZE:], preferred_element_type=jnp.float32
    )
    out[:, :HEAD_SIZE] = sums + jnp.dot(
        new.astype(jnp.bfloat16), new_value, preferred_element_type=jnp.float32
    )
    half = (QPK * STEPS, HEAD_SIZE // 2)
    out[:, HEAD_SIZE : HEAD_SIZE + half[1]] = jnp.broadcast_to(top, half)
    out[:, HEAD_SIZE + half[1] :] = jnp.broadcast_to(total, half)


def joined_kernel(place, mine, theirs, out):
    share = QPK // 2
    area = pl.ds(place[2] % 2 * share * STEPS, share * STEPS)
    last = HEAD_SIZE + HEAD_SIZE // 2
    sums, tops, totals = [], [], []
    for ref in (mine, theirs):
        sums.append(ref[area, :HEAD_SIZE])
        tops.append(ref[area, HEAD_SIZE : HEAD_SIZE + 1])
        totals.append(ref[area, last : last + 1])
    top = jnp.maximum(tops[0], tops[1])
    scales = [jnp.exp(one - top) for one in tops]
    total = totals[0] * scales[0] + totals[1] * scales[1]
    value = (sums[0] * scales[0] + sums[1] * scales[1]) / total
    for j in range(share):
        rows = value[j * STEPS : (j + 1) * STEPS]
        out[:, j * HEAD_SIZE : (j + 1) * HEAD_SIZE] = rows.astype(jnp.bfloat16)


def copied(cache):
    def kernel(source, out, sem):
        fetch(source, out, sem.at[0]).wait()

    return pl.pallas_call(
        kernel,
        in_specs=[VMEM_REF],
        out_specs=ANY_REF,
        out_shape=jax.ShapeDtypeStruct(cache.shape, cache.dtype),
        scratch_shapes=[pltpu.SemaphoreType.DMA((1,))],
        compiler_params=SMALL,
        cost_estimate=cost(1000, 1000),
        name="copied",
    )(cache)


def decoded(place, lengths, owner, cache, dec_query, dec_key, dec_value, tables):
    mine = pl.pallas_call(
        decode_kernel,
        in_specs=[SMEM_REF] * 3 + [VMEM_REF] * 8,
        out_specs=VMEM_REF,
        out_shape=jax.ShapeDtypeStruct((STEPS * QPK, 2 * HEAD_SIZE), jnp.float32),
        compiler_params=SMALL,
        cost_estimate=cost(1000, 1000),
        name="decode",
    )(place, lengths, owner, cache, dec_query, dec_key, dec_value, *tables[:4])
    return pl.pallas_call(
        joined_kernel,
        in_specs=[SMEM_REF] + [VMEM_REF] * 2,
        out_specs=VMEM_REF,
        out_shape=jax.ShapeDtypeStruct((STEPS, QPK // 2 * HEAD_SIZE), jnp.bfloat16),
        compiler_params=SMALL,
        cost_estimate=cost(1000, 1000),
        name="joined",
    )(place, mine, moved(mine, to_core))


HERE, THERE = 3, 7


def body(hidden, key_weight, value_weight, lengths, owner, dec_query, dec_key, dec_value):
    count_requests, count_rows, width = hidden.shape
    device_id = lax.axis_index("seq")
    group_id = lax.axis_index("groups")
    seq = lax.axis_size("seq")
    planned = seq == 16 and lax.axis_size("groups") == 2
    decode_peers = count_requests * KEY_VALUE_HEADS
    split_point = seq // decode_peers
    tree_levels = split_point.bit_length() - 1
    rows_per_peer = count_rows // split_point
    positions = device_id * count_rows + jnp.arange(count_rows, dtype=jnp.int32)
    total_rows = count_requests * count_rows
    flat = hidden.reshape(total_rows, width)
    if planned:
        core = device_id % 2
        z, y = device_id // 4, device_id // 2 % 2
        layers = [z, z ^ 1, jnp.where(z < 2, 2, 1), jnp.where(z < 2, 3, 0)]
        is_end = (z == 0) | (z == 3)
        place = [group_id, core, device_id]
        place += [layer * 2 + y for layer in layers]
        place += [layer * 2 + 1 - y for layer in layers]
        place = jnp.stack([jnp.asarray(entry, jnp.int32) for entry in place])
    else:
        widened = flat.astype(jnp.float32)
        normed = (
            widened * lax.rsqrt(jnp.mean(widened * widened, -1, keepdims=True) + 1e-05)
        ).astype(jnp.bfloat16)

        def project(weight):
            whole = lax.all_gather(weight, "seq", axis=0, tiled=True)
            return jnp.dot(normed, whole, preferred_element_type=jnp.float32)

    pair_ids = jnp.arange(decode_peers, dtype=jnp.int32)
    matches = owner[None, :] == pair_ids[:, None]
    inverse_order = jnp.sum(jnp.where(matches, pair_ids[None, :], 0), axis=1)
    live_rows = positions[None, :] < lengths[:, None]

    def handed_over(rows):
        rows = jnp.where(live_rows[:, :, None, None], rows, jnp.zeros_like(rows))
        pair_rows = jnp.transpose(rows, (0, 2, 1, 3)).reshape(decode_peers, count_rows, HEAD_SIZE)
        sorted_rows = pair_rows[inverse_order].reshape(
            decode_peers, rows_per_peer, split_point, HEAD_SIZE
        )
        outgoing = jnp.transpose(sorted_rows, (0, 2, 1, 3)).reshape(
            decode_peers * split_point, rows_per_peer, HEAD_SIZE
        )
        return lax.all_to_all(outgoing, "seq", split_axis=0, concat_axis=1, tiled=True)[0]

    if planned:
        depth = key_weight.shape[0] // 2

        def half_block(first):
            halves = [
                lax.dynamic_slice_in_dim(weight, first, depth, 0)
                for weight in (key_weight, value_weight)
            ]
            return jnp.concatenate(halves, 1)

        sent = half_block(group_id * depth)
        tables = turn_tables(count_rows * seq + STEPS, count_rows)
        near = moved(sent, to_pair)
        middle = moved(sent, to_middle)
        across = moved(sent, to_row)
        mine, kept = prepared(place, flat, seq // 2)
        rest = half_block(depth - group_id * depth)
        came = (near, middle, across, mine, rest)
        passed = moved(after(middle, *came), to_end)
        middle_c = moved(after(near, *came), to_middle)
        near_y = moved(after(near, *came), to_row)
        across_x = moved(after(across, *came), to_group)
        other = moved(after(kept, *came), to_core)
        came = (passed, middle_c, near_y, across_x, other)
        far = moved(after(middle_c, *came), to_end)
        block_b = jnp.where(is_end, after(passed, *came), middle)
        block_yb = moved(block_b, to_row)
        block_xb = moved(block_b, to_group)
        pieces = [(HERE, 0, sent), (HERE, 1, rest), (THERE, 0, across)]
        pieces += [(THERE, 1, across_x), (HERE + 1, 0, near), (THERE + 1, 0, near_y)]
        totals = product(place, after(mine, *came), other, pieces, (), 3)
        came = (far, block_yb, block_xb, totals[0])
        near_rest = moved(after(rest, *came), to_pair)
        block_c = jnp.where(is_end, after(far, *came), middle_c)
        block_xc = moved(block_c, to_group)
        block_yc = moved(block_c, to_row)
        pieces = [(HERE + 2, 0, block_b), (HERE + 2, 1, block_xb)]
        pieces += [(THERE + 2, 0, block_yb), (HERE + 3, 0, block_c)]
        totals = product(place, after(mine, *came), other, pieces, totals, 4)
        came = (near_rest, block_xc, block_yc, totals[0])
        end_a = moved(after(across_x, *came), to_pair)
        ends = [moved(after(block_yb, *came), to_group), moved(after(block_xc, *came), to_row)]
        pieces = [(HERE + 1, 1, near_rest), (HERE + 3, 1, block_xc), (THERE + 3, 0, block_yc)]
        totals = product(place, after(mine, *came), other, pieces, totals, 3)
        came = (end_a, *ends, *totals)
        pieces = [(THERE + 1, 1, end_a), (THERE + 2, 1, ends[0]), (THERE + 3, 1, ends[1])]
        total, given = product(place, after(mine, *came), other, pieces, totals, 3)
        outgoing = outgoing_rows(place, lengths, owner, total, moved(given, to_core), tables)
        incoming = lax.all_to_all(outgoing, "seq", split_axis=0, concat_axis=1, tiled=True)
        attended = decoded(
            place, lengths, owner, incoming[0], dec_query, dec_key, dec_value, tables
        )
        return (copied(incoming[0])[None], attended)
    else:
        cosine, sine_part = rope_table(positions, HEAD_SIZE)
        shape = (count_requests, count_rows, KEY_VALUE_HEADS, HEAD_SIZE)
        unrotated_key = project(key_weight).reshape(shape)
        key_rows = rotate(
            unrotated_key, cosine[:, None, :], sine_part[:, None, :]
        ).astype(jnp.bfloat16)
        cache_keys = handed_over(key_rows)
        cache_values = handed_over(project(value_weight).astype(jnp.bfloat16).reshape(shape))
    slot_count = cache_keys.shape[0]
    decode_peer = device_id // split_point
    block = device_id % split_point
    source_pair = jnp.sum(jnp.where(owner == decode_peer, pair_ids, 0))
    source_request = source_pair // KEY_VALUE_HEADS
    length = jnp.sum(
        jnp.where(jnp.arange(count_requests, dtype=jnp.int32) == source_request, lengths, 0)
    )
    query = lax.dynamic_index_in_dim(dec_query, decode_peer, 0, keepdims=False)
    new_key = lax.dynamic_index_in_dim(dec_key, decode_peer, 0, keepdims=False)
    new_value = lax.dynamic_index_in_dim(dec_value, decode_peer, 0, keepdims=False)
    step_pos = length + jnp.arange(STEPS, dtype=jnp.int32)
    step_cos, step_sin = rope_table(step_pos, HEAD_SIZE)
    query_rot = rotate(
        query.astype(jnp.float32).reshape(STEPS, QPK, HEAD_SIZE),
        step_cos[:, None, :],
        step_sin[:, None, :],
    ).astype(jnp.bfloat16)
    new_keys = rotate(new_key.astype(jnp.float32), step_cos, step_sin).astype(jnp.bfloat16)
    score_scale = 1.0 / HEAD_SIZE**0.5
    old_scores = (
        jnp.einsum(
            "sjd,id->sji", query_rot, cache_keys, preferred_element_type=jnp.float32
        )
        * score_scale
    )
    new_scores = (
        jnp.einsum("sjd,td->sjt", query_rot, new_keys, preferred_element_type=jnp.float32)
        * score_scale
    )
    slot_ids = jnp.arange(slot_count, dtype=jnp.int32) * split_point + block
    old_live = slot_ids < length
    new_live = (jnp.arange(STEPS)[None, :] <= jnp.arange(STEPS)[:, None]) & (block == 0)
    old_scores = jnp.where(old_live[None, None, :], old_scores, -1e30)
    new_scores = jnp.where(new_live[:, None, :], new_scores, -1e30)
    row_max = jnp.maximum(jnp.max(old_scores, -1), jnp.max(new_scores, -1))
    for bit in range(tree_levels):
        row_max = jnp.maximum(row_max, swapped(row_max, "seq", bit))
    old_exp = jnp.exp(old_scores - row_max[..., None])
    new_exp = jnp.exp(new_scores - row_max[..., None])
    denom = jnp.sum(old_exp, -1) + jnp.sum(new_exp, -1)
    for bit in range(tree_levels):
        denom = denom + swapped(denom, "seq", bit)
    old_probs = (old_exp / denom[..., None]).astype(jnp.bfloat16)
    new_probs = (new_exp / denom[..., None]).astype(jnp.bfloat16)
    partial_sum = jnp.einsum(
        "sji,id->sjd", old_probs, cache_values, preferred_element_type=jnp.float32
    )
    partial_sum = partial_sum + jnp.einsum(
        "sjt,td->sjd", new_probs, new_value, preferred_element_type=jnp.float32
    )
    flat_rows = partial_sum.reshape(STEPS, QPK * HEAD_SIZE)
    for bit in range(tree_levels):
        flat_rows = flat_rows + swapped(flat_rows, "seq", bit)
    share = flat_rows.shape[1] // split_point
    mine = lax.dynamic_slice_in_dim(flat_rows, block * share, share, 1)
    cache = jnp.concatenate([cache_keys, cache_values], 1)[None]
    return (cache, mine.astype(jnp.bfloat16))


def solution(mesh):
    placed = (
        P("groups", "seq", None),
        P("seq", None),
        P("seq", None),
        P("groups"),
        P("groups"),
        P("groups", None, None),
        P("groups", None, None),
        P("groups", None, None),
    )
    return jax.shard_map(
        body,
        mesh=mesh,
        in_specs=placed,
        out_specs=(P(("groups", "seq"), None, None), P("groups", "seq")),
        check_vma=False,
    )
```

```python
import functools

import jax
import jax.numpy as jnp
import numpy as np
from jax import lax
from jax.experimental import pallas as pl
from jax.experimental.pallas import tpu as pltpu
from jax.sharding import PartitionSpec as P

HEAD_SIZE = 128
KEY_VALUE_HEADS = 4
QPK = 8
STEPS = 4


ROPE_BASE = 500000.0


def swapped(block, axis, bit):
    count = lax.axis_size(axis)
    route = []
    for low in range(count):
        high = low | 1 << bit
        if high != low and high < count:
            route += [(low, high), (high, low)]
    return lax.ppermute(block, axis, route)


def rope_table(positions, head_dim):
    freq = ROPE_BASE ** (-(np.arange(head_dim // 2, dtype=np.float64) * 2.0) / head_dim)
    angle = positions.astype(jnp.float32)[:, None] * jnp.asarray(freq, jnp.float32)[None, :]
    return (jnp.cos(angle), jnp.sin(angle))


def rotate(values_in, cosine, sine_part):
    half_dim = values_in.shape[-1] // 2
    lower_half = values_in[..., :half_dim]
    upper_half = values_in[..., half_dim:]
    return jnp.concatenate(
        [
            lower_half * cosine - upper_half * sine_part,
            upper_half * cosine + lower_half * sine_part,
        ],
        -1,
    )


def spread(count):
    side = 1
    while side * side < count:
        side *= 2
    return (side, count // side)


def moved(block, rule):
    groups, seq = lax.axis_size("groups"), lax.axis_size("seq")
    low = spread(seq // 2)[1]
    route = []
    for g in range(groups):
        for s in range(seq):
            place = rule(g, s // 2 // low, s // 2 % low, s % 2)
            if place is not None:
                tg, tz, ty, tc = place
                route.append((g * seq + s, tg * seq + (tz * low + ty) * 2 + tc))
    return lax.ppermute(block, ("groups", "seq"), route)


def to_core(g, z, y, c):
    return (g, z, y, 1 - c)


def to_row(g, z, y, c):
    return (g, z, 1 - y, c)


def to_group(g, z, y, c):
    return (1 - g, z, y, c)


def to_pair(g, z, y, c):
    return (g, z ^ 1, y, c)


def to_middle(g, z, y, c):
    return (g, 3 - z, y, c) if z in (1, 2) else None


def to_end(g, z, y, c):
    return (g, 0 if z == 1 else 3, y, c) if z in (1, 2) else None


VMEM_REF = pl.BlockSpec(memory_space=pltpu.VMEM)
SMEM_REF = pl.BlockSpec(memory_space=pltpu.SMEM)
ANY_REF = pl.BlockSpec(memory_space=pl.ANY)
PARAMS = pltpu.CompilerParams(vmem_limit_bytes=20 << 20)
LARGE = pltpu.CompilerParams(vmem_limit_bytes=58 << 20)
SMALL = pltpu.CompilerParams(vmem_limit_bytes=16 << 20)


def cost(flops, moved_bytes):
    return pl.CostEstimate(flops=flops, bytes_accessed=moved_bytes, transcendentals=0)


def fetch(source, target, sem):
    copy = pltpu.make_async_copy(source, target, sem)
    copy.start()
    return copy


def prepare_kernel(place, *refs):
    depth = refs[2].shape[2]
    for rows_in, target in zip(refs[:2], refs[2:]):
        rows, width = rows_in.shape
        square = jnp.zeros((rows, depth), jnp.float32)
        for first in range(0, width, depth):
            part = rows_in[:, first : first + depth].astype(jnp.float32)
            square += part * part
        scale = lax.rsqrt(jnp.sum(square, -1, keepdims=True) / width + 1e-05)
        for core in range(2):

            @pl.when(place[1] == core)
            def _():
                for k in range(width // (2 * depth)):
                    first = (k // 2 * 4 + core * 2 + k % 2) * depth
                    part = rows_in[:, first : first + depth].astype(jnp.float32)
                    target[k] = (part * scale).astype(jnp.bfloat16)


def prepared(place, mine, other, blocks):
    rows, width = mine.shape
    depth = width // (4 * blocks)
    tile = 80 if rows % 80 == 0 else rows
    out = jax.ShapeDtypeStruct((2 * blocks, rows, depth), jnp.bfloat16)
    taken = pl.BlockSpec((tile, width), lambda i, place: (i, 0))
    given = pl.BlockSpec((2 * blocks, tile, depth), lambda i, place: (0, i, 0))
    return pl.pallas_call(
        prepare_kernel,
        grid_spec=pltpu.PrefetchScalarGridSpec(
            num_scalar_prefetch=1,
            grid=(rows // tile,),
            in_specs=[taken, taken],
            out_specs=[given, given],
        ),
        out_shape=[out, out],
        compiler_params=LARGE,
        cost_estimate=cost(1000, 1000),
        name="normed_halves",
    )(place, mine, other)


def after(value, *events):
    return lax.optimization_barrier((value, *events))[0]


def half_index(place, entry, kind):
    half = {0: place[0], 1: 1 - place[0], 2: 0, 3: 1}[kind]
    return place[entry] * 2 + half


def product_kernel(plan, group, with_total, place, mine, other, *refs):
    count = len(plan)
    outs = refs[-7:-5]
    left, right, total, sems, total_sems = refs[-5:]
    rows, depth = mine.shape[1], mine.shape[2]
    waits = []
    for k, (entry, kind) in enumerate(plan):
        area = pl.ds((k % group) * depth, depth)
        slot = k // group
        index = half_index(place, entry, kind)
        sources = (mine.at[index], other.at[index], refs[k])
        targets = (left.at[slot, 0, :, area], left.at[slot, 1, :, area], right.at[slot, area])
        waits.append(
            [fetch(a, b, sems.at[3 * k + i]) for i, (a, b) in enumerate(zip(sources, targets))]
        )
    carried = [
        fetch(ref, total.at[pl.ds(k * rows, rows)], total_sems.at[k])
        for k, ref in enumerate(refs[count : count + 2 * with_total])
    ]
    for slot in range(count // group):
        for copies in waits[slot * group : (slot + 1) * group]:
            for copy in copies:
                copy.wait()
        stacked = left[slot].reshape(2 * rows, group * depth)
        value = jnp.dot(stacked, right[slot], preferred_element_type=jnp.float32)
        if slot == 0:
            for copy in carried:
                copy.wait()
        if slot or with_total:
            value += total[...]
        if slot + 1 < count // group:
            total[...] = value
        else:
            outs[0][...] = value[:rows]
            outs[1][...] = value[rows:]


def product(place, mine, other, pieces, totals, group, moved_bytes=1000):
    _, rows, depth = mine.shape
    columns = pieces[0][2].shape[1]
    plan = [(entry, kind) for entry, kind, _ in pieces]
    count = len(plan)
    out = jax.ShapeDtypeStruct((rows, columns), jnp.float32)
    return pl.pallas_call(
        functools.partial(product_kernel, plan, group, bool(totals)),
        in_specs=[SMEM_REF] + [ANY_REF] * (2 + count + len(totals)),
        out_specs=[VMEM_REF] * 2,
        out_shape=[out] * 2,
        scratch_shapes=[
            pltpu.VMEM((count // group, 2, rows, group * depth), mine.dtype),
            pltpu.VMEM((count // group, group * depth, columns), mine.dtype),
            pltpu.VMEM((2 * rows, columns), jnp.float32),
            pltpu.SemaphoreType.DMA((3 * count,)),
            pltpu.SemaphoreType.DMA((2,)),
        ],
        compiler_params=PARAMS,
        cost_estimate=cost(1000, moved_bytes),
        name="add_product",
    )(place, mine, other, *[array for _, _, array in pieces], *totals)


LOW = 64


def turn_tables(positions, rows):
    freq = ROPE_BASE ** (-(np.arange(HEAD_SIZE // 2) * 2.0) / HEAD_SIZE)
    tables = []
    for places in (np.arange(0, positions, LOW), np.arange(LOW), np.arange(rows)):
        angle = places[:, None] * freq[None, :]
        tables.append(np.concatenate([np.cos(angle), np.cos(angle)], 1))
        tables.append(np.concatenate([-np.sin(angle), np.sin(angle)], 1))
    return [jnp.asarray(table, jnp.float32) for table in tables]


def turned_by(start, tables, cosine, sine):
    high, low = pl.ds(start // LOW, 1), pl.ds(start % LOW, 1)
    for cos_row, sin_row in (
        (tables[0][high], tables[1][high]),
        (tables[2][low], tables[3][low]),
    ):
        cosine, sine = cosine * cos_row - sine * sin_row, sine * cos_row + cosine * sin_row
    return cosine, sine


def rotated(rows, cosine, sine):
    half = HEAD_SIZE // 2
    return rows * cosine + jnp.concatenate([rows[:, half:], rows[:, :half]], 1) * sine


def rows_kernel(place, lengths, owner, *refs):
    total, came, *tables, out, scratch = refs
    columns = total.shape[1] // 2
    count_requests, count_rows = lengths.shape[0], scratch.shape[0]
    cosine, sine = turned_by(place[2] * count_rows, tables, tables[4][...], tables[5][...])
    index = place[2] * count_rows + lax.broadcasted_iota(jnp.int32, scratch.shape, 0)
    for r in range(count_requests):
        live = index < lengths[r]
        for h in range(KEY_VALUE_HEADS):
            for part in range(2):
                first = part * columns + h * HEAD_SIZE
                area = (
                    slice(r * count_rows, (r + 1) * count_rows),
                    slice(first, first + HEAD_SIZE),
                )
                rows = total[area] + came[area]
                if part == 0:
                    rows = rotated(rows, cosine, sine)
                scratch[...] = jnp.where(live, rows, 0.0)
                peer = owner[r * KEY_VALUE_HEADS + h]
                lanes = slice(part * HEAD_SIZE, (part + 1) * HEAD_SIZE)
                for b in range(2):
                    picked = scratch[pl.ds(b, count_rows // 2, stride=2), :]
                    out[peer * 2 + b, :, lanes] = picked.astype(jnp.bfloat16)


def outgoing_rows(place, lengths, owner, total, came, tables):
    count_rows = total.shape[0] // lengths.shape[0]
    out = (owner.shape[0] * 2, count_rows // 2, 2 * HEAD_SIZE)
    return pl.pallas_call(
        rows_kernel,
        in_specs=[SMEM_REF] * 3 + [VMEM_REF] * 8,
        out_specs=VMEM_REF,
        out_shape=jax.ShapeDtypeStruct(out, jnp.bfloat16),
        scratch_shapes=[pltpu.VMEM((count_rows, HEAD_SIZE), jnp.float32)],
        compiler_params=SMALL,
        cost_estimate=cost(1000, 1000),
        name="cache_rows",
    )(place, lengths, owner, total, came, *tables)


def decode_kernel(place, lengths, owner, cache, dec_query, dec_key, dec_value, *refs):
    tables, out = refs[:4], refs[4]
    peer, block = place[2] // 2, place[2] % 2
    length = lengths[0]
    for pair in range(owner.shape[0]):
        length = jnp.where(owner[pair] == peer, lengths[pair // KEY_VALUE_HEADS], length)
    cosine, sine = turned_by(length, tables, tables[2][:STEPS], tables[3][:STEPS])

    def turned(rows):
        return rotated(rows.astype(jnp.float32), cosine, sine)

    def padded(rows):
        return jnp.concatenate([rows, jnp.zeros((16 - STEPS, HEAD_SIZE), jnp.float32)], 0)

    raw = dec_query[peer]
    heads = [raw[:, j * HEAD_SIZE : (j + 1) * HEAD_SIZE] for j in range(QPK)]
    query = jnp.concatenate([turned(head) for head in heads], 0).astype(jnp.bfloat16)
    new_keys = padded(turned(dec_key[peer])).astype(jnp.bfloat16)
    new_value = padded(dec_value[peer].astype(jnp.float32)).astype(jnp.bfloat16)
    contract = (((1,), (1,)), ((), ()))
    scale = 1.0 / HEAD_SIZE**0.5
    old = lax.dot_general(
        query, cache[:, :HEAD_SIZE], contract, preferred_element_type=jnp.float32
    )
    slot = lax.broadcasted_iota(jnp.int32, old.shape, 1) * 2 + block
    old = jnp.where(slot < length, old * scale, -1e30)
    new = lax.dot_general(query, new_keys, contract, preferred_element_type=jnp.float32)
    step = lax.broadcasted_iota(jnp.int32, new.shape, 0) % STEPS
    token = lax.broadcasted_iota(jnp.int32, new.shape, 1)
    new = jnp.where((token <= step) & (block == 0), new * scale, -1e30)
    top = jnp.maximum(jnp.max(old, 1, keepdims=True), jnp.max(new, 1, keepdims=True))
    old, new = jnp.exp(old - top), jnp.exp(new - top)
    total = jnp.sum(old, 1, keepdims=True) + jnp.sum(new, 1, keepdims=True)
    sums = jnp.dot(
        old.astype(jnp.bfloat16), cache[:, HEAD_SIZE:], preferred_element_type=jnp.float32
    )
    out[:, :HEAD_SIZE] = sums + jnp.dot(
        new.astype(jnp.bfloat16), new_value, preferred_element_type=jnp.float32
    )
    half = (QPK * STEPS, HEAD_SIZE // 2)
    out[:, HEAD_SIZE : HEAD_SIZE + half[1]] = jnp.broadcast_to(top, half)
    out[:, HEAD_SIZE + half[1] :] = jnp.broadcast_to(total, half)


def joined_kernel(place, mine, theirs, out):
    share = QPK // 2
    area = pl.ds(place[2] % 2 * share * STEPS, share * STEPS)
    last = HEAD_SIZE + HEAD_SIZE // 2
    sums, tops, totals = [], [], []
    for ref in (mine, theirs):
        sums.append(ref[area, :HEAD_SIZE])
        tops.append(ref[area, HEAD_SIZE : HEAD_SIZE + 1])
        totals.append(ref[area, last : last + 1])
    top = jnp.maximum(tops[0], tops[1])
    scales = [jnp.exp(one - top) for one in tops]
    total = totals[0] * scales[0] + totals[1] * scales[1]
    value = (sums[0] * scales[0] + sums[1] * scales[1]) / total
    for j in range(share):
        rows = value[j * STEPS : (j + 1) * STEPS]
        out[:, j * HEAD_SIZE : (j + 1) * HEAD_SIZE] = rows.astype(jnp.bfloat16)


def copied(cache):
    def kernel(source, out, sem):
        fetch(source, out, sem.at[0]).wait()

    return pl.pallas_call(
        kernel,
        in_specs=[VMEM_REF],
        out_specs=ANY_REF,
        out_shape=jax.ShapeDtypeStruct(cache.shape, cache.dtype),
        scratch_shapes=[pltpu.SemaphoreType.DMA((1,))],
        compiler_params=SMALL,
        cost_estimate=cost(1000, 1000),
        name="copied",
    )(cache)


def decoded(place, lengths, owner, cache, dec_query, dec_key, dec_value, tables):
    mine = pl.pallas_call(
        decode_kernel,
        in_specs=[SMEM_REF] * 3 + [VMEM_REF] * 8,
        out_specs=VMEM_REF,
        out_shape=jax.ShapeDtypeStruct((STEPS * QPK, 2 * HEAD_SIZE), jnp.float32),
        compiler_params=SMALL,
        cost_estimate=cost(1000, 1000),
        name="decode",
    )(place, lengths, owner, cache, dec_query, dec_key, dec_value, *tables[:4])
    return pl.pallas_call(
        joined_kernel,
        in_specs=[SMEM_REF] + [VMEM_REF] * 2,
        out_specs=VMEM_REF,
        out_shape=jax.ShapeDtypeStruct((STEPS, QPK // 2 * HEAD_SIZE), jnp.bfloat16),
        compiler_params=SMALL,
        cost_estimate=cost(1000, 1000),
        name="joined",
    )(place, mine, moved(mine, to_core))


HERE, THERE = 3, 7


def body(hidden, key_weight, value_weight, lengths, owner, dec_query, dec_key, dec_value):
    count_requests, count_rows, width = hidden.shape
    device_id = lax.axis_index("seq")
    group_id = lax.axis_index("groups")
    seq = lax.axis_size("seq")
    planned = seq == 16 and lax.axis_size("groups") == 2
    decode_peers = count_requests * KEY_VALUE_HEADS
    split_point = seq // decode_peers
    tree_levels = split_point.bit_length() - 1
    rows_per_peer = count_rows // split_point
    positions = device_id * count_rows + jnp.arange(count_rows, dtype=jnp.int32)
    total_rows = count_requests * count_rows
    flat = hidden.reshape(total_rows, width)
    if planned:
        core = device_id % 2
        z, y = device_id // 4, device_id // 2 % 2
        layers = [z, z ^ 1, jnp.where(z < 2, 2, 1), jnp.where(z < 2, 3, 0)]
        is_end = (z == 0) | (z == 3)
        place = [group_id, core, device_id]
        place += [layer * 2 + y for layer in layers]
        place += [layer * 2 + 1 - y for layer in layers]
        place = jnp.stack([jnp.asarray(entry, jnp.int32) for entry in place])
    else:
        widened = flat.astype(jnp.float32)
        normed = (
            widened * lax.rsqrt(jnp.mean(widened * widened, -1, keepdims=True) + 1e-05)
        ).astype(jnp.bfloat16)

        def project(weight):
            whole = lax.all_gather(weight, "seq", axis=0, tiled=True)
            return jnp.dot(normed, whole, preferred_element_type=jnp.float32)

    pair_ids = jnp.arange(decode_peers, dtype=jnp.int32)
    matches = owner[None, :] == pair_ids[:, None]
    inverse_order = jnp.sum(jnp.where(matches, pair_ids[None, :], 0), axis=1)
    live_rows = positions[None, :] < lengths[:, None]

    def handed_over(rows):
        rows = jnp.where(live_rows[:, :, None, None], rows, jnp.zeros_like(rows))
        pair_rows = jnp.transpose(rows, (0, 2, 1, 3)).reshape(decode_peers, count_rows, HEAD_SIZE)
        sorted_rows = pair_rows[inverse_order].reshape(
            decode_peers, rows_per_peer, split_point, HEAD_SIZE
        )
        outgoing = jnp.transpose(sorted_rows, (0, 2, 1, 3)).reshape(
            decode_peers * split_point, rows_per_peer, HEAD_SIZE
        )
        return lax.all_to_all(outgoing, "seq", split_axis=0, concat_axis=1, tiled=True)[0]

    if planned:
        depth = key_weight.shape[0] // 2

        def half_block(first):
            halves = [
                lax.dynamic_slice_in_dim(weight, first, depth, 0)
                for weight in (key_weight, value_weight)
            ]
            return jnp.concatenate(halves, 1)

        raw = moved(flat, to_core)
        sent = half_block(group_id * depth)
        tables = turn_tables(count_rows * seq + STEPS, count_rows)
        near = moved(sent, to_pair)
        middle = moved(sent, to_middle)
        across = moved(sent, to_row)
        rest = half_block(depth - group_id * depth)
        came = (near, middle, across, raw, rest)
        passed = moved(after(middle, *came), to_end)
        middle_c = moved(after(near, *came), to_middle)
        near_y = moved(after(near, *came), to_row)
        across_x = moved(after(across, *came), to_group)
        mine, other = prepared(place, after(flat, *came), raw, seq // 2)
        came = (passed, middle_c, near_y, across_x, mine)
        far = moved(after(middle_c, *came), to_end)
        block_b = jnp.where(is_end, after(passed, *came), middle)
        block_yb = moved(block_b, to_row)
        block_xb = moved(block_b, to_group)
        pieces = [(HERE, 0, sent), (HERE, 1, rest), (THERE, 0, across)]
        pieces += [(THERE, 1, across_x), (HERE + 1, 0, near), (THERE + 1, 0, near_y)]
        totals = product(place, after(mine, *came), other, pieces, (), 3)
        came = (far, block_yb, block_xb, totals[0])
        near_rest = moved(after(rest, *came), to_pair)
        block_c = jnp.where(is_end, after(far, *came), middle_c)
        block_xc = moved(block_c, to_group)
        block_yc = moved(block_c, to_row)
        pieces = [(HERE + 2, 0, block_b), (HERE + 2, 1, block_xb)]
        pieces += [(THERE + 2, 0, block_yb), (HERE + 3, 0, block_c)]
        totals = product(place, after(mine, *came), other, pieces, totals, 4)
        came = (near_rest, block_xc, block_yc, totals[0])
        end_a = moved(after(across_x, *came), to_pair)
        ends = [moved(after(block_yb, *came), to_group), moved(after(block_xc, *came), to_row)]
        pieces = [(HERE + 1, 1, near_rest), (HERE + 3, 1, block_xc), (THERE + 3, 0, block_yc)]
        totals = product(place, after(mine, *came), other, pieces, totals, 3)
        came = (end_a, *ends, *totals)
        pieces = [(THERE + 1, 1, end_a), (THERE + 2, 1, ends[0]), (THERE + 3, 1, ends[1])]
        total, given = product(place, after(mine, *came), other, pieces, totals, 3)
        outgoing = outgoing_rows(place, lengths, owner, total, moved(given, to_core), tables)
        incoming = lax.all_to_all(outgoing, "seq", split_axis=0, concat_axis=1, tiled=True)
        attended = decoded(
            place, lengths, owner, incoming[0], dec_query, dec_key, dec_value, tables
        )
        return (copied(incoming[0])[None], attended)
    else:
        cosine, sine_part = rope_table(positions, HEAD_SIZE)
        shape = (count_requests, count_rows, KEY_VALUE_HEADS, HEAD_SIZE)
        unrotated_key = project(key_weight).reshape(shape)
        key_rows = rotate(
            unrotated_key, cosine[:, None, :], sine_part[:, None, :]
        ).astype(jnp.bfloat16)
        cache_keys = handed_over(key_rows)
        cache_values = handed_over(project(value_weight).astype(jnp.bfloat16).reshape(shape))
    slot_count = cache_keys.shape[0]
    decode_peer = device_id // split_point
    block = device_id % split_point
    source_pair = jnp.sum(jnp.where(owner == decode_peer, pair_ids, 0))
    source_request = source_pair // KEY_VALUE_HEADS
    length = jnp.sum(
        jnp.where(jnp.arange(count_requests, dtype=jnp.int32) == source_request, lengths, 0)
    )
    query = lax.dynamic_index_in_dim(dec_query, decode_peer, 0, keepdims=False)
    new_key = lax.dynamic_index_in_dim(dec_key, decode_peer, 0, keepdims=False)
    new_value = lax.dynamic_index_in_dim(dec_value, decode_peer, 0, keepdims=False)
    step_pos = length + jnp.arange(STEPS, dtype=jnp.int32)
    step_cos, step_sin = rope_table(step_pos, HEAD_SIZE)
    query_rot = rotate(
        query.astype(jnp.float32).reshape(STEPS, QPK, HEAD_SIZE),
        step_cos[:, None, :],
        step_sin[:, None, :],
    ).astype(jnp.bfloat16)
    new_keys = rotate(new_key.astype(jnp.float32), step_cos, step_sin).astype(jnp.bfloat16)
    score_scale = 1.0 / HEAD_SIZE**0.5
    old_scores = (
        jnp.einsum(
            "sjd,id->sji", query_rot, cache_keys, preferred_element_type=jnp.float32
        )
        * score_scale
    )
    new_scores = (
        jnp.einsum("sjd,td->sjt", query_rot, new_keys, preferred_element_type=jnp.float32)
        * score_scale
    )
    slot_ids = jnp.arange(slot_count, dtype=jnp.int32) * split_point + block
    old_live = slot_ids < length
    new_live = (jnp.arange(STEPS)[None, :] <= jnp.arange(STEPS)[:, None]) & (block == 0)
    old_scores = jnp.where(old_live[None, None, :], old_scores, -1e30)
    new_scores = jnp.where(new_live[:, None, :], new_scores, -1e30)
    row_max = jnp.maximum(jnp.max(old_scores, -1), jnp.max(new_scores, -1))
    for bit in range(tree_levels):
        row_max = jnp.maximum(row_max, swapped(row_max, "seq", bit))
    old_exp = jnp.exp(old_scores - row_max[..., None])
    new_exp = jnp.exp(new_scores - row_max[..., None])
    denom = jnp.sum(old_exp, -1) + jnp.sum(new_exp, -1)
    for bit in range(tree_levels):
        denom = denom + swapped(denom, "seq", bit)
    old_probs = (old_exp / denom[..., None]).astype(jnp.bfloat16)
    new_probs = (new_exp / denom[..., None]).astype(jnp.bfloat16)
    partial_sum = jnp.einsum(
        "sji,id->sjd", old_probs, cache_values, preferred_element_type=jnp.float32
    )
    partial_sum = partial_sum + jnp.einsum(
        "sjt,td->sjd", new_probs, new_value, preferred_element_type=jnp.float32
    )
    flat_rows = partial_sum.reshape(STEPS, QPK * HEAD_SIZE)
    for bit in range(tree_levels):
        flat_rows = flat_rows + swapped(flat_rows, "seq", bit)
    share = flat_rows.shape[1] // split_point
    mine = lax.dynamic_slice_in_dim(flat_rows, block * share, share, 1)
    cache = jnp.concatenate([cache_keys, cache_values], 1)[None]
    return (cache, mine.astype(jnp.bfloat16))


def solution(mesh):
    placed = (
        P("groups", "seq", None),
        P("seq", None),
        P("seq", None),
        P("groups"),
        P("groups"),
        P("groups", None, None),
        P("groups", None, None),
        P("groups", None, None),
    )
    return jax.shard_map(
        body,
        mesh=mesh,
        in_specs=placed,
        out_specs=(P(("groups", "seq"), None, None), P("groups", "seq")),
        check_vma=False,
    )
```

```python
import functools

import jax
import jax.numpy as jnp
import numpy as np
from jax import lax
from jax.experimental import pallas as pl
from jax.experimental.pallas import tpu as pltpu
from jax.sharding import PartitionSpec as P

HEAD_SIZE = 128
KEY_VALUE_HEADS = 4
QPK = 8
STEPS = 4


ROPE_BASE = 500000.0


def swapped(block, axis, bit):
    count = lax.axis_size(axis)
    route = []
    for low in range(count):
        high = low | 1 << bit
        if high != low and high < count:
            route += [(low, high), (high, low)]
    return lax.ppermute(block, axis, route)


def rope_table(positions, head_dim):
    freq = ROPE_BASE ** (-(np.arange(head_dim // 2, dtype=np.float64) * 2.0) / head_dim)
    angle = positions.astype(jnp.float32)[:, None] * jnp.asarray(freq, jnp.float32)[None, :]
    return (jnp.cos(angle), jnp.sin(angle))


def rotate(values_in, cosine, sine_part):
    half_dim = values_in.shape[-1] // 2
    lower_half = values_in[..., :half_dim]
    upper_half = values_in[..., half_dim:]
    return jnp.concatenate(
        [
            lower_half * cosine - upper_half * sine_part,
            upper_half * cosine + lower_half * sine_part,
        ],
        -1,
    )


def spread(count):
    side = 1
    while side * side < count:
        side *= 2
    return (side, count // side)


def moved(block, rule):
    groups, seq = lax.axis_size("groups"), lax.axis_size("seq")
    low = spread(seq // 2)[1]
    route = []
    for g in range(groups):
        for s in range(seq):
            place = rule(g, s // 2 // low, s // 2 % low, s % 2)
            if place is not None:
                tg, tz, ty, tc = place
                route.append((g * seq + s, tg * seq + (tz * low + ty) * 2 + tc))
    return lax.ppermute(block, ("groups", "seq"), route)


def to_core(g, z, y, c):
    return (g, z, y, 1 - c)


def to_row(g, z, y, c):
    return (g, z, 1 - y, c)


def to_group(g, z, y, c):
    return (1 - g, z, y, c)


def to_pair(g, z, y, c):
    return (g, z ^ 1, y, c)


def to_middle(g, z, y, c):
    return (g, 3 - z, y, c) if z in (1, 2) else None


def to_end(g, z, y, c):
    return (g, 0 if z == 1 else 3, y, c) if z in (1, 2) else None


VMEM_REF = pl.BlockSpec(memory_space=pltpu.VMEM)
SMEM_REF = pl.BlockSpec(memory_space=pltpu.SMEM)
ANY_REF = pl.BlockSpec(memory_space=pl.ANY)
PARAMS = pltpu.CompilerParams(vmem_limit_bytes=20 << 20)
LARGE = pltpu.CompilerParams(vmem_limit_bytes=58 << 20)
SMALL = pltpu.CompilerParams(vmem_limit_bytes=16 << 20)


def cost(flops, moved_bytes):
    return pl.CostEstimate(flops=flops, bytes_accessed=moved_bytes, transcendentals=0)


def fetch(source, target, sem):
    copy = pltpu.make_async_copy(source, target, sem)
    copy.start()
    return copy


def prepare_kernel(place, *refs):
    depth = refs[2].shape[2]
    for rows_in, target in zip(refs[:2], refs[2:]):
        rows, width = rows_in.shape
        square = jnp.zeros((rows, depth), jnp.float32)
        for first in range(0, width, depth):
            part = rows_in[:, first : first + depth].astype(jnp.float32)
            square += part * part
        scale = lax.rsqrt(jnp.sum(square, -1, keepdims=True) / width + 1e-05)
        for core in range(2):

            @pl.when(place[1] == core)
            def _():
                for k in range(width // (2 * depth)):
                    first = (k // 2 * 4 + core * 2 + k % 2) * depth
                    part = rows_in[:, first : first + depth].astype(jnp.float32)
                    target[k] = (part * scale).astype(jnp.bfloat16)


def prepared(place, mine, other, blocks):
    rows, width = mine.shape
    depth = width // (4 * blocks)
    tile = 80 if rows % 80 == 0 else rows
    out = jax.ShapeDtypeStruct((2 * blocks, rows, depth), jnp.bfloat16)
    taken = pl.BlockSpec((tile, width), lambda i, place: (i, 0))
    given = pl.BlockSpec((2 * blocks, tile, depth), lambda i, place: (0, i, 0))
    return pl.pallas_call(
        prepare_kernel,
        grid_spec=pltpu.PrefetchScalarGridSpec(
            num_scalar_prefetch=1,
            grid=(rows // tile,),
            in_specs=[taken, taken],
            out_specs=[given, given],
        ),
        out_shape=[out, out],
        compiler_params=LARGE,
        cost_estimate=cost(1000, 1000),
        name="normed_halves",
    )(place, mine, other)


def after(value, *events):
    return lax.optimization_barrier((value, *events))[0]


def half_index(place, entry, kind):
    half = {0: place[0], 1: 1 - place[0], 2: 0, 3: 1}[kind]
    return place[entry] * 2 + half


def product_kernel(plan, group, with_total, place, mine, other, *refs):
    count = len(plan)
    outs = refs[-7:-5]
    left, right, total, sems, total_sems = refs[-5:]
    rows, depth = mine.shape[1], mine.shape[2]
    waits = []
    for k, (entry, kind) in enumerate(plan):
        area = pl.ds((k % group) * depth, depth)
        slot = k // group
        index = half_index(place, entry, kind)
        sources = (mine.at[index], other.at[index], refs[k])
        targets = (left.at[slot, 0, :, area], left.at[slot, 1, :, area], right.at[slot, area])
        waits.append(
            [fetch(a, b, sems.at[3 * k + i]) for i, (a, b) in enumerate(zip(sources, targets))]
        )
    carried = [
        fetch(ref, total.at[pl.ds(k * rows, rows)], total_sems.at[k])
        for k, ref in enumerate(refs[count : count + 2 * with_total])
    ]
    for slot in range(count // group):
        for copies in waits[slot * group : (slot + 1) * group]:
            for copy in copies:
                copy.wait()
        stacked = left[slot].reshape(2 * rows, group * depth)
        value = jnp.dot(stacked, right[slot], preferred_element_type=jnp.float32)
        if slot == 0:
            for copy in carried:
                copy.wait()
        if slot or with_total:
            value += total[...]
        if slot + 1 < count // group:
            total[...] = value
        else:
            outs[0][...] = value[:rows]
            outs[1][...] = value[rows:]


def product(place, mine, other, pieces, totals, group, moved_bytes=1000):
    _, rows, depth = mine.shape
    columns = pieces[0][2].shape[1]
    plan = [(entry, kind) for entry, kind, _ in pieces]
    count = len(plan)
    out = jax.ShapeDtypeStruct((rows, columns), jnp.float32)
    return pl.pallas_call(
        functools.partial(product_kernel, plan, group, bool(totals)),
        in_specs=[SMEM_REF] + [ANY_REF] * (2 + count + len(totals)),
        out_specs=[VMEM_REF] * 2,
        out_shape=[out] * 2,
        scratch_shapes=[
            pltpu.VMEM((count // group, 2, rows, group * depth), mine.dtype),
            pltpu.VMEM((count // group, group * depth, columns), mine.dtype),
            pltpu.VMEM((2 * rows, columns), jnp.float32),
            pltpu.SemaphoreType.DMA((3 * count,)),
            pltpu.SemaphoreType.DMA((2,)),
        ],
        compiler_params=PARAMS,
        cost_estimate=cost(1000, moved_bytes),
        name="add_product",
    )(place, mine, other, *[array for _, _, array in pieces], *totals)


LOW = 64


def turn_tables(positions, rows):
    freq = ROPE_BASE ** (-(np.arange(HEAD_SIZE // 2) * 2.0) / HEAD_SIZE)
    tables = []
    for places in (np.arange(0, positions, LOW), np.arange(LOW), np.arange(rows)):
        angle = places[:, None] * freq[None, :]
        tables.append(np.concatenate([np.cos(angle), np.cos(angle)], 1))
        tables.append(np.concatenate([-np.sin(angle), np.sin(angle)], 1))
    return [jnp.asarray(table, jnp.float32) for table in tables]


def turned_by(start, tables, cosine, sine):
    high, low = pl.ds(start // LOW, 1), pl.ds(start % LOW, 1)
    for cos_row, sin_row in (
        (tables[0][high], tables[1][high]),
        (tables[2][low], tables[3][low]),
    ):
        cosine, sine = cosine * cos_row - sine * sin_row, sine * cos_row + cosine * sin_row
    return cosine, sine


def rotated(rows, cosine, sine):
    half = HEAD_SIZE // 2
    return rows * cosine + jnp.concatenate([rows[:, half:], rows[:, :half]], 1) * sine


def rows_kernel(place, lengths, owner, *refs):
    total, came, *tables, out, scratch = refs
    columns = total.shape[1] // 2
    count_requests, count_rows = lengths.shape[0], scratch.shape[0]
    cosine, sine = turned_by(place[2] * count_rows, tables, tables[4][...], tables[5][...])
    index = place[2] * count_rows + lax.broadcasted_iota(jnp.int32, scratch.shape, 0)
    for r in range(count_requests):
        live = index < lengths[r]
        for h in range(KEY_VALUE_HEADS):
            for part in range(2):
                first = part * columns + h * HEAD_SIZE
                area = (
                    slice(r * count_rows, (r + 1) * count_rows),
                    slice(first, first + HEAD_SIZE),
                )
                rows = total[area] + came[area]
                if part == 0:
                    rows = rotated(rows, cosine, sine)
                scratch[...] = jnp.where(live, rows, 0.0)
                peer = owner[r * KEY_VALUE_HEADS + h]
                lanes = slice(part * HEAD_SIZE, (part + 1) * HEAD_SIZE)
                for b in range(2):
                    picked = scratch[pl.ds(b, count_rows // 2, stride=2), :]
                    out[peer * 2 + b, :, lanes] = picked.astype(jnp.bfloat16)


def outgoing_rows(place, lengths, owner, total, came, tables):
    count_rows = total.shape[0] // lengths.shape[0]
    out = (owner.shape[0] * 2, count_rows // 2, 2 * HEAD_SIZE)
    return pl.pallas_call(
        rows_kernel,
        in_specs=[SMEM_REF] * 3 + [VMEM_REF] * 8,
        out_specs=VMEM_REF,
        out_shape=jax.ShapeDtypeStruct(out, jnp.bfloat16),
        scratch_shapes=[pltpu.VMEM((count_rows, HEAD_SIZE), jnp.float32)],
        compiler_params=SMALL,
        cost_estimate=cost(1000, 1000),
        name="cache_rows",
    )(place, lengths, owner, total, came, *tables)


def decode_kernel(place, lengths, owner, cache, dec_query, dec_key, dec_value, *refs):
    tables, out = refs[:4], refs[4]
    peer, block = place[2] // 2, place[2] % 2
    length = lengths[0]
    for pair in range(owner.shape[0]):
        length = jnp.where(owner[pair] == peer, lengths[pair // KEY_VALUE_HEADS], length)
    cosine, sine = turned_by(length, tables, tables[2][:STEPS], tables[3][:STEPS])

    def turned(rows):
        return rotated(rows.astype(jnp.float32), cosine, sine)

    def padded(rows):
        return jnp.concatenate([rows, jnp.zeros((16 - STEPS, HEAD_SIZE), jnp.float32)], 0)

    raw = dec_query[peer]
    heads = [raw[:, j * HEAD_SIZE : (j + 1) * HEAD_SIZE] for j in range(QPK)]
    query = jnp.concatenate([turned(head) for head in heads], 0).astype(jnp.bfloat16)
    new_keys = padded(turned(dec_key[peer])).astype(jnp.bfloat16)
    new_value = padded(dec_value[peer].astype(jnp.float32)).astype(jnp.bfloat16)
    contract = (((1,), (1,)), ((), ()))
    scale = 1.0 / HEAD_SIZE**0.5
    old = lax.dot_general(
        query, cache[:, :HEAD_SIZE], contract, preferred_element_type=jnp.float32
    )
    slot = lax.broadcasted_iota(jnp.int32, old.shape, 1) * 2 + block
    old = jnp.where(slot < length, old * scale, -1e30)
    new = lax.dot_general(query, new_keys, contract, preferred_element_type=jnp.float32)
    step = lax.broadcasted_iota(jnp.int32, new.shape, 0) % STEPS
    token = lax.broadcasted_iota(jnp.int32, new.shape, 1)
    new = jnp.where((token <= step) & (block == 0), new * scale, -1e30)
    top = jnp.maximum(jnp.max(old, 1, keepdims=True), jnp.max(new, 1, keepdims=True))
    old, new = jnp.exp(old - top), jnp.exp(new - top)
    total = jnp.sum(old, 1, keepdims=True) + jnp.sum(new, 1, keepdims=True)
    sums = jnp.dot(
        old.astype(jnp.bfloat16), cache[:, HEAD_SIZE:], preferred_element_type=jnp.float32
    )
    out[:, :HEAD_SIZE] = sums + jnp.dot(
        new.astype(jnp.bfloat16), new_value, preferred_element_type=jnp.float32
    )
    half = (QPK * STEPS, HEAD_SIZE // 2)
    out[:, HEAD_SIZE : HEAD_SIZE + half[1]] = jnp.broadcast_to(top, half)
    out[:, HEAD_SIZE + half[1] :] = jnp.broadcast_to(total, half)


def joined_kernel(place, mine, theirs, out):
    share = QPK // 2
    area = pl.ds(place[2] % 2 * share * STEPS, share * STEPS)
    last = HEAD_SIZE + HEAD_SIZE // 2
    sums, tops, totals = [], [], []
    for ref in (mine, theirs):
        sums.append(ref[area, :HEAD_SIZE])
        tops.append(ref[area, HEAD_SIZE : HEAD_SIZE + 1])
        totals.append(ref[area, last : last + 1])
    top = jnp.maximum(tops[0], tops[1])
    scales = [jnp.exp(one - top) for one in tops]
    total = totals[0] * scales[0] + totals[1] * scales[1]
    value = (sums[0] * scales[0] + sums[1] * scales[1]) / total
    for j in range(share):
        rows = value[j * STEPS : (j + 1) * STEPS]
        out[:, j * HEAD_SIZE : (j + 1) * HEAD_SIZE] = rows.astype(jnp.bfloat16)


def copied(cache):
    def kernel(source, out, sem):
        fetch(source, out, sem.at[0]).wait()

    return pl.pallas_call(
        kernel,
        in_specs=[VMEM_REF],
        out_specs=ANY_REF,
        out_shape=jax.ShapeDtypeStruct(cache.shape, cache.dtype),
        scratch_shapes=[pltpu.SemaphoreType.DMA((1,))],
        compiler_params=SMALL,
        cost_estimate=cost(1000, 1000),
        name="copied",
    )(cache)


def decoded(place, lengths, owner, cache, dec_query, dec_key, dec_value, tables):
    mine = pl.pallas_call(
        decode_kernel,
        in_specs=[SMEM_REF] * 3 + [VMEM_REF] * 8,
        out_specs=VMEM_REF,
        out_shape=jax.ShapeDtypeStruct((STEPS * QPK, 2 * HEAD_SIZE), jnp.float32),
        compiler_params=SMALL,
        cost_estimate=cost(1000, 1000),
        name="decode",
    )(place, lengths, owner, cache, dec_query, dec_key, dec_value, *tables[:4])
    return pl.pallas_call(
        joined_kernel,
        in_specs=[SMEM_REF] + [VMEM_REF] * 2,
        out_specs=VMEM_REF,
        out_shape=jax.ShapeDtypeStruct((STEPS, QPK // 2 * HEAD_SIZE), jnp.bfloat16),
        compiler_params=SMALL,
        cost_estimate=cost(1000, 1000),
        name="joined",
    )(place, mine, moved(mine, to_core))


HERE, THERE = 3, 7


def body(hidden, key_weight, value_weight, lengths, owner, dec_query, dec_key, dec_value):
    count_requests, count_rows, width = hidden.shape
    device_id = lax.axis_index("seq")
    group_id = lax.axis_index("groups")
    seq = lax.axis_size("seq")
    planned = seq == 16 and lax.axis_size("groups") == 2
    decode_peers = count_requests * KEY_VALUE_HEADS
    split_point = seq // decode_peers
    tree_levels = split_point.bit_length() - 1
    rows_per_peer = count_rows // split_point
    positions = device_id * count_rows + jnp.arange(count_rows, dtype=jnp.int32)
    total_rows = count_requests * count_rows
    flat = hidden.reshape(total_rows, width)
    if planned:
        core = device_id % 2
        z, y = device_id // 4, device_id // 2 % 2
        layers = [z, z ^ 1, jnp.where(z < 2, 2, 1), jnp.where(z < 2, 3, 0)]
        is_end = (z == 0) | (z == 3)
        place = [group_id, core, device_id]
        place += [layer * 2 + y for layer in layers]
        place += [layer * 2 + 1 - y for layer in layers]
        place = jnp.stack([jnp.asarray(entry, jnp.int32) for entry in place])
    else:
        widened = flat.astype(jnp.float32)
        normed = (
            widened * lax.rsqrt(jnp.mean(widened * widened, -1, keepdims=True) + 1e-05)
        ).astype(jnp.bfloat16)

        def project(weight):
            whole = lax.all_gather(weight, "seq", axis=0, tiled=True)
            return jnp.dot(normed, whole, preferred_element_type=jnp.float32)

    pair_ids = jnp.arange(decode_peers, dtype=jnp.int32)
    matches = owner[None, :] == pair_ids[:, None]
    inverse_order = jnp.sum(jnp.where(matches, pair_ids[None, :], 0), axis=1)
    live_rows = positions[None, :] < lengths[:, None]

    def handed_over(rows):
        rows = jnp.where(live_rows[:, :, None, None], rows, jnp.zeros_like(rows))
        pair_rows = jnp.transpose(rows, (0, 2, 1, 3)).reshape(decode_peers, count_rows, HEAD_SIZE)
        sorted_rows = pair_rows[inverse_order].reshape(
            decode_peers, rows_per_peer, split_point, HEAD_SIZE
        )
        outgoing = jnp.transpose(sorted_rows, (0, 2, 1, 3)).reshape(
            decode_peers * split_point, rows_per_peer, HEAD_SIZE
        )
        return lax.all_to_all(outgoing, "seq", split_axis=0, concat_axis=1, tiled=True)[0]

    if planned:
        depth = key_weight.shape[0] // 2

        def half_block(first):
            halves = [
                lax.dynamic_slice_in_dim(weight, first, depth, 0)
                for weight in (key_weight, value_weight)
            ]
            return jnp.concatenate(halves, 1)

        raw = moved(flat, to_core)
        sent = half_block(group_id * depth)
        tables = turn_tables(count_rows * seq + STEPS, count_rows)
        near = moved(sent, to_pair)
        middle = moved(sent, to_middle)
        across = moved(sent, to_row)
        rest = half_block(depth - group_id * depth)
        layers, rows = (near, middle), (near, middle, across, raw, rest)
        passed = moved(after(middle, *layers), to_end)
        middle_c = moved(after(near, *layers), to_middle)
        near_y = moved(after(near, *rows), to_row)
        across_x = moved(after(across, *rows), to_group)
        mine, other = prepared(place, after(flat, *rows), raw, seq // 2)
        layers, rows = (passed, middle_c), (near_y, across_x, mine, passed)
        far = moved(after(middle_c, *layers), to_end)
        block_b = jnp.where(is_end, after(passed, *rows), middle)
        block_yb = moved(block_b, to_row)
        block_xb = moved(block_b, to_group)
        layers, rows = (far, near_y), (block_yb, block_xb, far)
        near_rest = moved(after(rest, *layers), to_pair)
        block_c = jnp.where(is_end, after(far, *rows), middle_c)
        block_xc = moved(block_c, to_group)
        block_yc = moved(block_c, to_row)
        pieces = [(HERE, 0, sent), (HERE, 1, rest), (THERE, 0, across)]
        pieces += [(THERE, 1, across_x), (HERE + 1, 0, near), (THERE + 1, 0, near_y)]
        totals = product(place, after(mine, block_c), other, pieces, (), 3)
        layers, rows = (near_rest, block_yb), (block_xc, block_yc, near_rest, totals[0])
        end_a = moved(after(across_x, *layers), to_pair)
        ends = [moved(after(block_yb, *rows), to_group), moved(after(block_xc, *rows), to_row)]
        pieces = [(HERE + 2, 0, block_b), (HERE + 2, 1, block_xb), (THERE + 2, 0, block_yb)]
        pieces += [(HERE + 3, 0, block_c), (HERE + 1, 1, near_rest)]
        pieces += [(HERE + 3, 1, block_xc), (THERE + 3, 0, block_yc)]
        totals = product(place, after(mine, *rows), other, pieces, totals, 7)
        came = (end_a, *ends, *totals)
        pieces = [(THERE + 1, 1, end_a), (THERE + 2, 1, ends[0]), (THERE + 3, 1, ends[1])]
        total, given = product(place, after(mine, *came), other, pieces, totals, 3)
        outgoing = outgoing_rows(place, lengths, owner, total, moved(given, to_core), tables)
        incoming = lax.all_to_all(outgoing, "seq", split_axis=0, concat_axis=1, tiled=True)
        attended = decoded(
            place, lengths, owner, incoming[0], dec_query, dec_key, dec_value, tables
        )
        return (copied(incoming[0])[None], attended)
    else:
        cosine, sine_part = rope_table(positions, HEAD_SIZE)
        shape = (count_requests, count_rows, KEY_VALUE_HEADS, HEAD_SIZE)
        unrotated_key = project(key_weight).reshape(shape)
        key_rows = rotate(
            unrotated_key, cosine[:, None, :], sine_part[:, None, :]
        ).astype(jnp.bfloat16)
        cache_keys = handed_over(key_rows)
        cache_values = handed_over(project(value_weight).astype(jnp.bfloat16).reshape(shape))
    slot_count = cache_keys.shape[0]
    decode_peer = device_id // split_point
    block = device_id % split_point
    source_pair = jnp.sum(jnp.where(owner == decode_peer, pair_ids, 0))
    source_request = source_pair // KEY_VALUE_HEADS
    length = jnp.sum(
        jnp.where(jnp.arange(count_requests, dtype=jnp.int32) == source_request, lengths, 0)
    )
    query = lax.dynamic_index_in_dim(dec_query, decode_peer, 0, keepdims=False)
    new_key = lax.dynamic_index_in_dim(dec_key, decode_peer, 0, keepdims=False)
    new_value = lax.dynamic_index_in_dim(dec_value, decode_peer, 0, keepdims=False)
    step_pos = length + jnp.arange(STEPS, dtype=jnp.int32)
    step_cos, step_sin = rope_table(step_pos, HEAD_SIZE)
    query_rot = rotate(
        query.astype(jnp.float32).reshape(STEPS, QPK, HEAD_SIZE),
        step_cos[:, None, :],
        step_sin[:, None, :],
    ).astype(jnp.bfloat16)
    new_keys = rotate(new_key.astype(jnp.float32), step_cos, step_sin).astype(jnp.bfloat16)
    score_scale = 1.0 / HEAD_SIZE**0.5
    old_scores = (
        jnp.einsum(
            "sjd,id->sji", query_rot, cache_keys, preferred_element_type=jnp.float32
        )
        * score_scale
    )
    new_scores = (
        jnp.einsum("sjd,td->sjt", query_rot, new_keys, preferred_element_type=jnp.float32)
        * score_scale
    )
    slot_ids = jnp.arange(slot_count, dtype=jnp.int32) * split_point + block
    old_live = slot_ids < length
    new_live = (jnp.arange(STEPS)[None, :] <= jnp.arange(STEPS)[:, None]) & (block == 0)
    old_scores = jnp.where(old_live[None, None, :], old_scores, -1e30)
    new_scores = jnp.where(new_live[:, None, :], new_scores, -1e30)
    row_max = jnp.maximum(jnp.max(old_scores, -1), jnp.max(new_scores, -1))
    for bit in range(tree_levels):
        row_max = jnp.maximum(row_max, swapped(row_max, "seq", bit))
    old_exp = jnp.exp(old_scores - row_max[..., None])
    new_exp = jnp.exp(new_scores - row_max[..., None])
    denom = jnp.sum(old_exp, -1) + jnp.sum(new_exp, -1)
    for bit in range(tree_levels):
        denom = denom + swapped(denom, "seq", bit)
    old_probs = (old_exp / denom[..., None]).astype(jnp.bfloat16)
    new_probs = (new_exp / denom[..., None]).astype(jnp.bfloat16)
    partial_sum = jnp.einsum(
        "sji,id->sjd", old_probs, cache_values, preferred_element_type=jnp.float32
    )
    partial_sum = partial_sum + jnp.einsum(
        "sjt,td->sjd", new_probs, new_value, preferred_element_type=jnp.float32
    )
    flat_rows = partial_sum.reshape(STEPS, QPK * HEAD_SIZE)
    for bit in range(tree_levels):
        flat_rows = flat_rows + swapped(flat_rows, "seq", bit)
    share = flat_rows.shape[1] // split_point
    mine = lax.dynamic_slice_in_dim(flat_rows, block * share, share, 1)
    cache = jnp.concatenate([cache_keys, cache_values], 1)[None]
    return (cache, mine.astype(jnp.bfloat16))


def solution(mesh):
    placed = (
        P("groups", "seq", None),
        P("seq", None),
        P("seq", None),
        P("groups"),
        P("groups"),
        P("groups", None, None),
        P("groups", None, None),
        P("groups", None, None),
    )
    return jax.shard_map(
        body,
        mesh=mesh,
        in_specs=placed,
        out_specs=(P(("groups", "seq"), None, None), P("groups", "seq")),
        check_vma=False,
    )
```

```python
import functools

import jax
import jax.numpy as jnp
import numpy as np
from jax import lax
from jax.experimental import pallas as pl
from jax.experimental.pallas import tpu as pltpu
from jax.sharding import PartitionSpec as P

HEAD_SIZE = 128
KEY_VALUE_HEADS = 4
QPK = 8
STEPS = 4


ROPE_BASE = 500000.0


def swapped(block, axis, bit):
    count = lax.axis_size(axis)
    route = []
    for low in range(count):
        high = low | 1 << bit
        if high != low and high < count:
            route += [(low, high), (high, low)]
    return lax.ppermute(block, axis, route)


def rope_table(positions, head_dim):
    freq = ROPE_BASE ** (-(np.arange(head_dim // 2, dtype=np.float64) * 2.0) / head_dim)
    angle = positions.astype(jnp.float32)[:, None] * jnp.asarray(freq, jnp.float32)[None, :]
    return (jnp.cos(angle), jnp.sin(angle))


def rotate(values_in, cosine, sine_part):
    half_dim = values_in.shape[-1] // 2
    lower_half = values_in[..., :half_dim]
    upper_half = values_in[..., half_dim:]
    return jnp.concatenate(
        [
            lower_half * cosine - upper_half * sine_part,
            upper_half * cosine + lower_half * sine_part,
        ],
        -1,
    )


def spread(count):
    side = 1
    while side * side < count:
        side *= 2
    return (side, count // side)


def moved(block, rule):
    groups, seq = lax.axis_size("groups"), lax.axis_size("seq")
    low = spread(seq // 2)[1]
    route = []
    for g in range(groups):
        for s in range(seq):
            place = rule(g, s // 2 // low, s // 2 % low, s % 2)
            if place is not None:
                tg, tz, ty, tc = place
                route.append((g * seq + s, tg * seq + (tz * low + ty) * 2 + tc))
    return lax.ppermute(block, ("groups", "seq"), route)


def to_core(g, z, y, c):
    return (g, z, y, 1 - c)


def to_row(g, z, y, c):
    return (g, z, 1 - y, c)


def to_group(g, z, y, c):
    return (1 - g, z, y, c)


def to_pair(g, z, y, c):
    return (g, z ^ 1, y, c)


def to_middle(g, z, y, c):
    return (g, 3 - z, y, c) if z in (1, 2) else None


def to_end(g, z, y, c):
    return (g, 0 if z == 1 else 3, y, c) if z in (1, 2) else None


VMEM_REF = pl.BlockSpec(memory_space=pltpu.VMEM)
SMEM_REF = pl.BlockSpec(memory_space=pltpu.SMEM)
ANY_REF = pl.BlockSpec(memory_space=pl.ANY)
PARAMS = pltpu.CompilerParams(vmem_limit_bytes=20 << 20)
LARGE = pltpu.CompilerParams(vmem_limit_bytes=58 << 20)
SMALL = pltpu.CompilerParams(vmem_limit_bytes=16 << 20)


def cost(flops, moved_bytes):
    return pl.CostEstimate(flops=flops, bytes_accessed=moved_bytes, transcendentals=0)


def fetch(source, target, sem):
    copy = pltpu.make_async_copy(source, target, sem)
    copy.start()
    return copy


def prepare_kernel(place, *refs):
    depth = refs[2].shape[2]
    for rows_in, target in zip(refs[:2], refs[2:]):
        rows, width = rows_in.shape
        square = jnp.zeros((rows, depth), jnp.float32)
        for first in range(0, width, depth):
            part = rows_in[:, first : first + depth].astype(jnp.float32)
            square += part * part
        scale = lax.rsqrt(jnp.sum(square, -1, keepdims=True) / width + 1e-05)
        for core in range(2):

            @pl.when(place[1] == core)
            def _():
                for k in range(width // (2 * depth)):
                    first = (k // 2 * 4 + core * 2 + k % 2) * depth
                    part = rows_in[:, first : first + depth].astype(jnp.float32)
                    target[k] = (part * scale).astype(jnp.bfloat16)


def prepared(place, mine, other, blocks):
    rows, width = mine.shape
    depth = width // (4 * blocks)
    tile = 80 if rows % 80 == 0 else rows
    out = jax.ShapeDtypeStruct((2 * blocks, rows, depth), jnp.bfloat16)
    taken = pl.BlockSpec((tile, width), lambda i, place: (i, 0))
    given = pl.BlockSpec((2 * blocks, tile, depth), lambda i, place: (0, i, 0))
    return pl.pallas_call(
        prepare_kernel,
        grid_spec=pltpu.PrefetchScalarGridSpec(
            num_scalar_prefetch=1,
            grid=(rows // tile,),
            in_specs=[taken, taken],
            out_specs=[given, given],
        ),
        out_shape=[out, out],
        compiler_params=LARGE,
        cost_estimate=cost(1000, 1000),
        name="normed_halves",
    )(place, mine, other)


def after(value, *events):
    return lax.optimization_barrier((value, *events))[0]


def half_index(place, entry, kind):
    half = {0: place[0], 1: 1 - place[0], 2: 0, 3: 1}[kind]
    return place[entry] * 2 + half


def product_kernel(plan, group, with_total, place, mine, other, *refs):
    count = len(plan)
    outs = refs[-7:-5]
    left, right, total, sems, total_sems = refs[-5:]
    rows, depth = mine.shape[1], mine.shape[2]
    waits = []
    for k, (entry, kind) in enumerate(plan):
        area = pl.ds((k % group) * depth, depth)
        slot = k // group
        index = half_index(place, entry, kind)
        sources = (mine.at[index], other.at[index], refs[k])
        targets = (left.at[slot, 0, :, area], left.at[slot, 1, :, area], right.at[slot, area])
        waits.append(
            [fetch(a, b, sems.at[3 * k + i]) for i, (a, b) in enumerate(zip(sources, targets))]
        )
    carried = [
        fetch(ref, total.at[pl.ds(k * rows, rows)], total_sems.at[k])
        for k, ref in enumerate(refs[count : count + 2 * with_total])
    ]
    for slot in range(count // group):
        for copies in waits[slot * group : (slot + 1) * group]:
            for copy in copies:
                copy.wait()
        stacked = left[slot].reshape(2 * rows, group * depth)
        value = jnp.dot(stacked, right[slot], preferred_element_type=jnp.float32)
        if slot == 0:
            for copy in carried:
                copy.wait()
        if slot or with_total:
            value += total[...]
        if slot + 1 < count // group:
            total[...] = value
        else:
            outs[0][...] = value[:rows]
            outs[1][...] = value[rows:]


def product(place, mine, other, pieces, totals, group, moved_bytes=1000):
    _, rows, depth = mine.shape
    columns = pieces[0][2].shape[1]
    plan = [(entry, kind) for entry, kind, _ in pieces]
    count = len(plan)
    out = jax.ShapeDtypeStruct((rows, columns), jnp.float32)
    return pl.pallas_call(
        functools.partial(product_kernel, plan, group, bool(totals)),
        in_specs=[SMEM_REF] + [ANY_REF] * (2 + count + len(totals)),
        out_specs=[VMEM_REF] * 2,
        out_shape=[out] * 2,
        scratch_shapes=[
            pltpu.VMEM((count // group, 2, rows, group * depth), mine.dtype),
            pltpu.VMEM((count // group, group * depth, columns), mine.dtype),
            pltpu.VMEM((2 * rows, columns), jnp.float32),
            pltpu.SemaphoreType.DMA((3 * count,)),
            pltpu.SemaphoreType.DMA((2,)),
        ],
        compiler_params=PARAMS,
        cost_estimate=cost(1000, moved_bytes),
        name="add_product",
    )(place, mine, other, *[array for _, _, array in pieces], *totals)


LOW = 64


def turn_tables(positions, rows):
    freq = ROPE_BASE ** (-(np.arange(HEAD_SIZE // 2) * 2.0) / HEAD_SIZE)
    tables = []
    for places in (np.arange(0, positions, LOW), np.arange(LOW), np.arange(rows)):
        angle = places[:, None] * freq[None, :]
        tables.append(np.concatenate([np.cos(angle), np.cos(angle)], 1))
        tables.append(np.concatenate([-np.sin(angle), np.sin(angle)], 1))
    return [jnp.asarray(table, jnp.float32) for table in tables]


def turned_by(start, tables, cosine, sine):
    high, low = pl.ds(start // LOW, 1), pl.ds(start % LOW, 1)
    for cos_row, sin_row in (
        (tables[0][high], tables[1][high]),
        (tables[2][low], tables[3][low]),
    ):
        cosine, sine = cosine * cos_row - sine * sin_row, sine * cos_row + cosine * sin_row
    return cosine, sine


def rotated(rows, cosine, sine):
    half = HEAD_SIZE // 2
    return rows * cosine + jnp.concatenate([rows[:, half:], rows[:, :half]], 1) * sine


def rows_kernel(place, lengths, owner, *refs):
    total, came, *tables, out, scratch = refs
    columns = total.shape[1] // 2
    count_requests, count_rows = lengths.shape[0], scratch.shape[0]
    cosine, sine = turned_by(place[2] * count_rows, tables, tables[4][...], tables[5][...])
    index = place[2] * count_rows + lax.broadcasted_iota(jnp.int32, scratch.shape, 0)
    for r in range(count_requests):
        live = index < lengths[r]
        for h in range(KEY_VALUE_HEADS):
            for part in range(2):
                first = part * columns + h * HEAD_SIZE
                area = (
                    slice(r * count_rows, (r + 1) * count_rows),
                    slice(first, first + HEAD_SIZE),
                )
                rows = total[area] + came[area]
                if part == 0:
                    rows = rotated(rows, cosine, sine)
                scratch[...] = jnp.where(live, rows, 0.0)
                peer = owner[r * KEY_VALUE_HEADS + h]
                lanes = slice(part * HEAD_SIZE, (part + 1) * HEAD_SIZE)
                for b in range(2):
                    picked = scratch[pl.ds(b, count_rows // 2, stride=2), :]
                    out[peer * 2 + b, :, lanes] = picked.astype(jnp.bfloat16)


def outgoing_rows(place, lengths, owner, total, came, tables):
    count_rows = total.shape[0] // lengths.shape[0]
    out = (owner.shape[0] * 2, count_rows // 2, 2 * HEAD_SIZE)
    return pl.pallas_call(
        rows_kernel,
        in_specs=[SMEM_REF] * 3 + [VMEM_REF] * 8,
        out_specs=VMEM_REF,
        out_shape=jax.ShapeDtypeStruct(out, jnp.bfloat16),
        scratch_shapes=[pltpu.VMEM((count_rows, HEAD_SIZE), jnp.float32)],
        compiler_params=SMALL,
        cost_estimate=cost(1000, 1000),
        name="cache_rows",
    )(place, lengths, owner, total, came, *tables)


def decode_kernel(place, lengths, owner, cache, dec_query, dec_key, dec_value, *refs):
    tables, out = refs[:4], refs[4]
    peer, block = place[2] // 2, place[2] % 2
    length = lengths[0]
    for pair in range(owner.shape[0]):
        length = jnp.where(owner[pair] == peer, lengths[pair // KEY_VALUE_HEADS], length)
    cosine, sine = turned_by(length, tables, tables[2][:STEPS], tables[3][:STEPS])

    def turned(rows):
        return rotated(rows.astype(jnp.float32), cosine, sine)

    def padded(rows):
        return jnp.concatenate([rows, jnp.zeros((16 - STEPS, HEAD_SIZE), jnp.float32)], 0)

    raw = dec_query[peer]
    heads = [raw[:, j * HEAD_SIZE : (j + 1) * HEAD_SIZE] for j in range(QPK)]
    query = jnp.concatenate([turned(head) for head in heads], 0).astype(jnp.bfloat16)
    new_keys = padded(turned(dec_key[peer])).astype(jnp.bfloat16)
    new_value = padded(dec_value[peer].astype(jnp.float32)).astype(jnp.bfloat16)
    contract = (((1,), (1,)), ((), ()))
    scale = 1.0 / HEAD_SIZE**0.5
    old = lax.dot_general(
        query, cache[:, :HEAD_SIZE], contract, preferred_element_type=jnp.float32
    )
    slot = lax.broadcasted_iota(jnp.int32, old.shape, 1) * 2 + block
    old = jnp.where(slot < length, old * scale, -1e30)
    new = lax.dot_general(query, new_keys, contract, preferred_element_type=jnp.float32)
    step = lax.broadcasted_iota(jnp.int32, new.shape, 0) % STEPS
    token = lax.broadcasted_iota(jnp.int32, new.shape, 1)
    new = jnp.where((token <= step) & (block == 0), new * scale, -1e30)
    top = jnp.maximum(jnp.max(old, 1, keepdims=True), jnp.max(new, 1, keepdims=True))
    old, new = jnp.exp(old - top), jnp.exp(new - top)
    total = jnp.sum(old, 1, keepdims=True) + jnp.sum(new, 1, keepdims=True)
    sums = jnp.dot(
        old.astype(jnp.bfloat16), cache[:, HEAD_SIZE:], preferred_element_type=jnp.float32
    )
    out[:, :HEAD_SIZE] = sums + jnp.dot(
        new.astype(jnp.bfloat16), new_value, preferred_element_type=jnp.float32
    )
    half = (QPK * STEPS, HEAD_SIZE // 2)
    out[:, HEAD_SIZE : HEAD_SIZE + half[1]] = jnp.broadcast_to(top, half)
    out[:, HEAD_SIZE + half[1] :] = jnp.broadcast_to(total, half)


def joined_kernel(place, mine, theirs, out):
    share = QPK // 2
    area = pl.ds(place[2] % 2 * share * STEPS, share * STEPS)
    last = HEAD_SIZE + HEAD_SIZE // 2
    sums, tops, totals = [], [], []
    for ref in (mine, theirs):
        sums.append(ref[area, :HEAD_SIZE])
        tops.append(ref[area, HEAD_SIZE : HEAD_SIZE + 1])
        totals.append(ref[area, last : last + 1])
    top = jnp.maximum(tops[0], tops[1])
    scales = [jnp.exp(one - top) for one in tops]
    total = totals[0] * scales[0] + totals[1] * scales[1]
    value = (sums[0] * scales[0] + sums[1] * scales[1]) / total
    for j in range(share):
        rows = value[j * STEPS : (j + 1) * STEPS]
        out[:, j * HEAD_SIZE : (j + 1) * HEAD_SIZE] = rows.astype(jnp.bfloat16)


def copied(cache):
    def kernel(source, out, sem):
        fetch(source, out, sem.at[0]).wait()

    return pl.pallas_call(
        kernel,
        in_specs=[VMEM_REF],
        out_specs=ANY_REF,
        out_shape=jax.ShapeDtypeStruct(cache.shape, cache.dtype),
        scratch_shapes=[pltpu.SemaphoreType.DMA((1,))],
        compiler_params=SMALL,
        cost_estimate=cost(1000, 1000),
        name="copied",
    )(cache)


def decoded(place, lengths, owner, cache, dec_query, dec_key, dec_value, tables):
    mine = pl.pallas_call(
        decode_kernel,
        in_specs=[SMEM_REF] * 3 + [VMEM_REF] * 8,
        out_specs=VMEM_REF,
        out_shape=jax.ShapeDtypeStruct((STEPS * QPK, 2 * HEAD_SIZE), jnp.float32),
        compiler_params=SMALL,
        cost_estimate=cost(1000, 1000),
        name="decode",
    )(place, lengths, owner, cache, dec_query, dec_key, dec_value, *tables[:4])
    return pl.pallas_call(
        joined_kernel,
        in_specs=[SMEM_REF] + [VMEM_REF] * 2,
        out_specs=VMEM_REF,
        out_shape=jax.ShapeDtypeStruct((STEPS, QPK // 2 * HEAD_SIZE), jnp.bfloat16),
        compiler_params=SMALL,
        cost_estimate=cost(1000, 1000),
        name="joined",
    )(place, mine, moved(mine, to_core))


HERE, THERE = 3, 7


def body(hidden, key_weight, value_weight, lengths, owner, dec_query, dec_key, dec_value):
    count_requests, count_rows, width = hidden.shape
    device_id = lax.axis_index("seq")
    group_id = lax.axis_index("groups")
    seq = lax.axis_size("seq")
    planned = seq == 16 and lax.axis_size("groups") == 2
    decode_peers = count_requests * KEY_VALUE_HEADS
    split_point = seq // decode_peers
    tree_levels = split_point.bit_length() - 1
    rows_per_peer = count_rows // split_point
    positions = device_id * count_rows + jnp.arange(count_rows, dtype=jnp.int32)
    total_rows = count_requests * count_rows
    flat = hidden.reshape(total_rows, width)
    if planned:
        core = device_id % 2
        z, y = device_id // 4, device_id // 2 % 2
        layers = [z, z ^ 1, jnp.where(z < 2, 2, 1), jnp.where(z < 2, 3, 0)]
        is_end = (z == 0) | (z == 3)
        place = [group_id, core, device_id]
        place += [layer * 2 + y for layer in layers]
        place += [layer * 2 + 1 - y for layer in layers]
        place = jnp.stack([jnp.asarray(entry, jnp.int32) for entry in place])
    else:
        widened = flat.astype(jnp.float32)
        normed = (
            widened * lax.rsqrt(jnp.mean(widened * widened, -1, keepdims=True) + 1e-05)
        ).astype(jnp.bfloat16)

        def project(weight):
            whole = lax.all_gather(weight, "seq", axis=0, tiled=True)
            return jnp.dot(normed, whole, preferred_element_type=jnp.float32)

    pair_ids = jnp.arange(decode_peers, dtype=jnp.int32)
    matches = owner[None, :] == pair_ids[:, None]
    inverse_order = jnp.sum(jnp.where(matches, pair_ids[None, :], 0), axis=1)
    live_rows = positions[None, :] < lengths[:, None]

    def handed_over(rows):
        rows = jnp.where(live_rows[:, :, None, None], rows, jnp.zeros_like(rows))
        pair_rows = jnp.transpose(rows, (0, 2, 1, 3)).reshape(decode_peers, count_rows, HEAD_SIZE)
        sorted_rows = pair_rows[inverse_order].reshape(
            decode_peers, rows_per_peer, split_point, HEAD_SIZE
        )
        outgoing = jnp.transpose(sorted_rows, (0, 2, 1, 3)).reshape(
            decode_peers * split_point, rows_per_peer, HEAD_SIZE
        )
        return lax.all_to_all(outgoing, "seq", split_axis=0, concat_axis=1, tiled=True)[0]

    if planned:
        depth = key_weight.shape[0] // 2

        def half_block(first):
            halves = [
                lax.dynamic_slice_in_dim(weight, first, depth, 0)
                for weight in (key_weight, value_weight)
            ]
            return jnp.concatenate(halves, 1)

        raw = moved(flat, to_core)
        sent = half_block(group_id * depth)
        tables = turn_tables(count_rows * seq + STEPS, count_rows)
        near = moved(sent, to_pair)
        middle = moved(sent, to_middle)
        across = moved(sent, to_row)
        rest = half_block(depth - group_id * depth)
        layers, rows = (near, middle), (near, middle, across, raw, rest)
        passed = moved(after(middle, *layers), to_end)
        middle_c = moved(after(near, *layers), to_middle)
        near_y = moved(after(near, *rows), to_row)
        across_x = moved(after(across, *rows), to_group)
        mine, other = prepared(place, after(flat, *rows), raw, seq // 2)
        layers, rows = (passed, middle_c, mine), (near_y, across_x, mine, passed)
        far = moved(after(middle_c, *layers), to_end)
        block_b = jnp.where(is_end, after(passed, *rows), middle)
        block_yb = moved(block_b, to_row)
        block_xb = moved(block_b, to_group)
        layers, rows = (far, near_y), (block_yb, block_xb, far)
        near_rest = moved(after(rest, *layers), to_pair)
        block_c = jnp.where(is_end, after(far, *rows), middle_c)
        block_xc = moved(block_c, to_group)
        block_yc = moved(block_c, to_row)
        pieces = [(HERE, 0, sent), (HERE, 1, rest), (THERE, 0, across)]
        pieces += [(THERE, 1, across_x), (HERE + 1, 0, near), (THERE + 1, 0, near_y)]
        totals = product(place, after(mine, block_c), other, pieces, (), 3)
        layers, rows = (near_rest, block_yb), (block_xc, block_yc, near_rest, totals[0])
        end_a = moved(after(across_x, *layers), to_pair)
        ends = [moved(after(block_yb, *rows), to_group), moved(after(block_xc, *rows), to_row)]
        pieces = [(HERE + 2, 0, block_b), (HERE + 2, 1, block_xb), (THERE + 2, 0, block_yb)]
        pieces += [(HERE + 3, 0, block_c), (HERE + 1, 1, near_rest)]
        pieces += [(HERE + 3, 1, block_xc), (THERE + 3, 0, block_yc)]
        totals = product(place, after(mine, *rows), other, pieces, totals, 7)
        came = (end_a, *ends, *totals)
        pieces = [(THERE + 1, 1, end_a), (THERE + 2, 1, ends[0]), (THERE + 3, 1, ends[1])]
        total, given = product(place, after(mine, *came), other, pieces, totals, 3)
        outgoing = outgoing_rows(place, lengths, owner, total, moved(given, to_core), tables)
        incoming = lax.all_to_all(outgoing, "seq", split_axis=0, concat_axis=1, tiled=True)
        attended = decoded(
            place, lengths, owner, incoming[0], dec_query, dec_key, dec_value, tables
        )
        return (copied(incoming[0])[None], attended)
    else:
        cosine, sine_part = rope_table(positions, HEAD_SIZE)
        shape = (count_requests, count_rows, KEY_VALUE_HEADS, HEAD_SIZE)
        unrotated_key = project(key_weight).reshape(shape)
        key_rows = rotate(
            unrotated_key, cosine[:, None, :], sine_part[:, None, :]
        ).astype(jnp.bfloat16)
        cache_keys = handed_over(key_rows)
        cache_values = handed_over(project(value_weight).astype(jnp.bfloat16).reshape(shape))
    slot_count = cache_keys.shape[0]
    decode_peer = device_id // split_point
    block = device_id % split_point
    source_pair = jnp.sum(jnp.where(owner == decode_peer, pair_ids, 0))
    source_request = source_pair // KEY_VALUE_HEADS
    length = jnp.sum(
        jnp.where(jnp.arange(count_requests, dtype=jnp.int32) == source_request, lengths, 0)
    )
    query = lax.dynamic_index_in_dim(dec_query, decode_peer, 0, keepdims=False)
    new_key = lax.dynamic_index_in_dim(dec_key, decode_peer, 0, keepdims=False)
    new_value = lax.dynamic_index_in_dim(dec_value, decode_peer, 0, keepdims=False)
    step_pos = length + jnp.arange(STEPS, dtype=jnp.int32)
    step_cos, step_sin = rope_table(step_pos, HEAD_SIZE)
    query_rot = rotate(
        query.astype(jnp.float32).reshape(STEPS, QPK, HEAD_SIZE),
        step_cos[:, None, :],
        step_sin[:, None, :],
    ).astype(jnp.bfloat16)
    new_keys = rotate(new_key.astype(jnp.float32), step_cos, step_sin).astype(jnp.bfloat16)
    score_scale = 1.0 / HEAD_SIZE**0.5
    old_scores = (
        jnp.einsum(
            "sjd,id->sji", query_rot, cache_keys, preferred_element_type=jnp.float32
        )
        * score_scale
    )
    new_scores = (
        jnp.einsum("sjd,td->sjt", query_rot, new_keys, preferred_element_type=jnp.float32)
        * score_scale
    )
    slot_ids = jnp.arange(slot_count, dtype=jnp.int32) * split_point + block
    old_live = slot_ids < length
    new_live = (jnp.arange(STEPS)[None, :] <= jnp.arange(STEPS)[:, None]) & (block == 0)
    old_scores = jnp.where(old_live[None, None, :], old_scores, -1e30)
    new_scores = jnp.where(new_live[:, None, :], new_scores, -1e30)
    row_max = jnp.maximum(jnp.max(old_scores, -1), jnp.max(new_scores, -1))
    for bit in range(tree_levels):
        row_max = jnp.maximum(row_max, swapped(row_max, "seq", bit))
    old_exp = jnp.exp(old_scores - row_max[..., None])
    new_exp = jnp.exp(new_scores - row_max[..., None])
    denom = jnp.sum(old_exp, -1) + jnp.sum(new_exp, -1)
    for bit in range(tree_levels):
        denom = denom + swapped(denom, "seq", bit)
    old_probs = (old_exp / denom[..., None]).astype(jnp.bfloat16)
    new_probs = (new_exp / denom[..., None]).astype(jnp.bfloat16)
    partial_sum = jnp.einsum(
        "sji,id->sjd", old_probs, cache_values, preferred_element_type=jnp.float32
    )
    partial_sum = partial_sum + jnp.einsum(
        "sjt,td->sjd", new_probs, new_value, preferred_element_type=jnp.float32
    )
    flat_rows = partial_sum.reshape(STEPS, QPK * HEAD_SIZE)
    for bit in range(tree_levels):
        flat_rows = flat_rows + swapped(flat_rows, "seq", bit)
    share = flat_rows.shape[1] // split_point
    mine = lax.dynamic_slice_in_dim(flat_rows, block * share, share, 1)
    cache = jnp.concatenate([cache_keys, cache_values], 1)[None]
    return (cache, mine.astype(jnp.bfloat16))


def solution(mesh):
    placed = (
        P("groups", "seq", None),
        P("seq", None),
        P("seq", None),
        P("groups"),
        P("groups"),
        P("groups", None, None),
        P("groups", None, None),
        P("groups", None, None),
    )
    return jax.shard_map(
        body,
        mesh=mesh,
        in_specs=placed,
        out_specs=(P(("groups", "seq"), None, None), P("groups", "seq")),
        check_vma=False,
    )
```

```python
import functools

import jax
import jax.numpy as jnp
import numpy as np
from jax import lax
from jax.experimental import pallas as pl
from jax.experimental.pallas import tpu as pltpu
from jax.sharding import PartitionSpec as P

HEAD_SIZE = 128
KEY_VALUE_HEADS = 4
QPK = 8
STEPS = 4


ROPE_BASE = 500000.0


def swapped(block, axis, bit):
    count = lax.axis_size(axis)
    route = []
    for low in range(count):
        high = low | 1 << bit
        if high != low and high < count:
            route += [(low, high), (high, low)]
    return lax.ppermute(block, axis, route)


def rope_table(positions, head_dim):
    freq = ROPE_BASE ** (-(np.arange(head_dim // 2, dtype=np.float64) * 2.0) / head_dim)
    angle = positions.astype(jnp.float32)[:, None] * jnp.asarray(freq, jnp.float32)[None, :]
    return (jnp.cos(angle), jnp.sin(angle))


def rotate(values_in, cosine, sine_part):
    half_dim = values_in.shape[-1] // 2
    lower_half = values_in[..., :half_dim]
    upper_half = values_in[..., half_dim:]
    return jnp.concatenate(
        [
            lower_half * cosine - upper_half * sine_part,
            upper_half * cosine + lower_half * sine_part,
        ],
        -1,
    )


def spread(count):
    side = 1
    while side * side < count:
        side *= 2
    return (side, count // side)


def moved(block, rule):
    groups, seq = lax.axis_size("groups"), lax.axis_size("seq")
    low = spread(seq // 2)[1]
    route = []
    for g in range(groups):
        for s in range(seq):
            place = rule(g, s // 2 // low, s // 2 % low, s % 2)
            if place is not None:
                tg, tz, ty, tc = place
                route.append((g * seq + s, tg * seq + (tz * low + ty) * 2 + tc))
    return lax.ppermute(block, ("groups", "seq"), route)


def to_core(g, z, y, c):
    return (g, z, y, 1 - c)


def to_row(g, z, y, c):
    return (g, z, 1 - y, c)


def to_group(g, z, y, c):
    return (1 - g, z, y, c)


def to_pair(g, z, y, c):
    return (g, z ^ 1, y, c)


def to_middle(g, z, y, c):
    return (g, 3 - z, y, c) if z in (1, 2) else None


def to_end(g, z, y, c):
    return (g, 0 if z == 1 else 3, y, c) if z in (1, 2) else None


VMEM_REF = pl.BlockSpec(memory_space=pltpu.VMEM)
SMEM_REF = pl.BlockSpec(memory_space=pltpu.SMEM)
ANY_REF = pl.BlockSpec(memory_space=pl.ANY)
PARAMS = pltpu.CompilerParams(vmem_limit_bytes=20 << 20)
LARGE = pltpu.CompilerParams(vmem_limit_bytes=58 << 20)
SMALL = pltpu.CompilerParams(vmem_limit_bytes=16 << 20)


def cost(flops, moved_bytes):
    return pl.CostEstimate(flops=flops, bytes_accessed=moved_bytes, transcendentals=0)


def fetch(source, target, sem):
    copy = pltpu.make_async_copy(source, target, sem)
    copy.start()
    return copy


def prepare_kernel(place, *refs):
    depth = refs[2].shape[2]
    for rows_in, target in zip(refs[:2], refs[2:]):
        rows, width = rows_in.shape
        square = jnp.zeros((rows, depth), jnp.float32)
        for first in range(0, width, depth):
            part = rows_in[:, first : first + depth].astype(jnp.float32)
            square += part * part
        scale = lax.rsqrt(jnp.sum(square, -1, keepdims=True) / width + 1e-05)
        for core in range(2):

            @pl.when(place[1] == core)
            def _():
                for k in range(width // (2 * depth)):
                    first = (k // 2 * 4 + core * 2 + k % 2) * depth
                    part = rows_in[:, first : first + depth].astype(jnp.float32)
                    target[k] = (part * scale).astype(jnp.bfloat16)


def prepared(place, mine, other, blocks):
    rows, width = mine.shape
    depth = width // (4 * blocks)
    tile = 80 if rows % 80 == 0 else rows
    out = jax.ShapeDtypeStruct((2 * blocks, rows, depth), jnp.bfloat16)
    taken = pl.BlockSpec((tile, width), lambda i, place: (i, 0))
    given = pl.BlockSpec((2 * blocks, tile, depth), lambda i, place: (0, i, 0))
    return pl.pallas_call(
        prepare_kernel,
        grid_spec=pltpu.PrefetchScalarGridSpec(
            num_scalar_prefetch=1,
            grid=(rows // tile,),
            in_specs=[taken, taken],
            out_specs=[given, given],
        ),
        out_shape=[out, out],
        compiler_params=LARGE,
        cost_estimate=cost(1000, 1000),
        name="normed_halves",
    )(place, mine, other)


def after(value, *events):
    return lax.optimization_barrier((value, *events))[0]


def half_index(place, entry, kind):
    half = {0: place[0], 1: 1 - place[0], 2: 0, 3: 1}[kind]
    return place[entry] * 2 + half


def product_kernel(plan, group, with_total, place, mine, other, *refs):
    count = len(plan)
    outs = refs[-7:-5]
    left, right, total, sems, total_sems = refs[-5:]
    rows, depth = mine.shape[1], mine.shape[2]
    waits = []
    for k, (entry, kind) in enumerate(plan):
        area = pl.ds((k % group) * depth, depth)
        slot = k // group
        index = half_index(place, entry, kind)
        sources = (mine.at[index], other.at[index], refs[k])
        targets = (left.at[slot, 0, :, area], left.at[slot, 1, :, area], right.at[slot, area])
        waits.append(
            [fetch(a, b, sems.at[3 * k + i]) for i, (a, b) in enumerate(zip(sources, targets))]
        )
    carried = [
        fetch(ref, total.at[pl.ds(k * rows, rows)], total_sems.at[k])
        for k, ref in enumerate(refs[count : count + 2 * with_total])
    ]
    for slot in range(count // group):
        for copies in waits[slot * group : (slot + 1) * group]:
            for copy in copies:
                copy.wait()
        stacked = left[slot].reshape(2 * rows, group * depth)
        value = jnp.dot(stacked, right[slot], preferred_element_type=jnp.float32)
        if slot == 0:
            for copy in carried:
                copy.wait()
        if slot or with_total:
            value += total[...]
        if slot + 1 < count // group:
            total[...] = value
        else:
            outs[0][...] = value[:rows]
            outs[1][...] = value[rows:]


def product(place, mine, other, pieces, totals, group, moved_bytes=1000):
    _, rows, depth = mine.shape
    columns = pieces[0][2].shape[1]
    plan = [(entry, kind) for entry, kind, _ in pieces]
    count = len(plan)
    out = jax.ShapeDtypeStruct((rows, columns), jnp.float32)
    return pl.pallas_call(
        functools.partial(product_kernel, plan, group, bool(totals)),
        in_specs=[SMEM_REF] + [ANY_REF] * (2 + count + len(totals)),
        out_specs=[VMEM_REF] * 2,
        out_shape=[out] * 2,
        scratch_shapes=[
            pltpu.VMEM((count // group, 2, rows, group * depth), mine.dtype),
            pltpu.VMEM((count // group, group * depth, columns), mine.dtype),
            pltpu.VMEM((2 * rows, columns), jnp.float32),
            pltpu.SemaphoreType.DMA((3 * count,)),
            pltpu.SemaphoreType.DMA((2,)),
        ],
        compiler_params=PARAMS,
        cost_estimate=cost(1000, moved_bytes),
        name="add_product",
    )(place, mine, other, *[array for _, _, array in pieces], *totals)


LOW = 64


def turn_tables(positions, rows):
    freq = ROPE_BASE ** (-(np.arange(HEAD_SIZE // 2) * 2.0) / HEAD_SIZE)
    tables = []
    for places in (np.arange(0, positions, LOW), np.arange(LOW), np.arange(rows)):
        angle = places[:, None] * freq[None, :]
        tables.append(np.concatenate([np.cos(angle), np.cos(angle)], 1))
        tables.append(np.concatenate([-np.sin(angle), np.sin(angle)], 1))
    return [jnp.asarray(table, jnp.float32) for table in tables]


def turned_by(start, tables, cosine, sine):
    high, low = pl.ds(start // LOW, 1), pl.ds(start % LOW, 1)
    for cos_row, sin_row in (
        (tables[0][high], tables[1][high]),
        (tables[2][low], tables[3][low]),
    ):
        cosine, sine = cosine * cos_row - sine * sin_row, sine * cos_row + cosine * sin_row
    return cosine, sine


def rotated(rows, cosine, sine):
    half = HEAD_SIZE // 2
    return rows * cosine + jnp.concatenate([rows[:, half:], rows[:, :half]], 1) * sine


def rows_kernel(place, lengths, owner, *refs):
    total, came, *tables, out, scratch = refs
    columns = total.shape[1] // 2
    count_requests, count_rows = lengths.shape[0], scratch.shape[0]
    cosine, sine = turned_by(place[2] * count_rows, tables, tables[4][...], tables[5][...])
    index = place[2] * count_rows + lax.broadcasted_iota(jnp.int32, scratch.shape, 0)
    for r in range(count_requests):
        live = index < lengths[r]
        for h in range(KEY_VALUE_HEADS):
            for part in range(2):
                first = part * columns + h * HEAD_SIZE
                area = (
                    slice(r * count_rows, (r + 1) * count_rows),
                    slice(first, first + HEAD_SIZE),
                )
                rows = total[area] + came[area]
                if part == 0:
                    rows = rotated(rows, cosine, sine)
                scratch[...] = jnp.where(live, rows, 0.0)
                peer = owner[r * KEY_VALUE_HEADS + h]
                lanes = slice(part * HEAD_SIZE, (part + 1) * HEAD_SIZE)
                for b in range(2):
                    picked = scratch[pl.ds(b, count_rows // 2, stride=2), :]
                    out[peer * 2 + b, :, lanes] = picked.astype(jnp.bfloat16)


def outgoing_rows(place, lengths, owner, total, came, tables):
    count_rows = total.shape[0] // lengths.shape[0]
    out = (owner.shape[0] * 2, count_rows // 2, 2 * HEAD_SIZE)
    return pl.pallas_call(
        rows_kernel,
        in_specs=[SMEM_REF] * 3 + [VMEM_REF] * 8,
        out_specs=VMEM_REF,
        out_shape=jax.ShapeDtypeStruct(out, jnp.bfloat16),
        scratch_shapes=[pltpu.VMEM((count_rows, HEAD_SIZE), jnp.float32)],
        compiler_params=SMALL,
        cost_estimate=cost(1000, 1000),
        name="cache_rows",
    )(place, lengths, owner, total, came, *tables)


def decode_kernel(place, lengths, owner, cache, dec_query, dec_key, dec_value, *refs):
    tables, out = refs[:4], refs[4]
    peer, block = place[2] // 2, place[2] % 2
    length = lengths[0]
    for pair in range(owner.shape[0]):
        length = jnp.where(owner[pair] == peer, lengths[pair // KEY_VALUE_HEADS], length)
    cosine, sine = turned_by(length, tables, tables[2][:STEPS], tables[3][:STEPS])

    def turned(rows):
        return rotated(rows.astype(jnp.float32), cosine, sine)

    def padded(rows):
        return jnp.concatenate([rows, jnp.zeros((16 - STEPS, HEAD_SIZE), jnp.float32)], 0)

    raw = dec_query[peer]
    heads = [raw[:, j * HEAD_SIZE : (j + 1) * HEAD_SIZE] for j in range(QPK)]
    query = jnp.concatenate([turned(head) for head in heads], 0).astype(jnp.bfloat16)
    new_keys = padded(turned(dec_key[peer])).astype(jnp.bfloat16)
    new_value = padded(dec_value[peer].astype(jnp.float32)).astype(jnp.bfloat16)
    contract = (((1,), (1,)), ((), ()))
    scale = 1.0 / HEAD_SIZE**0.5
    old = lax.dot_general(
        query, cache[:, :HEAD_SIZE], contract, preferred_element_type=jnp.float32
    )
    slot = lax.broadcasted_iota(jnp.int32, old.shape, 1) * 2 + block
    old = jnp.where(slot < length, old * scale, -1e30)
    new = lax.dot_general(query, new_keys, contract, preferred_element_type=jnp.float32)
    step = lax.broadcasted_iota(jnp.int32, new.shape, 0) % STEPS
    token = lax.broadcasted_iota(jnp.int32, new.shape, 1)
    new = jnp.where((token <= step) & (block == 0), new * scale, -1e30)
    top = jnp.maximum(jnp.max(old, 1, keepdims=True), jnp.max(new, 1, keepdims=True))
    old, new = jnp.exp(old - top), jnp.exp(new - top)
    total = jnp.sum(old, 1, keepdims=True) + jnp.sum(new, 1, keepdims=True)
    sums = jnp.dot(
        old.astype(jnp.bfloat16), cache[:, HEAD_SIZE:], preferred_element_type=jnp.float32
    )
    out[:, :HEAD_SIZE] = sums + jnp.dot(
        new.astype(jnp.bfloat16), new_value, preferred_element_type=jnp.float32
    )
    half = (QPK * STEPS, HEAD_SIZE // 2)
    out[:, HEAD_SIZE : HEAD_SIZE + half[1]] = jnp.broadcast_to(top, half)
    out[:, HEAD_SIZE + half[1] :] = jnp.broadcast_to(total, half)


def joined_kernel(place, mine, theirs, out):
    share = QPK // 2
    area = pl.ds(place[2] % 2 * share * STEPS, share * STEPS)
    last = HEAD_SIZE + HEAD_SIZE // 2
    sums, tops, totals = [], [], []
    for ref in (mine, theirs):
        sums.append(ref[area, :HEAD_SIZE])
        tops.append(ref[area, HEAD_SIZE : HEAD_SIZE + 1])
        totals.append(ref[area, last : last + 1])
    top = jnp.maximum(tops[0], tops[1])
    scales = [jnp.exp(one - top) for one in tops]
    total = totals[0] * scales[0] + totals[1] * scales[1]
    value = (sums[0] * scales[0] + sums[1] * scales[1]) / total
    for j in range(share):
        rows = value[j * STEPS : (j + 1) * STEPS]
        out[:, j * HEAD_SIZE : (j + 1) * HEAD_SIZE] = rows.astype(jnp.bfloat16)


def copied(cache):
    def kernel(source, out, sem):
        fetch(source, out, sem.at[0]).wait()

    return pl.pallas_call(
        kernel,
        in_specs=[VMEM_REF],
        out_specs=ANY_REF,
        out_shape=jax.ShapeDtypeStruct(cache.shape, cache.dtype),
        scratch_shapes=[pltpu.SemaphoreType.DMA((1,))],
        compiler_params=SMALL,
        cost_estimate=cost(1000, 1000),
        name="copied",
    )(cache)


def decoded(place, lengths, owner, cache, dec_query, dec_key, dec_value, tables):
    mine = pl.pallas_call(
        decode_kernel,
        in_specs=[SMEM_REF] * 3 + [VMEM_REF] * 8,
        out_specs=VMEM_REF,
        out_shape=jax.ShapeDtypeStruct((STEPS * QPK, 2 * HEAD_SIZE), jnp.float32),
        compiler_params=SMALL,
        cost_estimate=cost(1000, 1000),
        name="decode",
    )(place, lengths, owner, cache, dec_query, dec_key, dec_value, *tables[:4])
    return pl.pallas_call(
        joined_kernel,
        in_specs=[SMEM_REF] + [VMEM_REF] * 2,
        out_specs=VMEM_REF,
        out_shape=jax.ShapeDtypeStruct((STEPS, QPK // 2 * HEAD_SIZE), jnp.bfloat16),
        compiler_params=SMALL,
        cost_estimate=cost(1000, 1000),
        name="joined",
    )(place, mine, moved(mine, to_core))


HERE, THERE = 3, 7


def body(hidden, key_weight, value_weight, lengths, owner, dec_query, dec_key, dec_value):
    count_requests, count_rows, width = hidden.shape
    device_id = lax.axis_index("seq")
    group_id = lax.axis_index("groups")
    seq = lax.axis_size("seq")
    planned = seq == 16 and lax.axis_size("groups") == 2
    decode_peers = count_requests * KEY_VALUE_HEADS
    split_point = seq // decode_peers
    tree_levels = split_point.bit_length() - 1
    rows_per_peer = count_rows // split_point
    positions = device_id * count_rows + jnp.arange(count_rows, dtype=jnp.int32)
    total_rows = count_requests * count_rows
    flat = hidden.reshape(total_rows, width)
    if planned:
        core = device_id % 2
        z, y = device_id // 4, device_id // 2 % 2
        layers = [z, z ^ 1, jnp.where(z < 2, 2, 1), jnp.where(z < 2, 3, 0)]
        is_end = (z == 0) | (z == 3)
        place = [group_id, core, device_id]
        place += [layer * 2 + y for layer in layers]
        place += [layer * 2 + 1 - y for layer in layers]
        place = jnp.stack([jnp.asarray(entry, jnp.int32) for entry in place])
    else:
        widened = flat.astype(jnp.float32)
        normed = (
            widened * lax.rsqrt(jnp.mean(widened * widened, -1, keepdims=True) + 1e-05)
        ).astype(jnp.bfloat16)

        def project(weight):
            whole = lax.all_gather(weight, "seq", axis=0, tiled=True)
            return jnp.dot(normed, whole, preferred_element_type=jnp.float32)

    pair_ids = jnp.arange(decode_peers, dtype=jnp.int32)
    matches = owner[None, :] == pair_ids[:, None]
    inverse_order = jnp.sum(jnp.where(matches, pair_ids[None, :], 0), axis=1)
    live_rows = positions[None, :] < lengths[:, None]

    def handed_over(rows):
        rows = jnp.where(live_rows[:, :, None, None], rows, jnp.zeros_like(rows))
        pair_rows = jnp.transpose(rows, (0, 2, 1, 3)).reshape(decode_peers, count_rows, HEAD_SIZE)
        sorted_rows = pair_rows[inverse_order].reshape(
            decode_peers, rows_per_peer, split_point, HEAD_SIZE
        )
        outgoing = jnp.transpose(sorted_rows, (0, 2, 1, 3)).reshape(
            decode_peers * split_point, rows_per_peer, HEAD_SIZE
        )
        return lax.all_to_all(outgoing, "seq", split_axis=0, concat_axis=1, tiled=True)[0]

    if planned:
        depth = key_weight.shape[0] // 2

        def half_block(first):
            halves = [
                lax.dynamic_slice_in_dim(weight, first, depth, 0)
                for weight in (key_weight, value_weight)
            ]
            return jnp.concatenate(halves, 1)

        raw = moved(flat, to_core)
        sent = half_block(group_id * depth)
        tables = turn_tables(count_rows * seq + STEPS, count_rows)
        near = moved(sent, to_pair)
        middle = moved(sent, to_middle)
        across = moved(sent, to_row)
        rest = half_block(depth - group_id * depth)
        layers, rows = (near, middle), (near, middle, across, raw, rest)
        passed = moved(after(middle, *layers), to_end)
        middle_c = moved(after(near, *layers), to_middle)
        near_y = moved(after(near, *rows), to_row)
        across_x = moved(after(across, *rows), to_group)
        mine, other = prepared(place, after(flat, *rows), raw, seq // 2)
        layers, rows = (passed, middle_c, mine), (near_y, across_x, mine, passed)
        far = moved(after(middle_c, *layers), to_end)
        block_b = jnp.where(is_end, after(passed, *rows), middle)
        block_yb = moved(block_b, to_row)
        block_xb = moved(block_b, to_group)
        layers, rows = (far, near_y), (block_yb, block_xb, far)
        near_rest = moved(after(rest, *layers), to_pair)
        block_c = jnp.where(is_end, after(far, *rows), middle_c)
        block_xc = moved(block_c, to_group)
        block_yc = moved(block_c, to_row)
        pieces = [(HERE, 0, sent), (HERE, 1, rest), (THERE, 0, across)]
        pieces += [(THERE, 1, across_x), (HERE + 1, 0, near), (THERE + 1, 0, near_y)]
        totals = product(place, after(mine, block_c), other, pieces, (), 3)
        layers, rows = (near_rest, block_yb, totals[0]), (block_xc, block_yc, near_rest, totals[0])
        end_a = moved(after(across_x, *layers), to_pair)
        ends = [moved(after(block_yb, *rows), to_group), moved(after(block_xc, *rows), to_row)]
        pieces = [(HERE + 2, 0, block_b), (HERE + 2, 1, block_xb), (THERE + 2, 0, block_yb)]
        pieces += [(HERE + 3, 0, block_c), (HERE + 1, 1, near_rest)]
        pieces += [(HERE + 3, 1, block_xc), (THERE + 3, 0, block_yc)]
        totals = product(place, after(mine, *rows), other, pieces, totals, 7)
        came = (end_a, *ends, *totals)
        pieces = [(THERE + 1, 1, end_a), (THERE + 2, 1, ends[0]), (THERE + 3, 1, ends[1])]
        total, given = product(place, after(mine, *came), other, pieces, totals, 3)
        outgoing = outgoing_rows(place, lengths, owner, total, moved(given, to_core), tables)
        incoming = lax.all_to_all(outgoing, "seq", split_axis=0, concat_axis=1, tiled=True)
        attended = decoded(
            place, lengths, owner, incoming[0], dec_query, dec_key, dec_value, tables
        )
        return (copied(incoming[0])[None], attended)
    else:
        cosine, sine_part = rope_table(positions, HEAD_SIZE)
        shape = (count_requests, count_rows, KEY_VALUE_HEADS, HEAD_SIZE)
        unrotated_key = project(key_weight).reshape(shape)
        key_rows = rotate(
            unrotated_key, cosine[:, None, :], sine_part[:, None, :]
        ).astype(jnp.bfloat16)
        cache_keys = handed_over(key_rows)
        cache_values = handed_over(project(value_weight).astype(jnp.bfloat16).reshape(shape))
    slot_count = cache_keys.shape[0]
    decode_peer = device_id // split_point
    block = device_id % split_point
    source_pair = jnp.sum(jnp.where(owner == decode_peer, pair_ids, 0))
    source_request = source_pair // KEY_VALUE_HEADS
    length = jnp.sum(
        jnp.where(jnp.arange(count_requests, dtype=jnp.int32) == source_request, lengths, 0)
    )
    query = lax.dynamic_index_in_dim(dec_query, decode_peer, 0, keepdims=False)
    new_key = lax.dynamic_index_in_dim(dec_key, decode_peer, 0, keepdims=False)
    new_value = lax.dynamic_index_in_dim(dec_value, decode_peer, 0, keepdims=False)
    step_pos = length + jnp.arange(STEPS, dtype=jnp.int32)
    step_cos, step_sin = rope_table(step_pos, HEAD_SIZE)
    query_rot = rotate(
        query.astype(jnp.float32).reshape(STEPS, QPK, HEAD_SIZE),
        step_cos[:, None, :],
        step_sin[:, None, :],
    ).astype(jnp.bfloat16)
    new_keys = rotate(new_key.astype(jnp.float32), step_cos, step_sin).astype(jnp.bfloat16)
    score_scale = 1.0 / HEAD_SIZE**0.5
    old_scores = (
        jnp.einsum(
            "sjd,id->sji", query_rot, cache_keys, preferred_element_type=jnp.float32
        )
        * score_scale
    )
    new_scores = (
        jnp.einsum("sjd,td->sjt", query_rot, new_keys, preferred_element_type=jnp.float32)
        * score_scale
    )
    slot_ids = jnp.arange(slot_count, dtype=jnp.int32) * split_point + block
    old_live = slot_ids < length
    new_live = (jnp.arange(STEPS)[None, :] <= jnp.arange(STEPS)[:, None]) & (block == 0)
    old_scores = jnp.where(old_live[None, None, :], old_scores, -1e30)
    new_scores = jnp.where(new_live[:, None, :], new_scores, -1e30)
    row_max = jnp.maximum(jnp.max(old_scores, -1), jnp.max(new_scores, -1))
    for bit in range(tree_levels):
        row_max = jnp.maximum(row_max, swapped(row_max, "seq", bit))
    old_exp = jnp.exp(old_scores - row_max[..., None])
    new_exp = jnp.exp(new_scores - row_max[..., None])
    denom = jnp.sum(old_exp, -1) + jnp.sum(new_exp, -1)
    for bit in range(tree_levels):
        denom = denom + swapped(denom, "seq", bit)
    old_probs = (old_exp / denom[..., None]).astype(jnp.bfloat16)
    new_probs = (new_exp / denom[..., None]).astype(jnp.bfloat16)
    partial_sum = jnp.einsum(
        "sji,id->sjd", old_probs, cache_values, preferred_element_type=jnp.float32
    )
    partial_sum = partial_sum + jnp.einsum(
        "sjt,td->sjd", new_probs, new_value, preferred_element_type=jnp.float32
    )
    flat_rows = partial_sum.reshape(STEPS, QPK * HEAD_SIZE)
    for bit in range(tree_levels):
        flat_rows = flat_rows + swapped(flat_rows, "seq", bit)
    share = flat_rows.shape[1] // split_point
    mine = lax.dynamic_slice_in_dim(flat_rows, block * share, share, 1)
    cache = jnp.concatenate([cache_keys, cache_values], 1)[None]
    return (cache, mine.astype(jnp.bfloat16))


def solution(mesh):
    placed = (
        P("groups", "seq", None),
        P("seq", None),
        P("seq", None),
        P("groups"),
        P("groups"),
        P("groups", None, None),
        P("groups", None, None),
        P("groups", None, None),
    )
    return jax.shard_map(
        body,
        mesh=mesh,
        in_specs=placed,
        out_specs=(P(("groups", "seq"), None, None), P("groups", "seq")),
        check_vma=False,
    )
```

```python
import functools

import jax
import jax.numpy as jnp
import numpy as np
from jax import lax
from jax.experimental import pallas as pl
from jax.experimental.pallas import tpu as pltpu
from jax.sharding import PartitionSpec as P

HEAD_SIZE = 128
KEY_VALUE_HEADS = 4
QPK = 8
STEPS = 4


ROPE_BASE = 500000.0


def swapped(block, axis, bit):
    count = lax.axis_size(axis)
    route = []
    for low in range(count):
        high = low | 1 << bit
        if high != low and high < count:
            route += [(low, high), (high, low)]
    return lax.ppermute(block, axis, route)


def rope_table(positions, head_dim):
    freq = ROPE_BASE ** (-(np.arange(head_dim // 2, dtype=np.float64) * 2.0) / head_dim)
    angle = positions.astype(jnp.float32)[:, None] * jnp.asarray(freq, jnp.float32)[None, :]
    return (jnp.cos(angle), jnp.sin(angle))


def rotate(values_in, cosine, sine_part):
    half_dim = values_in.shape[-1] // 2
    lower_half = values_in[..., :half_dim]
    upper_half = values_in[..., half_dim:]
    return jnp.concatenate(
        [
            lower_half * cosine - upper_half * sine_part,
            upper_half * cosine + lower_half * sine_part,
        ],
        -1,
    )


def spread(count):
    side = 1
    while side * side < count:
        side *= 2
    return (side, count // side)


def moved(block, rule):
    groups, seq = lax.axis_size("groups"), lax.axis_size("seq")
    low = spread(seq // 2)[1]
    route = []
    for g in range(groups):
        for s in range(seq):
            place = rule(g, s // 2 // low, s // 2 % low, s % 2)
            if place is not None:
                tg, tz, ty, tc = place
                route.append((g * seq + s, tg * seq + (tz * low + ty) * 2 + tc))
    return lax.ppermute(block, ("groups", "seq"), route)


def to_core(g, z, y, c):
    return (g, z, y, 1 - c)


def to_row(g, z, y, c):
    return (g, z, 1 - y, c)


def to_group(g, z, y, c):
    return (1 - g, z, y, c)


def to_pair(g, z, y, c):
    return (g, z ^ 1, y, c)


def to_middle(g, z, y, c):
    return (g, 3 - z, y, c) if z in (1, 2) else None


def to_end(g, z, y, c):
    return (g, 0 if z == 1 else 3, y, c) if z in (1, 2) else None


VMEM_REF = pl.BlockSpec(memory_space=pltpu.VMEM)
SMEM_REF = pl.BlockSpec(memory_space=pltpu.SMEM)
ANY_REF = pl.BlockSpec(memory_space=pl.ANY)
PARAMS = pltpu.CompilerParams(vmem_limit_bytes=20 << 20)
LARGE = pltpu.CompilerParams(vmem_limit_bytes=53 << 20)
SMALL = pltpu.CompilerParams(vmem_limit_bytes=16 << 20)


def cost(flops, moved_bytes):
    return pl.CostEstimate(flops=flops, bytes_accessed=moved_bytes, transcendentals=0)


def fetch(source, target, sem):
    copy = pltpu.make_async_copy(source, target, sem)
    copy.start()
    return copy


def prepare_kernel(place, *refs):
    depth = refs[2].shape[2]
    for rows_in, target in zip(refs[:2], refs[2:]):
        rows, width = rows_in.shape
        square = jnp.zeros((rows, depth), jnp.float32)
        for first in range(0, width, depth):
            part = rows_in[:, first : first + depth].astype(jnp.float32)
            square += part * part
        scale = lax.rsqrt(jnp.sum(square, -1, keepdims=True) / width + 1e-05)
        for core in range(2):

            @pl.when(place[1] == core)
            def _():
                for k in range(width // (2 * depth)):
                    first = (k // 2 * 4 + core * 2 + k % 2) * depth
                    part = rows_in[:, first : first + depth].astype(jnp.float32)
                    target[k] = (part * scale).astype(jnp.bfloat16)


def prepared(place, mine, other, blocks):
    rows, width = mine.shape
    depth = width // (4 * blocks)
    tile = 80 if rows % 80 == 0 else rows
    out = jax.ShapeDtypeStruct((2 * blocks, rows, depth), jnp.bfloat16)
    taken = pl.BlockSpec((tile, width), lambda i, place: (i, 0))
    given = pl.BlockSpec((2 * blocks, tile, depth), lambda i, place: (0, i, 0))
    return pl.pallas_call(
        prepare_kernel,
        grid_spec=pltpu.PrefetchScalarGridSpec(
            num_scalar_prefetch=1,
            grid=(rows // tile,),
            in_specs=[taken, taken],
            out_specs=[given, given],
        ),
        out_shape=[out, out],
        compiler_params=LARGE,
        cost_estimate=cost(1000, 1000),
        name="normed_halves",
    )(place, mine, other)


def after(value, *events):
    return lax.optimization_barrier((value, *events))[0]


def half_index(place, entry, kind):
    half = {0: place[0], 1: 1 - place[0], 2: 0, 3: 1}[kind]
    return place[entry] * 2 + half


def product_kernel(plan, group, with_total, place, mine, other, *refs):
    count = len(plan)
    outs = refs[-7:-5]
    left, right, total, sems, total_sems = refs[-5:]
    rows, depth = mine.shape[1], mine.shape[2]
    waits = []
    for k, (entry, kind) in enumerate(plan):
        area = pl.ds((k % group) * depth, depth)
        slot = k // group
        index = half_index(place, entry, kind)
        sources = (mine.at[index], other.at[index], refs[k])
        targets = (left.at[slot, 0, :, area], left.at[slot, 1, :, area], right.at[slot, area])
        waits.append(
            [fetch(a, b, sems.at[3 * k + i]) for i, (a, b) in enumerate(zip(sources, targets))]
        )
    carried = [
        fetch(ref, total.at[pl.ds(k * rows, rows)], total_sems.at[k])
        for k, ref in enumerate(refs[count : count + 2 * with_total])
    ]
    for slot in range(count // group):
        for copies in waits[slot * group : (slot + 1) * group]:
            for copy in copies:
                copy.wait()
        stacked = left[slot].reshape(2 * rows, group * depth)
        value = jnp.dot(stacked, right[slot], preferred_element_type=jnp.float32)
        if slot == 0:
            for copy in carried:
                copy.wait()
        if slot or with_total:
            value += total[...]
        if slot + 1 < count // group:
            total[...] = value
        else:
            outs[0][...] = value[:rows]
            outs[1][...] = value[rows:]


def product(place, mine, other, pieces, totals, group, moved_bytes=1000):
    _, rows, depth = mine.shape
    columns = pieces[0][2].shape[1]
    plan = [(entry, kind) for entry, kind, _ in pieces]
    count = len(plan)
    out = jax.ShapeDtypeStruct((rows, columns), jnp.float32)
    return pl.pallas_call(
        functools.partial(product_kernel, plan, group, bool(totals)),
        in_specs=[SMEM_REF] + [ANY_REF] * (2 + count + len(totals)),
        out_specs=[VMEM_REF] * 2,
        out_shape=[out] * 2,
        scratch_shapes=[
            pltpu.VMEM((count // group, 2, rows, group * depth), mine.dtype),
            pltpu.VMEM((count // group, group * depth, columns), mine.dtype),
            pltpu.VMEM((2 * rows, columns), jnp.float32),
            pltpu.SemaphoreType.DMA((3 * count,)),
            pltpu.SemaphoreType.DMA((2,)),
        ],
        compiler_params=PARAMS,
        cost_estimate=cost(1000, moved_bytes),
        name="add_product",
    )(place, mine, other, *[array for _, _, array in pieces], *totals)


LOW = 64


def turn_tables(positions, rows):
    freq = ROPE_BASE ** (-(np.arange(HEAD_SIZE // 2) * 2.0) / HEAD_SIZE)
    tables = []
    for places in (np.arange(0, positions, LOW), np.arange(LOW), np.arange(rows)):
        angle = places[:, None] * freq[None, :]
        tables.append(np.concatenate([np.cos(angle), np.cos(angle)], 1))
        tables.append(np.concatenate([-np.sin(angle), np.sin(angle)], 1))
    return [jnp.asarray(table, jnp.float32) for table in tables]


def turned_by(start, tables, cosine, sine):
    high, low = pl.ds(start // LOW, 1), pl.ds(start % LOW, 1)
    for cos_row, sin_row in (
        (tables[0][high], tables[1][high]),
        (tables[2][low], tables[3][low]),
    ):
        cosine, sine = cosine * cos_row - sine * sin_row, sine * cos_row + cosine * sin_row
    return cosine, sine


def rotated(rows, cosine, sine):
    half = HEAD_SIZE // 2
    return rows * cosine + jnp.concatenate([rows[:, half:], rows[:, :half]], 1) * sine


def rows_kernel(place, lengths, owner, *refs):
    total, came, *tables, out, scratch = refs
    columns = total.shape[1] // 2
    count_requests, count_rows = lengths.shape[0], scratch.shape[0]
    cosine, sine = turned_by(place[2] * count_rows, tables, tables[4][...], tables[5][...])
    index = place[2] * count_rows + lax.broadcasted_iota(jnp.int32, scratch.shape, 0)
    for r in range(count_requests):
        live = index < lengths[r]
        for h in range(KEY_VALUE_HEADS):
            for part in range(2):
                first = part * columns + h * HEAD_SIZE
                area = (
                    slice(r * count_rows, (r + 1) * count_rows),
                    slice(first, first + HEAD_SIZE),
                )
                rows = total[area] + came[area]
                if part == 0:
                    rows = rotated(rows, cosine, sine)
                scratch[...] = jnp.where(live, rows, 0.0)
                peer = owner[r * KEY_VALUE_HEADS + h]
                lanes = slice(part * HEAD_SIZE, (part + 1) * HEAD_SIZE)
                for b in range(2):
                    picked = scratch[pl.ds(b, count_rows // 2, stride=2), :]
                    out[peer * 2 + b, :, lanes] = picked.astype(jnp.bfloat16)


def outgoing_rows(place, lengths, owner, total, came, tables):
    count_rows = total.shape[0] // lengths.shape[0]
    out = (owner.shape[0] * 2, count_rows // 2, 2 * HEAD_SIZE)
    return pl.pallas_call(
        rows_kernel,
        in_specs=[SMEM_REF] * 3 + [VMEM_REF] * 8,
        out_specs=VMEM_REF,
        out_shape=jax.ShapeDtypeStruct(out, jnp.bfloat16),
        scratch_shapes=[pltpu.VMEM((count_rows, HEAD_SIZE), jnp.float32)],
        compiler_params=SMALL,
        cost_estimate=cost(1000, 1000),
        name="cache_rows",
    )(place, lengths, owner, total, came, *tables)


def decode_kernel(place, lengths, owner, cache, dec_query, dec_key, dec_value, *refs):
    tables, out = refs[:4], refs[4]
    peer, block = place[2] // 2, place[2] % 2
    length = lengths[0]
    for pair in range(owner.shape[0]):
        length = jnp.where(owner[pair] == peer, lengths[pair // KEY_VALUE_HEADS], length)
    cosine, sine = turned_by(length, tables, tables[2][:STEPS], tables[3][:STEPS])

    def turned(rows):
        return rotated(rows.astype(jnp.float32), cosine, sine)

    def padded(rows):
        return jnp.concatenate([rows, jnp.zeros((16 - STEPS, HEAD_SIZE), jnp.float32)], 0)

    raw = dec_query[peer]
    heads = [raw[:, j * HEAD_SIZE : (j + 1) * HEAD_SIZE] for j in range(QPK)]
    query = jnp.concatenate([turned(head) for head in heads], 0).astype(jnp.bfloat16)
    new_keys = padded(turned(dec_key[peer])).astype(jnp.bfloat16)
    new_value = padded(dec_value[peer].astype(jnp.float32)).astype(jnp.bfloat16)
    contract = (((1,), (1,)), ((), ()))
    scale = 1.0 / HEAD_SIZE**0.5
    old = lax.dot_general(
        query, cache[:, :HEAD_SIZE], contract, preferred_element_type=jnp.float32
    )
    slot = lax.broadcasted_iota(jnp.int32, old.shape, 1) * 2 + block
    old = jnp.where(slot < length, old * scale, -1e30)
    new = lax.dot_general(query, new_keys, contract, preferred_element_type=jnp.float32)
    step = lax.broadcasted_iota(jnp.int32, new.shape, 0) % STEPS
    token = lax.broadcasted_iota(jnp.int32, new.shape, 1)
    new = jnp.where((token <= step) & (block == 0), new * scale, -1e30)
    top = jnp.maximum(jnp.max(old, 1, keepdims=True), jnp.max(new, 1, keepdims=True))
    old, new = jnp.exp(old - top), jnp.exp(new - top)
    total = jnp.sum(old, 1, keepdims=True) + jnp.sum(new, 1, keepdims=True)
    sums = jnp.dot(
        old.astype(jnp.bfloat16), cache[:, HEAD_SIZE:], preferred_element_type=jnp.float32
    )
    out[:, :HEAD_SIZE] = sums + jnp.dot(
        new.astype(jnp.bfloat16), new_value, preferred_element_type=jnp.float32
    )
    half = (QPK * STEPS, HEAD_SIZE // 2)
    out[:, HEAD_SIZE : HEAD_SIZE + half[1]] = jnp.broadcast_to(top, half)
    out[:, HEAD_SIZE + half[1] :] = jnp.broadcast_to(total, half)


def copied(cache):
    def kernel(source, out, sem):
        fetch(source, out, sem.at[0]).wait()

    return pl.pallas_call(
        kernel,
        in_specs=[VMEM_REF],
        out_specs=ANY_REF,
        out_shape=jax.ShapeDtypeStruct(cache.shape, cache.dtype),
        scratch_shapes=[pltpu.SemaphoreType.DMA((1,))],
        compiler_params=SMALL,
        cost_estimate=cost(1000, 1000),
        name="copied",
    )(cache)


def decoded(place, lengths, owner, cache, dec_query, dec_key, dec_value, tables):
    mine = pl.pallas_call(
        decode_kernel,
        in_specs=[SMEM_REF] * 3 + [VMEM_REF] * 8,
        out_specs=VMEM_REF,
        out_shape=jax.ShapeDtypeStruct((STEPS * QPK, 2 * HEAD_SIZE), jnp.float32),
        compiler_params=SMALL,
        cost_estimate=cost(1000, 1000),
        name="decode",
    )(place, lengths, owner, cache, dec_query, dec_key, dec_value, *tables[:4])
    theirs = moved(mine, to_core)
    share = QPK // 2
    last = HEAD_SIZE + HEAD_SIZE // 2

    def heads(array):
        array = array.reshape(QPK, STEPS, 2 * HEAD_SIZE)
        array = lax.dynamic_slice_in_dim(array, place[2] % 2 * share, share, 0)
        return array[..., :HEAD_SIZE], array[..., HEAD_SIZE : HEAD_SIZE + 1], array[..., last : last + 1]

    sums_a, top_a, total_a = heads(mine)
    sums_b, top_b, total_b = heads(theirs)
    top = jnp.maximum(top_a, top_b)
    scale_a, scale_b = jnp.exp(top_a - top), jnp.exp(top_b - top)
    value = (sums_a * scale_a + sums_b * scale_b) / (total_a * scale_a + total_b * scale_b)
    return jnp.transpose(value, (1, 0, 2)).reshape(STEPS, share * HEAD_SIZE).astype(jnp.bfloat16)


HERE, THERE = 3, 7


def body(hidden, key_weight, value_weight, lengths, owner, dec_query, dec_key, dec_value):
    count_requests, count_rows, width = hidden.shape
    device_id = lax.axis_index("seq")
    group_id = lax.axis_index("groups")
    seq = lax.axis_size("seq")
    planned = seq == 16 and lax.axis_size("groups") == 2
    decode_peers = count_requests * KEY_VALUE_HEADS
    split_point = seq // decode_peers
    tree_levels = split_point.bit_length() - 1
    rows_per_peer = count_rows // split_point
    positions = device_id * count_rows + jnp.arange(count_rows, dtype=jnp.int32)
    total_rows = count_requests * count_rows
    flat = hidden.reshape(total_rows, width)
    if planned:
        core = device_id % 2
        z, y = device_id // 4, device_id // 2 % 2
        layers = [z, z ^ 1, jnp.where(z < 2, 2, 1), jnp.where(z < 2, 3, 0)]
        is_end = (z == 0) | (z == 3)
        place = [group_id, core, device_id]
        place += [layer * 2 + y for layer in layers]
        place += [layer * 2 + 1 - y for layer in layers]
        place = jnp.stack([jnp.asarray(entry, jnp.int32) for entry in place])
    else:
        widened = flat.astype(jnp.float32)
        normed = (
            widened * lax.rsqrt(jnp.mean(widened * widened, -1, keepdims=True) + 1e-05)
        ).astype(jnp.bfloat16)

        def project(weight):
            whole = lax.all_gather(weight, "seq", axis=0, tiled=True)
            return jnp.dot(normed, whole, preferred_element_type=jnp.float32)

    pair_ids = jnp.arange(decode_peers, dtype=jnp.int32)
    matches = owner[None, :] == pair_ids[:, None]
    inverse_order = jnp.sum(jnp.where(matches, pair_ids[None, :], 0), axis=1)
    live_rows = positions[None, :] < lengths[:, None]

    def handed_over(rows):
        rows = jnp.where(live_rows[:, :, None, None], rows, jnp.zeros_like(rows))
        pair_rows = jnp.transpose(rows, (0, 2, 1, 3)).reshape(decode_peers, count_rows, HEAD_SIZE)
        sorted_rows = pair_rows[inverse_order].reshape(
            decode_peers, rows_per_peer, split_point, HEAD_SIZE
        )
        outgoing = jnp.transpose(sorted_rows, (0, 2, 1, 3)).reshape(
            decode_peers * split_point, rows_per_peer, HEAD_SIZE
        )
        return lax.all_to_all(outgoing, "seq", split_axis=0, concat_axis=1, tiled=True)[0]

    if planned:
        depth = key_weight.shape[0] // 2

        def half_block(first):
            halves = [
                lax.dynamic_slice_in_dim(weight, first, depth, 0)
                for weight in (key_weight, value_weight)
            ]
            return jnp.concatenate(halves, 1)

        raw = moved(flat, to_core)
        sent = half_block(group_id * depth)
        tables = turn_tables(count_rows * seq + STEPS, count_rows)
        near = moved(sent, to_pair)
        middle = moved(sent, to_middle)
        across = moved(sent, to_row)
        rest = half_block(depth - group_id * depth)
        layers, rows = (near, middle), (near, middle, across, raw, rest)
        passed = moved(after(middle, *layers), to_end)
        middle_c = moved(near, to_middle)
        near_y = moved(after(near, *rows), to_row)
        across_x = moved(after(across, *rows), to_group)
        mine, other = prepared(place, after(flat, *rows), raw, seq // 2)
        layers, rows = (passed, middle_c, mine), (near_y, across_x, mine, passed)
        far = moved(after(middle_c, *layers), to_end)
        block_b = jnp.where(is_end, after(passed, *rows), middle)
        block_yb = moved(block_b, to_row)
        block_xb = moved(block_b, to_group)
        layers, rows = (far, near_y), (block_yb, block_xb, far)
        near_rest = moved(after(rest, *layers), to_pair)
        block_c = jnp.where(is_end, after(far, *rows), middle_c)
        block_xc = moved(block_c, to_group)
        block_yc = moved(block_c, to_row)
        pieces = [(HERE, 0, sent), (HERE, 1, rest), (THERE, 0, across)]
        pieces += [(THERE, 1, across_x), (HERE + 1, 0, near), (THERE + 1, 0, near_y)]
        totals = product(place, after(mine, block_c), other, pieces, (), 3)
        layers, rows = (near_rest, block_yb, totals[0]), (block_xc, block_yc, near_rest, totals[0])
        end_a = moved(after(across_x, *layers), to_pair)
        ends = [moved(after(block_yb, *rows), to_group), moved(after(block_xc, *rows), to_row)]
        pieces = [(HERE + 2, 0, block_b), (HERE + 2, 1, block_xb), (THERE + 2, 0, block_yb)]
        pieces += [(HERE + 3, 0, block_c), (HERE + 1, 1, near_rest)]
        pieces += [(HERE + 3, 1, block_xc), (THERE + 3, 0, block_yc)]
        totals = product(place, after(mine, *rows), other, pieces, totals, 7)
        came = (end_a, *ends, *totals)
        pieces = [(THERE + 1, 1, end_a), (THERE + 2, 1, ends[0]), (THERE + 3, 1, ends[1])]
        total, given = product(place, after(mine, *came), other, pieces, totals, 3)
        outgoing = outgoing_rows(place, lengths, owner, total, moved(given, to_core), tables)
        incoming = lax.all_to_all(outgoing, "seq", split_axis=0, concat_axis=1, tiled=True)
        attended = decoded(
            place, lengths, owner, incoming[0], dec_query, dec_key, dec_value, tables
        )
        return (copied(incoming[0])[None], attended)
    else:
        cosine, sine_part = rope_table(positions, HEAD_SIZE)
        shape = (count_requests, count_rows, KEY_VALUE_HEADS, HEAD_SIZE)
        unrotated_key = project(key_weight).reshape(shape)
        key_rows = rotate(
            unrotated_key, cosine[:, None, :], sine_part[:, None, :]
        ).astype(jnp.bfloat16)
        cache_keys = handed_over(key_rows)
        cache_values = handed_over(project(value_weight).astype(jnp.bfloat16).reshape(shape))
    slot_count = cache_keys.shape[0]
    decode_peer = device_id // split_point
    block = device_id % split_point
    source_pair = jnp.sum(jnp.where(owner == decode_peer, pair_ids, 0))
    source_request = source_pair // KEY_VALUE_HEADS
    length = jnp.sum(
        jnp.where(jnp.arange(count_requests, dtype=jnp.int32) == source_request, lengths, 0)
    )
    query = lax.dynamic_index_in_dim(dec_query, decode_peer, 0, keepdims=False)
    new_key = lax.dynamic_index_in_dim(dec_key, decode_peer, 0, keepdims=False)
    new_value = lax.dynamic_index_in_dim(dec_value, decode_peer, 0, keepdims=False)
    step_pos = length + jnp.arange(STEPS, dtype=jnp.int32)
    step_cos, step_sin = rope_table(step_pos, HEAD_SIZE)
    query_rot = rotate(
        query.astype(jnp.float32).reshape(STEPS, QPK, HEAD_SIZE),
        step_cos[:, None, :],
        step_sin[:, None, :],
    ).astype(jnp.bfloat16)
    new_keys = rotate(new_key.astype(jnp.float32), step_cos, step_sin).astype(jnp.bfloat16)
    score_scale = 1.0 / HEAD_SIZE**0.5
    old_scores = (
        jnp.einsum(
            "sjd,id->sji", query_rot, cache_keys, preferred_element_type=jnp.float32
        )
        * score_scale
    )
    new_scores = (
        jnp.einsum("sjd,td->sjt", query_rot, new_keys, preferred_element_type=jnp.float32)
        * score_scale
    )
    slot_ids = jnp.arange(slot_count, dtype=jnp.int32) * split_point + block
    old_live = slot_ids < length
    new_live = (jnp.arange(STEPS)[None, :] <= jnp.arange(STEPS)[:, None]) & (block == 0)
    old_scores = jnp.where(old_live[None, None, :], old_scores, -1e30)
    new_scores = jnp.where(new_live[:, None, :], new_scores, -1e30)
    row_max = jnp.maximum(jnp.max(old_scores, -1), jnp.max(new_scores, -1))
    for bit in range(tree_levels):
        row_max = jnp.maximum(row_max, swapped(row_max, "seq", bit))
    old_exp = jnp.exp(old_scores - row_max[..., None])
    new_exp = jnp.exp(new_scores - row_max[..., None])
    denom = jnp.sum(old_exp, -1) + jnp.sum(new_exp, -1)
    for bit in range(tree_levels):
        denom = denom + swapped(denom, "seq", bit)
    old_probs = (old_exp / denom[..., None]).astype(jnp.bfloat16)
    new_probs = (new_exp / denom[..., None]).astype(jnp.bfloat16)
    partial_sum = jnp.einsum(
        "sji,id->sjd", old_probs, cache_values, preferred_element_type=jnp.float32
    )
    partial_sum = partial_sum + jnp.einsum(
        "sjt,td->sjd", new_probs, new_value, preferred_element_type=jnp.float32
    )
    flat_rows = partial_sum.reshape(STEPS, QPK * HEAD_SIZE)
    for bit in range(tree_levels):
        flat_rows = flat_rows + swapped(flat_rows, "seq", bit)
    share = flat_rows.shape[1] // split_point
    mine = lax.dynamic_slice_in_dim(flat_rows, block * share, share, 1)
    cache = jnp.concatenate([cache_keys, cache_values], 1)[None]
    return (cache, mine.astype(jnp.bfloat16))


def solution(mesh):
    placed = (
        P("groups", "seq", None),
        P("seq", None),
        P("seq", None),
        P("groups"),
        P("groups"),
        P("groups", None, None),
        P("groups", None, None),
        P("groups", None, None),
    )
    return jax.shard_map(
        body,
        mesh=mesh,
        in_specs=placed,
        out_specs=(P(("groups", "seq"), None, None), P("groups", "seq")),
        check_vma=False,
    )
```

```python
import functools

import jax
import jax.numpy as jnp
import numpy as np
from jax import lax
from jax.experimental import pallas as pl
from jax.experimental.pallas import tpu as pltpu
from jax.sharding import PartitionSpec as P

HEAD_SIZE = 128
KEY_VALUE_HEADS = 4
QPK = 8
STEPS = 4


ROPE_BASE = 500000.0


def swapped(block, axis, bit):
    count = lax.axis_size(axis)
    route = []
    for low in range(count):
        high = low | 1 << bit
        if high != low and high < count:
            route += [(low, high), (high, low)]
    return lax.ppermute(block, axis, route)


def rope_table(positions, head_dim):
    freq = ROPE_BASE ** (-(np.arange(head_dim // 2, dtype=np.float64) * 2.0) / head_dim)
    angle = positions.astype(jnp.float32)[:, None] * jnp.asarray(freq, jnp.float32)[None, :]
    return (jnp.cos(angle), jnp.sin(angle))


def rotate(values_in, cosine, sine_part):
    half_dim = values_in.shape[-1] // 2
    lower_half = values_in[..., :half_dim]
    upper_half = values_in[..., half_dim:]
    return jnp.concatenate(
        [
            lower_half * cosine - upper_half * sine_part,
            upper_half * cosine + lower_half * sine_part,
        ],
        -1,
    )


def spread(count):
    side = 1
    while side * side < count:
        side *= 2
    return (side, count // side)


def moved(block, rule):
    groups, seq = lax.axis_size("groups"), lax.axis_size("seq")
    low = spread(seq // 2)[1]
    route = []
    for g in range(groups):
        for s in range(seq):
            place = rule(g, s // 2 // low, s // 2 % low, s % 2)
            if place is not None:
                tg, tz, ty, tc = place
                route.append((g * seq + s, tg * seq + (tz * low + ty) * 2 + tc))
    return lax.ppermute(block, ("groups", "seq"), route)


def to_core(g, z, y, c):
    return (g, z, y, 1 - c)


def to_row(g, z, y, c):
    return (g, z, 1 - y, c)


def to_group(g, z, y, c):
    return (1 - g, z, y, c)


def to_pair(g, z, y, c):
    return (g, z ^ 1, y, c)


def to_next(g, z, y, c):
    return (g, z ^ 2, y, c)


def to_middle(g, z, y, c):
    return (g, 3 - z, y, c) if z in (1, 2) else None


def to_end(g, z, y, c):
    return (g, 0 if z == 1 else 3, y, c) if z in (1, 2) else None


VMEM_REF = pl.BlockSpec(memory_space=pltpu.VMEM)
SMEM_REF = pl.BlockSpec(memory_space=pltpu.SMEM)
ANY_REF = pl.BlockSpec(memory_space=pl.ANY)
PARAMS = pltpu.CompilerParams(vmem_limit_bytes=20 << 20)
LARGE = pltpu.CompilerParams(vmem_limit_bytes=53 << 20)
SMALL = pltpu.CompilerParams(vmem_limit_bytes=16 << 20)


def cost(flops, moved_bytes):
    return pl.CostEstimate(flops=flops, bytes_accessed=moved_bytes, transcendentals=0)


def fetch(source, target, sem):
    copy = pltpu.make_async_copy(source, target, sem)
    copy.start()
    return copy


def prepare_kernel(place, *refs):
    depth = refs[2].shape[2]
    for rows_in, target in zip(refs[:2], refs[2:]):
        rows, width = rows_in.shape
        square = jnp.zeros((rows, depth), jnp.float32)
        for first in range(0, width, depth):
            part = rows_in[:, first : first + depth].astype(jnp.float32)
            square += part * part
        scale = lax.rsqrt(jnp.sum(square, -1, keepdims=True) / width + 1e-05)
        for core in range(2):

            @pl.when(place[1] == core)
            def _():
                for k in range(width // (2 * depth)):
                    first = (k // 2 * 4 + core * 2 + k % 2) * depth
                    part = rows_in[:, first : first + depth].astype(jnp.float32)
                    target[k] = (part * scale).astype(jnp.bfloat16)


def prepared(place, mine, other, blocks):
    rows, width = mine.shape
    depth = width // (4 * blocks)
    tile = 80 if rows % 80 == 0 else rows
    out = jax.ShapeDtypeStruct((2 * blocks, rows, depth), jnp.bfloat16)
    taken = pl.BlockSpec((tile, width), lambda i, place: (i, 0))
    given = pl.BlockSpec((2 * blocks, tile, depth), lambda i, place: (0, i, 0))
    return pl.pallas_call(
        prepare_kernel,
        grid_spec=pltpu.PrefetchScalarGridSpec(
            num_scalar_prefetch=1,
            grid=(rows // tile,),
            in_specs=[taken, taken],
            out_specs=[given, given],
        ),
        out_shape=[out, out],
        compiler_params=LARGE,
        cost_estimate=cost(1000, 1000),
        name="normed_halves",
    )(place, mine, other)


def after(value, *events):
    return lax.optimization_barrier((value, *events))[0]


def half_index(place, entry, kind):
    half = {0: place[0], 1: 1 - place[0], 2: 0, 3: 1}[kind]
    return place[entry] * 2 + half


def product_kernel(plan, group, with_total, place, mine, other, *refs):
    count = len(plan)
    outs = refs[-7:-5]
    left, right, total, sems, total_sems = refs[-5:]
    rows, depth = mine.shape[1], mine.shape[2]
    waits = []
    for k, (entry, kind) in enumerate(plan):
        area = pl.ds((k % group) * depth, depth)
        slot = k // group
        index = half_index(place, entry, kind)
        sources = (mine.at[index], other.at[index], refs[k])
        targets = (left.at[slot, 0, :, area], left.at[slot, 1, :, area], right.at[slot, area])
        waits.append(
            [fetch(a, b, sems.at[3 * k + i]) for i, (a, b) in enumerate(zip(sources, targets))]
        )
    carried = [
        fetch(ref, total.at[pl.ds(k * rows, rows)], total_sems.at[k])
        for k, ref in enumerate(refs[count : count + 2 * with_total])
    ]
    for slot in range(count // group):
        for copies in waits[slot * group : (slot + 1) * group]:
            for copy in copies:
                copy.wait()
        stacked = left[slot].reshape(2 * rows, group * depth)
        value = jnp.dot(stacked, right[slot], preferred_element_type=jnp.float32)
        if slot == 0:
            for copy in carried:
                copy.wait()
        if slot or with_total:
            value += total[...]
        if slot + 1 < count // group:
            total[...] = value
        else:
            outs[0][...] = value[:rows]
            outs[1][...] = value[rows:]


def product(place, mine, other, pieces, totals, group, moved_bytes=1000):
    _, rows, depth = mine.shape
    columns = pieces[0][2].shape[1]
    plan = [(entry, kind) for entry, kind, _ in pieces]
    count = len(plan)
    out = jax.ShapeDtypeStruct((rows, columns), jnp.float32)
    return pl.pallas_call(
        functools.partial(product_kernel, plan, group, bool(totals)),
        in_specs=[SMEM_REF] + [ANY_REF] * (2 + count + len(totals)),
        out_specs=[VMEM_REF] * 2,
        out_shape=[out] * 2,
        scratch_shapes=[
            pltpu.VMEM((count // group, 2, rows, group * depth), mine.dtype),
            pltpu.VMEM((count // group, group * depth, columns), mine.dtype),
            pltpu.VMEM((2 * rows, columns), jnp.float32),
            pltpu.SemaphoreType.DMA((3 * count,)),
            pltpu.SemaphoreType.DMA((2,)),
        ],
        compiler_params=PARAMS,
        cost_estimate=cost(1000, moved_bytes),
        name="add_product",
    )(place, mine, other, *[array for _, _, array in pieces], *totals)


LOW = 64


def turn_tables(positions, rows):
    freq = ROPE_BASE ** (-(np.arange(HEAD_SIZE // 2) * 2.0) / HEAD_SIZE)
    tables = []
    for places in (np.arange(0, positions, LOW), np.arange(LOW), np.arange(rows)):
        angle = places[:, None] * freq[None, :]
        tables.append(np.concatenate([np.cos(angle), np.cos(angle)], 1))
        tables.append(np.concatenate([-np.sin(angle), np.sin(angle)], 1))
    return [jnp.asarray(table, jnp.float32) for table in tables]


def turned_by(start, tables, cosine, sine):
    high, low = pl.ds(start // LOW, 1), pl.ds(start % LOW, 1)
    for cos_row, sin_row in (
        (tables[0][high], tables[1][high]),
        (tables[2][low], tables[3][low]),
    ):
        cosine, sine = cosine * cos_row - sine * sin_row, sine * cos_row + cosine * sin_row
    return cosine, sine


def rotated(rows, cosine, sine):
    half = HEAD_SIZE // 2
    return rows * cosine + jnp.concatenate([rows[:, half:], rows[:, :half]], 1) * sine


def rows_kernel(place, lengths, owner, *refs):
    total, came, *tables, out, scratch = refs
    columns = total.shape[1] // 2
    count_requests, count_rows = lengths.shape[0], scratch.shape[0]
    cosine, sine = turned_by(place[2] * count_rows, tables, tables[4][...], tables[5][...])
    index = place[2] * count_rows + lax.broadcasted_iota(jnp.int32, scratch.shape, 0)
    for r in range(count_requests):
        live = index < lengths[r]
        for h in range(KEY_VALUE_HEADS):
            for part in range(2):
                first = part * columns + h * HEAD_SIZE
                area = (
                    slice(r * count_rows, (r + 1) * count_rows),
                    slice(first, first + HEAD_SIZE),
                )
                rows = total[area] + came[area]
                if part == 0:
                    rows = rotated(rows, cosine, sine)
                scratch[...] = jnp.where(live, rows, 0.0)
                peer = owner[r * KEY_VALUE_HEADS + h]
                lanes = slice(part * HEAD_SIZE, (part + 1) * HEAD_SIZE)
                for b in range(2):
                    picked = scratch[pl.ds(b, count_rows // 2, stride=2), :]
                    out[peer * 2 + b, :, lanes] = picked.astype(jnp.bfloat16)


def outgoing_rows(place, lengths, owner, total, came, tables):
    count_rows = total.shape[0] // lengths.shape[0]
    out = (owner.shape[0] * 2, count_rows // 2, 2 * HEAD_SIZE)
    return pl.pallas_call(
        rows_kernel,
        in_specs=[SMEM_REF] * 3 + [VMEM_REF] * 8,
        out_specs=VMEM_REF,
        out_shape=jax.ShapeDtypeStruct(out, jnp.bfloat16),
        scratch_shapes=[pltpu.VMEM((count_rows, HEAD_SIZE), jnp.float32)],
        compiler_params=SMALL,
        cost_estimate=cost(1000, 1000),
        name="cache_rows",
    )(place, lengths, owner, total, came, *tables)


def decode_kernel(place, lengths, owner, cache, dec_query, dec_key, dec_value, *refs):
    tables, out = refs[:4], refs[4]
    peer, block = place[2] // 2, place[2] % 2
    length = lengths[0]
    for pair in range(owner.shape[0]):
        length = jnp.where(owner[pair] == peer, lengths[pair // KEY_VALUE_HEADS], length)
    cosine, sine = turned_by(length, tables, tables[2][:STEPS], tables[3][:STEPS])

    def turned(rows):
        return rotated(rows.astype(jnp.float32), cosine, sine)

    def padded(rows):
        return jnp.concatenate([rows, jnp.zeros((16 - STEPS, HEAD_SIZE), jnp.float32)], 0)

    raw = dec_query[peer]
    heads = [raw[:, j * HEAD_SIZE : (j + 1) * HEAD_SIZE] for j in range(QPK)]
    query = jnp.concatenate([turned(head) for head in heads], 0).astype(jnp.bfloat16)
    new_keys = padded(turned(dec_key[peer])).astype(jnp.bfloat16)
    new_value = padded(dec_value[peer].astype(jnp.float32)).astype(jnp.bfloat16)
    contract = (((1,), (1,)), ((), ()))
    scale = 1.0 / HEAD_SIZE**0.5
    old = lax.dot_general(
        query, cache[:, :HEAD_SIZE], contract, preferred_element_type=jnp.float32
    )
    slot = lax.broadcasted_iota(jnp.int32, old.shape, 1) * 2 + block
    old = jnp.where(slot < length, old * scale, -1e30)
    new = lax.dot_general(query, new_keys, contract, preferred_element_type=jnp.float32)
    step = lax.broadcasted_iota(jnp.int32, new.shape, 0) % STEPS
    token = lax.broadcasted_iota(jnp.int32, new.shape, 1)
    new = jnp.where((token <= step) & (block == 0), new * scale, -1e30)
    top = jnp.maximum(jnp.max(old, 1, keepdims=True), jnp.max(new, 1, keepdims=True))
    old, new = jnp.exp(old - top), jnp.exp(new - top)
    total = jnp.sum(old, 1, keepdims=True) + jnp.sum(new, 1, keepdims=True)
    sums = jnp.dot(
        old.astype(jnp.bfloat16), cache[:, HEAD_SIZE:], preferred_element_type=jnp.float32
    )
    out[:, :HEAD_SIZE] = sums + jnp.dot(
        new.astype(jnp.bfloat16), new_value, preferred_element_type=jnp.float32
    )
    half = (QPK * STEPS, HEAD_SIZE // 2)
    out[:, HEAD_SIZE : HEAD_SIZE + half[1]] = jnp.broadcast_to(top, half)
    out[:, HEAD_SIZE + half[1] :] = jnp.broadcast_to(total, half)


def copied(cache):
    def kernel(source, out, sem):
        fetch(source, out, sem.at[0]).wait()

    return pl.pallas_call(
        kernel,
        in_specs=[VMEM_REF],
        out_specs=ANY_REF,
        out_shape=jax.ShapeDtypeStruct(cache.shape, cache.dtype),
        scratch_shapes=[pltpu.SemaphoreType.DMA((1,))],
        compiler_params=SMALL,
        cost_estimate=cost(1000, 1000),
        name="copied",
    )(cache)


def decoded(place, lengths, owner, cache, dec_query, dec_key, dec_value, tables):
    mine = pl.pallas_call(
        decode_kernel,
        in_specs=[SMEM_REF] * 3 + [VMEM_REF] * 8,
        out_specs=VMEM_REF,
        out_shape=jax.ShapeDtypeStruct((STEPS * QPK, 2 * HEAD_SIZE), jnp.float32),
        compiler_params=SMALL,
        cost_estimate=cost(1000, 1000),
        name="decode",
    )(place, lengths, owner, cache, dec_query, dec_key, dec_value, *tables[:4])
    theirs = moved(mine, to_core)
    share = QPK // 2
    last = HEAD_SIZE + HEAD_SIZE // 2

    def heads(array):
        array = array.reshape(QPK, STEPS, 2 * HEAD_SIZE)
        array = lax.dynamic_slice_in_dim(array, place[2] % 2 * share, share, 0)
        return array[..., :HEAD_SIZE], array[..., HEAD_SIZE : HEAD_SIZE + 1], array[..., last : last + 1]

    sums_a, top_a, total_a = heads(mine)
    sums_b, top_b, total_b = heads(theirs)
    top = jnp.maximum(top_a, top_b)
    scale_a, scale_b = jnp.exp(top_a - top), jnp.exp(top_b - top)
    value = (sums_a * scale_a + sums_b * scale_b) / (total_a * scale_a + total_b * scale_b)
    return jnp.transpose(value, (1, 0, 2)).reshape(STEPS, share * HEAD_SIZE).astype(jnp.bfloat16)


HERE, THERE = 3, 7


def body(hidden, key_weight, value_weight, lengths, owner, dec_query, dec_key, dec_value):
    count_requests, count_rows, width = hidden.shape
    device_id = lax.axis_index("seq")
    group_id = lax.axis_index("groups")
    seq = lax.axis_size("seq")
    planned = seq == 16 and lax.axis_size("groups") == 2
    decode_peers = count_requests * KEY_VALUE_HEADS
    split_point = seq // decode_peers
    tree_levels = split_point.bit_length() - 1
    rows_per_peer = count_rows // split_point
    positions = device_id * count_rows + jnp.arange(count_rows, dtype=jnp.int32)
    total_rows = count_requests * count_rows
    flat = hidden.reshape(total_rows, width)
    if planned:
        core = device_id % 2
        z, y = device_id // 4, device_id // 2 % 2
        layers = [z, z ^ 1, jnp.where(z < 2, 2, 1), jnp.where(z < 2, 3, 0)]
        is_end = (z == 0) | (z == 3)
        place = [group_id, core, device_id]
        place += [layer * 2 + y for layer in layers]
        place += [layer * 2 + 1 - y for layer in layers]
        place = jnp.stack([jnp.asarray(entry, jnp.int32) for entry in place])
    else:
        widened = flat.astype(jnp.float32)
        normed = (
            widened * lax.rsqrt(jnp.mean(widened * widened, -1, keepdims=True) + 1e-05)
        ).astype(jnp.bfloat16)

        def project(weight):
            whole = lax.all_gather(weight, "seq", axis=0, tiled=True)
            return jnp.dot(normed, whole, preferred_element_type=jnp.float32)

    pair_ids = jnp.arange(decode_peers, dtype=jnp.int32)
    matches = owner[None, :] == pair_ids[:, None]
    inverse_order = jnp.sum(jnp.where(matches, pair_ids[None, :], 0), axis=1)
    live_rows = positions[None, :] < lengths[:, None]

    def handed_over(rows):
        rows = jnp.where(live_rows[:, :, None, None], rows, jnp.zeros_like(rows))
        pair_rows = jnp.transpose(rows, (0, 2, 1, 3)).reshape(decode_peers, count_rows, HEAD_SIZE)
        sorted_rows = pair_rows[inverse_order].reshape(
            decode_peers, rows_per_peer, split_point, HEAD_SIZE
        )
        outgoing = jnp.transpose(sorted_rows, (0, 2, 1, 3)).reshape(
            decode_peers * split_point, rows_per_peer, HEAD_SIZE
        )
        return lax.all_to_all(outgoing, "seq", split_axis=0, concat_axis=1, tiled=True)[0]

    if planned:
        depth = key_weight.shape[0] // 2

        def half_block(first):
            halves = [
                lax.dynamic_slice_in_dim(weight, first, depth, 0)
                for weight in (key_weight, value_weight)
            ]
            return jnp.concatenate(halves, 1)

        raw = moved(flat, to_core)
        sent = half_block(group_id * depth)
        tables = turn_tables(count_rows * seq + STEPS, count_rows)
        near = moved(sent, to_pair)
        middle = moved(sent, to_middle)
        beyond = moved(sent, to_next)
        across = moved(sent, to_row)
        rest = half_block(depth - group_id * depth)
        rows = (near, across, raw, rest)
        near_y = moved(after(near, *rows), to_row)
        across_x = moved(after(across, *rows), to_group)
        mine, other = prepared(place, after(flat, *rows), raw, seq // 2)
        far = moved(after(beyond, middle, mine), to_end)
        block_b = after(jnp.where(is_end, beyond, middle), near_y, across_x, mine)
        block_yb = moved(block_b, to_row)
        block_xb = moved(block_b, to_group)
        layers, rows = (far, near_y), (block_yb, block_xb, far)
        near_rest = moved(after(rest, *layers), to_pair)
        block_c = jnp.where(is_end, after(far, *rows), beyond)
        block_xc = moved(block_c, to_group)
        block_yc = moved(block_c, to_row)
        pieces = [(HERE, 0, sent), (HERE, 1, rest), (THERE, 0, across)]
        pieces += [(THERE, 1, across_x), (HERE + 1, 0, near), (THERE + 1, 0, near_y)]
        totals = product(place, after(mine, block_c), other, pieces, (), 3)
        layers, rows = (near_rest, block_yb, totals[0]), (block_xc, block_yc, near_rest, totals[0])
        end_a = moved(after(across_x, *layers), to_pair)
        ends = [moved(after(block_yb, *rows), to_group), moved(after(block_xc, *rows), to_row)]
        pieces = [(HERE + 2, 0, block_b), (HERE + 2, 1, block_xb), (THERE + 2, 0, block_yb)]
        pieces += [(HERE + 3, 0, block_c), (HERE + 1, 1, near_rest)]
        pieces += [(HERE + 3, 1, block_xc), (THERE + 3, 0, block_yc)]
        totals = product(place, after(mine, *rows), other, pieces, totals, 7)
        came = (end_a, *ends, *totals)
        pieces = [(THERE + 1, 1, end_a), (THERE + 2, 1, ends[0]), (THERE + 3, 1, ends[1])]
        total, given = product(place, after(mine, *came), other, pieces, totals, 3)
        outgoing = outgoing_rows(place, lengths, owner, total, moved(given, to_core), tables)
        incoming = lax.all_to_all(outgoing, "seq", split_axis=0, concat_axis=1, tiled=True)
        attended = decoded(
            place, lengths, owner, incoming[0], dec_query, dec_key, dec_value, tables
        )
        return (copied(incoming[0])[None], attended)
    else:
        cosine, sine_part = rope_table(positions, HEAD_SIZE)
        shape = (count_requests, count_rows, KEY_VALUE_HEADS, HEAD_SIZE)
        unrotated_key = project(key_weight).reshape(shape)
        key_rows = rotate(
            unrotated_key, cosine[:, None, :], sine_part[:, None, :]
        ).astype(jnp.bfloat16)
        cache_keys = handed_over(key_rows)
        cache_values = handed_over(project(value_weight).astype(jnp.bfloat16).reshape(shape))
    slot_count = cache_keys.shape[0]
    decode_peer = device_id // split_point
    block = device_id % split_point
    source_pair = jnp.sum(jnp.where(owner == decode_peer, pair_ids, 0))
    source_request = source_pair // KEY_VALUE_HEADS
    length = jnp.sum(
        jnp.where(jnp.arange(count_requests, dtype=jnp.int32) == source_request, lengths, 0)
    )
    query = lax.dynamic_index_in_dim(dec_query, decode_peer, 0, keepdims=False)
    new_key = lax.dynamic_index_in_dim(dec_key, decode_peer, 0, keepdims=False)
    new_value = lax.dynamic_index_in_dim(dec_value, decode_peer, 0, keepdims=False)
    step_pos = length + jnp.arange(STEPS, dtype=jnp.int32)
    step_cos, step_sin = rope_table(step_pos, HEAD_SIZE)
    query_rot = rotate(
        query.astype(jnp.float32).reshape(STEPS, QPK, HEAD_SIZE),
        step_cos[:, None, :],
        step_sin[:, None, :],
    ).astype(jnp.bfloat16)
    new_keys = rotate(new_key.astype(jnp.float32), step_cos, step_sin).astype(jnp.bfloat16)
    score_scale = 1.0 / HEAD_SIZE**0.5
    old_scores = (
        jnp.einsum(
            "sjd,id->sji", query_rot, cache_keys, preferred_element_type=jnp.float32
        )
        * score_scale
    )
    new_scores = (
        jnp.einsum("sjd,td->sjt", query_rot, new_keys, preferred_element_type=jnp.float32)
        * score_scale
    )
    slot_ids = jnp.arange(slot_count, dtype=jnp.int32) * split_point + block
    old_live = slot_ids < length
    new_live = (jnp.arange(STEPS)[None, :] <= jnp.arange(STEPS)[:, None]) & (block == 0)
    old_scores = jnp.where(old_live[None, None, :], old_scores, -1e30)
    new_scores = jnp.where(new_live[:, None, :], new_scores, -1e30)
    row_max = jnp.maximum(jnp.max(old_scores, -1), jnp.max(new_scores, -1))
    for bit in range(tree_levels):
        row_max = jnp.maximum(row_max, swapped(row_max, "seq", bit))
    old_exp = jnp.exp(old_scores - row_max[..., None])
    new_exp = jnp.exp(new_scores - row_max[..., None])
    denom = jnp.sum(old_exp, -1) + jnp.sum(new_exp, -1)
    for bit in range(tree_levels):
        denom = denom + swapped(denom, "seq", bit)
    old_probs = (old_exp / denom[..., None]).astype(jnp.bfloat16)
    new_probs = (new_exp / denom[..., None]).astype(jnp.bfloat16)
    partial_sum = jnp.einsum(
        "sji,id->sjd", old_probs, cache_values, preferred_element_type=jnp.float32
    )
    partial_sum = partial_sum + jnp.einsum(
        "sjt,td->sjd", new_probs, new_value, preferred_element_type=jnp.float32
    )
    flat_rows = partial_sum.reshape(STEPS, QPK * HEAD_SIZE)
    for bit in range(tree_levels):
        flat_rows = flat_rows + swapped(flat_rows, "seq", bit)
    share = flat_rows.shape[1] // split_point
    mine = lax.dynamic_slice_in_dim(flat_rows, block * share, share, 1)
    cache = jnp.concatenate([cache_keys, cache_values], 1)[None]
    return (cache, mine.astype(jnp.bfloat16))


def solution(mesh):
    placed = (
        P("groups", "seq", None),
        P("seq", None),
        P("seq", None),
        P("groups"),
        P("groups"),
        P("groups", None, None),
        P("groups", None, None),
        P("groups", None, None),
    )
    return jax.shard_map(
        body,
        mesh=mesh,
        in_specs=placed,
        out_specs=(P(("groups", "seq"), None, None), P("groups", "seq")),
        check_vma=False,
    )
```

```python
import functools

import jax
import jax.numpy as jnp
import numpy as np
from jax import lax
from jax.experimental import pallas as pl
from jax.experimental.pallas import tpu as pltpu
from jax.sharding import PartitionSpec as P

HEAD_SIZE = 128
KEY_VALUE_HEADS = 4
QPK = 8
STEPS = 4


ROPE_BASE = 500000.0


def swapped(block, axis, bit):
    count = lax.axis_size(axis)
    route = []
    for low in range(count):
        high = low | 1 << bit
        if high != low and high < count:
            route += [(low, high), (high, low)]
    return lax.ppermute(block, axis, route)


def rope_table(positions, head_dim):
    freq = ROPE_BASE ** (-(np.arange(head_dim // 2, dtype=np.float64) * 2.0) / head_dim)
    angle = positions.astype(jnp.float32)[:, None] * jnp.asarray(freq, jnp.float32)[None, :]
    return (jnp.cos(angle), jnp.sin(angle))


def rotate(values_in, cosine, sine_part):
    half_dim = values_in.shape[-1] // 2
    lower_half = values_in[..., :half_dim]
    upper_half = values_in[..., half_dim:]
    return jnp.concatenate(
        [
            lower_half * cosine - upper_half * sine_part,
            upper_half * cosine + lower_half * sine_part,
        ],
        -1,
    )


def spread(count):
    side = 1
    while side * side < count:
        side *= 2
    return (side, count // side)


def moved(block, rule):
    groups, seq = lax.axis_size("groups"), lax.axis_size("seq")
    low = spread(seq // 2)[1]
    route = []
    for g in range(groups):
        for s in range(seq):
            place = rule(g, s // 2 // low, s // 2 % low, s % 2)
            if place is not None:
                tg, tz, ty, tc = place
                route.append((g * seq + s, tg * seq + (tz * low + ty) * 2 + tc))
    return lax.ppermute(block, ("groups", "seq"), route)


def to_core(g, z, y, c):
    return (g, z, y, 1 - c)


def to_row(g, z, y, c):
    return (g, z, 1 - y, c)


def to_group(g, z, y, c):
    return (1 - g, z, y, c)


def to_pair(g, z, y, c):
    return (g, z ^ 1, y, c)


def to_middle(g, z, y, c):
    return (g, 3 - z, y, c) if z in (1, 2) else None


def to_end(g, z, y, c):
    return (g, 0 if z == 1 else 3, y, c) if z in (1, 2) else None


VMEM_REF = pl.BlockSpec(memory_space=pltpu.VMEM)
SMEM_REF = pl.BlockSpec(memory_space=pltpu.SMEM)
ANY_REF = pl.BlockSpec(memory_space=pl.ANY)
PARAMS = pltpu.CompilerParams(vmem_limit_bytes=20 << 20)
LARGE = pltpu.CompilerParams(vmem_limit_bytes=58 << 20)
SMALL = pltpu.CompilerParams(vmem_limit_bytes=16 << 20)


def cost(flops, moved_bytes):
    return pl.CostEstimate(flops=flops, bytes_accessed=moved_bytes, transcendentals=0)


def fetch(source, target, sem):
    copy = pltpu.make_async_copy(source, target, sem)
    copy.start()
    return copy


def prepare_kernel(place, *refs):
    depth = refs[2].shape[2]
    for rows_in, target in zip(refs[:2], refs[2:]):
        rows, width = rows_in.shape
        square = jnp.zeros((rows, depth), jnp.float32)
        for first in range(0, width, depth):
            part = rows_in[:, first : first + depth].astype(jnp.float32)
            square += part * part
        scale = lax.rsqrt(jnp.sum(square, -1, keepdims=True) / width + 1e-05)
        for core in range(2):

            @pl.when(place[1] == core)
            def _():
                for k in range(width // (2 * depth)):
                    first = (k // 2 * 4 + core * 2 + k % 2) * depth
                    part = rows_in[:, first : first + depth].astype(jnp.float32)
                    target[k] = (part * scale).astype(jnp.bfloat16)


def prepared(place, mine, other, blocks):
    rows, width = mine.shape
    depth = width // (4 * blocks)
    tile = 80 if rows % 80 == 0 else rows
    out = jax.ShapeDtypeStruct((2 * blocks, rows, depth), jnp.bfloat16)
    taken = pl.BlockSpec((tile, width), lambda i, place: (i, 0))
    given = pl.BlockSpec((2 * blocks, tile, depth), lambda i, place: (0, i, 0))
    return pl.pallas_call(
        prepare_kernel,
        grid_spec=pltpu.PrefetchScalarGridSpec(
            num_scalar_prefetch=1,
            grid=(rows // tile,),
            in_specs=[taken, taken],
            out_specs=[given, given],
        ),
        out_shape=[out, out],
        compiler_params=LARGE,
        cost_estimate=cost(1000, 1000),
        name="normed_halves",
    )(place, mine, other)


def after(value, *events):
    return lax.optimization_barrier((value, *events))[0]


def half_index(place, entry, kind):
    half = {0: place[0], 1: 1 - place[0], 2: 0, 3: 1}[kind]
    return place[entry] * 2 + half


def product_kernel(plan, group, with_total, place, mine, other, *refs):
    count = len(plan)
    outs = refs[-7:-5]
    left, right, total, sems, total_sems = refs[-5:]
    rows, depth = mine.shape[1], mine.shape[2]
    waits = []
    for k, (entry, kind) in enumerate(plan):
        area = pl.ds((k % group) * depth, depth)
        slot = k // group
        index = half_index(place, entry, kind)
        sources = (mine.at[index], other.at[index], refs[k])
        targets = (left.at[slot, 0, :, area], left.at[slot, 1, :, area], right.at[slot, area])
        waits.append(
            [fetch(a, b, sems.at[3 * k + i]) for i, (a, b) in enumerate(zip(sources, targets))]
        )
    carried = [
        fetch(ref, total.at[pl.ds(k * rows, rows)], total_sems.at[k])
        for k, ref in enumerate(refs[count : count + 2 * with_total])
    ]
    for slot in range(count // group):
        for copies in waits[slot * group : (slot + 1) * group]:
            for copy in copies:
                copy.wait()
        stacked = left[slot].reshape(2 * rows, group * depth)
        value = jnp.dot(stacked, right[slot], preferred_element_type=jnp.float32)
        if slot == 0:
            for copy in carried:
                copy.wait()
        if slot or with_total:
            value += total[...]
        if slot + 1 < count // group:
            total[...] = value
        else:
            outs[0][...] = value[:rows]
            outs[1][...] = value[rows:]


def product(place, mine, other, pieces, totals, group, moved_bytes=1000):
    _, rows, depth = mine.shape
    columns = pieces[0][2].shape[1]
    plan = [(entry, kind) for entry, kind, _ in pieces]
    count = len(plan)
    out = jax.ShapeDtypeStruct((rows, columns), jnp.float32)
    return pl.pallas_call(
        functools.partial(product_kernel, plan, group, bool(totals)),
        in_specs=[SMEM_REF] + [ANY_REF] * (2 + count + len(totals)),
        out_specs=[VMEM_REF] * 2,
        out_shape=[out] * 2,
        scratch_shapes=[
            pltpu.VMEM((count // group, 2, rows, group * depth), mine.dtype),
            pltpu.VMEM((count // group, group * depth, columns), mine.dtype),
            pltpu.VMEM((2 * rows, columns), jnp.float32),
            pltpu.SemaphoreType.DMA((3 * count,)),
            pltpu.SemaphoreType.DMA((2,)),
        ],
        compiler_params=PARAMS,
        cost_estimate=cost(1000, moved_bytes),
        name="add_product",
    )(place, mine, other, *[array for _, _, array in pieces], *totals)


LOW = 64


def turn_tables(positions, rows):
    freq = ROPE_BASE ** (-(np.arange(HEAD_SIZE // 2) * 2.0) / HEAD_SIZE)
    tables = []
    for places in (np.arange(0, positions, LOW), np.arange(LOW), np.arange(rows)):
        angle = places[:, None] * freq[None, :]
        tables.append(np.concatenate([np.cos(angle), np.cos(angle)], 1))
        tables.append(np.concatenate([-np.sin(angle), np.sin(angle)], 1))
    return [jnp.asarray(table, jnp.float32) for table in tables]


def turned_by(start, tables, cosine, sine):
    high, low = pl.ds(start // LOW, 1), pl.ds(start % LOW, 1)
    for cos_row, sin_row in (
        (tables[0][high], tables[1][high]),
        (tables[2][low], tables[3][low]),
    ):
        cosine, sine = cosine * cos_row - sine * sin_row, sine * cos_row + cosine * sin_row
    return cosine, sine


def rotated(rows, cosine, sine):
    half = HEAD_SIZE // 2
    return rows * cosine + jnp.concatenate([rows[:, half:], rows[:, :half]], 1) * sine


def rows_kernel(place, lengths, owner, *refs):
    total, came, *tables, out, scratch = refs
    columns = total.shape[1] // 2
    count_requests, count_rows = lengths.shape[0], scratch.shape[0]
    cosine, sine = turned_by(place[2] * count_rows, tables, tables[4][...], tables[5][...])
    index = place[2] * count_rows + lax.broadcasted_iota(jnp.int32, scratch.shape, 0)
    for r in range(count_requests):
        live = index < lengths[r]
        for h in range(KEY_VALUE_HEADS):
            for part in range(2):
                first = part * columns + h * HEAD_SIZE
                area = (
                    slice(r * count_rows, (r + 1) * count_rows),
                    slice(first, first + HEAD_SIZE),
                )
                rows = total[area] + came[area]
                if part == 0:
                    rows = rotated(rows, cosine, sine)
                scratch[...] = jnp.where(live, rows, 0.0)
                peer = owner[r * KEY_VALUE_HEADS + h]
                lanes = slice(part * HEAD_SIZE, (part + 1) * HEAD_SIZE)
                for b in range(2):
                    picked = scratch[pl.ds(b, count_rows // 2, stride=2), :]
                    out[peer * 2 + b, :, lanes] = picked.astype(jnp.bfloat16)


def outgoing_rows(place, lengths, owner, total, came, tables):
    count_rows = total.shape[0] // lengths.shape[0]
    out = (owner.shape[0] * 2, count_rows // 2, 2 * HEAD_SIZE)
    return pl.pallas_call(
        rows_kernel,
        in_specs=[SMEM_REF] * 3 + [VMEM_REF] * 8,
        out_specs=VMEM_REF,
        out_shape=jax.ShapeDtypeStruct(out, jnp.bfloat16),
        scratch_shapes=[pltpu.VMEM((count_rows, HEAD_SIZE), jnp.float32)],
        compiler_params=SMALL,
        cost_estimate=cost(1000, 1000),
        name="cache_rows",
    )(place, lengths, owner, total, came, *tables)


def decode_kernel(place, lengths, owner, cache, dec_query, dec_key, dec_value, *refs):
    tables, out = refs[:4], refs[4]
    peer, block = place[2] // 2, place[2] % 2
    length = lengths[0]
    for pair in range(owner.shape[0]):
        length = jnp.where(owner[pair] == peer, lengths[pair // KEY_VALUE_HEADS], length)
    cosine, sine = turned_by(length, tables, tables[2][:STEPS], tables[3][:STEPS])

    def turned(rows):
        return rotated(rows.astype(jnp.float32), cosine, sine)

    def padded(rows):
        return jnp.concatenate([rows, jnp.zeros((16 - STEPS, HEAD_SIZE), jnp.float32)], 0)

    raw = dec_query[peer]
    heads = [raw[:, j * HEAD_SIZE : (j + 1) * HEAD_SIZE] for j in range(QPK)]
    query = jnp.concatenate([turned(head) for head in heads], 0).astype(jnp.bfloat16)
    new_keys = padded(turned(dec_key[peer])).astype(jnp.bfloat16)
    new_value = padded(dec_value[peer].astype(jnp.float32)).astype(jnp.bfloat16)
    contract = (((1,), (1,)), ((), ()))
    scale = 1.0 / HEAD_SIZE**0.5
    old = lax.dot_general(
        query, cache[:, :HEAD_SIZE], contract, preferred_element_type=jnp.float32
    )
    slot = lax.broadcasted_iota(jnp.int32, old.shape, 1) * 2 + block
    old = jnp.where(slot < length, old * scale, -1e30)
    new = lax.dot_general(query, new_keys, contract, preferred_element_type=jnp.float32)
    step = lax.broadcasted_iota(jnp.int32, new.shape, 0) % STEPS
    token = lax.broadcasted_iota(jnp.int32, new.shape, 1)
    new = jnp.where((token <= step) & (block == 0), new * scale, -1e30)
    top = jnp.maximum(jnp.max(old, 1, keepdims=True), jnp.max(new, 1, keepdims=True))
    old, new = jnp.exp(old - top), jnp.exp(new - top)
    total = jnp.sum(old, 1, keepdims=True) + jnp.sum(new, 1, keepdims=True)
    sums = jnp.dot(
        old.astype(jnp.bfloat16), cache[:, HEAD_SIZE:], preferred_element_type=jnp.float32
    )
    out[:, :HEAD_SIZE] = sums + jnp.dot(
        new.astype(jnp.bfloat16), new_value, preferred_element_type=jnp.float32
    )
    half = (QPK * STEPS, HEAD_SIZE // 2)
    out[:, HEAD_SIZE : HEAD_SIZE + half[1]] = jnp.broadcast_to(top, half)
    out[:, HEAD_SIZE + half[1] :] = jnp.broadcast_to(total, half)


def joined_kernel(place, mine, theirs, out):
    share = QPK // 2
    area = pl.ds(place[2] % 2 * share * STEPS, share * STEPS)
    last = HEAD_SIZE + HEAD_SIZE // 2
    sums, tops, totals = [], [], []
    for ref in (mine, theirs):
        sums.append(ref[area, :HEAD_SIZE])
        tops.append(ref[area, HEAD_SIZE : HEAD_SIZE + 1])
        totals.append(ref[area, last : last + 1])
    top = jnp.maximum(tops[0], tops[1])
    scales = [jnp.exp(one - top) for one in tops]
    total = totals[0] * scales[0] + totals[1] * scales[1]
    value = (sums[0] * scales[0] + sums[1] * scales[1]) / total
    for j in range(share):
        rows = value[j * STEPS : (j + 1) * STEPS]
        out[:, j * HEAD_SIZE : (j + 1) * HEAD_SIZE] = rows.astype(jnp.bfloat16)


def copied(cache):
    def kernel(source, out, sem):
        fetch(source, out, sem.at[0]).wait()

    return pl.pallas_call(
        kernel,
        in_specs=[VMEM_REF],
        out_specs=ANY_REF,
        out_shape=jax.ShapeDtypeStruct(cache.shape, cache.dtype),
        scratch_shapes=[pltpu.SemaphoreType.DMA((1,))],
        compiler_params=SMALL,
        cost_estimate=cost(1000, 1000),
        name="copied",
    )(cache)


def decoded(place, lengths, owner, cache, dec_query, dec_key, dec_value, tables):
    mine = pl.pallas_call(
        decode_kernel,
        in_specs=[SMEM_REF] * 3 + [VMEM_REF] * 8,
        out_specs=VMEM_REF,
        out_shape=jax.ShapeDtypeStruct((STEPS * QPK, 2 * HEAD_SIZE), jnp.float32),
        compiler_params=SMALL,
        cost_estimate=cost(1000, 1000),
        name="decode",
    )(place, lengths, owner, cache, dec_query, dec_key, dec_value, *tables[:4])
    return pl.pallas_call(
        joined_kernel,
        in_specs=[SMEM_REF] + [VMEM_REF] * 2,
        out_specs=VMEM_REF,
        out_shape=jax.ShapeDtypeStruct((STEPS, QPK // 2 * HEAD_SIZE), jnp.bfloat16),
        compiler_params=SMALL,
        cost_estimate=cost(1000, 1000),
        name="joined",
    )(place, mine, moved(mine, to_core))


HERE, THERE = 3, 7


def body(hidden, key_weight, value_weight, lengths, owner, dec_query, dec_key, dec_value):
    count_requests, count_rows, width = hidden.shape
    device_id = lax.axis_index("seq")
    group_id = lax.axis_index("groups")
    seq = lax.axis_size("seq")
    planned = seq == 16 and lax.axis_size("groups") == 2
    decode_peers = count_requests * KEY_VALUE_HEADS
    split_point = seq // decode_peers
    tree_levels = split_point.bit_length() - 1
    rows_per_peer = count_rows // split_point
    positions = device_id * count_rows + jnp.arange(count_rows, dtype=jnp.int32)
    total_rows = count_requests * count_rows
    flat = hidden.reshape(total_rows, width)
    if planned:
        core = device_id % 2
        z, y = device_id // 4, device_id // 2 % 2
        layers = [z, z ^ 1, jnp.where(z < 2, 2, 1), jnp.where(z < 2, 3, 0)]
        is_end = (z == 0) | (z == 3)
        place = [group_id, core, device_id]
        place += [layer * 2 + y for layer in layers]
        place += [layer * 2 + 1 - y for layer in layers]
        place = jnp.stack([jnp.asarray(entry, jnp.int32) for entry in place])
    else:
        widened = flat.astype(jnp.float32)
        normed = (
            widened * lax.rsqrt(jnp.mean(widened * widened, -1, keepdims=True) + 1e-05)
        ).astype(jnp.bfloat16)

        def project(weight):
            whole = lax.all_gather(weight, "seq", axis=0, tiled=True)
            return jnp.dot(normed, whole, preferred_element_type=jnp.float32)

    pair_ids = jnp.arange(decode_peers, dtype=jnp.int32)
    matches = owner[None, :] == pair_ids[:, None]
    inverse_order = jnp.sum(jnp.where(matches, pair_ids[None, :], 0), axis=1)
    live_rows = positions[None, :] < lengths[:, None]

    def handed_over(rows):
        rows = jnp.where(live_rows[:, :, None, None], rows, jnp.zeros_like(rows))
        pair_rows = jnp.transpose(rows, (0, 2, 1, 3)).reshape(decode_peers, count_rows, HEAD_SIZE)
        sorted_rows = pair_rows[inverse_order].reshape(
            decode_peers, rows_per_peer, split_point, HEAD_SIZE
        )
        outgoing = jnp.transpose(sorted_rows, (0, 2, 1, 3)).reshape(
            decode_peers * split_point, rows_per_peer, HEAD_SIZE
        )
        return lax.all_to_all(outgoing, "seq", split_axis=0, concat_axis=1, tiled=True)[0]

    if planned:
        depth = key_weight.shape[0] // 2

        def half_block(first):
            halves = [
                lax.dynamic_slice_in_dim(weight, first, depth, 0)
                for weight in (key_weight, value_weight)
            ]
            return jnp.concatenate(halves, 1)

        raw = moved(flat, to_core)
        sent = half_block(group_id * depth)
        tables = turn_tables(count_rows * seq + STEPS, count_rows)
        near = moved(sent, to_pair)
        middle = moved(sent, to_middle)
        across = moved(sent, to_row)
        rest = half_block(depth - group_id * depth)
        layers, rows = (near, middle), (near, middle, across, raw, rest)
        passed = moved(after(middle, *layers), to_end)
        middle_c = moved(near, to_middle)
        near_y = moved(after(near, across), to_row)
        across_x = moved(across, to_group)
        mine, other = prepared(place, after(flat, *rows), raw, seq // 2)
        layers, rows = (passed, middle_c, mine), (near_y, across_x, mine, passed)
        far = moved(after(middle_c, *layers), to_end)
        block_b = jnp.where(is_end, after(passed, *rows), middle)
        block_yb = moved(block_b, to_row)
        block_xb = moved(block_b, to_group)
        layers, rows = (far, near_y), (block_yb, block_xb, far)
        near_rest = moved(after(rest, *layers), to_pair)
        block_c = jnp.where(is_end, after(far, *rows), middle_c)
        block_xc = moved(block_c, to_group)
        block_yc = moved(block_c, to_row)
        pieces = [(HERE, 0, sent), (HERE, 1, rest), (THERE, 0, across)]
        pieces += [(THERE, 1, across_x), (HERE + 1, 0, near), (THERE + 1, 0, near_y)]
        totals = product(place, after(mine, block_c), other, pieces, (), 3)
        layers, rows = (near_rest, block_yb, totals[0]), (block_xc, block_yc, near_rest, totals[0])
        end_a = moved(after(across_x, *layers), to_pair)
        ends = [moved(after(block_yb, *rows), to_group), moved(after(block_xc, *rows), to_row)]
        pieces = [(HERE + 2, 0, block_b), (HERE + 2, 1, block_xb), (THERE + 2, 0, block_yb)]
        pieces += [(HERE + 3, 0, block_c), (HERE + 1, 1, near_rest)]
        pieces += [(HERE + 3, 1, block_xc), (THERE + 3, 0, block_yc)]
        totals = product(place, after(mine, *rows), other, pieces, totals, 7)
        came = (end_a, *ends, *totals)
        pieces = [(THERE + 1, 1, end_a), (THERE + 2, 1, ends[0]), (THERE + 3, 1, ends[1])]
        total, given = product(place, after(mine, *came), other, pieces, totals, 3)
        outgoing = outgoing_rows(place, lengths, owner, total, moved(given, to_core), tables)
        incoming = lax.all_to_all(outgoing, "seq", split_axis=0, concat_axis=1, tiled=True)
        attended = decoded(
            place, lengths, owner, incoming[0], dec_query, dec_key, dec_value, tables
        )
        return (copied(incoming[0])[None], attended)
    else:
        cosine, sine_part = rope_table(positions, HEAD_SIZE)
        shape = (count_requests, count_rows, KEY_VALUE_HEADS, HEAD_SIZE)
        unrotated_key = project(key_weight).reshape(shape)
        key_rows = rotate(
            unrotated_key, cosine[:, None, :], sine_part[:, None, :]
        ).astype(jnp.bfloat16)
        cache_keys = handed_over(key_rows)
        cache_values = handed_over(project(value_weight).astype(jnp.bfloat16).reshape(shape))
    slot_count = cache_keys.shape[0]
    decode_peer = device_id // split_point
    block = device_id % split_point
    source_pair = jnp.sum(jnp.where(owner == decode_peer, pair_ids, 0))
    source_request = source_pair // KEY_VALUE_HEADS
    length = jnp.sum(
        jnp.where(jnp.arange(count_requests, dtype=jnp.int32) == source_request, lengths, 0)
    )
    query = lax.dynamic_index_in_dim(dec_query, decode_peer, 0, keepdims=False)
    new_key = lax.dynamic_index_in_dim(dec_key, decode_peer, 0, keepdims=False)
    new_value = lax.dynamic_index_in_dim(dec_value, decode_peer, 0, keepdims=False)
    step_pos = length + jnp.arange(STEPS, dtype=jnp.int32)
    step_cos, step_sin = rope_table(step_pos, HEAD_SIZE)
    query_rot = rotate(
        query.astype(jnp.float32).reshape(STEPS, QPK, HEAD_SIZE),
        step_cos[:, None, :],
        step_sin[:, None, :],
    ).astype(jnp.bfloat16)
    new_keys = rotate(new_key.astype(jnp.float32), step_cos, step_sin).astype(jnp.bfloat16)
    score_scale = 1.0 / HEAD_SIZE**0.5
    old_scores = (
        jnp.einsum(
            "sjd,id->sji", query_rot, cache_keys, preferred_element_type=jnp.float32
        )
        * score_scale
    )
    new_scores = (
        jnp.einsum("sjd,td->sjt", query_rot, new_keys, preferred_element_type=jnp.float32)
        * score_scale
    )
    slot_ids = jnp.arange(slot_count, dtype=jnp.int32) * split_point + block
    old_live = slot_ids < length
    new_live = (jnp.arange(STEPS)[None, :] <= jnp.arange(STEPS)[:, None]) & (block == 0)
    old_scores = jnp.where(old_live[None, None, :], old_scores, -1e30)
    new_scores = jnp.where(new_live[:, None, :], new_scores, -1e30)
    row_max = jnp.maximum(jnp.max(old_scores, -1), jnp.max(new_scores, -1))
    for bit in range(tree_levels):
        row_max = jnp.maximum(row_max, swapped(row_max, "seq", bit))
    old_exp = jnp.exp(old_scores - row_max[..., None])
    new_exp = jnp.exp(new_scores - row_max[..., None])
    denom = jnp.sum(old_exp, -1) + jnp.sum(new_exp, -1)
    for bit in range(tree_levels):
        denom = denom + swapped(denom, "seq", bit)
    old_probs = (old_exp / denom[..., None]).astype(jnp.bfloat16)
    new_probs = (new_exp / denom[..., None]).astype(jnp.bfloat16)
    partial_sum = jnp.einsum(
        "sji,id->sjd", old_probs, cache_values, preferred_element_type=jnp.float32
    )
    partial_sum = partial_sum + jnp.einsum(
        "sjt,td->sjd", new_probs, new_value, preferred_element_type=jnp.float32
    )
    flat_rows = partial_sum.reshape(STEPS, QPK * HEAD_SIZE)
    for bit in range(tree_levels):
        flat_rows = flat_rows + swapped(flat_rows, "seq", bit)
    share = flat_rows.shape[1] // split_point
    mine = lax.dynamic_slice_in_dim(flat_rows, block * share, share, 1)
    cache = jnp.concatenate([cache_keys, cache_values], 1)[None]
    return (cache, mine.astype(jnp.bfloat16))


def solution(mesh):
    placed = (
        P("groups", "seq", None),
        P("seq", None),
        P("seq", None),
        P("groups"),
        P("groups"),
        P("groups", None, None),
        P("groups", None, None),
        P("groups", None, None),
    )
    return jax.shard_map(
        body,
        mesh=mesh,
        in_specs=placed,
        out_specs=(P(("groups", "seq"), None, None), P("groups", "seq")),
        check_vma=False,
    )
```

```python
import functools

import jax
import jax.numpy as jnp
import numpy as np
from jax import lax
from jax.experimental import pallas as pl
from jax.experimental.pallas import tpu as pltpu
from jax.sharding import PartitionSpec as P

HEAD_SIZE = 128
KEY_VALUE_HEADS = 4
QPK = 8
STEPS = 4


ROPE_BASE = 500000.0


def swapped(block, axis, bit):
    count = lax.axis_size(axis)
    route = []
    for low in range(count):
        high = low | 1 << bit
        if high != low and high < count:
            route += [(low, high), (high, low)]
    return lax.ppermute(block, axis, route)


def rope_table(positions, head_dim):
    freq = ROPE_BASE ** (-(np.arange(head_dim // 2, dtype=np.float64) * 2.0) / head_dim)
    angle = positions.astype(jnp.float32)[:, None] * jnp.asarray(freq, jnp.float32)[None, :]
    return (jnp.cos(angle), jnp.sin(angle))


def rotate(values_in, cosine, sine_part):
    half_dim = values_in.shape[-1] // 2
    lower_half = values_in[..., :half_dim]
    upper_half = values_in[..., half_dim:]
    return jnp.concatenate(
        [
            lower_half * cosine - upper_half * sine_part,
            upper_half * cosine + lower_half * sine_part,
        ],
        -1,
    )


def spread(count):
    side = 1
    while side * side < count:
        side *= 2
    return (side, count // side)


def moved(block, rule):
    groups, seq = lax.axis_size("groups"), lax.axis_size("seq")
    low = spread(seq // 2)[1]
    route = []
    for g in range(groups):
        for s in range(seq):
            place = rule(g, s // 2 // low, s // 2 % low, s % 2)
            if place is not None:
                tg, tz, ty, tc = place
                route.append((g * seq + s, tg * seq + (tz * low + ty) * 2 + tc))
    return lax.ppermute(block, ("groups", "seq"), route)


def to_core(g, z, y, c):
    return (g, z, y, 1 - c)


def to_row(g, z, y, c):
    return (g, z, 1 - y, c)


def to_group(g, z, y, c):
    return (1 - g, z, y, c)


def to_pair(g, z, y, c):
    return (g, z ^ 1, y, c)


def to_middle(g, z, y, c):
    return (g, 3 - z, y, c) if z in (1, 2) else None


def to_end(g, z, y, c):
    return (g, 0 if z == 1 else 3, y, c) if z in (1, 2) else None


VMEM_REF = pl.BlockSpec(memory_space=pltpu.VMEM)
SMEM_REF = pl.BlockSpec(memory_space=pltpu.SMEM)
ANY_REF = pl.BlockSpec(memory_space=pl.ANY)
PARAMS = pltpu.CompilerParams(vmem_limit_bytes=20 << 20)
LARGE = pltpu.CompilerParams(vmem_limit_bytes=58 << 20)
SMALL = pltpu.CompilerParams(vmem_limit_bytes=16 << 20)


def cost(flops, moved_bytes):
    return pl.CostEstimate(flops=flops, bytes_accessed=moved_bytes, transcendentals=0)


def fetch(source, target, sem):
    copy = pltpu.make_async_copy(source, target, sem)
    copy.start()
    return copy


def prepare_kernel(place, *refs):
    depth = refs[2].shape[2]
    for rows_in, target in zip(refs[:2], refs[2:]):
        rows, width = rows_in.shape
        square = jnp.zeros((rows, depth), jnp.float32)
        for first in range(0, width, depth):
            part = rows_in[:, first : first + depth].astype(jnp.float32)
            square += part * part
        scale = lax.rsqrt(jnp.sum(square, -1, keepdims=True) / width + 1e-05)
        for core in range(2):

            @pl.when(place[1] == core)
            def _():
                for k in range(width // (2 * depth)):
                    first = (k // 2 * 4 + core * 2 + k % 2) * depth
                    part = rows_in[:, first : first + depth].astype(jnp.float32)
                    target[k] = (part * scale).astype(jnp.bfloat16)


def prepared(place, mine, other, blocks):
    rows, width = mine.shape
    depth = width // (4 * blocks)
    tile = 80 if rows % 80 == 0 else rows
    out = jax.ShapeDtypeStruct((2 * blocks, rows, depth), jnp.bfloat16)
    taken = pl.BlockSpec((tile, width), lambda i, place: (i, 0))
    given = pl.BlockSpec((2 * blocks, tile, depth), lambda i, place: (0, i, 0))
    return pl.pallas_call(
        prepare_kernel,
        grid_spec=pltpu.PrefetchScalarGridSpec(
            num_scalar_prefetch=1,
            grid=(rows // tile,),
            in_specs=[taken, taken],
            out_specs=[given, given],
        ),
        out_shape=[out, out],
        compiler_params=LARGE,
        cost_estimate=cost(1000, 1000),
        name="normed_halves",
    )(place, mine, other)


def after(value, *events):
    return lax.optimization_barrier((value, *events))[0]


def half_index(place, entry, kind):
    half = {0: place[0], 1: 1 - place[0], 2: 0, 3: 1}[kind]
    return place[entry] * 2 + half


def product_kernel(plan, group, with_total, place, mine, other, *refs):
    count = len(plan)
    outs = refs[-7:-5]
    left, right, total, sems, total_sems = refs[-5:]
    rows, depth = mine.shape[1], mine.shape[2]
    waits = []
    for k, (entry, kind) in enumerate(plan):
        area = pl.ds((k % group) * depth, depth)
        slot = k // group
        index = half_index(place, entry, kind)
        sources = (mine.at[index], other.at[index], refs[k])
        targets = (left.at[slot, 0, :, area], left.at[slot, 1, :, area], right.at[slot, area])
        waits.append(
            [fetch(a, b, sems.at[3 * k + i]) for i, (a, b) in enumerate(zip(sources, targets))]
        )
    carried = [
        fetch(ref, total.at[pl.ds(k * rows, rows)], total_sems.at[k])
        for k, ref in enumerate(refs[count : count + 2 * with_total])
    ]
    for slot in range(count // group):
        for copies in waits[slot * group : (slot + 1) * group]:
            for copy in copies:
                copy.wait()
        stacked = left[slot].reshape(2 * rows, group * depth)
        value = jnp.dot(stacked, right[slot], preferred_element_type=jnp.float32)
        if slot == 0:
            for copy in carried:
                copy.wait()
        if slot or with_total:
            value += total[...]
        if slot + 1 < count // group:
            total[...] = value
        else:
            outs[0][...] = value[:rows]
            outs[1][...] = value[rows:]


def product(place, mine, other, pieces, totals, group, moved_bytes=1000):
    _, rows, depth = mine.shape
    columns = pieces[0][2].shape[1]
    plan = [(entry, kind) for entry, kind, _ in pieces]
    count = len(plan)
    out = jax.ShapeDtypeStruct((rows, columns), jnp.float32)
    return pl.pallas_call(
        functools.partial(product_kernel, plan, group, bool(totals)),
        in_specs=[SMEM_REF] + [ANY_REF] * (2 + count + len(totals)),
        out_specs=[VMEM_REF] * 2,
        out_shape=[out] * 2,
        scratch_shapes=[
            pltpu.VMEM((count // group, 2, rows, group * depth), mine.dtype),
            pltpu.VMEM((count // group, group * depth, columns), mine.dtype),
            pltpu.VMEM((2 * rows, columns), jnp.float32),
            pltpu.SemaphoreType.DMA((3 * count,)),
            pltpu.SemaphoreType.DMA((2,)),
        ],
        compiler_params=PARAMS,
        cost_estimate=cost(1000, moved_bytes),
        name="add_product",
    )(place, mine, other, *[array for _, _, array in pieces], *totals)


LOW = 64


def turn_tables(positions, rows):
    freq = ROPE_BASE ** (-(np.arange(HEAD_SIZE // 2) * 2.0) / HEAD_SIZE)
    tables = []
    for places in (np.arange(0, positions, LOW), np.arange(LOW), np.arange(rows)):
        angle = places[:, None] * freq[None, :]
        tables.append(np.concatenate([np.cos(angle), np.cos(angle)], 1))
        tables.append(np.concatenate([-np.sin(angle), np.sin(angle)], 1))
    return [jnp.asarray(table, jnp.float32) for table in tables]


def turned_by(start, tables, cosine, sine):
    high, low = pl.ds(start // LOW, 1), pl.ds(start % LOW, 1)
    for cos_row, sin_row in (
        (tables[0][high], tables[1][high]),
        (tables[2][low], tables[3][low]),
    ):
        cosine, sine = cosine * cos_row - sine * sin_row, sine * cos_row + cosine * sin_row
    return cosine, sine


def rotated(rows, cosine, sine):
    half = HEAD_SIZE // 2
    return rows * cosine + jnp.concatenate([rows[:, half:], rows[:, :half]], 1) * sine


def rows_kernel(place, lengths, owner, *refs):
    total, came, *tables, out, scratch = refs
    columns = total.shape[1] // 2
    count_requests, count_rows = lengths.shape[0], scratch.shape[0]
    cosine, sine = turned_by(place[2] * count_rows, tables, tables[4][...], tables[5][...])
    index = place[2] * count_rows + lax.broadcasted_iota(jnp.int32, scratch.shape, 0)
    for r in range(count_requests):
        live = index < lengths[r]
        for h in range(KEY_VALUE_HEADS):
            for part in range(2):
                first = part * columns + h * HEAD_SIZE
                area = (
                    slice(r * count_rows, (r + 1) * count_rows),
                    slice(first, first + HEAD_SIZE),
                )
                rows = total[area] + came[area]
                if part == 0:
                    rows = rotated(rows, cosine, sine)
                scratch[...] = jnp.where(live, rows, 0.0)
                peer = owner[r * KEY_VALUE_HEADS + h]
                lanes = slice(part * HEAD_SIZE, (part + 1) * HEAD_SIZE)
                for b in range(2):
                    picked = scratch[pl.ds(b, count_rows // 2, stride=2), :]
                    out[peer * 2 + b, :, lanes] = picked.astype(jnp.bfloat16)


def outgoing_rows(place, lengths, owner, total, came, tables):
    count_rows = total.shape[0] // lengths.shape[0]
    out = (owner.shape[0] * 2, count_rows // 2, 2 * HEAD_SIZE)
    return pl.pallas_call(
        rows_kernel,
        in_specs=[SMEM_REF] * 3 + [VMEM_REF] * 8,
        out_specs=VMEM_REF,
        out_shape=jax.ShapeDtypeStruct(out, jnp.bfloat16),
        scratch_shapes=[pltpu.VMEM((count_rows, HEAD_SIZE), jnp.float32)],
        compiler_params=SMALL,
        cost_estimate=cost(1000, 1000),
        name="cache_rows",
    )(place, lengths, owner, total, came, *tables)


def decode_kernel(place, lengths, owner, cache, dec_query, dec_key, dec_value, *refs):
    tables, out = refs[:4], refs[4]
    peer, block = place[2] // 2, place[2] % 2
    length = lengths[0]
    for pair in range(owner.shape[0]):
        length = jnp.where(owner[pair] == peer, lengths[pair // KEY_VALUE_HEADS], length)
    cosine, sine = turned_by(length, tables, tables[2][:STEPS], tables[3][:STEPS])

    def turned(rows):
        return rotated(rows.astype(jnp.float32), cosine, sine)

    def padded(rows):
        return jnp.concatenate([rows, jnp.zeros((16 - STEPS, HEAD_SIZE), jnp.float32)], 0)

    raw = dec_query[peer]
    heads = [raw[:, j * HEAD_SIZE : (j + 1) * HEAD_SIZE] for j in range(QPK)]
    query = jnp.concatenate([turned(head) for head in heads], 0).astype(jnp.bfloat16)
    new_keys = padded(turned(dec_key[peer])).astype(jnp.bfloat16)
    new_value = padded(dec_value[peer].astype(jnp.float32)).astype(jnp.bfloat16)
    contract = (((1,), (1,)), ((), ()))
    scale = 1.0 / HEAD_SIZE**0.5
    old = lax.dot_general(
        query, cache[:, :HEAD_SIZE], contract, preferred_element_type=jnp.float32
    )
    slot = lax.broadcasted_iota(jnp.int32, old.shape, 1) * 2 + block
    old = jnp.where(slot < length, old * scale, -1e30)
    new = lax.dot_general(query, new_keys, contract, preferred_element_type=jnp.float32)
    step = lax.broadcasted_iota(jnp.int32, new.shape, 0) % STEPS
    token = lax.broadcasted_iota(jnp.int32, new.shape, 1)
    new = jnp.where((token <= step) & (block == 0), new * scale, -1e30)
    top = jnp.maximum(jnp.max(old, 1, keepdims=True), jnp.max(new, 1, keepdims=True))
    old, new = jnp.exp(old - top), jnp.exp(new - top)
    total = jnp.sum(old, 1, keepdims=True) + jnp.sum(new, 1, keepdims=True)
    sums = jnp.dot(
        old.astype(jnp.bfloat16), cache[:, HEAD_SIZE:], preferred_element_type=jnp.float32
    )
    out[:, :HEAD_SIZE] = sums + jnp.dot(
        new.astype(jnp.bfloat16), new_value, preferred_element_type=jnp.float32
    )
    half = (QPK * STEPS, HEAD_SIZE // 2)
    out[:, HEAD_SIZE : HEAD_SIZE + half[1]] = jnp.broadcast_to(top, half)
    out[:, HEAD_SIZE + half[1] :] = jnp.broadcast_to(total, half)


def joined_kernel(place, mine, theirs, out):
    share = QPK // 2
    area = pl.ds(place[2] % 2 * share * STEPS, share * STEPS)
    last = HEAD_SIZE + HEAD_SIZE // 2
    sums, tops, totals = [], [], []
    for ref in (mine, theirs):
        sums.append(ref[area, :HEAD_SIZE])
        tops.append(ref[area, HEAD_SIZE : HEAD_SIZE + 1])
        totals.append(ref[area, last : last + 1])
    top = jnp.maximum(tops[0], tops[1])
    scales = [jnp.exp(one - top) for one in tops]
    total = totals[0] * scales[0] + totals[1] * scales[1]
    value = (sums[0] * scales[0] + sums[1] * scales[1]) / total
    for j in range(share):
        rows = value[j * STEPS : (j + 1) * STEPS]
        out[:, j * HEAD_SIZE : (j + 1) * HEAD_SIZE] = rows.astype(jnp.bfloat16)


def copied(cache):
    def kernel(source, out, sem):
        fetch(source, out, sem.at[0]).wait()

    return pl.pallas_call(
        kernel,
        in_specs=[VMEM_REF],
        out_specs=ANY_REF,
        out_shape=jax.ShapeDtypeStruct(cache.shape, cache.dtype),
        scratch_shapes=[pltpu.SemaphoreType.DMA((1,))],
        compiler_params=SMALL,
        cost_estimate=cost(1000, 1000),
        name="copied",
    )(cache)


def decoded(place, lengths, owner, cache, dec_query, dec_key, dec_value, tables):
    mine = pl.pallas_call(
        decode_kernel,
        in_specs=[SMEM_REF] * 3 + [VMEM_REF] * 8,
        out_specs=VMEM_REF,
        out_shape=jax.ShapeDtypeStruct((STEPS * QPK, 2 * HEAD_SIZE), jnp.float32),
        compiler_params=SMALL,
        cost_estimate=cost(1000, 1000),
        name="decode",
    )(place, lengths, owner, cache, dec_query, dec_key, dec_value, *tables[:4])
    return pl.pallas_call(
        joined_kernel,
        in_specs=[SMEM_REF] + [VMEM_REF] * 2,
        out_specs=VMEM_REF,
        out_shape=jax.ShapeDtypeStruct((STEPS, QPK // 2 * HEAD_SIZE), jnp.bfloat16),
        compiler_params=SMALL,
        cost_estimate=cost(1000, 1000),
        name="joined",
    )(place, mine, moved(mine, to_core))


HERE, THERE = 3, 7


def body(hidden, key_weight, value_weight, lengths, owner, dec_query, dec_key, dec_value):
    count_requests, count_rows, width = hidden.shape
    device_id = lax.axis_index("seq")
    group_id = lax.axis_index("groups")
    seq = lax.axis_size("seq")
    planned = seq == 16 and lax.axis_size("groups") == 2
    decode_peers = count_requests * KEY_VALUE_HEADS
    split_point = seq // decode_peers
    tree_levels = split_point.bit_length() - 1
    rows_per_peer = count_rows // split_point
    positions = device_id * count_rows + jnp.arange(count_rows, dtype=jnp.int32)
    total_rows = count_requests * count_rows
    flat = hidden.reshape(total_rows, width)
    if planned:
        core = device_id % 2
        z, y = device_id // 4, device_id // 2 % 2
        layers = [z, z ^ 1, jnp.where(z < 2, 2, 1), jnp.where(z < 2, 3, 0)]
        is_end = (z == 0) | (z == 3)
        place = [group_id, core, device_id]
        place += [layer * 2 + y for layer in layers]
        place += [layer * 2 + 1 - y for layer in layers]
        place = jnp.stack([jnp.asarray(entry, jnp.int32) for entry in place])
    else:
        widened = flat.astype(jnp.float32)
        normed = (
            widened * lax.rsqrt(jnp.mean(widened * widened, -1, keepdims=True) + 1e-05)
        ).astype(jnp.bfloat16)

        def project(weight):
            whole = lax.all_gather(weight, "seq", axis=0, tiled=True)
            return jnp.dot(normed, whole, preferred_element_type=jnp.float32)

    pair_ids = jnp.arange(decode_peers, dtype=jnp.int32)
    matches = owner[None, :] == pair_ids[:, None]
    inverse_order = jnp.sum(jnp.where(matches, pair_ids[None, :], 0), axis=1)
    live_rows = positions[None, :] < lengths[:, None]

    def handed_over(rows):
        rows = jnp.where(live_rows[:, :, None, None], rows, jnp.zeros_like(rows))
        pair_rows = jnp.transpose(rows, (0, 2, 1, 3)).reshape(decode_peers, count_rows, HEAD_SIZE)
        sorted_rows = pair_rows[inverse_order].reshape(
            decode_peers, rows_per_peer, split_point, HEAD_SIZE
        )
        outgoing = jnp.transpose(sorted_rows, (0, 2, 1, 3)).reshape(
            decode_peers * split_point, rows_per_peer, HEAD_SIZE
        )
        return lax.all_to_all(outgoing, "seq", split_axis=0, concat_axis=1, tiled=True)[0]

    if planned:
        depth = key_weight.shape[0] // 2

        def half_block(first):
            halves = [
                lax.dynamic_slice_in_dim(weight, first, depth, 0)
                for weight in (key_weight, value_weight)
            ]
            return jnp.concatenate(halves, 1)

        raw = moved(flat, to_core)
        sent = half_block(group_id * depth)
        tables = turn_tables(count_rows * seq + STEPS, count_rows)
        near = moved(sent, to_pair)
        middle = moved(sent, to_middle)
        across = moved(sent, to_row)
        rest = half_block(depth - group_id * depth)
        layers, rows = (near, middle), (near, middle, across, raw, rest)
        passed = moved(after(middle, *layers), to_end)
        middle_c = moved(after(near, *layers), to_middle)
        near_y = moved(after(near, *rows), to_row)
        across_x = moved(across, to_group)
        mine, other = prepared(place, after(flat, *rows), raw, seq // 2)
        layers, rows = (passed, middle_c, mine), (near_y, across_x, mine, passed)
        far = moved(after(middle_c, *layers), to_end)
        block_b = jnp.where(is_end, after(passed, *rows), middle)
        block_yb = moved(block_b, to_row)
        block_xb = moved(block_b, to_group)
        layers, rows = (far, near_y), (block_yb, block_xb, far)
        near_rest = moved(after(rest, *layers), to_pair)
        block_c = jnp.where(is_end, after(far, *rows), middle_c)
        block_xc = moved(block_c, to_group)
        block_yc = moved(block_c, to_row)
        pieces = [(HERE, 0, sent), (HERE, 1, rest), (THERE, 0, across)]
        pieces += [(THERE, 1, across_x), (HERE + 1, 0, near), (THERE + 1, 0, near_y)]
        totals = product(place, after(mine, block_c), other, pieces, (), 3)
        layers, rows = (near_rest, block_yb, totals[0]), (block_xc, block_yc, near_rest, totals[0])
        end_a = moved(after(across_x, *layers), to_pair)
        ends = [moved(after(block_yb, *rows), to_group), moved(after(block_xc, *rows), to_row)]
        pieces = [(HERE + 2, 0, block_b), (HERE + 2, 1, block_xb), (THERE + 2, 0, block_yb)]
        pieces += [(HERE + 3, 0, block_c), (HERE + 1, 1, near_rest)]
        pieces += [(HERE + 3, 1, block_xc), (THERE + 3, 0, block_yc)]
        totals = product(place, after(mine, *rows), other, pieces, totals, 7)
        came = (end_a, *ends, *totals)
        pieces = [(THERE + 1, 1, end_a), (THERE + 2, 1, ends[0]), (THERE + 3, 1, ends[1])]
        total, given = product(place, after(mine, *came), other, pieces, totals, 3)
        outgoing = outgoing_rows(place, lengths, owner, total, moved(given, to_core), tables)
        incoming = lax.all_to_all(outgoing, "seq", split_axis=0, concat_axis=1, tiled=True)
        attended = decoded(
            place, lengths, owner, incoming[0], dec_query, dec_key, dec_value, tables
        )
        return (copied(incoming[0])[None], attended)
    else:
        cosine, sine_part = rope_table(positions, HEAD_SIZE)
        shape = (count_requests, count_rows, KEY_VALUE_HEADS, HEAD_SIZE)
        unrotated_key = project(key_weight).reshape(shape)
        key_rows = rotate(
            unrotated_key, cosine[:, None, :], sine_part[:, None, :]
        ).astype(jnp.bfloat16)
        cache_keys = handed_over(key_rows)
        cache_values = handed_over(project(value_weight).astype(jnp.bfloat16).reshape(shape))
    slot_count = cache_keys.shape[0]
    decode_peer = device_id // split_point
    block = device_id % split_point
    source_pair = jnp.sum(jnp.where(owner == decode_peer, pair_ids, 0))
    source_request = source_pair // KEY_VALUE_HEADS
    length = jnp.sum(
        jnp.where(jnp.arange(count_requests, dtype=jnp.int32) == source_request, lengths, 0)
    )
    query = lax.dynamic_index_in_dim(dec_query, decode_peer, 0, keepdims=False)
    new_key = lax.dynamic_index_in_dim(dec_key, decode_peer, 0, keepdims=False)
    new_value = lax.dynamic_index_in_dim(dec_value, decode_peer, 0, keepdims=False)
    step_pos = length + jnp.arange(STEPS, dtype=jnp.int32)
    step_cos, step_sin = rope_table(step_pos, HEAD_SIZE)
    query_rot = rotate(
        query.astype(jnp.float32).reshape(STEPS, QPK, HEAD_SIZE),
        step_cos[:, None, :],
        step_sin[:, None, :],
    ).astype(jnp.bfloat16)
    new_keys = rotate(new_key.astype(jnp.float32), step_cos, step_sin).astype(jnp.bfloat16)
    score_scale = 1.0 / HEAD_SIZE**0.5
    old_scores = (
        jnp.einsum(
            "sjd,id->sji", query_rot, cache_keys, preferred_element_type=jnp.float32
        )
        * score_scale
    )
    new_scores = (
        jnp.einsum("sjd,td->sjt", query_rot, new_keys, preferred_element_type=jnp.float32)
        * score_scale
    )
    slot_ids = jnp.arange(slot_count, dtype=jnp.int32) * split_point + block
    old_live = slot_ids < length
    new_live = (jnp.arange(STEPS)[None, :] <= jnp.arange(STEPS)[:, None]) & (block == 0)
    old_scores = jnp.where(old_live[None, None, :], old_scores, -1e30)
    new_scores = jnp.where(new_live[:, None, :], new_scores, -1e30)
    row_max = jnp.maximum(jnp.max(old_scores, -1), jnp.max(new_scores, -1))
    for bit in range(tree_levels):
        row_max = jnp.maximum(row_max, swapped(row_max, "seq", bit))
    old_exp = jnp.exp(old_scores - row_max[..., None])
    new_exp = jnp.exp(new_scores - row_max[..., None])
    denom = jnp.sum(old_exp, -1) + jnp.sum(new_exp, -1)
    for bit in range(tree_levels):
        denom = denom + swapped(denom, "seq", bit)
    old_probs = (old_exp / denom[..., None]).astype(jnp.bfloat16)
    new_probs = (new_exp / denom[..., None]).astype(jnp.bfloat16)
    partial_sum = jnp.einsum(
        "sji,id->sjd", old_probs, cache_values, preferred_element_type=jnp.float32
    )
    partial_sum = partial_sum + jnp.einsum(
        "sjt,td->sjd", new_probs, new_value, preferred_element_type=jnp.float32
    )
    flat_rows = partial_sum.reshape(STEPS, QPK * HEAD_SIZE)
    for bit in range(tree_levels):
        flat_rows = flat_rows + swapped(flat_rows, "seq", bit)
    share = flat_rows.shape[1] // split_point
    mine = lax.dynamic_slice_in_dim(flat_rows, block * share, share, 1)
    cache = jnp.concatenate([cache_keys, cache_values], 1)[None]
    return (cache, mine.astype(jnp.bfloat16))


def solution(mesh):
    placed = (
        P("groups", "seq", None),
        P("seq", None),
        P("seq", None),
        P("groups"),
        P("groups"),
        P("groups", None, None),
        P("groups", None, None),
        P("groups", None, None),
    )
    return jax.shard_map(
        body,
        mesh=mesh,
        in_specs=placed,
        out_specs=(P(("groups", "seq"), None, None), P("groups", "seq")),
        check_vma=False,
    )
```

```python
import functools

import jax
import jax.numpy as jnp
import numpy as np
from jax import lax
from jax.experimental import pallas as pl
from jax.experimental.pallas import tpu as pltpu
from jax.sharding import PartitionSpec as P

HEAD_SIZE = 128
KEY_VALUE_HEADS = 4
QPK = 8
STEPS = 4


ROPE_BASE = 500000.0


def swapped(block, axis, bit):
    count = lax.axis_size(axis)
    route = []
    for low in range(count):
        high = low | 1 << bit
        if high != low and high < count:
            route += [(low, high), (high, low)]
    return lax.ppermute(block, axis, route)


def rope_table(positions, head_dim):
    freq = ROPE_BASE ** (-(np.arange(head_dim // 2, dtype=np.float64) * 2.0) / head_dim)
    angle = positions.astype(jnp.float32)[:, None] * jnp.asarray(freq, jnp.float32)[None, :]
    return (jnp.cos(angle), jnp.sin(angle))


def rotate(values_in, cosine, sine_part):
    half_dim = values_in.shape[-1] // 2
    lower_half = values_in[..., :half_dim]
    upper_half = values_in[..., half_dim:]
    return jnp.concatenate(
        [
            lower_half * cosine - upper_half * sine_part,
            upper_half * cosine + lower_half * sine_part,
        ],
        -1,
    )


def spread(count):
    side = 1
    while side * side < count:
        side *= 2
    return (side, count // side)


def moved(block, rule):
    groups, seq = lax.axis_size("groups"), lax.axis_size("seq")
    low = spread(seq // 2)[1]
    route = []
    for g in range(groups):
        for s in range(seq):
            place = rule(g, s // 2 // low, s // 2 % low, s % 2)
            if place is not None:
                tg, tz, ty, tc = place
                route.append((g * seq + s, tg * seq + (tz * low + ty) * 2 + tc))
    return lax.ppermute(block, ("groups", "seq"), route)


def to_core(g, z, y, c):
    return (g, z, y, 1 - c)


def to_row(g, z, y, c):
    return (g, z, 1 - y, c)


def to_group(g, z, y, c):
    return (1 - g, z, y, c)


def to_pair(g, z, y, c):
    return (g, z ^ 1, y, c)


def to_middle(g, z, y, c):
    return (g, 3 - z, y, c) if z in (1, 2) else None


def to_end(g, z, y, c):
    return (g, 0 if z == 1 else 3, y, c) if z in (1, 2) else None


VMEM_REF = pl.BlockSpec(memory_space=pltpu.VMEM)
SMEM_REF = pl.BlockSpec(memory_space=pltpu.SMEM)
ANY_REF = pl.BlockSpec(memory_space=pl.ANY)
PARAMS = pltpu.CompilerParams(vmem_limit_bytes=20 << 20)
LARGE = pltpu.CompilerParams(vmem_limit_bytes=40 << 20)
SMALL = pltpu.CompilerParams(vmem_limit_bytes=16 << 20)


def cost(flops, moved_bytes):
    return pl.CostEstimate(flops=flops, bytes_accessed=moved_bytes, transcendentals=0)


def fetch(source, target, sem):
    copy = pltpu.make_async_copy(source, target, sem)
    copy.start()
    return copy


def prepare_kernel(place, *refs):
    depth = refs[2].shape[2]
    for rows_in, target in zip(refs[:2], refs[2:]):
        rows, width = rows_in.shape
        square = jnp.zeros((rows, depth), jnp.float32)
        for first in range(0, width, depth):
            part = rows_in[:, first : first + depth].astype(jnp.float32)
            square += part * part
        scale = lax.rsqrt(jnp.sum(square, -1, keepdims=True) / width + 1e-05)
        for core in range(2):

            @pl.when(place[1] == core)
            def _():
                for k in range(width // (2 * depth)):
                    first = (k // 2 * 4 + core * 2 + k % 2) * depth
                    part = rows_in[:, first : first + depth].astype(jnp.float32)
                    target[k] = (part * scale).astype(jnp.bfloat16)


def prepared(place, mine, other, blocks):
    rows, width = mine.shape
    depth = width // (4 * blocks)
    tile = 80 if rows % 80 == 0 else rows
    out = jax.ShapeDtypeStruct((2 * blocks, rows, depth), jnp.bfloat16)
    taken = pl.BlockSpec((tile, width), lambda i, place: (i, 0))
    given = pl.BlockSpec((2 * blocks, tile, depth), lambda i, place: (0, i, 0))
    return pl.pallas_call(
        prepare_kernel,
        grid_spec=pltpu.PrefetchScalarGridSpec(
            num_scalar_prefetch=1,
            grid=(rows // tile,),
            in_specs=[taken, taken],
            out_specs=[given, given],
        ),
        out_shape=[out, out],
        compiler_params=LARGE,
        cost_estimate=cost(1000, 1000),
        name="normed_halves",
    )(place, mine, other)


def after(value, *events):
    return lax.optimization_barrier((value, *events))[0]


def half_index(place, entry, kind):
    half = {0: place[0], 1: 1 - place[0], 2: 0, 3: 1}[kind]
    return place[entry] * 2 + half


def product_kernel(plan, group, with_total, place, mine, other, *refs):
    count = len(plan)
    outs = refs[-7:-5]
    left, right, total, sems, total_sems = refs[-5:]
    rows, depth = mine.shape[1], mine.shape[2]
    waits = []
    for k, (entry, kind) in enumerate(plan):
        area = pl.ds((k % group) * depth, depth)
        slot = k // group
        index = half_index(place, entry, kind)
        sources = (mine.at[index], other.at[index], refs[k])
        targets = (left.at[slot, 0, :, area], left.at[slot, 1, :, area], right.at[slot, area])
        waits.append(
            [fetch(a, b, sems.at[3 * k + i]) for i, (a, b) in enumerate(zip(sources, targets))]
        )
    carried = [
        fetch(ref, total.at[pl.ds(k * rows, rows)], total_sems.at[k])
        for k, ref in enumerate(refs[count : count + 2 * with_total])
    ]
    for slot in range(count // group):
        for copies in waits[slot * group : (slot + 1) * group]:
            for copy in copies:
                copy.wait()
        stacked = left[slot].reshape(2 * rows, group * depth)
        value = jnp.dot(stacked, right[slot], preferred_element_type=jnp.float32)
        if slot == 0:
            for copy in carried:
                copy.wait()
        if slot or with_total:
            value += total[...]
        if slot + 1 < count // group:
            total[...] = value
        else:
            outs[0][...] = value[:rows]
            outs[1][...] = value[rows:]


def product(place, mine, other, pieces, totals, group, moved_bytes=1000):
    _, rows, depth = mine.shape
    columns = pieces[0][2].shape[1]
    plan = [(entry, kind) for entry, kind, _ in pieces]
    count = len(plan)
    out = jax.ShapeDtypeStruct((rows, columns), jnp.float32)
    return pl.pallas_call(
        functools.partial(product_kernel, plan, group, bool(totals)),
        in_specs=[SMEM_REF] + [ANY_REF] * (2 + count + len(totals)),
        out_specs=[VMEM_REF] * 2,
        out_shape=[out] * 2,
        scratch_shapes=[
            pltpu.VMEM((count // group, 2, rows, group * depth), mine.dtype),
            pltpu.VMEM((count // group, group * depth, columns), mine.dtype),
            pltpu.VMEM((2 * rows, columns), jnp.float32),
            pltpu.SemaphoreType.DMA((3 * count,)),
            pltpu.SemaphoreType.DMA((2,)),
        ],
        compiler_params=PARAMS,
        cost_estimate=cost(1000, moved_bytes),
        name="add_product",
    )(place, mine, other, *[array for _, _, array in pieces], *totals)


LOW = 64


def turn_tables(positions, rows):
    freq = ROPE_BASE ** (-(np.arange(HEAD_SIZE // 2) * 2.0) / HEAD_SIZE)
    tables = []
    for places in (np.arange(0, positions, LOW), np.arange(LOW), np.arange(rows)):
        angle = places[:, None] * freq[None, :]
        tables.append(np.concatenate([np.cos(angle), np.cos(angle)], 1))
        tables.append(np.concatenate([-np.sin(angle), np.sin(angle)], 1))
    return [jnp.asarray(table, jnp.float32) for table in tables]


def turned_by(start, tables, cosine, sine):
    high, low = pl.ds(start // LOW, 1), pl.ds(start % LOW, 1)
    for cos_row, sin_row in (
        (tables[0][high], tables[1][high]),
        (tables[2][low], tables[3][low]),
    ):
        cosine, sine = cosine * cos_row - sine * sin_row, sine * cos_row + cosine * sin_row
    return cosine, sine


def rotated(rows, cosine, sine):
    half = HEAD_SIZE // 2
    return rows * cosine + jnp.concatenate([rows[:, half:], rows[:, :half]], 1) * sine


def rows_kernel(place, lengths, owner, *refs):
    total, came, *tables, out, scratch = refs
    columns = total.shape[1] // 2
    count_requests, count_rows = lengths.shape[0], scratch.shape[0]
    cosine, sine = turned_by(place[2] * count_rows, tables, tables[4][...], tables[5][...])
    index = place[2] * count_rows + lax.broadcasted_iota(jnp.int32, scratch.shape, 0)
    for r in range(count_requests):
        live = index < lengths[r]
        for h in range(KEY_VALUE_HEADS):
            for part in range(2):
                first = part * columns + h * HEAD_SIZE
                area = (
                    slice(r * count_rows, (r + 1) * count_rows),
                    slice(first, first + HEAD_SIZE),
                )
                rows = total[area] + came[area]
                if part == 0:
                    rows = rotated(rows, cosine, sine)
                scratch[...] = jnp.where(live, rows, 0.0)
                peer = owner[r * KEY_VALUE_HEADS + h]
                lanes = slice(part * HEAD_SIZE, (part + 1) * HEAD_SIZE)
                for b in range(2):
                    picked = scratch[pl.ds(b, count_rows // 2, stride=2), :]
                    out[peer * 2 + b, :, lanes] = picked.astype(jnp.bfloat16)


def outgoing_rows(place, lengths, owner, total, came, tables):
    count_rows = total.shape[0] // lengths.shape[0]
    out = (owner.shape[0] * 2, count_rows // 2, 2 * HEAD_SIZE)
    return pl.pallas_call(
        rows_kernel,
        in_specs=[SMEM_REF] * 3 + [VMEM_REF] * 8,
        out_specs=VMEM_REF,
        out_shape=jax.ShapeDtypeStruct(out, jnp.bfloat16),
        scratch_shapes=[pltpu.VMEM((count_rows, HEAD_SIZE), jnp.float32)],
        compiler_params=SMALL,
        cost_estimate=cost(1000, 1000),
        name="cache_rows",
    )(place, lengths, owner, total, came, *tables)


def decode_kernel(place, lengths, owner, cache, dec_query, dec_key, dec_value, *refs):
    tables, out = refs[:4], refs[4]
    peer, block = place[2] // 2, place[2] % 2
    length = lengths[0]
    for pair in range(owner.shape[0]):
        length = jnp.where(owner[pair] == peer, lengths[pair // KEY_VALUE_HEADS], length)
    cosine, sine = turned_by(length, tables, tables[2][:STEPS], tables[3][:STEPS])

    def turned(rows):
        return rotated(rows.astype(jnp.float32), cosine, sine)

    def padded(rows):
        return jnp.concatenate([rows, jnp.zeros((16 - STEPS, HEAD_SIZE), jnp.float32)], 0)

    raw = dec_query[peer]
    heads = [raw[:, j * HEAD_SIZE : (j + 1) * HEAD_SIZE] for j in range(QPK)]
    query = jnp.concatenate([turned(head) for head in heads], 0).astype(jnp.bfloat16)
    new_keys = padded(turned(dec_key[peer])).astype(jnp.bfloat16)
    new_value = padded(dec_value[peer].astype(jnp.float32)).astype(jnp.bfloat16)
    contract = (((1,), (1,)), ((), ()))
    scale = 1.0 / HEAD_SIZE**0.5
    old = lax.dot_general(
        query, cache[:, :HEAD_SIZE], contract, preferred_element_type=jnp.float32
    )
    slot = lax.broadcasted_iota(jnp.int32, old.shape, 1) * 2 + block
    old = jnp.where(slot < length, old * scale, -1e30)
    new = lax.dot_general(query, new_keys, contract, preferred_element_type=jnp.float32)
    step = lax.broadcasted_iota(jnp.int32, new.shape, 0) % STEPS
    token = lax.broadcasted_iota(jnp.int32, new.shape, 1)
    new = jnp.where((token <= step) & (block == 0), new * scale, -1e30)
    top = jnp.maximum(jnp.max(old, 1, keepdims=True), jnp.max(new, 1, keepdims=True))
    old, new = jnp.exp(old - top), jnp.exp(new - top)
    total = jnp.sum(old, 1, keepdims=True) + jnp.sum(new, 1, keepdims=True)
    sums = jnp.dot(
        old.astype(jnp.bfloat16), cache[:, HEAD_SIZE:], preferred_element_type=jnp.float32
    )
    out[:, :HEAD_SIZE] = sums + jnp.dot(
        new.astype(jnp.bfloat16), new_value, preferred_element_type=jnp.float32
    )
    half = (QPK * STEPS, HEAD_SIZE // 2)
    out[:, HEAD_SIZE : HEAD_SIZE + half[1]] = jnp.broadcast_to(top, half)
    out[:, HEAD_SIZE + half[1] :] = jnp.broadcast_to(total, half)


def joined_kernel(place, mine, theirs, out):
    share = QPK // 2
    area = pl.ds(place[2] % 2 * share * STEPS, share * STEPS)
    last = HEAD_SIZE + HEAD_SIZE // 2
    sums, tops, totals = [], [], []
    for ref in (mine, theirs):
        sums.append(ref[area, :HEAD_SIZE])
        tops.append(ref[area, HEAD_SIZE : HEAD_SIZE + 1])
        totals.append(ref[area, last : last + 1])
    top = jnp.maximum(tops[0], tops[1])
    scales = [jnp.exp(one - top) for one in tops]
    total = totals[0] * scales[0] + totals[1] * scales[1]
    value = (sums[0] * scales[0] + sums[1] * scales[1]) / total
    for j in range(share):
        rows = value[j * STEPS : (j + 1) * STEPS]
        out[:, j * HEAD_SIZE : (j + 1) * HEAD_SIZE] = rows.astype(jnp.bfloat16)


def copied(cache):
    def kernel(source, out, sem):
        fetch(source, out, sem.at[0]).wait()

    return pl.pallas_call(
        kernel,
        in_specs=[VMEM_REF],
        out_specs=ANY_REF,
        out_shape=jax.ShapeDtypeStruct(cache.shape, cache.dtype),
        scratch_shapes=[pltpu.SemaphoreType.DMA((1,))],
        compiler_params=SMALL,
        cost_estimate=cost(1000, 1000),
        name="copied",
    )(cache)


def decoded(place, lengths, owner, cache, dec_query, dec_key, dec_value, tables):
    mine = pl.pallas_call(
        decode_kernel,
        in_specs=[SMEM_REF] * 3 + [VMEM_REF] * 8,
        out_specs=VMEM_REF,
        out_shape=jax.ShapeDtypeStruct((STEPS * QPK, 2 * HEAD_SIZE), jnp.float32),
        compiler_params=SMALL,
        cost_estimate=cost(1000, 1000),
        name="decode",
    )(place, lengths, owner, cache, dec_query, dec_key, dec_value, *tables[:4])
    return pl.pallas_call(
        joined_kernel,
        in_specs=[SMEM_REF] + [VMEM_REF] * 2,
        out_specs=VMEM_REF,
        out_shape=jax.ShapeDtypeStruct((STEPS, QPK // 2 * HEAD_SIZE), jnp.bfloat16),
        compiler_params=SMALL,
        cost_estimate=cost(1000, 1000),
        name="joined",
    )(place, mine, moved(mine, to_core))


HERE, THERE = 3, 7


def body(hidden, key_weight, value_weight, lengths, owner, dec_query, dec_key, dec_value):
    count_requests, count_rows, width = hidden.shape
    device_id = lax.axis_index("seq")
    group_id = lax.axis_index("groups")
    seq = lax.axis_size("seq")
    planned = seq == 16 and lax.axis_size("groups") == 2
    decode_peers = count_requests * KEY_VALUE_HEADS
    split_point = seq // decode_peers
    tree_levels = split_point.bit_length() - 1
    rows_per_peer = count_rows // split_point
    positions = device_id * count_rows + jnp.arange(count_rows, dtype=jnp.int32)
    total_rows = count_requests * count_rows
    flat = hidden.reshape(total_rows, width)
    if planned:
        core = device_id % 2
        z, y = device_id // 4, device_id // 2 % 2
        layers = [z, z ^ 1, jnp.where(z < 2, 2, 1), jnp.where(z < 2, 3, 0)]
        is_end = (z == 0) | (z == 3)
        place = [group_id, core, device_id]
        place += [layer * 2 + y for layer in layers]
        place += [layer * 2 + 1 - y for layer in layers]
        place = jnp.stack([jnp.asarray(entry, jnp.int32) for entry in place])
    else:
        widened = flat.astype(jnp.float32)
        normed = (
            widened * lax.rsqrt(jnp.mean(widened * widened, -1, keepdims=True) + 1e-05)
        ).astype(jnp.bfloat16)

        def project(weight):
            whole = lax.all_gather(weight, "seq", axis=0, tiled=True)
            return jnp.dot(normed, whole, preferred_element_type=jnp.float32)

    pair_ids = jnp.arange(decode_peers, dtype=jnp.int32)
    matches = owner[None, :] == pair_ids[:, None]
    inverse_order = jnp.sum(jnp.where(matches, pair_ids[None, :], 0), axis=1)
    live_rows = positions[None, :] < lengths[:, None]

    def handed_over(rows):
        rows = jnp.where(live_rows[:, :, None, None], rows, jnp.zeros_like(rows))
        pair_rows = jnp.transpose(rows, (0, 2, 1, 3)).reshape(decode_peers, count_rows, HEAD_SIZE)
        sorted_rows = pair_rows[inverse_order].reshape(
            decode_peers, rows_per_peer, split_point, HEAD_SIZE
        )
        outgoing = jnp.transpose(sorted_rows, (0, 2, 1, 3)).reshape(
            decode_peers * split_point, rows_per_peer, HEAD_SIZE
        )
        return lax.all_to_all(outgoing, "seq", split_axis=0, concat_axis=1, tiled=True)[0]

    if planned:
        depth = key_weight.shape[0] // 2

        def half_block(first):
            halves = [
                lax.dynamic_slice_in_dim(weight, first, depth, 0)
                for weight in (key_weight, value_weight)
            ]
            return jnp.concatenate(halves, 1)

        raw = moved(flat, to_core)
        sent = half_block(group_id * depth)
        tables = turn_tables(count_rows * seq + STEPS, count_rows)
        near = moved(sent, to_pair)
        middle = moved(sent, to_middle)
        across = moved(sent, to_row)
        rest = half_block(depth - group_id * depth)
        layers, rows = (near, middle), (near, middle, across, raw, rest)
        passed = moved(after(middle, *layers), to_end)
        middle_c = moved(near, to_middle)
        near_y = moved(after(near, across), to_row)
        across_x = moved(across, to_group)
        mine, other = prepared(place, after(flat, *rows), raw, seq // 2)
        layers, rows = (passed, middle_c, mine), (near_y, across_x, mine, passed)
        far = moved(after(middle_c, *layers), to_end)
        block_b = jnp.where(is_end, after(passed, *rows), middle)
        block_yb = moved(block_b, to_row)
        block_xb = moved(block_b, to_group)
        layers, rows = (far, near_y), (block_yb, block_xb, far)
        near_rest = moved(after(rest, *layers), to_pair)
        block_c = jnp.where(is_end, after(far, *rows), middle_c)
        block_xc = moved(block_c, to_group)
        block_yc = moved(block_c, to_row)
        pieces = [(HERE, 0, sent), (HERE, 1, rest), (THERE, 0, across)]
        pieces += [(THERE, 1, across_x), (HERE + 1, 0, near), (THERE + 1, 0, near_y)]
        totals = product(place, after(mine, block_c), other, pieces, (), 3)
        layers, rows = (near_rest, block_yb, totals[0]), (block_xc, block_yc, near_rest, totals[0])
        end_a = moved(after(across_x, *layers), to_pair)
        ends = [moved(after(block_yb, *rows), to_group), moved(after(block_xc, *rows), to_row)]
        pieces = [(HERE + 2, 0, block_b), (HERE + 2, 1, block_xb), (THERE + 2, 0, block_yb)]
        pieces += [(HERE + 3, 0, block_c), (HERE + 1, 1, near_rest)]
        pieces += [(HERE + 3, 1, block_xc), (THERE + 3, 0, block_yc)]
        totals = product(place, after(mine, *rows), other, pieces, totals, 7)
        came = (end_a, *ends, *totals)
        pieces = [(THERE + 1, 1, end_a), (THERE + 2, 1, ends[0]), (THERE + 3, 1, ends[1])]
        total, given = product(place, after(mine, *came), other, pieces, totals, 3)
        outgoing = outgoing_rows(place, lengths, owner, total, moved(given, to_core), tables)
        incoming = lax.all_to_all(outgoing, "seq", split_axis=0, concat_axis=1, tiled=True)
        attended = decoded(
            place, lengths, owner, incoming[0], dec_query, dec_key, dec_value, tables
        )
        return (copied(incoming[0])[None], attended)
    else:
        cosine, sine_part = rope_table(positions, HEAD_SIZE)
        shape = (count_requests, count_rows, KEY_VALUE_HEADS, HEAD_SIZE)
        unrotated_key = project(key_weight).reshape(shape)
        key_rows = rotate(
            unrotated_key, cosine[:, None, :], sine_part[:, None, :]
        ).astype(jnp.bfloat16)
        cache_keys = handed_over(key_rows)
        cache_values = handed_over(project(value_weight).astype(jnp.bfloat16).reshape(shape))
    slot_count = cache_keys.shape[0]
    decode_peer = device_id // split_point
    block = device_id % split_point
    source_pair = jnp.sum(jnp.where(owner == decode_peer, pair_ids, 0))
    source_request = source_pair // KEY_VALUE_HEADS
    length = jnp.sum(
        jnp.where(jnp.arange(count_requests, dtype=jnp.int32) == source_request, lengths, 0)
    )
    query = lax.dynamic_index_in_dim(dec_query, decode_peer, 0, keepdims=False)
    new_key = lax.dynamic_index_in_dim(dec_key, decode_peer, 0, keepdims=False)
    new_value = lax.dynamic_index_in_dim(dec_value, decode_peer, 0, keepdims=False)
    step_pos = length + jnp.arange(STEPS, dtype=jnp.int32)
    step_cos, step_sin = rope_table(step_pos, HEAD_SIZE)
    query_rot = rotate(
        query.astype(jnp.float32).reshape(STEPS, QPK, HEAD_SIZE),
        step_cos[:, None, :],
        step_sin[:, None, :],
    ).astype(jnp.bfloat16)
    new_keys = rotate(new_key.astype(jnp.float32), step_cos, step_sin).astype(jnp.bfloat16)
    score_scale = 1.0 / HEAD_SIZE**0.5
    old_scores = (
        jnp.einsum(
            "sjd,id->sji", query_rot, cache_keys, preferred_element_type=jnp.float32
        )
        * score_scale
    )
    new_scores = (
        jnp.einsum("sjd,td->sjt", query_rot, new_keys, preferred_element_type=jnp.float32)
        * score_scale
    )
    slot_ids = jnp.arange(slot_count, dtype=jnp.int32) * split_point + block
    old_live = slot_ids < length
    new_live = (jnp.arange(STEPS)[None, :] <= jnp.arange(STEPS)[:, None]) & (block == 0)
    old_scores = jnp.where(old_live[None, None, :], old_scores, -1e30)
    new_scores = jnp.where(new_live[:, None, :], new_scores, -1e30)
    row_max = jnp.maximum(jnp.max(old_scores, -1), jnp.max(new_scores, -1))
    for bit in range(tree_levels):
        row_max = jnp.maximum(row_max, swapped(row_max, "seq", bit))
    old_exp = jnp.exp(old_scores - row_max[..., None])
    new_exp = jnp.exp(new_scores - row_max[..., None])
    denom = jnp.sum(old_exp, -1) + jnp.sum(new_exp, -1)
    for bit in range(tree_levels):
        denom = denom + swapped(denom, "seq", bit)
    old_probs = (old_exp / denom[..., None]).astype(jnp.bfloat16)
    new_probs = (new_exp / denom[..., None]).astype(jnp.bfloat16)
    partial_sum = jnp.einsum(
        "sji,id->sjd", old_probs, cache_values, preferred_element_type=jnp.float32
    )
    partial_sum = partial_sum + jnp.einsum(
        "sjt,td->sjd", new_probs, new_value, preferred_element_type=jnp.float32
    )
    flat_rows = partial_sum.reshape(STEPS, QPK * HEAD_SIZE)
    for bit in range(tree_levels):
        flat_rows = flat_rows + swapped(flat_rows, "seq", bit)
    share = flat_rows.shape[1] // split_point
    mine = lax.dynamic_slice_in_dim(flat_rows, block * share, share, 1)
    cache = jnp.concatenate([cache_keys, cache_values], 1)[None]
    return (cache, mine.astype(jnp.bfloat16))


def solution(mesh):
    placed = (
        P("groups", "seq", None),
        P("seq", None),
        P("seq", None),
        P("groups"),
        P("groups"),
        P("groups", None, None),
        P("groups", None, None),
        P("groups", None, None),
    )
    return jax.shard_map(
        body,
        mesh=mesh,
        in_specs=placed,
        out_specs=(P(("groups", "seq"), None, None), P("groups", "seq")),
        check_vma=False,
    )
```

```python
import functools

import jax
import jax.numpy as jnp
import numpy as np
from jax import lax
from jax.experimental import pallas as pl
from jax.experimental.pallas import tpu as pltpu
from jax.sharding import PartitionSpec as P

HEAD_SIZE = 128
KEY_VALUE_HEADS = 4
QPK = 8
STEPS = 4


ROPE_BASE = 500000.0


def swapped(block, axis, bit):
    count = lax.axis_size(axis)
    route = []
    for low in range(count):
        high = low | 1 << bit
        if high != low and high < count:
            route += [(low, high), (high, low)]
    return lax.ppermute(block, axis, route)


def rope_table(positions, head_dim):
    freq = ROPE_BASE ** (-(np.arange(head_dim // 2, dtype=np.float64) * 2.0) / head_dim)
    angle = positions.astype(jnp.float32)[:, None] * jnp.asarray(freq, jnp.float32)[None, :]
    return (jnp.cos(angle), jnp.sin(angle))


def rotate(values_in, cosine, sine_part):
    half_dim = values_in.shape[-1] // 2
    lower_half = values_in[..., :half_dim]
    upper_half = values_in[..., half_dim:]
    return jnp.concatenate(
        [
            lower_half * cosine - upper_half * sine_part,
            upper_half * cosine + lower_half * sine_part,
        ],
        -1,
    )


def spread(count):
    side = 1
    while side * side < count:
        side *= 2
    return (side, count // side)


def moved(block, rule):
    groups, seq = lax.axis_size("groups"), lax.axis_size("seq")
    low = spread(seq // 2)[1]
    route = []
    for g in range(groups):
        for s in range(seq):
            place = rule(g, s // 2 // low, s // 2 % low, s % 2)
            if place is not None:
                tg, tz, ty, tc = place
                route.append((g * seq + s, tg * seq + (tz * low + ty) * 2 + tc))
    return lax.ppermute(block, ("groups", "seq"), route)


def to_core(g, z, y, c):
    return (g, z, y, 1 - c)


def to_row(g, z, y, c):
    return (g, z, 1 - y, c)


def to_group(g, z, y, c):
    return (1 - g, z, y, c)


def to_pair(g, z, y, c):
    return (g, z ^ 1, y, c)


def to_middle(g, z, y, c):
    return (g, 3 - z, y, c) if z in (1, 2) else None


def to_end(g, z, y, c):
    return (g, 0 if z == 1 else 3, y, c) if z in (1, 2) else None


VMEM_REF = pl.BlockSpec(memory_space=pltpu.VMEM)
SMEM_REF = pl.BlockSpec(memory_space=pltpu.SMEM)
ANY_REF = pl.BlockSpec(memory_space=pl.ANY)
PARAMS = pltpu.CompilerParams(vmem_limit_bytes=20 << 20)
LARGE = pltpu.CompilerParams(vmem_limit_bytes=58 << 20)
SMALL = pltpu.CompilerParams(vmem_limit_bytes=16 << 20)


def cost(flops, moved_bytes):
    return pl.CostEstimate(flops=flops, bytes_accessed=moved_bytes, transcendentals=0)


def fetch(source, target, sem):
    copy = pltpu.make_async_copy(source, target, sem)
    copy.start()
    return copy


def prepare_kernel(place, *refs):
    depth = refs[2].shape[2]
    for rows_in, target in zip(refs[:2], refs[2:]):
        rows, width = rows_in.shape
        square = jnp.zeros((rows, depth), jnp.float32)
        for first in range(0, width, depth):
            part = rows_in[:, first : first + depth].astype(jnp.float32)
            square += part * part
        scale = lax.rsqrt(jnp.sum(square, -1, keepdims=True) / width + 1e-05)
        for core in range(2):

            @pl.when(place[1] == core)
            def _():
                for k in range(width // (2 * depth)):
                    first = (k // 2 * 4 + core * 2 + k % 2) * depth
                    part = rows_in[:, first : first + depth].astype(jnp.float32)
                    target[k] = (part * scale).astype(jnp.bfloat16)


def prepared(place, mine, other, blocks):
    rows, width = mine.shape
    depth = width // (4 * blocks)
    tile = 80 if rows % 80 == 0 else rows
    out = jax.ShapeDtypeStruct((2 * blocks, rows, depth), jnp.bfloat16)
    taken = pl.BlockSpec((tile, width), lambda i, place: (i, 0))
    given = pl.BlockSpec((2 * blocks, tile, depth), lambda i, place: (0, i, 0))
    return pl.pallas_call(
        prepare_kernel,
        grid_spec=pltpu.PrefetchScalarGridSpec(
            num_scalar_prefetch=1,
            grid=(rows // tile,),
            in_specs=[taken, taken],
            out_specs=[given, given],
        ),
        out_shape=[out, out],
        compiler_params=LARGE,
        cost_estimate=cost(1000, 1000),
        name="normed_halves",
    )(place, mine, other)


def after(value, *events):
    return lax.optimization_barrier((value, *events))[0]


def half_index(place, entry, kind):
    half = {0: place[0], 1: 1 - place[0], 2: 0, 3: 1}[kind]
    return place[entry] * 2 + half


def product_kernel(plan, group, part, with_total, place, mine, other, *refs):
    count = len(plan)
    outs = refs[-7:-5]
    left, right, total, sems, total_sems = refs[-5:]
    rows, depth = mine.shape[1], mine.shape[2]
    columns = right.shape[2]
    taken = pl.ds(part, columns)
    waits = []
    for k, (entry, kind) in enumerate(plan):
        area = pl.ds((k % group) * depth, depth)
        slot = k // group
        index = half_index(place, entry, kind)
        sources = (mine.at[index], other.at[index], refs[k].at[:, taken])
        targets = (left.at[slot, 0, :, area], left.at[slot, 1, :, area], right.at[slot, area])
        waits.append(
            [fetch(a, b, sems.at[3 * k + i]) for i, (a, b) in enumerate(zip(sources, targets))]
        )
    carried = [
        fetch(ref.at[:, taken], total.at[pl.ds(k * rows, rows)], total_sems.at[k])
        for k, ref in enumerate(refs[count : count + 2 * with_total])
    ]
    for slot in range(count // group):
        for copies in waits[slot * group : (slot + 1) * group]:
            for copy in copies:
                copy.wait()
        stacked = left[slot].reshape(2 * rows, group * depth)
        value = jnp.dot(stacked, right[slot], preferred_element_type=jnp.float32)
        if slot == 0:
            for copy in carried:
                copy.wait()
        if slot or with_total:
            value += total[...]
        if slot + 1 < count // group:
            total[...] = value
        else:
            outs[0][...] = value[:rows]
            outs[1][...] = value[rows:]


def product(place, mine, other, pieces, totals, group, part=0, columns=None):
    _, rows, depth = mine.shape
    columns = columns or pieces[0][2].shape[1]
    plan = [(entry, kind) for entry, kind, _ in pieces]
    count = len(plan)
    out = jax.ShapeDtypeStruct((rows, columns), jnp.float32)
    return pl.pallas_call(
        functools.partial(product_kernel, plan, group, part, bool(totals)),
        in_specs=[SMEM_REF] + [ANY_REF] * (2 + count + len(totals)),
        out_specs=[VMEM_REF] * 2,
        out_shape=[out] * 2,
        scratch_shapes=[
            pltpu.VMEM((count // group, 2, rows, group * depth), mine.dtype),
            pltpu.VMEM((count // group, group * depth, columns), mine.dtype),
            pltpu.VMEM((2 * rows, columns), jnp.float32),
            pltpu.SemaphoreType.DMA((3 * count,)),
            pltpu.SemaphoreType.DMA((2,)),
        ],
        compiler_params=PARAMS,
        cost_estimate=cost(1000, 1000),
        name="add_product",
    )(place, mine, other, *[array for _, _, array in pieces], *totals)


LOW = 64


def turn_tables(positions, rows):
    freq = ROPE_BASE ** (-(np.arange(HEAD_SIZE // 2) * 2.0) / HEAD_SIZE)
    tables = []
    for places in (np.arange(0, positions, LOW), np.arange(LOW), np.arange(rows)):
        angle = places[:, None] * freq[None, :]
        tables.append(np.concatenate([np.cos(angle), np.cos(angle)], 1))
        tables.append(np.concatenate([-np.sin(angle), np.sin(angle)], 1))
    return [jnp.asarray(table, jnp.float32) for table in tables]


def turned_by(start, tables, cosine, sine):
    high, low = pl.ds(start // LOW, 1), pl.ds(start % LOW, 1)
    for cos_row, sin_row in (
        (tables[0][high], tables[1][high]),
        (tables[2][low], tables[3][low]),
    ):
        cosine, sine = cosine * cos_row - sine * sin_row, sine * cos_row + cosine * sin_row
    return cosine, sine


def rotated(rows, cosine, sine):
    half = HEAD_SIZE // 2
    return rows * cosine + jnp.concatenate([rows[:, half:], rows[:, :half]], 1) * sine


def rows_kernel(place, lengths, owner, *refs):
    totals, came, tables, (out, scratch) = refs[:2], refs[2:4], refs[4:10], refs[10:]
    count_requests, count_rows = lengths.shape[0], scratch.shape[0]
    cosine, sine = turned_by(place[2] * count_rows, tables, tables[4][...], tables[5][...])
    index = place[2] * count_rows + lax.broadcasted_iota(jnp.int32, scratch.shape, 0)
    for r in range(count_requests):
        live = index < lengths[r]
        for h in range(KEY_VALUE_HEADS):
            for part in range(2):
                first = (part * KEY_VALUE_HEADS + h) * HEAD_SIZE
                which = int(first >= totals[0].shape[1])
                first -= which * totals[0].shape[1]
                area = (
                    slice(r * count_rows, (r + 1) * count_rows),
                    slice(first, first + HEAD_SIZE),
                )
                rows = totals[which][area] + came[which][area]
                if part == 0:
                    rows = rotated(rows, cosine, sine)
                scratch[...] = jnp.where(live, rows, 0.0)
                peer = owner[r * KEY_VALUE_HEADS + h]
                lanes = slice(part * HEAD_SIZE, (part + 1) * HEAD_SIZE)
                for b in range(2):
                    picked = scratch[pl.ds(b, count_rows // 2, stride=2), :]
                    out[peer * 2 + b, :, lanes] = picked.astype(jnp.bfloat16)


def outgoing_rows(place, lengths, owner, totals, came, tables):
    count_rows = totals[0].shape[0] // lengths.shape[0]
    out = (owner.shape[0] * 2, count_rows // 2, 2 * HEAD_SIZE)
    return pl.pallas_call(
        rows_kernel,
        in_specs=[SMEM_REF] * 3 + [VMEM_REF] * 10,
        out_specs=VMEM_REF,
        out_shape=jax.ShapeDtypeStruct(out, jnp.bfloat16),
        scratch_shapes=[pltpu.VMEM((count_rows, HEAD_SIZE), jnp.float32)],
        compiler_params=SMALL,
        cost_estimate=cost(1000, 1000),
        name="cache_rows",
    )(place, lengths, owner, *totals, *came, *tables)


def decode_kernel(place, lengths, owner, cache, dec_query, dec_key, dec_value, *refs):
    tables, out = refs[:4], refs[4]
    peer, block = place[2] // 2, place[2] % 2
    length = lengths[0]
    for pair in range(owner.shape[0]):
        length = jnp.where(owner[pair] == peer, lengths[pair // KEY_VALUE_HEADS], length)
    cosine, sine = turned_by(length, tables, tables[2][:STEPS], tables[3][:STEPS])

    def turned(rows):
        return rotated(rows.astype(jnp.float32), cosine, sine)

    def padded(rows):
        return jnp.concatenate([rows, jnp.zeros((16 - STEPS, HEAD_SIZE), jnp.float32)], 0)

    raw = dec_query[peer]
    heads = [raw[:, j * HEAD_SIZE : (j + 1) * HEAD_SIZE] for j in range(QPK)]
    query = jnp.concatenate([turned(head) for head in heads], 0).astype(jnp.bfloat16)
    new_keys = padded(turned(dec_key[peer])).astype(jnp.bfloat16)
    new_value = padded(dec_value[peer].astype(jnp.float32)).astype(jnp.bfloat16)
    contract = (((1,), (1,)), ((), ()))
    scale = 1.0 / HEAD_SIZE**0.5
    old = lax.dot_general(
        query, cache[:, :HEAD_SIZE], contract, preferred_element_type=jnp.float32
    )
    slot = lax.broadcasted_iota(jnp.int32, old.shape, 1) * 2 + block
    old = jnp.where(slot < length, old * scale, -1e30)
    new = lax.dot_general(query, new_keys, contract, preferred_element_type=jnp.float32)
    step = lax.broadcasted_iota(jnp.int32, new.shape, 0) % STEPS
    token = lax.broadcasted_iota(jnp.int32, new.shape, 1)
    new = jnp.where((token <= step) & (block == 0), new * scale, -1e30)
    top = jnp.maximum(jnp.max(old, 1, keepdims=True), jnp.max(new, 1, keepdims=True))
    old, new = jnp.exp(old - top), jnp.exp(new - top)
    total = jnp.sum(old, 1, keepdims=True) + jnp.sum(new, 1, keepdims=True)
    sums = jnp.dot(
        old.astype(jnp.bfloat16), cache[:, HEAD_SIZE:], preferred_element_type=jnp.float32
    )
    out[:, :HEAD_SIZE] = sums + jnp.dot(
        new.astype(jnp.bfloat16), new_value, preferred_element_type=jnp.float32
    )
    half = (QPK * STEPS, HEAD_SIZE // 2)
    out[:, HEAD_SIZE : HEAD_SIZE + half[1]] = jnp.broadcast_to(top, half)
    out[:, HEAD_SIZE + half[1] :] = jnp.broadcast_to(total, half)


def joined_kernel(place, mine, theirs, out):
    share = QPK // 2
    area = pl.ds(place[2] % 2 * share * STEPS, share * STEPS)
    last = HEAD_SIZE + HEAD_SIZE // 2
    sums, tops, totals = [], [], []
    for ref in (mine, theirs):
        sums.append(ref[area, :HEAD_SIZE])
        tops.append(ref[area, HEAD_SIZE : HEAD_SIZE + 1])
        totals.append(ref[area, last : last + 1])
    top = jnp.maximum(tops[0], tops[1])
    scales = [jnp.exp(one - top) for one in tops]
    total = totals[0] * scales[0] + totals[1] * scales[1]
    value = (sums[0] * scales[0] + sums[1] * scales[1]) / total
    for j in range(share):
        rows = value[j * STEPS : (j + 1) * STEPS]
        out[:, j * HEAD_SIZE : (j + 1) * HEAD_SIZE] = rows.astype(jnp.bfloat16)


def copied(cache):
    def kernel(source, out, sem):
        fetch(source, out, sem.at[0]).wait()

    return pl.pallas_call(
        kernel,
        in_specs=[VMEM_REF],
        out_specs=ANY_REF,
        out_shape=jax.ShapeDtypeStruct(cache.shape, cache.dtype),
        scratch_shapes=[pltpu.SemaphoreType.DMA((1,))],
        compiler_params=SMALL,
        cost_estimate=cost(1000, 1000),
        name="copied",
    )(cache)


def decoded(place, lengths, owner, cache, dec_query, dec_key, dec_value, tables):
    mine = pl.pallas_call(
        decode_kernel,
        in_specs=[SMEM_REF] * 3 + [VMEM_REF] * 8,
        out_specs=VMEM_REF,
        out_shape=jax.ShapeDtypeStruct((STEPS * QPK, 2 * HEAD_SIZE), jnp.float32),
        compiler_params=SMALL,
        cost_estimate=cost(1000, 1000),
        name="decode",
    )(place, lengths, owner, cache, dec_query, dec_key, dec_value, *tables[:4])
    return pl.pallas_call(
        joined_kernel,
        in_specs=[SMEM_REF] + [VMEM_REF] * 2,
        out_specs=VMEM_REF,
        out_shape=jax.ShapeDtypeStruct((STEPS, QPK // 2 * HEAD_SIZE), jnp.bfloat16),
        compiler_params=SMALL,
        cost_estimate=cost(1000, 1000),
        name="joined",
    )(place, mine, moved(mine, to_core))


HERE, THERE = 3, 7


def body(hidden, key_weight, value_weight, lengths, owner, dec_query, dec_key, dec_value):
    count_requests, count_rows, width = hidden.shape
    device_id = lax.axis_index("seq")
    group_id = lax.axis_index("groups")
    seq = lax.axis_size("seq")
    planned = seq == 16 and lax.axis_size("groups") == 2
    decode_peers = count_requests * KEY_VALUE_HEADS
    split_point = seq // decode_peers
    tree_levels = split_point.bit_length() - 1
    rows_per_peer = count_rows // split_point
    positions = device_id * count_rows + jnp.arange(count_rows, dtype=jnp.int32)
    total_rows = count_requests * count_rows
    flat = hidden.reshape(total_rows, width)
    if planned:
        core = device_id % 2
        z, y = device_id // 4, device_id // 2 % 2
        layers = [z, z ^ 1, jnp.where(z < 2, 2, 1), jnp.where(z < 2, 3, 0)]
        is_end = (z == 0) | (z == 3)
        place = [group_id, core, device_id]
        place += [layer * 2 + y for layer in layers]
        place += [layer * 2 + 1 - y for layer in layers]
        place = jnp.stack([jnp.asarray(entry, jnp.int32) for entry in place])
    else:
        widened = flat.astype(jnp.float32)
        normed = (
            widened * lax.rsqrt(jnp.mean(widened * widened, -1, keepdims=True) + 1e-05)
        ).astype(jnp.bfloat16)

        def project(weight):
            whole = lax.all_gather(weight, "seq", axis=0, tiled=True)
            return jnp.dot(normed, whole, preferred_element_type=jnp.float32)

    pair_ids = jnp.arange(decode_peers, dtype=jnp.int32)
    matches = owner[None, :] == pair_ids[:, None]
    inverse_order = jnp.sum(jnp.where(matches, pair_ids[None, :], 0), axis=1)
    live_rows = positions[None, :] < lengths[:, None]

    def handed_over(rows):
        rows = jnp.where(live_rows[:, :, None, None], rows, jnp.zeros_like(rows))
        pair_rows = jnp.transpose(rows, (0, 2, 1, 3)).reshape(decode_peers, count_rows, HEAD_SIZE)
        sorted_rows = pair_rows[inverse_order].reshape(
            decode_peers, rows_per_peer, split_point, HEAD_SIZE
        )
        outgoing = jnp.transpose(sorted_rows, (0, 2, 1, 3)).reshape(
            decode_peers * split_point, rows_per_peer, HEAD_SIZE
        )
        return lax.all_to_all(outgoing, "seq", split_axis=0, concat_axis=1, tiled=True)[0]

    if planned:
        depth = key_weight.shape[0] // 2

        def half_block(first):
            halves = [
                lax.dynamic_slice_in_dim(weight, first, depth, 0)
                for weight in (key_weight, value_weight)
            ]
            return jnp.concatenate(halves, 1)

        raw = moved(flat, to_core)
        sent = half_block(group_id * depth)
        tables = turn_tables(count_rows * seq + STEPS, count_rows)
        near = moved(sent, to_pair)
        middle = moved(sent, to_middle)
        across = moved(sent, to_row)
        rest = half_block(depth - group_id * depth)
        layers, rows = (near, middle), (near, middle, across, raw, rest)
        passed = moved(after(middle, *layers), to_end)
        middle_c = moved(near, to_middle)
        near_y = moved(after(near, across), to_row)
        across_x = moved(across, to_group)
        mine, other = prepared(place, after(flat, *rows), raw, seq // 2)
        layers, rows = (passed, middle_c, mine), (near_y, across_x, mine, passed)
        far = moved(after(middle_c, *layers), to_end)
        block_b = jnp.where(is_end, after(passed, *rows), middle)
        block_yb = moved(block_b, to_row)
        block_xb = moved(block_b, to_group)
        layers, rows = (far, near_y), (block_yb, block_xb, far)
        near_rest = moved(after(rest, *layers), to_pair)
        block_c = jnp.where(is_end, after(far, *rows), middle_c)
        block_xc = moved(block_c, to_group)
        block_yc = moved(block_c, to_row)
        pieces = [(HERE, 0, sent), (HERE, 1, rest), (THERE, 0, across)]
        pieces += [(THERE, 1, across_x), (HERE + 1, 0, near), (THERE + 1, 0, near_y)]
        totals = product(place, after(mine, block_c), other, pieces, (), 3)
        layers, rows = (near_rest, block_yb, totals[0]), (block_xc, block_yc, near_rest, totals[0])
        end_a = moved(after(across_x, *layers), to_pair)
        ends = [moved(after(block_yb, *rows), to_group), moved(after(block_xc, *rows), to_row)]
        pieces = [(HERE + 2, 0, block_b), (HERE + 2, 1, block_xb), (THERE + 2, 0, block_yb)]
        pieces += [(HERE + 3, 0, block_c), (HERE + 1, 1, near_rest)]
        pieces += [(HERE + 3, 1, block_xc), (THERE + 3, 0, block_yc)]
        totals = product(place, after(mine, *rows), other, pieces, totals, 7)
        came = (end_a, *ends, *totals)
        pieces = [(THERE + 1, 1, end_a), (THERE + 2, 1, ends[0]), (THERE + 3, 1, ends[1])]
        sums, given = [], []
        width = end_a.shape[1]
        split = width * 3 // 4
        for first, columns in ((0, split), (split, width - split)):
            left = after(mine, *came, *sums)
            total, theirs = product(place, left, other, pieces, totals, 3, first, columns)
            sums.append(total)
            given.append(moved(theirs, to_core))
        outgoing = outgoing_rows(place, lengths, owner, sums, given, tables)
        incoming = lax.all_to_all(outgoing, "seq", split_axis=0, concat_axis=1, tiled=True)
        attended = decoded(
            place, lengths, owner, incoming[0], dec_query, dec_key, dec_value, tables
        )
        return (copied(incoming[0])[None], attended)
    else:
        cosine, sine_part = rope_table(positions, HEAD_SIZE)
        shape = (count_requests, count_rows, KEY_VALUE_HEADS, HEAD_SIZE)
        unrotated_key = project(key_weight).reshape(shape)
        key_rows = rotate(
            unrotated_key, cosine[:, None, :], sine_part[:, None, :]
        ).astype(jnp.bfloat16)
        cache_keys = handed_over(key_rows)
        cache_values = handed_over(project(value_weight).astype(jnp.bfloat16).reshape(shape))
    slot_count = cache_keys.shape[0]
    decode_peer = device_id // split_point
    block = device_id % split_point
    source_pair = jnp.sum(jnp.where(owner == decode_peer, pair_ids, 0))
    source_request = source_pair // KEY_VALUE_HEADS
    length = jnp.sum(
        jnp.where(jnp.arange(count_requests, dtype=jnp.int32) == source_request, lengths, 0)
    )
    query = lax.dynamic_index_in_dim(dec_query, decode_peer, 0, keepdims=False)
    new_key = lax.dynamic_index_in_dim(dec_key, decode_peer, 0, keepdims=False)
    new_value = lax.dynamic_index_in_dim(dec_value, decode_peer, 0, keepdims=False)
    step_pos = length + jnp.arange(STEPS, dtype=jnp.int32)
    step_cos, step_sin = rope_table(step_pos, HEAD_SIZE)
    query_rot = rotate(
        query.astype(jnp.float32).reshape(STEPS, QPK, HEAD_SIZE),
        step_cos[:, None, :],
        step_sin[:, None, :],
    ).astype(jnp.bfloat16)
    new_keys = rotate(new_key.astype(jnp.float32), step_cos, step_sin).astype(jnp.bfloat16)
    score_scale = 1.0 / HEAD_SIZE**0.5
    old_scores = (
        jnp.einsum(
            "sjd,id->sji", query_rot, cache_keys, preferred_element_type=jnp.float32
        )
        * score_scale
    )
    new_scores = (
        jnp.einsum("sjd,td->sjt", query_rot, new_keys, preferred_element_type=jnp.float32)
        * score_scale
    )
    slot_ids = jnp.arange(slot_count, dtype=jnp.int32) * split_point + block
    old_live = slot_ids < length
    new_live = (jnp.arange(STEPS)[None, :] <= jnp.arange(STEPS)[:, None]) & (block == 0)
    old_scores = jnp.where(old_live[None, None, :], old_scores, -1e30)
    new_scores = jnp.where(new_live[:, None, :], new_scores, -1e30)
    row_max = jnp.maximum(jnp.max(old_scores, -1), jnp.max(new_scores, -1))
    for bit in range(tree_levels):
        row_max = jnp.maximum(row_max, swapped(row_max, "seq", bit))
    old_exp = jnp.exp(old_scores - row_max[..., None])
    new_exp = jnp.exp(new_scores - row_max[..., None])
    denom = jnp.sum(old_exp, -1) + jnp.sum(new_exp, -1)
    for bit in range(tree_levels):
        denom = denom + swapped(denom, "seq", bit)
    old_probs = (old_exp / denom[..., None]).astype(jnp.bfloat16)
    new_probs = (new_exp / denom[..., None]).astype(jnp.bfloat16)
    partial_sum = jnp.einsum(
        "sji,id->sjd", old_probs, cache_values, preferred_element_type=jnp.float32
    )
    partial_sum = partial_sum + jnp.einsum(
        "sjt,td->sjd", new_probs, new_value, preferred_element_type=jnp.float32
    )
    flat_rows = partial_sum.reshape(STEPS, QPK * HEAD_SIZE)
    for bit in range(tree_levels):
        flat_rows = flat_rows + swapped(flat_rows, "seq", bit)
    share = flat_rows.shape[1] // split_point
    mine = lax.dynamic_slice_in_dim(flat_rows, block * share, share, 1)
    cache = jnp.concatenate([cache_keys, cache_values], 1)[None]
    return (cache, mine.astype(jnp.bfloat16))


def solution(mesh):
    placed = (
        P("groups", "seq", None),
        P("seq", None),
        P("seq", None),
        P("groups"),
        P("groups"),
        P("groups", None, None),
        P("groups", None, None),
        P("groups", None, None),
    )
    return jax.shard_map(
        body,
        mesh=mesh,
        in_specs=placed,
        out_specs=(P(("groups", "seq"), None, None), P("groups", "seq")),
        check_vma=False,
    )
```

```python
import functools

import jax
import jax.numpy as jnp
import numpy as np
from jax import lax
from jax.experimental import pallas as pl
from jax.experimental.pallas import tpu as pltpu
from jax.sharding import PartitionSpec as P

HEAD_SIZE = 128
KEY_VALUE_HEADS = 4
QPK = 8
STEPS = 4


ROPE_BASE = 500000.0


def swapped(block, axis, bit):
    count = lax.axis_size(axis)
    route = []
    for low in range(count):
        high = low | 1 << bit
        if high != low and high < count:
            route += [(low, high), (high, low)]
    return lax.ppermute(block, axis, route)


def rope_table(positions, head_dim):
    freq = ROPE_BASE ** (-(np.arange(head_dim // 2, dtype=np.float64) * 2.0) / head_dim)
    angle = positions.astype(jnp.float32)[:, None] * jnp.asarray(freq, jnp.float32)[None, :]
    return (jnp.cos(angle), jnp.sin(angle))


def rotate(values_in, cosine, sine_part):
    half_dim = values_in.shape[-1] // 2
    lower_half = values_in[..., :half_dim]
    upper_half = values_in[..., half_dim:]
    return jnp.concatenate(
        [
            lower_half * cosine - upper_half * sine_part,
            upper_half * cosine + lower_half * sine_part,
        ],
        -1,
    )


def spread(count):
    side = 1
    while side * side < count:
        side *= 2
    return (side, count // side)


def moved(block, rule):
    groups, seq = lax.axis_size("groups"), lax.axis_size("seq")
    low = spread(seq // 2)[1]
    route = []
    for g in range(groups):
        for s in range(seq):
            place = rule(g, s // 2 // low, s // 2 % low, s % 2)
            if place is not None:
                tg, tz, ty, tc = place
                route.append((g * seq + s, tg * seq + (tz * low + ty) * 2 + tc))
    return lax.ppermute(block, ("groups", "seq"), route)


def to_core(g, z, y, c):
    return (g, z, y, 1 - c)


def to_row(g, z, y, c):
    return (g, z, 1 - y, c)


def to_group(g, z, y, c):
    return (1 - g, z, y, c)


def to_pair(g, z, y, c):
    return (g, z ^ 1, y, c)


def to_middle(g, z, y, c):
    return (g, 3 - z, y, c) if z in (1, 2) else None


def to_end(g, z, y, c):
    return (g, 0 if z == 1 else 3, y, c) if z in (1, 2) else None


VMEM_REF = pl.BlockSpec(memory_space=pltpu.VMEM)
SMEM_REF = pl.BlockSpec(memory_space=pltpu.SMEM)
ANY_REF = pl.BlockSpec(memory_space=pl.ANY)
PARAMS = pltpu.CompilerParams(vmem_limit_bytes=20 << 20)
LARGE = pltpu.CompilerParams(vmem_limit_bytes=58 << 20)
SMALL = pltpu.CompilerParams(vmem_limit_bytes=16 << 20)


def cost(flops, moved_bytes):
    return pl.CostEstimate(flops=flops, bytes_accessed=moved_bytes, transcendentals=0)


def fetch(source, target, sem):
    copy = pltpu.make_async_copy(source, target, sem)
    copy.start()
    return copy


def prepare_kernel(place, *refs):
    depth = refs[2].shape[2]
    for rows_in, target in zip(refs[:2], refs[2:]):
        rows, width = rows_in.shape
        square = jnp.zeros((rows, depth), jnp.float32)
        for first in range(0, width, depth):
            part = rows_in[:, first : first + depth].astype(jnp.float32)
            square += part * part
        scale = lax.rsqrt(jnp.sum(square, -1, keepdims=True) / width + 1e-05)
        for core in range(2):

            @pl.when(place[1] == core)
            def _():
                for k in range(width // (2 * depth)):
                    first = (k // 2 * 4 + core * 2 + k % 2) * depth
                    part = rows_in[:, first : first + depth].astype(jnp.float32)
                    target[k] = (part * scale).astype(jnp.bfloat16)


def prepared(place, mine, other, blocks):
    rows, width = mine.shape
    depth = width // (4 * blocks)
    tile = 80 if rows % 80 == 0 else rows
    out = jax.ShapeDtypeStruct((2 * blocks, rows, depth), jnp.bfloat16)
    taken = pl.BlockSpec((tile, width), lambda i, place: (i, 0))
    given = pl.BlockSpec((2 * blocks, tile, depth), lambda i, place: (0, i, 0))
    return pl.pallas_call(
        prepare_kernel,
        grid_spec=pltpu.PrefetchScalarGridSpec(
            num_scalar_prefetch=1,
            grid=(rows // tile,),
            in_specs=[taken, taken],
            out_specs=[given, given],
        ),
        out_shape=[out, out],
        compiler_params=LARGE,
        cost_estimate=cost(1000, 1000),
        name="normed_halves",
    )(place, mine, other)


def after(value, *events):
    return lax.optimization_barrier((value, *events))[0]


def half_index(place, entry, kind):
    half = {0: place[0], 1: 1 - place[0], 2: 0, 3: 1}[kind]
    return place[entry] * 2 + half


def product_kernel(plan, group, part, with_total, place, mine, other, *refs):
    count = len(plan)
    outs = refs[-7:-5]
    left, right, total, sems, total_sems = refs[-5:]
    rows, depth = mine.shape[1], mine.shape[2]
    columns = right.shape[2]
    taken = pl.ds(part, columns)
    waits = []
    for k, (entry, kind) in enumerate(plan):
        area = pl.ds((k % group) * depth, depth)
        slot = k // group
        index = half_index(place, entry, kind)
        sources = (mine.at[index], other.at[index], refs[k].at[:, taken])
        targets = (left.at[slot, 0, :, area], left.at[slot, 1, :, area], right.at[slot, area])
        waits.append(
            [fetch(a, b, sems.at[3 * k + i]) for i, (a, b) in enumerate(zip(sources, targets))]
        )
    carried = [
        fetch(ref.at[:, taken], total.at[pl.ds(k * rows, rows)], total_sems.at[k])
        for k, ref in enumerate(refs[count : count + 2 * with_total])
    ]
    for slot in range(count // group):
        for copies in waits[slot * group : (slot + 1) * group]:
            for copy in copies:
                copy.wait()
        stacked = left[slot].reshape(2 * rows, group * depth)
        value = jnp.dot(stacked, right[slot], preferred_element_type=jnp.float32)
        if slot == 0:
            for copy in carried:
                copy.wait()
        if slot or with_total:
            value += total[...]
        if slot + 1 < count // group:
            total[...] = value
        else:
            outs[0][...] = value[:rows]
            outs[1][...] = value[rows:]


def product(place, mine, other, pieces, totals, group, part=0, columns=None):
    _, rows, depth = mine.shape
    columns = columns or pieces[0][2].shape[1]
    plan = [(entry, kind) for entry, kind, _ in pieces]
    count = len(plan)
    out = jax.ShapeDtypeStruct((rows, columns), jnp.float32)
    return pl.pallas_call(
        functools.partial(product_kernel, plan, group, part, bool(totals)),
        in_specs=[SMEM_REF] + [ANY_REF] * (2 + count + len(totals)),
        out_specs=[VMEM_REF] * 2,
        out_shape=[out] * 2,
        scratch_shapes=[
            pltpu.VMEM((count // group, 2, rows, group * depth), mine.dtype),
            pltpu.VMEM((count // group, group * depth, columns), mine.dtype),
            pltpu.VMEM((2 * rows, columns), jnp.float32),
            pltpu.SemaphoreType.DMA((3 * count,)),
            pltpu.SemaphoreType.DMA((2,)),
        ],
        compiler_params=PARAMS,
        cost_estimate=cost(1000, 1000),
        name="add_product",
    )(place, mine, other, *[array for _, _, array in pieces], *totals)


LOW = 64


def turn_tables(positions, rows):
    freq = ROPE_BASE ** (-(np.arange(HEAD_SIZE // 2) * 2.0) / HEAD_SIZE)
    tables = []
    for places in (np.arange(0, positions, LOW), np.arange(LOW), np.arange(rows)):
        angle = places[:, None] * freq[None, :]
        tables.append(np.concatenate([np.cos(angle), np.cos(angle)], 1))
        tables.append(np.concatenate([-np.sin(angle), np.sin(angle)], 1))
    return [jnp.asarray(table, jnp.float32) for table in tables]


def turned_by(start, tables, cosine, sine):
    high, low = pl.ds(start // LOW, 1), pl.ds(start % LOW, 1)
    for cos_row, sin_row in (
        (tables[0][high], tables[1][high]),
        (tables[2][low], tables[3][low]),
    ):
        cosine, sine = cosine * cos_row - sine * sin_row, sine * cos_row + cosine * sin_row
    return cosine, sine


def rotated(rows, cosine, sine):
    half = HEAD_SIZE // 2
    return rows * cosine + jnp.concatenate([rows[:, half:], rows[:, :half]], 1) * sine


def rows_kernel(place, lengths, owner, *refs):
    totals, came, tables, (out, scratch) = refs[:2], refs[2:4], refs[4:10], refs[10:]
    count_requests, count_rows = lengths.shape[0], scratch.shape[0]
    cosine, sine = turned_by(place[2] * count_rows, tables, tables[4][...], tables[5][...])
    index = place[2] * count_rows + lax.broadcasted_iota(jnp.int32, scratch.shape, 0)
    for r in range(count_requests):
        live = index < lengths[r]
        for h in range(KEY_VALUE_HEADS):
            for part in range(2):
                first = (part * KEY_VALUE_HEADS + h) * HEAD_SIZE
                which = int(first >= totals[0].shape[1])
                first -= which * totals[0].shape[1]
                area = (
                    slice(r * count_rows, (r + 1) * count_rows),
                    slice(first, first + HEAD_SIZE),
                )
                rows = totals[which][area] + came[which][area]
                if part == 0:
                    rows = rotated(rows, cosine, sine)
                scratch[...] = jnp.where(live, rows, 0.0)
                peer = owner[r * KEY_VALUE_HEADS + h]
                lanes = slice(part * HEAD_SIZE, (part + 1) * HEAD_SIZE)
                for b in range(2):
                    picked = scratch[pl.ds(b, count_rows // 2, stride=2), :]
                    out[peer * 2 + b, :, lanes] = picked.astype(jnp.bfloat16)


def outgoing_rows(place, lengths, owner, totals, came, tables):
    count_rows = totals[0].shape[0] // lengths.shape[0]
    out = (owner.shape[0] * 2, count_rows // 2, 2 * HEAD_SIZE)
    return pl.pallas_call(
        rows_kernel,
        in_specs=[SMEM_REF] * 3 + [VMEM_REF] * 10,
        out_specs=VMEM_REF,
        out_shape=jax.ShapeDtypeStruct(out, jnp.bfloat16),
        scratch_shapes=[pltpu.VMEM((count_rows, HEAD_SIZE), jnp.float32)],
        compiler_params=SMALL,
        cost_estimate=cost(1000, 1000),
        name="cache_rows",
    )(place, lengths, owner, *totals, *came, *tables)


def decode_kernel(place, lengths, owner, cache, dec_query, dec_key, dec_value, *refs):
    tables, out = refs[:4], refs[4]
    peer, block = place[2] // 2, place[2] % 2
    length = lengths[0]
    for pair in range(owner.shape[0]):
        length = jnp.where(owner[pair] == peer, lengths[pair // KEY_VALUE_HEADS], length)
    cosine, sine = turned_by(length, tables, tables[2][:STEPS], tables[3][:STEPS])

    def turned(rows):
        return rotated(rows.astype(jnp.float32), cosine, sine)

    def padded(rows):
        return jnp.concatenate([rows, jnp.zeros((16 - STEPS, HEAD_SIZE), jnp.float32)], 0)

    raw = dec_query[peer]
    heads = [raw[:, j * HEAD_SIZE : (j + 1) * HEAD_SIZE] for j in range(QPK)]
    query = jnp.concatenate([turned(head) for head in heads], 0).astype(jnp.bfloat16)
    new_keys = padded(turned(dec_key[peer])).astype(jnp.bfloat16)
    new_value = padded(dec_value[peer].astype(jnp.float32)).astype(jnp.bfloat16)
    contract = (((1,), (1,)), ((), ()))
    scale = 1.0 / HEAD_SIZE**0.5
    old = lax.dot_general(
        query, cache[:, :HEAD_SIZE], contract, preferred_element_type=jnp.float32
    )
    slot = lax.broadcasted_iota(jnp.int32, old.shape, 1) * 2 + block
    old = jnp.where(slot < length, old * scale, -1e30)
    new = lax.dot_general(query, new_keys, contract, preferred_element_type=jnp.float32)
    step = lax.broadcasted_iota(jnp.int32, new.shape, 0) % STEPS
    token = lax.broadcasted_iota(jnp.int32, new.shape, 1)
    new = jnp.where((token <= step) & (block == 0), new * scale, -1e30)
    top = jnp.maximum(jnp.max(old, 1, keepdims=True), jnp.max(new, 1, keepdims=True))
    old, new = jnp.exp(old - top), jnp.exp(new - top)
    total = jnp.sum(old, 1, keepdims=True) + jnp.sum(new, 1, keepdims=True)
    sums = jnp.dot(
        old.astype(jnp.bfloat16), cache[:, HEAD_SIZE:], preferred_element_type=jnp.float32
    )
    out[:, :HEAD_SIZE] = sums + jnp.dot(
        new.astype(jnp.bfloat16), new_value, preferred_element_type=jnp.float32
    )
    half = (QPK * STEPS, HEAD_SIZE // 2)
    out[:, HEAD_SIZE : HEAD_SIZE + half[1]] = jnp.broadcast_to(top, half)
    out[:, HEAD_SIZE + half[1] :] = jnp.broadcast_to(total, half)


def joined_kernel(place, mine, theirs, out):
    share = QPK // 2
    area = pl.ds(place[2] % 2 * share * STEPS, share * STEPS)
    last = HEAD_SIZE + HEAD_SIZE // 2
    sums, tops, totals = [], [], []
    for ref in (mine, theirs):
        sums.append(ref[area, :HEAD_SIZE])
        tops.append(ref[area, HEAD_SIZE : HEAD_SIZE + 1])
        totals.append(ref[area, last : last + 1])
    top = jnp.maximum(tops[0], tops[1])
    scales = [jnp.exp(one - top) for one in tops]
    total = totals[0] * scales[0] + totals[1] * scales[1]
    value = (sums[0] * scales[0] + sums[1] * scales[1]) / total
    for j in range(share):
        rows = value[j * STEPS : (j + 1) * STEPS]
        out[:, j * HEAD_SIZE : (j + 1) * HEAD_SIZE] = rows.astype(jnp.bfloat16)


def copied(cache):
    def kernel(source, out, sem):
        fetch(source, out, sem.at[0]).wait()

    return pl.pallas_call(
        kernel,
        in_specs=[VMEM_REF],
        out_specs=ANY_REF,
        out_shape=jax.ShapeDtypeStruct(cache.shape, cache.dtype),
        scratch_shapes=[pltpu.SemaphoreType.DMA((1,))],
        compiler_params=SMALL,
        cost_estimate=cost(1000, 1000),
        name="copied",
    )(cache)


def decoded(place, lengths, owner, cache, dec_query, dec_key, dec_value, tables):
    mine = pl.pallas_call(
        decode_kernel,
        in_specs=[SMEM_REF] * 3 + [VMEM_REF] * 8,
        out_specs=VMEM_REF,
        out_shape=jax.ShapeDtypeStruct((STEPS * QPK, 2 * HEAD_SIZE), jnp.float32),
        compiler_params=SMALL,
        cost_estimate=cost(1000, 1000),
        name="decode",
    )(place, lengths, owner, cache, dec_query, dec_key, dec_value, *tables[:4])
    return pl.pallas_call(
        joined_kernel,
        in_specs=[SMEM_REF] + [VMEM_REF] * 2,
        out_specs=VMEM_REF,
        out_shape=jax.ShapeDtypeStruct((STEPS, QPK // 2 * HEAD_SIZE), jnp.bfloat16),
        compiler_params=SMALL,
        cost_estimate=cost(1000, 1000),
        name="joined",
    )(place, mine, moved(mine, to_core))


HERE, THERE = 3, 7


def body(hidden, key_weight, value_weight, lengths, owner, dec_query, dec_key, dec_value):
    count_requests, count_rows, width = hidden.shape
    device_id = lax.axis_index("seq")
    group_id = lax.axis_index("groups")
    seq = lax.axis_size("seq")
    planned = seq == 16 and lax.axis_size("groups") == 2
    decode_peers = count_requests * KEY_VALUE_HEADS
    split_point = seq // decode_peers
    tree_levels = split_point.bit_length() - 1
    rows_per_peer = count_rows // split_point
    positions = device_id * count_rows + jnp.arange(count_rows, dtype=jnp.int32)
    total_rows = count_requests * count_rows
    flat = hidden.reshape(total_rows, width)
    if planned:
        core = device_id % 2
        z, y = device_id // 4, device_id // 2 % 2
        layers = [z, z ^ 1, jnp.where(z < 2, 2, 1), jnp.where(z < 2, 3, 0)]
        is_end = (z == 0) | (z == 3)
        place = [group_id, core, device_id]
        place += [layer * 2 + y for layer in layers]
        place += [layer * 2 + 1 - y for layer in layers]
        place = jnp.stack([jnp.asarray(entry, jnp.int32) for entry in place])
    else:
        widened = flat.astype(jnp.float32)
        normed = (
            widened * lax.rsqrt(jnp.mean(widened * widened, -1, keepdims=True) + 1e-05)
        ).astype(jnp.bfloat16)

        def project(weight):
            whole = lax.all_gather(weight, "seq", axis=0, tiled=True)
            return jnp.dot(normed, whole, preferred_element_type=jnp.float32)

    pair_ids = jnp.arange(decode_peers, dtype=jnp.int32)
    matches = owner[None, :] == pair_ids[:, None]
    inverse_order = jnp.sum(jnp.where(matches, pair_ids[None, :], 0), axis=1)
    live_rows = positions[None, :] < lengths[:, None]

    def handed_over(rows):
        rows = jnp.where(live_rows[:, :, None, None], rows, jnp.zeros_like(rows))
        pair_rows = jnp.transpose(rows, (0, 2, 1, 3)).reshape(decode_peers, count_rows, HEAD_SIZE)
        sorted_rows = pair_rows[inverse_order].reshape(
            decode_peers, rows_per_peer, split_point, HEAD_SIZE
        )
        outgoing = jnp.transpose(sorted_rows, (0, 2, 1, 3)).reshape(
            decode_peers * split_point, rows_per_peer, HEAD_SIZE
        )
        return lax.all_to_all(outgoing, "seq", split_axis=0, concat_axis=1, tiled=True)[0]

    if planned:
        depth = key_weight.shape[0] // 2

        def half_block(first):
            halves = [
                lax.dynamic_slice_in_dim(weight, first, depth, 0)
                for weight in (key_weight, value_weight)
            ]
            return jnp.concatenate(halves, 1)

        raw = moved(flat, to_core)
        sent = half_block(group_id * depth)
        tables = turn_tables(count_rows * seq + STEPS, count_rows)
        near = moved(sent, to_pair)
        middle = moved(sent, to_middle)
        across = moved(sent, to_row)
        rest = half_block(depth - group_id * depth)
        layers, rows = (near, middle), (near, middle, across, raw, rest)
        passed = moved(after(middle, *layers), to_end)
        middle_c = moved(near, to_middle)
        near_y = moved(near, to_row)
        across_x = moved(across, to_group)
        mine, other = prepared(place, after(flat, *rows), raw, seq // 2)
        layers, rows = (passed, middle_c, mine), (near_y, across_x, mine, passed)
        far = moved(after(middle_c, *layers), to_end)
        block_b = jnp.where(is_end, after(passed, *rows), middle)
        block_yb = moved(block_b, to_row)
        block_xb = moved(block_b, to_group)
        layers, rows = (far, near_y), (block_yb, block_xb, far)
        near_rest = moved(after(rest, *layers), to_pair)
        block_c = jnp.where(is_end, after(far, *rows), middle_c)
        block_xc = moved(block_c, to_group)
        block_yc = moved(block_c, to_row)
        pieces = [(HERE, 0, sent), (HERE, 1, rest), (THERE, 0, across)]
        pieces += [(THERE, 1, across_x), (HERE + 1, 0, near), (THERE + 1, 0, near_y)]
        totals = product(place, after(mine, block_c), other, pieces, (), 3)
        layers, rows = (near_rest, block_yb, totals[0]), (block_xc, block_yc, near_rest, totals[0])
        end_a = moved(after(across_x, *layers), to_pair)
        ends = [moved(after(block_yb, *rows), to_group), moved(after(block_xc, *rows), to_row)]
        pieces = [(HERE + 2, 0, block_b), (HERE + 2, 1, block_xb), (THERE + 2, 0, block_yb)]
        pieces += [(HERE + 3, 0, block_c), (HERE + 1, 1, near_rest)]
        pieces += [(HERE + 3, 1, block_xc), (THERE + 3, 0, block_yc)]
        totals = product(place, after(mine, *rows), other, pieces, totals, 7)
        came = (end_a, *ends, *totals)
        pieces = [(THERE + 1, 1, end_a), (THERE + 2, 1, ends[0]), (THERE + 3, 1, ends[1])]
        sums, given = [], []
        width = end_a.shape[1]
        split = width * 3 // 4
        for first, columns in ((0, split), (split, width - split)):
            left = after(mine, *came, *sums)
            total, theirs = product(place, left, other, pieces, totals, 3, first, columns)
            sums.append(total)
            given.append(moved(theirs, to_core))
        outgoing = outgoing_rows(place, lengths, owner, sums, given, tables)
        incoming = lax.all_to_all(outgoing, "seq", split_axis=0, concat_axis=1, tiled=True)
        attended = decoded(
            place, lengths, owner, incoming[0], dec_query, dec_key, dec_value, tables
        )
        return (copied(incoming[0])[None], attended)
    else:
        cosine, sine_part = rope_table(positions, HEAD_SIZE)
        shape = (count_requests, count_rows, KEY_VALUE_HEADS, HEAD_SIZE)
        unrotated_key = project(key_weight).reshape(shape)
        key_rows = rotate(
            unrotated_key, cosine[:, None, :], sine_part[:, None, :]
        ).astype(jnp.bfloat16)
        cache_keys = handed_over(key_rows)
        cache_values = handed_over(project(value_weight).astype(jnp.bfloat16).reshape(shape))
    slot_count = cache_keys.shape[0]
    decode_peer = device_id // split_point
    block = device_id % split_point
    source_pair = jnp.sum(jnp.where(owner == decode_peer, pair_ids, 0))
    source_request = source_pair // KEY_VALUE_HEADS
    length = jnp.sum(
        jnp.where(jnp.arange(count_requests, dtype=jnp.int32) == source_request, lengths, 0)
    )
    query = lax.dynamic_index_in_dim(dec_query, decode_peer, 0, keepdims=False)
    new_key = lax.dynamic_index_in_dim(dec_key, decode_peer, 0, keepdims=False)
    new_value = lax.dynamic_index_in_dim(dec_value, decode_peer, 0, keepdims=False)
    step_pos = length + jnp.arange(STEPS, dtype=jnp.int32)
    step_cos, step_sin = rope_table(step_pos, HEAD_SIZE)
    query_rot = rotate(
        query.astype(jnp.float32).reshape(STEPS, QPK, HEAD_SIZE),
        step_cos[:, None, :],
        step_sin[:, None, :],
    ).astype(jnp.bfloat16)
    new_keys = rotate(new_key.astype(jnp.float32), step_cos, step_sin).astype(jnp.bfloat16)
    score_scale = 1.0 / HEAD_SIZE**0.5
    old_scores = (
        jnp.einsum(
            "sjd,id->sji", query_rot, cache_keys, preferred_element_type=jnp.float32
        )
        * score_scale
    )
    new_scores = (
        jnp.einsum("sjd,td->sjt", query_rot, new_keys, preferred_element_type=jnp.float32)
        * score_scale
    )
    slot_ids = jnp.arange(slot_count, dtype=jnp.int32) * split_point + block
    old_live = slot_ids < length
    new_live = (jnp.arange(STEPS)[None, :] <= jnp.arange(STEPS)[:, None]) & (block == 0)
    old_scores = jnp.where(old_live[None, None, :], old_scores, -1e30)
    new_scores = jnp.where(new_live[:, None, :], new_scores, -1e30)
    row_max = jnp.maximum(jnp.max(old_scores, -1), jnp.max(new_scores, -1))
    for bit in range(tree_levels):
        row_max = jnp.maximum(row_max, swapped(row_max, "seq", bit))
    old_exp = jnp.exp(old_scores - row_max[..., None])
    new_exp = jnp.exp(new_scores - row_max[..., None])
    denom = jnp.sum(old_exp, -1) + jnp.sum(new_exp, -1)
    for bit in range(tree_levels):
        denom = denom + swapped(denom, "seq", bit)
    old_probs = (old_exp / denom[..., None]).astype(jnp.bfloat16)
    new_probs = (new_exp / denom[..., None]).astype(jnp.bfloat16)
    partial_sum = jnp.einsum(
        "sji,id->sjd", old_probs, cache_values, preferred_element_type=jnp.float32
    )
    partial_sum = partial_sum + jnp.einsum(
        "sjt,td->sjd", new_probs, new_value, preferred_element_type=jnp.float32
    )
    flat_rows = partial_sum.reshape(STEPS, QPK * HEAD_SIZE)
    for bit in range(tree_levels):
        flat_rows = flat_rows + swapped(flat_rows, "seq", bit)
    share = flat_rows.shape[1] // split_point
    mine = lax.dynamic_slice_in_dim(flat_rows, block * share, share, 1)
    cache = jnp.concatenate([cache_keys, cache_values], 1)[None]
    return (cache, mine.astype(jnp.bfloat16))


def solution(mesh):
    placed = (
        P("groups", "seq", None),
        P("seq", None),
        P("seq", None),
        P("groups"),
        P("groups"),
        P("groups", None, None),
        P("groups", None, None),
        P("groups", None, None),
    )
    return jax.shard_map(
        body,
        mesh=mesh,
        in_specs=placed,
        out_specs=(P(("groups", "seq"), None, None), P("groups", "seq")),
        check_vma=False,
    )
```
